32 devices in a mesh: dp: 4 (over z), ctx: 2 (over x), shard: 4 (over y, core).
Axes of the slice: x: 2, y: 2, z: 4, core: 2. Of those that a mesh axis runs over, the one named last changes fastest.
Arguments:
- tokens: bfloat16 [8192, 1024], P(('dp', 'ctx', 'shard')), may hold values from -6 to 6
- cotangent: bfloat16 [8192, 1024], P(('dp', 'ctx', 'shard')), may hold values from -6 to 6
- picture_starts: int32 [4, 7], P('dp'), may hold values from 0 to 1792, as said below
- matrices: bfloat16 [1024, 12288], replicated
- vectors: bfloat16 [12, 1024], replicated
- master_matrices: float32 [1024, 12288], P(('dp', 'ctx', 'shard')), may hold values from -0.1875 to 0.1875
- master_vectors: float32 [12, 1024], P(None, ('dp', 'ctx', 'shard')), may hold values from -4 to 4
- first_matrices: float32 [1024, 12288], P(('dp', 'ctx', 'shard')), may hold values from -4 to 4
- first_vectors: float32 [12, 1024], P(None, ('dp', 'ctx', 'shard')), may hold values from -4 to 4
- second_matrices: float32 [1024, 12288], P(('dp', 'ctx', 'shard')), may hold values from 0.01 to 1
- second_vectors: float32 [12, 1024], P(None, ('dp', 'ctx', 'shard')), may hold values from 0.01 to 1
Outputs:
- layer_output: bfloat16 [8192, 1024], P(('dp', 'ctx', 'shard'))
- token_grads: float32 [8192, 1024], P(('dp', 'ctx', 'shard'))
- momentum_matrices: float32 [1024, 12288], P(('dp', 'ctx', 'shard'))
- momentum_vectors: float32 [12, 1024], P(None, ('dp', 'ctx', 'shard'))
- variance_matrices: float32 [1024, 12288], P(('dp', 'ctx', 'shard'))
- variance_vectors: float32 [12, 1024], P(None, ('dp', 'ctx', 'shard'))
- updated_matrices: float32 [1024, 12288], P(('dp', 'ctx', 'shard'))
- updated_vectors: float32 [12, 1024], P(None, ('dp', 'ctx', 'shard'))
- copied_matrices: bfloat16 [1024, 12288], P(('dp', 'ctx'))
- copied_vectors: bfloat16 [12, 1024], P(None, ('dp', 'ctx'))
The draws below stay inside these ranges and needn't reach their ends.
Inputs may be any that keep to these rules, and one draw needn't show every extreme that they name: `picture_starts`: each sequence holds 7 picture blocks of 256 tokens given by their first positions in increasing order; blocks do not intersect and lie inside the sequence.
All inputs are finite; a program needn't handle non-finite values.
Results may differ from the reference program's by a relative error of at most 0.0095.
Values may be sent and summed in bfloat16 or wider, within the bound.
No kernel may reach another device: no remote copies, remote signals or barrier semaphores. Data moves between devices by JAX's collectives and lax.ppermute only.
A program may use at most 320 MiB of HBM per device.

```python
import math
import jax
import jax.numpy as jnp
from jax import lax

D = 1024
HEADS = 16
FF = 4096
PIC = 256
STEP = 2
SEQ = 2048
SEQS = 4
TOKENS = 8192
NPIC = 7
VROWS = 12


def draw_matrices(key, part):
    key = jax.random.fold_in(key, 11)
    values = jax.random.normal(key, (D, 4 * D + 2 * FF), jnp.float32)
    column = jnp.arange(4 * D + 2 * FF)
    scale = jnp.where(column < 3 * D, D ** (-0.5), jnp.where(column < 4 * D, 4.0 * D ** (-0.5), jnp.where(column < 4 * D + FF, D ** (-0.5), 1.5 * FF ** (-0.5))))
    return (values * scale[None, :]).astype(jnp.bfloat16)


def draw_vectors(key, part):
    key = jax.random.fold_in(key, 12)
    values = jax.random.normal(key, (8 + FF // D, D), jnp.float32)
    row = jnp.arange(8 + FF // D)[:, None]
    gains = (row == 0) | (row == 5)
    return jnp.where(gains, 1.0 + 0.15 * values, 0.3 * values).astype(jnp.bfloat16)


def draw_picture_starts(key, part):
    key = jax.random.fold_in(key, 13)
    text_count = SEQ - NPIC * PIC
    gaps = jnp.sort(jax.random.randint(key, (SEQS, NPIC), 0, text_count + 1), axis=1)
    return (gaps + jnp.arange(NPIC, dtype=jnp.int32)[None, :] * PIC).astype(jnp.int32)


def block_levels(stream_key, extent, cuts, least, largest):
    factor_of, own = 1.0, jax.random.fold_in(stream_key, 6)
    for dim, shards_of in cuts:
        steps = jnp.exp(jax.random.uniform(jax.random.fold_in(own, dim), (shards_of,), jnp.float32, least / len(cuts), largest / len(cuts)))
        factor_of = factor_of * jnp.repeat(steps, extent[dim] // shards_of).reshape([-1 if axis == dim else 1 for axis in range(len(extent))])
    return factor_of


def normal_values(rng, shape, deviation, bound, split=(), kind=jnp.bfloat16):
    gain = block_levels(rng, shape, split, -0.22, 0.18) if split else 1.0
    array = jax.random.normal(rng, shape, jnp.float32) * deviation * gain
    return jnp.minimum(jnp.maximum(array, -bound), bound).astype(kind)


def setup_inputs(seed: int = 0) -> dict:
    seeds = jax.random.split(jax.random.key(seed), 12)
    tokens = normal_values(seeds[0], (TOKENS, D), 1.0, 6.0, ((0, 32),))
    cotangent = normal_values(seeds[1], (TOKENS, D), 1.0, 6.0, ((0, 32),))
    picture_starts = draw_picture_starts(jax.random.fold_in(seeds[11], 71), 0)
    matrices = draw_matrices(jax.random.fold_in(seeds[11], 71), 0)
    vectors = draw_vectors(jax.random.fold_in(seeds[11], 71), 0)
    master_matrices = normal_values(seeds[5], (D, 4 * D + 2 * FF), D ** -0.5, 0.1875, ((0, 32),), jnp.float32)
    master_vectors = normal_values(seeds[6], (VROWS, D), 0.3, 4.0, ((1, 32),), jnp.float32)
    first_matrices = normal_values(seeds[7], (D, 4 * D + 2 * FF), 0.3, 4.0, ((0, 32),), jnp.float32)
    first_vectors = normal_values(seeds[8], (VROWS, D), 0.3, 4.0, ((1, 32),), jnp.float32)
    second_matrices = jnp.clip(jnp.exp(math.log(1.0) - 4.6051702 * jax.random.uniform(seeds[9], (D, 4 * D + 2 * FF), jnp.float32) ** block_levels(seeds[9], (D, 4 * D + 2 * FF), ((0, 32),), -0.2, 0.2)), 0.01, 1.0)
    second_vectors = jnp.clip(jnp.exp(math.log(1.0) - 4.6051702 * jax.random.uniform(seeds[10], (VROWS, D), jnp.float32) ** block_levels(seeds[10], (VROWS, D), ((1, 32),), -0.2, 0.2)), 0.01, 1.0)
    return dict(tokens=tokens, cotangent=cotangent, picture_starts=picture_starts, matrices=matrices, vectors=vectors, master_matrices=master_matrices, master_vectors=master_vectors, first_matrices=first_matrices, first_vectors=first_vectors, second_matrices=second_matrices, second_vectors=second_vectors)


EPSILON = 1e-05
NEGATIVE = -1e+30
BETA = 0.5
RATE = 0.03
DECAY_RATE = 0.1
ADAM_EPSILON = 1e-08

@jax.custom_vjp
def low(v):
    return lax.optimization_barrier(v.astype(jnp.bfloat16)).astype(jnp.float32)

@jax.custom_vjp
def low_back(v):
    return v

def low_keep(v):
    return (low(v), None)

def low_pass(kept, grad):
    return (grad,)

def back_keep(v):
    return (v, None)

def back_low(kept, grad):
    return (low(grad),)
low.defvjp(low_keep, low_pass)
low_back.defvjp(back_keep, back_low)

def token_tags(index, start_list, block_len):
    after = index[:, None] - start_list[None, :]
    inside = (after >= 0) & (after < block_len)
    offsets = lax.optimization_barrier(jnp.sum(jnp.clip(after, 0, block_len - 1), axis=1))
    number = jnp.arange(1, start_list.shape[0] + 1, dtype=jnp.int32)
    picture = lax.optimization_barrier(jnp.sum(jnp.where(inside, number[None, :], 0), axis=1)) - 1
    return ((index - offsets).astype(jnp.int32), picture.astype(jnp.int32))

def layer_norm(inputs):
    centered = inputs - lax.optimization_barrier(jnp.mean(inputs, axis=1, keepdims=True))
    inverse_std = lax.rsqrt(lax.optimization_barrier(jnp.mean(centered * centered, axis=1, keepdims=True)) + EPSILON)
    return centered * inverse_std

def activate(value):
    return jax.nn.gelu(value, approximate=True)

def layer(inputs, start_list, weights, vecs):
    head_width = D // HEADS
    factor = head_width ** (-0.5)
    normed = layer_norm(inputs)
    hidden = low(normed * vecs[0] + vecs[1])
    projected = jnp.dot(hidden, weights[:, :3 * D], precision=lax.Precision.HIGHEST)
    queries = low(low_back(projected[:, :D] + vecs[2]))
    keys = low(low_back(projected[:, D:2 * D]))
    values = low(low_back(projected[:, 2 * D:] + vecs[3]))
    index = jnp.arange(SEQ, dtype=jnp.int32)
    position, picture = token_tags(index, start_list, PIC)
    slopes = jnp.exp2(-8.0 * (jnp.arange(HEADS, dtype=jnp.float32) + 1.0) / HEADS)
    key_heads = keys.reshape(SEQ, HEADS, head_width)
    value_heads = values.reshape(SEQ, HEADS, head_width)
    block_rows = math.gcd(SEQ, 512)
    block_count = SEQ // block_rows

    def one_block(pieces):
        query_block, query_pos, query_pic, query_idx = pieces
        raw = jnp.einsum('qhd,khd->hqk', query_block, key_heads, precision=lax.Precision.HIGHEST)
        distance = (query_pos[:, None] - position[None, :]).astype(jnp.float32)
        logits = low_back(raw * factor - slopes[:, None, None] * distance[None, :, :])
        same = (query_pic[:, None] == picture[None, :]) & (query_pic[:, None] >= 0)
        visible = (index[None, :] <= query_idx[:, None]) | same
        probs = low(jax.nn.softmax(jnp.where(visible[None, :, :], logits, NEGATIVE), axis=-1))
        mixed = jnp.einsum('hqk,khd->qhd', probs, value_heads, precision=lax.Precision.HIGHEST)
        return mixed.reshape(block_rows, D)
    attended = lax.map(jax.checkpoint(one_block), (queries.reshape(block_count, block_rows, HEADS, head_width), position.reshape(block_count, block_rows), picture.reshape(block_count, block_rows), index.reshape(block_count, block_rows)))
    attended = low(low_back(attended.reshape(SEQ, D)))
    branch = low_back(jnp.dot(attended, weights[:, 3 * D:4 * D], precision=lax.Precision.HIGHEST))
    middle = inputs + branch + vecs[4]
    normed_two = layer_norm(middle)
    hidden_two = low(normed_two * vecs[5] + vecs[6])
    up_bias = vecs[8:].reshape(FF)
    pre = low_back(jnp.dot(hidden_two, weights[:, 4 * D:4 * D + FF], precision=lax.Precision.HIGHEST) + up_bias)
    act = low(activate(pre))
    down = jnp.dot(act, weights[:, 4 * D + FF:].T, precision=lax.Precision.HIGHEST)
    return middle + down + vecs[7]

def adam_update(master, first, second, gradient, correction, decay_rate):
    moment = BETA * first + (1.0 - BETA) * gradient
    variance = BETA * second + (1.0 - BETA) * gradient * gradient
    direction = moment / correction / (jnp.sqrt(variance / correction) + ADAM_EPSILON)
    return (moment, variance, master - RATE * (direction + decay_rate * master))

def reference(tokens, cotangent, picture_starts, matrices, vectors, master_matrices, master_vectors, first_matrices, first_vectors, second_matrices, second_vectors):

    def forward(inputs, weights, vecs):
        stacked = inputs.reshape(SEQS, SEQ, D)
        results = lax.map(lambda pair: layer(pair[0], pair[1], weights, vecs), (stacked, picture_starts))
        return results.reshape(TOKENS, D)
    outputs, pullback = jax.vjp(forward, tokens.astype(jnp.float32), matrices.astype(jnp.float32), vectors.astype(jnp.float32))
    token_grads, grad_weights, grad_vecs = pullback(cotangent.astype(jnp.float32))
    root = TOKENS ** (-0.5)
    correction = 1.0 - BETA ** STEP
    moment_w, variance_w, updated_w = adam_update(master_matrices, first_matrices, second_matrices, grad_weights * root, correction, DECAY_RATE)
    moment_v, variance_v, updated_v = adam_update(master_vectors, first_vectors, second_vectors, grad_vecs * root, correction, 0.0)
    return (outputs.astype(jnp.bfloat16), token_grads, moment_w, moment_v, variance_w, variance_v, updated_w, updated_v, updated_w.astype(jnp.bfloat16), updated_v.astype(jnp.bfloat16))
```

```python
import functools
import math

import jax
import jax.numpy as jnp
from jax import lax
from jax.experimental import pallas as pl
from jax.experimental.pallas import tpu as pltpu
from jax.sharding import PartitionSpec as P

HEADS = 16
PIC = 256
STEP = 2


EPSILON = 1e-05
NEGATIVE = -1e30
BETA = 0.5
RATE = 0.03
DECAY_RATE = 0.1
ADAM_EPSILON = 1e-08


def token_tags(index, start_list, block_len):
    after = index[:, None] - start_list[None, :]
    inside = (after >= 0) & (after < block_len)
    offsets = jnp.sum(jnp.clip(after, 0, block_len - 1), axis=1)
    number = jnp.arange(1, start_list.shape[0] + 1, dtype=jnp.int32)
    picture = jnp.sum(jnp.where(inside, number[None, :], 0), axis=1) - 1
    return (index - offsets, picture)


def block_scores(query_heads, query_index, key_heads, key_index, start_list, slopes, factor):
    query_pos, query_pic = token_tags(query_index, start_list, PIC)
    key_pos, key_pic = token_tags(key_index, start_list, PIC)
    raw = jnp.einsum("qhd,khd->hqk", query_heads, key_heads, preferred_element_type=jnp.float32)
    distance = (query_pos[:, None] - key_pos[None, :]).astype(jnp.float32)
    logits = raw * factor - slopes[:, None, None] * distance[None, :, :]
    same = (query_pic[:, None] == key_pic[None, :]) & (query_pic[:, None] >= 0)
    visible = (key_index[None, :] <= query_index[:, None]) | same
    return (logits, visible[None, :, :])


def layer_norm(inputs):
    centered = inputs - jnp.mean(inputs, axis=1, keepdims=True)
    inverse_std = lax.rsqrt(jnp.mean(centered * centered, axis=1, keepdims=True) + EPSILON)
    return (centered * inverse_std, inverse_std)


def norm_backward(grad_normed, gain, normed, inverse_std):
    scaled = grad_normed * gain
    return inverse_std * (
        scaled
        - jnp.mean(scaled, axis=1, keepdims=True)
        - normed * jnp.mean(scaled * normed, axis=1, keepdims=True)
    )


def activate(value):
    return jax.nn.gelu(value, approximate=True)


def regroup(array, dim, outer, inner):
    shape = array.shape
    split = array.reshape(
        shape[:dim] + (outer, inner, shape[dim] // (outer * inner)) + shape[dim + 1 :]
    )
    return jnp.swapaxes(split, dim, dim + 1).reshape(shape)


def adam_update(master, first, second, gradient, correction, decay_rate):
    moment = BETA * first + (1.0 - BETA) * gradient
    variance = BETA * second + (1.0 - BETA) * gradient * gradient
    direction = moment / correction / (jnp.sqrt(variance / correction) + ADAM_EPSILON)
    return (moment, variance, master - RATE * (direction + decay_rate * master))


def general_shards(
    tokens,
    cotangent,
    picture_starts,
    matrices,
    vectors,
    master_matrices,
    master_vectors,
    first_matrices,
    first_vectors,
    second_matrices,
    second_vectors,
):
    row_count, model_width = tokens.shape
    ff_width = (matrices.shape[1] - 4 * model_width) // 2
    head_count = HEADS
    head_width = model_width // head_count
    factor = head_width ** (-0.5)
    group_size = lax.axis_size("ctx") * lax.axis_size("shard")
    group_rank = lax.axis_index("ctx") * lax.axis_size("shard") + lax.axis_index("shard")
    seq_length = row_count * group_size
    first_row = group_rank * row_count
    start_list = picture_starts[0]
    slopes = jnp.exp2(-8.0 * (jnp.arange(head_count, dtype=jnp.float32) + 1.0) / head_count)
    block_rows = math.gcd(seq_length, 512)
    block_count = seq_length // block_rows
    w_qkv = matrices[:, : 3 * model_width]
    w_proj = matrices[:, 3 * model_width : 4 * model_width]
    w_up = matrices[:, 4 * model_width : 4 * model_width + ff_width]
    w_down = matrices[:, 4 * model_width + ff_width :]
    inputs = tokens.astype(jnp.float32)
    vector_rows = vectors.astype(jnp.float32)
    up_bias = vector_rows[8:].reshape(ff_width)
    normed, inverse_std = layer_norm(inputs)
    hidden = (normed * vector_rows[0] + vector_rows[1]).astype(jnp.bfloat16)
    projected = jnp.dot(hidden, w_qkv, preferred_element_type=jnp.float32)
    queries = (projected[:, :model_width] + vector_rows[2]).astype(jnp.bfloat16)
    kv_bias = jnp.concatenate([jnp.zeros((model_width,), jnp.float32), vector_rows[3]])
    kv_local = (projected[:, model_width:] + kv_bias).astype(jnp.bfloat16)
    gathered = lax.all_gather(kv_local, ("ctx", "shard"), axis=0, tiled=True)
    query_index = first_row + jnp.arange(row_count, dtype=jnp.int32)
    query_heads = queries.reshape(row_count, head_count, head_width)

    def key_block(index):
        piece = lax.dynamic_slice_in_dim(gathered, index * block_rows, block_rows, 0)
        key_heads = piece[:, :model_width].reshape(block_rows, head_count, head_width)
        value_heads = piece[:, model_width:].reshape(block_rows, head_count, head_width)
        key_index = index * block_rows + jnp.arange(block_rows, dtype=jnp.int32)
        logits, visible = block_scores(
            query_heads, query_index, key_heads, key_index, start_list, slopes, factor
        )
        return (logits, visible, key_heads, value_heads)

    def running_total(index, carry):
        highest, total = carry
        logits, visible, key_heads, value_heads = key_block(index)
        masked = jnp.where(visible, logits, NEGATIVE)
        updated = jnp.maximum(highest, jnp.max(masked, axis=2))
        weights = jnp.where(visible, jnp.exp(logits - updated[:, :, None]), 0.0)
        return (updated, total * jnp.exp(highest - updated) + jnp.sum(weights, axis=2))

    start_high = jnp.full((head_count, row_count), NEGATIVE, jnp.float32)
    start_total = jnp.zeros((head_count, row_count), jnp.float32)
    highest, total = lax.fori_loop(0, block_count, running_total, (start_high, start_total))
    log_total = highest + jnp.log(total)

    def weighted_sum(index, accum):
        logits, visible, key_heads, value_heads = key_block(index)
        probs = jnp.where(visible, jnp.exp(logits - log_total[:, :, None]), 0.0).astype(
            jnp.bfloat16
        )
        return accum + jnp.einsum(
            "hqk,khd->qhd", probs, value_heads, preferred_element_type=jnp.float32
        )

    attended = lax.fori_loop(
        0, block_count, weighted_sum, jnp.zeros((row_count, head_count, head_width), jnp.float32)
    )
    attended_low = attended.reshape(row_count, model_width).astype(jnp.bfloat16)
    middle = (
        inputs + jnp.dot(attended_low, w_proj, preferred_element_type=jnp.float32) + vector_rows[4]
    )
    normed_two, inverse_two = layer_norm(middle)
    hidden_two = (normed_two * vector_rows[5] + vector_rows[6]).astype(jnp.bfloat16)
    pre_act = jnp.dot(hidden_two, w_up, preferred_element_type=jnp.float32) + up_bias
    act_low = activate(pre_act).astype(jnp.bfloat16)
    down_out = lax.dot_general(
        act_low, w_down, (((1,), (1,)), ((), ())), preferred_element_type=jnp.float32
    )
    layer_output = (middle + down_out + vector_rows[7]).astype(jnp.bfloat16)
    upstream = cotangent.astype(jnp.float32)
    grad_act = jnp.dot(cotangent, w_down, preferred_element_type=jnp.float32)
    gelu_value, gelu_pull = jax.vjp(activate, pre_act)
    grad_pre = gelu_pull(grad_act)[0].astype(jnp.bfloat16)
    grad_up_w = lax.dot_general(
        hidden_two, grad_pre, (((0,), (0,)), ((), ())), preferred_element_type=jnp.float32
    )
    grad_down_w = lax.dot_general(
        cotangent, act_low, (((0,), (0,)), ((), ())), preferred_element_type=jnp.float32
    )
    grad_two = lax.dot_general(
        grad_pre, w_up, (((1,), (1,)), ((), ())), preferred_element_type=jnp.float32
    )
    grad_mid = upstream + norm_backward(grad_two, vector_rows[5], normed_two, inverse_two)
    grad_mid_low = grad_mid.astype(jnp.bfloat16)
    grad_proj = lax.dot_general(
        attended_low, grad_mid_low, (((0,), (0,)), ((), ())), preferred_element_type=jnp.float32
    )
    grad_out = lax.dot_general(
        grad_mid_low, w_proj, (((1,), (1,)), ((), ())), preferred_element_type=jnp.float32
    ).astype(jnp.bfloat16)
    grad_heads = grad_out.reshape(row_count, head_count, head_width)
    delta = jnp.sum(grad_heads.astype(jnp.float32) * attended, axis=2).T

    def score_grads(index):
        logits, visible, key_heads, value_heads = key_block(index)
        probs = jnp.where(visible, jnp.exp(logits - log_total[:, :, None]), 0.0)
        product = jnp.einsum(
            "qhd,khd->hqk", grad_heads, value_heads, preferred_element_type=jnp.float32
        )
        grad_logits = (probs * (product - delta[:, :, None])).astype(jnp.bfloat16)
        return (probs, grad_logits, key_heads)

    def both_grads(index, carry):
        accum, key_terms = carry
        probs, grad_logits, key_heads = score_grads(index)
        accum = (
            accum
            + jnp.einsum("hqk,khd->qhd", grad_logits, key_heads, preferred_element_type=jnp.float32)
            * factor
        )
        grad_key = (
            jnp.einsum("hqk,qhd->khd", grad_logits, query_heads, preferred_element_type=jnp.float32)
            * factor
        )
        grad_value = jnp.einsum(
            "hqk,qhd->khd",
            probs.astype(jnp.bfloat16),
            grad_heads,
            preferred_element_type=jnp.float32,
        )
        term = jnp.concatenate(
            [
                grad_key.reshape(block_rows, model_width),
                grad_value.reshape(block_rows, model_width),
            ],
            axis=1,
        )
        return (accum, lax.dynamic_update_slice_in_dim(key_terms, term, index * block_rows, 0))

    grad_query, key_terms = lax.fori_loop(
        0,
        block_count,
        both_grads,
        (
            jnp.zeros((row_count, head_count, head_width), jnp.float32),
            jnp.zeros((seq_length, 2 * model_width), jnp.float32),
        ),
    )
    own_key_grads = lax.psum_scatter(key_terms, ("ctx", "shard"), scatter_dimension=0, tiled=True)
    grad_qkv = jnp.concatenate(
        [grad_query.reshape(row_count, model_width), own_key_grads], axis=1
    ).astype(jnp.bfloat16)
    grad_qkv_weights = lax.dot_general(
        hidden, grad_qkv, (((0,), (0,)), ((), ())), preferred_element_type=jnp.float32
    )
    grad_hidden = lax.dot_general(
        grad_qkv, w_qkv, (((1,), (1,)), ((), ())), preferred_element_type=jnp.float32
    )
    query_bias_grad = jnp.sum(grad_qkv[:, :model_width].astype(jnp.float32), axis=0)
    value_bias_grad = jnp.sum(grad_qkv[:, 2 * model_width :].astype(jnp.float32), axis=0)
    grad_vectors = jnp.concatenate(
        [
            jnp.stack(
                [
                    jnp.sum(grad_hidden * normed, axis=0),
                    jnp.sum(grad_hidden, axis=0),
                    query_bias_grad,
                    value_bias_grad,
                    jnp.sum(grad_mid, axis=0),
                    jnp.sum(grad_two * normed_two, axis=0),
                    jnp.sum(grad_two, axis=0),
                    jnp.sum(upstream, axis=0),
                ]
            ),
            jnp.sum(grad_pre.astype(jnp.float32), axis=0).reshape(
                ff_width // model_width, model_width
            ),
        ],
        axis=0,
    )
    token_grads = grad_mid + norm_backward(grad_hidden, vector_rows[0], normed, inverse_std)
    grad_matrix = jnp.concatenate([grad_qkv_weights, grad_proj, grad_up_w, grad_down_w], axis=1)
    shard_count = lax.axis_size("shard")
    replicas = lax.axis_size("dp") * lax.axis_size("ctx")
    part_matrix, part_vec = (
        lax.psum_scatter(
            regroup(grad_matrix, 0, replicas, shard_count), "shard", scatter_dimension=0, tiled=True
        ),
        lax.psum_scatter(
            regroup(grad_vectors, 1, replicas, shard_count),
            "shard",
            scatter_dimension=1,
            tiled=True,
        ),
    )
    part_matrix, part_vec = (
        lax.psum_scatter(part_matrix, ("dp", "ctx"), scatter_dimension=0, tiled=True),
        lax.psum_scatter(part_vec, ("dp", "ctx"), scatter_dimension=1, tiled=True),
    )
    root = (row_count * lax.axis_size("dp") * group_size) ** (-0.5)
    correction = 1.0 - BETA**STEP
    moment_w, variance_w, updated_w = adam_update(
        master_matrices, first_matrices, second_matrices, part_matrix * root, correction, DECAY_RATE
    )
    moment_v, variance_v, updated_v = adam_update(
        master_vectors, first_vectors, second_vectors, part_vec * root, correction, 0.0
    )
    copied_w, copied_v = (
        lax.all_gather(updated_w.astype(jnp.bfloat16), "shard", axis=0, tiled=True),
        lax.all_gather(updated_v.astype(jnp.bfloat16), "shard", axis=1, tiled=True),
    )
    return (
        layer_output,
        token_grads,
        moment_w,
        moment_v,
        variance_w,
        variance_v,
        updated_w,
        updated_v,
        copied_w,
        copied_v,
    )


BLK=256
f32 = jnp.float32
bf16 = jnp.bfloat16
NT=(((1,),(1,)),((),()))

def split3(x):
    hi=x.astype(bf16).astype(f32)
    rest=x-hi
    mid=rest.astype(bf16).astype(f32)
    low=(rest-mid).astype(bf16).astype(f32)
    return hi,mid,low

def positions(index, starts_ref, count):
    pos=index
    for b in range(count):
        pos=pos-jnp.clip(index-starts_ref[0,b],0,PIC-1)
    return pos.astype(f32)

def limits(index, starts_ref, count):
    lim=index+1
    for b in range(count):
        s=starts_ref[0,b]
        lim=jnp.where((index>=s)&(index<s+PIC), s+PIC, lim)
    return lim

def head_lanes(shape,h,width):
    lane=lax.broadcasted_iota(jnp.int32,shape,1)
    inside=(lane<width) if h==0 else (lane>=width)
    extra=lane-width if h==0 else lane
    return inside,extra

def pick(extra,values,rest=0.0):
    out=jnp.full(extra.shape,rest,f32)
    for e,v in enumerate(values):
        out=jnp.where(extra==e,v,out)
    return out

def fwd_kernel(width, tile, count, rank_ref, starts_ref, slopes_ref, qkv_ref, att_ref, o_ref, lse_ref,
               qa, ka, va, m_ref, acc_ref):
    seq,lanes=att_ref.shape
    rank=rank_ref[0]
    factor=width**-0.5
    def prologue(t,_):
        src=pl.ds(pl.multiple_of((t^rank)*BLK,BLK),BLK)
        dst=pl.ds(pl.multiple_of(t*BLK,BLK),BLK)
        q=qkv_ref[src,0:lanes].astype(f32)*factor
        k=qkv_ref[src,lanes:2*lanes].astype(f32)
        v=qkv_ref[src,2*lanes:3*lanes].astype(f32)
        index=lax.broadcasted_iota(jnp.int32,(BLK,lanes),0)+t*BLK
        pos=positions(index,starts_ref,count)
        for h in range(2):
            inside,extra=head_lanes((BLK,lanes),h,width)
            hi,mid,low=split3(pos*slopes_ref[h])
            qa[h,dst,:]=jnp.where(inside,q,pick(extra,(1.0,1.0,1.0))).astype(bf16)
            ka[h,dst,:]=jnp.where(inside,k,pick(extra,(hi,mid,low))).astype(bf16)
            va[h,dst,:]=jnp.where(inside,v,pick(extra,(1.0,))).astype(bf16)
        return 0
    lax.fori_loop(0,seq//BLK,prologue,0)

    def update(h,rows,q,key_rows,mask_fn,local):
        k=ka[h,key_rows,:]
        v=va[h,key_rows,:]
        s=lax.dot_general(q,k,NT,preferred_element_type=f32)
        if mask_fn is not None:
            s=jnp.where(mask_fn(s.shape),s,NEGATIVE)
        old=m_ref[h,local,:]
        best=jnp.max(s,axis=1,keepdims=True)
        new=jnp.maximum(old,jnp.broadcast_to(best,old.shape))
        m_ref[h,local,:]=new
        p=jnp.exp(s-new[:,0:1]).astype(bf16)
        pv=jnp.dot(p,v,preferred_element_type=f32)
        acc_ref[h,local,:]=acc_ref[h,local,:]*jnp.exp(old-new)+pv

    for i in range(seq//tile):
        base=i*tile
        m_ref[...]=jnp.full(m_ref.shape,NEGATIVE,f32)
        acc_ref[...]=jnp.zeros(acc_ref.shape,f32)
        def full(j,_):
            for h in range(2):
                update(h,None,qa[h,base:base+tile,:],pl.ds(pl.multiple_of(j*tile,tile),tile),None,slice(0,tile))
            return 0
        if i>0:
            lax.fori_loop(0,i,full,0)
        def mask(first_row,first_col,shape):
            rows=lax.broadcasted_iota(jnp.int32,(shape[0],1),0)+first_row
            lim=limits(rows,starts_ref,count)
            cols=lax.broadcasted_iota(jnp.int32,shape,1)+first_col
            return cols<lim
        for h in range(2):
            update(h,None,qa[h,base:base+tile,:],slice(base,base+tile),functools.partial(mask,base,base),slice(0,tile))
        if base+tile<seq:
            for h in range(2):
                update(h,None,qa[h,base+tile-PIC:base+tile,:],slice(base+tile,base+tile+PIC),functools.partial(mask,base+tile-PIC,base+tile),slice(tile-PIC,tile))
        res=[];lses=[]
        for h in range(2):
            acc=acc_ref[h]
            col=width if h==0 else 0
            total=acc[:,col:col+1]
            res.append(acc/total)
            lses.append(m_ref[h]+jnp.log(total))
        inside,_=head_lanes((tile,lanes),0,width)
        out=jnp.where(inside,res[0],res[1])
        o_ref[base:base+tile,:]=out
        lse_ref[base:base+tile,:]=jnp.where(inside,lses[0],lses[1])
        att_ref[base:base+tile,:]=out.astype(bf16)

def attention_forward(qkv, rank, starts, slopes, tile=512):
    seq=qkv.shape[0]; lanes=qkv.shape[1]//3; width=lanes//2
    count=starts.shape[1]
    sm=pl.BlockSpec(memory_space=pltpu.SMEM)
    vm=pl.BlockSpec(memory_space=pltpu.VMEM)
    return pl.pallas_call(functools.partial(fwd_kernel,width,tile,count),
        out_shape=(jax.ShapeDtypeStruct((seq,lanes),bf16),jax.ShapeDtypeStruct((seq,lanes),f32),jax.ShapeDtypeStruct((seq,lanes),f32)),
        in_specs=[sm,sm,sm,vm], out_specs=(vm,vm,vm),
        scratch_shapes=[pltpu.VMEM((2,seq,lanes),bf16)]*3+[pltpu.VMEM((2,tile,lanes),f32)]*2,
        compiler_params=pltpu.CompilerParams(vmem_limit_bytes=40*2**20),
        name="attention_forward")(rank,starts,slopes,qkv)

def bwd_kernel(width, tile, count, rank_ref, starts_ref, slopes_ref, qkv_ref, do_ref, o_ref, lse_ref, abs_ref, rel_ref,
               qa, ka, va, da, kt, dq_ref, dk_ref, dv_ref):
    seq,lanes=do_ref.shape
    rank=rank_ref[0]
    factor=width**-0.5
    def prologue(t,_):
        src=pl.ds(pl.multiple_of((t^rank)*BLK,BLK),BLK)
        dst=pl.ds(pl.multiple_of(t*BLK,BLK),BLK)
        q=qkv_ref[src,0:lanes].astype(f32)*factor
        k=qkv_ref[src,lanes:2*lanes].astype(f32)
        v=qkv_ref[src,2*lanes:3*lanes].astype(f32)
        kt[:,dst]=k.T.astype(bf16)
        g=do_ref[dst,:].astype(f32)
        prod=g*o_ref[dst,:]
        index=lax.broadcasted_iota(jnp.int32,(BLK,lanes),0)+t*BLK
        pos=positions(index,starts_ref,count)
        lse=lse_ref[dst,:]
        for h in range(2):
            inside,extra=head_lanes((BLK,lanes),h,width)
            hi,mid,low=split3(pos*slopes_ref[h])
            delta=jnp.sum(jnp.where(inside,prod,0.0),axis=1,keepdims=True)
            delta=jnp.broadcast_to(delta,(BLK,lanes))
            lse_h=jnp.broadcast_to(lse[:,0:1] if h==0 else lse[:,width:width+1],(BLK,lanes))
            lhi,lmid,llow=split3(-lse_h)
            dhi,dmid,dlow=split3(-delta)
            qa[h,dst,:]=jnp.where(inside,q,pick(extra,(1.0,1.0,1.0,lhi,lmid,llow))).astype(bf16)
            ka[h,dst,:]=jnp.where(inside,k,pick(extra,(hi,mid,low,1.0,1.0,1.0))).astype(bf16)
            va[h,dst,:]=jnp.where(inside,v,pick(extra,(1.0,1.0,1.0))).astype(bf16)
            da[h,dst,:]=jnp.where(inside,g,pick(extra,(dhi,dmid,dlow))).astype(bf16)
        return 0
    lax.fori_loop(0,seq//BLK,prologue,0)
    dq_ref[...]=jnp.zeros(dq_ref.shape,f32)

    def pair(h,key_rows,query_rows,mask_fn,dkv_rows):
        st=lax.dot_general(ka[h,key_rows,:],qa[h,query_rows,:],NT,preferred_element_type=f32)
        pt=jnp.exp(st)
        if mask_fn is not None:
            pt=jnp.where(mask_fn(st.shape),pt,0.0)
        dpt=lax.dot_general(va[h,key_rows,:],da[h,query_rows,:],NT,preferred_element_type=f32)
        dst=(pt*dpt).astype(bf16)
        dv_ref[h,dkv_rows,:]+=jnp.dot(pt.astype(bf16),da[h,query_rows,:],preferred_element_type=f32)
        dk_ref[h,dkv_rows,:]+=jnp.dot(dst,qa[h,query_rows,:],preferred_element_type=f32)
        rows=slice(h*width,(h+1)*width)
        dq_ref[rows,query_rows]+=jnp.dot(kt[rows,key_rows],dst,preferred_element_type=f32)

    for j in range(seq//tile):
        base=j*tile
        dk_ref[...]=jnp.zeros(dk_ref.shape,f32)
        dv_ref[...]=jnp.zeros(dv_ref.shape,f32)
        def mask(first_key,first_query,shape):
            cols=lax.broadcasted_iota(jnp.int32,(1,shape[1]),1)+first_query
            lim=limits(cols,starts_ref,count)
            rows=lax.broadcasted_iota(jnp.int32,shape,0)+first_key
            return rows<lim
        if base>0:
            for h in range(2):
                pair(h,slice(base,base+PIC),slice(base-PIC,base),functools.partial(mask,base,base-PIC),slice(0,PIC))
        for h in range(2):
            pair(h,slice(base,base+tile),slice(base,base+tile),functools.partial(mask,base,base),slice(0,tile))
        def full(i,_):
            for h in range(2):
                pair(h,slice(base,base+tile),pl.ds(pl.multiple_of(i*tile,tile),tile),None,slice(0,tile))
            return 0
        if base+tile<seq:
            lax.fori_loop(j+1,seq//tile,full,0)
        inside,_=head_lanes((BLK,lanes),0,width)
        for t in range(tile//BLK):
            part=slice(t*BLK,(t+1)*BLK)
            dst=pl.ds(pl.multiple_of(((j*(tile//BLK)+t)^rank)*BLK,BLK),BLK)
            dk=jnp.where(inside,dk_ref[0,part,:],dk_ref[1,part,:]).astype(bf16)
            dv=jnp.where(inside,dv_ref[0,part,:],dv_ref[1,part,:]).astype(bf16)
            same=slice(base+t*BLK,base+(t+1)*BLK)
            for ref,rows in ((abs_ref,same),(rel_ref,dst)):
                ref[rows,lanes:2*lanes]=dk
                ref[rows,2*lanes:3*lanes]=dv
    for t in range(seq//BLK):
        dst=pl.ds(pl.multiple_of((t^rank)*BLK,BLK),BLK)
        dq=(dq_ref[:,t*BLK:(t+1)*BLK].T*factor).astype(bf16)
        abs_ref[t*BLK:(t+1)*BLK,0:lanes]=dq
        rel_ref[dst,0:lanes]=dq

def attention_backward(qkv, do, o, lse, rank, starts, slopes, tile=512):
    seq=qkv.shape[0]; lanes=qkv.shape[1]//3; width=lanes//2
    count=starts.shape[1]
    sm=pl.BlockSpec(memory_space=pltpu.SMEM)
    vm=pl.BlockSpec(memory_space=pltpu.VMEM)
    return pl.pallas_call(functools.partial(bwd_kernel,width,tile,count),
        out_shape=(jax.ShapeDtypeStruct((seq,3*lanes),bf16),)*2,
        in_specs=[sm,sm,sm,vm,vm,vm,vm], out_specs=(vm,vm),
        scratch_shapes=[pltpu.VMEM((2,seq,lanes),bf16)]*4+[pltpu.VMEM((lanes,seq),bf16),pltpu.VMEM((lanes,seq),f32)]+[pltpu.VMEM((2,tile,lanes),f32)]*2,
        compiler_params=pltpu.CompilerParams(vmem_limit_bytes=40*2**20),
        name="attention_backward")(rank,starts,slopes,qkv,do,o,lse)


def fits_sequence_plan(mesh):
    return mesh.shape["dp"] == 4 and mesh.shape["ctx"] == 2 and mesh.shape["shard"] == 4


def swap(array, axis, bit):
    count = lax.axis_size(axis)
    return lax.ppermute(array, axis, [(i, i ^ bit) for i in range(count)])


def gather_sequence(block):
    over_ctx = swap(block, "ctx", 1)
    over_y = swap(block, "shard", 2)
    over_core = swap(block, "shard", 1)
    core = lax.axis_index("shard") % 2
    relay = jnp.where(core == 0, over_ctx, over_y)
    opposite = lax.ppermute(
        relay, ("ctx", "shard"), [(i, i ^ (2 if i % 2 == 0 else 4)) for i in range(8)]
    )
    ctx_core = swap(over_ctx, "shard", 1)
    y_core = swap(over_y, "shard", 1)
    opposite_core = swap(opposite, "shard", 1)
    return jnp.concatenate(
        [block, over_core, over_y, y_core, over_ctx, ctx_core, opposite, opposite_core], axis=0
    )


def exchange(array):
    return lax.all_to_all(array, ("ctx", "shard"), 0, 0, tiled=True)


def dot_tn(left, right):
    return lax.dot_general(left, right, (((0,), (0,)), ((), ())), preferred_element_type=f32)


def dot_nt(left, right):
    return lax.dot_general(left, right, (((1,), (1,)), ((), ())), preferred_element_type=f32)


def dot_nn(left, right):
    return jnp.dot(left, right, preferred_element_type=f32)


def sum_over_dp(lhs, rhs, extra=None):
    quarter = lhs.shape[1] // 4
    send = dot_tn(lhs[:, : 2 * quarter], rhs).astype(bf16)
    got = lax.ppermute(send, "dp", [(i, i ^ 1) for i in range(4)])
    relay = (dot_tn(lhs[:, 2 * quarter : 3 * quarter], rhs) + got[quarter:].astype(f32)).astype(bf16)
    far = lax.ppermute(relay, "dp", [(i, 3 - i) for i in range(4)])
    return dot_tn(lhs[:, 3 * quarter :], rhs) + got[:quarter].astype(f32) + far.astype(f32)


def sequence_shards(
    tokens,
    cotangent,
    picture_starts,
    matrices,
    vectors,
    master_matrices,
    master_vectors,
    first_matrices,
    first_vectors,
    second_matrices,
    second_vectors,
):
    row_count, width = tokens.shape
    ff_width = (matrices.shape[1] - 4 * width) // 2
    head_width = width // HEADS
    group = 8
    rank = lax.axis_index("ctx") * 4 + lax.axis_index("shard")
    depth = lax.axis_index("dp")
    lanes = width // group
    units = ff_width // group
    heads_here = HEADS // group
    head = rank * heads_here + jnp.arange(heads_here)
    slopes = jnp.exp2(-8.0 * (head.astype(f32) + 1.0) / HEADS)
    rank_array = rank.astype(jnp.int32).reshape(1)
    quarter = width // 4
    near = depth ^ 1
    order = [near, 3 - near, 3 - depth, depth]

    def reorder(array, dim):
        return jnp.concatenate(
            [lax.dynamic_slice_in_dim(array, block * quarter, quarter, dim) for block in order],
            axis=dim,
        )

    def own(first, size):
        return reorder(lax.dynamic_slice_in_dim(matrices, first + rank * size, size, 1), 0)

    w_qkv = matrices[:, : 3 * width]
    w_proj = matrices[:, 3 * width : 4 * width]
    w_up = matrices[:, 4 * width : 4 * width + ff_width]
    w_down = matrices[:, 4 * width + ff_width :]
    inputs = tokens.astype(f32)
    vector_rows = vectors.astype(f32)
    up_bias = vector_rows[8:].reshape(ff_width)

    with jax.named_scope("norm_one"):
        normed, inverse_std = layer_norm(inputs)
        hidden = (normed * vector_rows[0] + vector_rows[1]).astype(bf16)
    with jax.named_scope("gather_hidden"):
        hidden_all = gather_sequence(reorder(hidden, 1))
    with jax.named_scope("project"):
        w_heads = jnp.concatenate([own(0, lanes), own(width, lanes), own(2 * width, lanes)], axis=1)
        bias = jnp.concatenate(
            [
                lax.dynamic_slice_in_dim(vector_rows[2], rank * lanes, lanes, 0),
                jnp.zeros((lanes,), f32),
                lax.dynamic_slice_in_dim(vector_rows[3], rank * lanes, lanes, 0),
            ]
        )
        qkv = (dot_nn(hidden_all, w_heads) + bias).astype(bf16)
    attended_heads, attended_wide, log_total = attention_forward(
        qkv, rank_array, picture_starts, slopes
    )
    with jax.named_scope("attended_exchange"):
        attended = (
            exchange(attended_heads.reshape(group, row_count, lanes))
            .transpose(1, 0, 2)
            .reshape(row_count, width)
        )
    with jax.named_scope("gather_cotangent"):
        cotangent_all = gather_sequence(reorder(cotangent, 1))
    with jax.named_scope("feed_forward"):
        middle = inputs + dot_nn(attended, w_proj) + vector_rows[4]
        normed_two, inverse_two = layer_norm(middle)
        hidden_two = (normed_two * vector_rows[5] + vector_rows[6]).astype(bf16)
        pre_act = dot_nn(hidden_two, w_up) + up_bias
        grad_act = dot_nn(cotangent, w_down)
        act, pull = jax.vjp(activate, pre_act)
        act_low = act.astype(bf16)
        grad_pre = pull(grad_act)[0].astype(bf16)
        grad_two = dot_nt(grad_pre, w_up)
        upstream = cotangent.astype(f32)
        grad_mid = upstream + norm_backward(grad_two, vector_rows[5], normed_two, inverse_two)
        grad_mid_low = grad_mid.astype(bf16)
        grad_attended = dot_nt(grad_mid_low, w_proj).astype(bf16)
    with jax.named_scope("grad_attended_exchange"):
        grad_heads = exchange(
            grad_attended.reshape(row_count, group, lanes).transpose(1, 0, 2)
        ).reshape(group * row_count, lanes)
    with jax.named_scope("layer_output"):
        layer_output = (middle + dot_nt(act_low, w_down) + vector_rows[7]).astype(bf16)
    with jax.named_scope("gather_hidden_two"):
        hidden_two_all = gather_sequence(reorder(hidden_two, 1))
    with jax.named_scope("own_units"):
        own_up = own(4 * width, units)
        own_down = own(4 * width + ff_width, units)
        own_pre = dot_nn(hidden_two_all, own_up) + lax.dynamic_slice_in_dim(
            up_bias, rank * units, units, 0
        )
        own_grad_act = dot_nn(cotangent_all, own_down)
        own_act, own_pull = jax.vjp(activate, own_pre)
        own_act_low = own_act.astype(bf16)
        own_grad_pre = own_pull(own_grad_act)[0].astype(bf16)
    with jax.named_scope("grad_down"):
        sum_down = sum_over_dp(cotangent_all, own_act_low)
    with jax.named_scope("grad_up"):
        sum_up = sum_over_dp(hidden_two_all, own_grad_pre)
    with jax.named_scope("grad_proj"):
        grad_proj = dot_tn(attended, grad_mid_low).astype(bf16)
        grad_proj = (
            grad_proj.reshape(4, group, 32, width).transpose(1, 0, 2, 3).reshape(group, 128, width)
        )
        part_proj = lax.psum_scatter(
            grad_proj.reshape(width, width), ("ctx", "shard"), scatter_dimension=0, tiled=True
        )
        part_proj = lax.psum_scatter(part_proj, "dp", scatter_dimension=0, tiled=True).astype(f32)
    grad_abs, grad_rel = attention_backward(
        qkv, grad_heads, attended_wide, log_total, rank_array, picture_starts, slopes
    )
    with jax.named_scope("grad_qkv_exchange"):
        grad_qkv = (
            exchange(grad_abs.reshape(group, row_count, 3 * lanes))
            .reshape(group, row_count, 3, lanes)
            .transpose(1, 2, 0, 3)
            .reshape(row_count, 3 * width)
        )
    with jax.named_scope("grad_qkv_weights"):
        sum_qkv = sum_over_dp(hidden_all, grad_rel)
        own_bias_grad = jnp.sum(grad_rel.astype(f32), axis=0)
    with jax.named_scope("grad_hidden"):
        grad_hidden = dot_nt(grad_qkv, w_qkv)
        token_grads = grad_mid + norm_backward(grad_hidden, vector_rows[0], normed, inverse_std)
    with jax.named_scope("grad_vectors"):

        def spread(values, total):
            return lax.dynamic_update_slice_in_dim(
                jnp.zeros((total,), f32), values, rank * values.shape[0], 0
            )

        grad_vectors = jnp.concatenate(
            [
                jnp.stack(
                    [
                        jnp.sum(grad_hidden * normed, axis=0),
                        jnp.sum(grad_hidden, axis=0),
                        spread(own_bias_grad[:lanes], width),
                        spread(own_bias_grad[2 * lanes :], width),
                        jnp.sum(grad_mid, axis=0),
                        jnp.sum(grad_two * normed_two, axis=0),
                        jnp.sum(grad_two, axis=0),
                        jnp.sum(upstream, axis=0),
                    ]
                ),
                spread(jnp.sum(own_grad_pre.astype(f32), axis=0), ff_width).reshape(-1, width),
            ],
            axis=0,
        )
        summed = lax.psum(grad_vectors, ("dp", "ctx", "shard"))
        part_vec = lax.dynamic_slice_in_dim(summed, (depth * group + rank) * 32, 32, 1)
    with jax.named_scope("rows_exchange"):

        def to_rows(array, parts):
            columns = array.shape[1]
            got = exchange(array.astype(bf16).reshape(group, 32, columns))
            got = got.reshape(group, 32, parts, columns // parts).transpose(1, 2, 0, 3)
            return got.reshape(32, group * columns).astype(f32)

        part_matrix = jnp.concatenate(
            [to_rows(sum_qkv, 3), part_proj, to_rows(sum_up, 1), to_rows(sum_down, 1)], axis=1
        )
    root = (row_count * lax.axis_size("dp") * group) ** (-0.5)
    correction = 1.0 - BETA**STEP
    with jax.named_scope("update"):
        moment_w, variance_w, updated_w = adam_update(
            master_matrices,
            first_matrices,
            second_matrices,
            part_matrix * root,
            correction,
            DECAY_RATE,
        )
        moment_v, variance_v, updated_v = adam_update(
            master_vectors, first_vectors, second_vectors, part_vec * root, correction, 0.0
        )
    with jax.named_scope("copies"):
        copied_w = lax.all_gather(updated_w.astype(bf16), "shard", axis=0, tiled=True)
        copied_v = lax.all_gather(updated_v.astype(bf16), "shard", axis=1, tiled=True)
    return (
        layer_output,
        token_grads,
        moment_w,
        moment_v,
        variance_w,
        variance_v,
        updated_w,
        updated_v,
        copied_w,
        copied_v,
    )


def solution(mesh):
    in_specs = (
        P(("dp", "ctx", "shard"), None),
        P(("dp", "ctx", "shard"), None),
        P("dp", None),
        P(),
        P(),
        P(("dp", "ctx", "shard"), None),
        P(None, ("dp", "ctx", "shard")),
        P(("dp", "ctx", "shard"), None),
        P(None, ("dp", "ctx", "shard")),
        P(("dp", "ctx", "shard"), None),
        P(None, ("dp", "ctx", "shard")),
    )
    out_specs = (
        P(("dp", "ctx", "shard"), None),
        P(("dp", "ctx", "shard"), None),
        P(("dp", "ctx", "shard"), None),
        P(None, ("dp", "ctx", "shard")),
        P(("dp", "ctx", "shard"), None),
        P(None, ("dp", "ctx", "shard")),
        P(("dp", "ctx", "shard"), None),
        P(None, ("dp", "ctx", "shard")),
        P(("dp", "ctx"), None),
        P(None, ("dp", "ctx")),
    )
    body = sequence_shards if fits_sequence_plan(mesh) else general_shards
    return jax.shard_map(body, mesh=mesh, in_specs=in_specs, out_specs=out_specs, check_vma=False)
```

```python
import functools
import math

import jax
import jax.numpy as jnp
from jax import lax
from jax.experimental import pallas as pl
from jax.experimental.pallas import tpu as pltpu
from jax.sharding import PartitionSpec as P

HEADS = 16
PIC = 256
STEP = 2


EPSILON = 1e-05
NEGATIVE = -1e30
BETA = 0.5
RATE = 0.03
DECAY_RATE = 0.1
ADAM_EPSILON = 1e-08


def token_tags(index, start_list, block_len):
    after = index[:, None] - start_list[None, :]
    inside = (after >= 0) & (after < block_len)
    offsets = jnp.sum(jnp.clip(after, 0, block_len - 1), axis=1)
    number = jnp.arange(1, start_list.shape[0] + 1, dtype=jnp.int32)
    picture = jnp.sum(jnp.where(inside, number[None, :], 0), axis=1) - 1
    return (index - offsets, picture)


def block_scores(query_heads, query_index, key_heads, key_index, start_list, slopes, factor):
    query_pos, query_pic = token_tags(query_index, start_list, PIC)
    key_pos, key_pic = token_tags(key_index, start_list, PIC)
    raw = jnp.einsum("qhd,khd->hqk", query_heads, key_heads, preferred_element_type=jnp.float32)
    distance = (query_pos[:, None] - key_pos[None, :]).astype(jnp.float32)
    logits = raw * factor - slopes[:, None, None] * distance[None, :, :]
    same = (query_pic[:, None] == key_pic[None, :]) & (query_pic[:, None] >= 0)
    visible = (key_index[None, :] <= query_index[:, None]) | same
    return (logits, visible[None, :, :])


def layer_norm(inputs):
    centered = inputs - jnp.mean(inputs, axis=1, keepdims=True)
    inverse_std = lax.rsqrt(jnp.mean(centered * centered, axis=1, keepdims=True) + EPSILON)
    return (centered * inverse_std, inverse_std)


def norm_backward(grad_normed, gain, normed, inverse_std):
    scaled = grad_normed * gain
    return inverse_std * (
        scaled
        - jnp.mean(scaled, axis=1, keepdims=True)
        - normed * jnp.mean(scaled * normed, axis=1, keepdims=True)
    )


def activate(value):
    return jax.nn.gelu(value, approximate=True)


def regroup(array, dim, outer, inner):
    shape = array.shape
    split = array.reshape(
        shape[:dim] + (outer, inner, shape[dim] // (outer * inner)) + shape[dim + 1 :]
    )
    return jnp.swapaxes(split, dim, dim + 1).reshape(shape)


def adam_update(master, first, second, gradient, correction, decay_rate):
    moment = BETA * first + (1.0 - BETA) * gradient
    variance = BETA * second + (1.0 - BETA) * gradient * gradient
    direction = moment / correction / (jnp.sqrt(variance / correction) + ADAM_EPSILON)
    return (moment, variance, master - RATE * (direction + decay_rate * master))


def general_shards(
    tokens,
    cotangent,
    picture_starts,
    matrices,
    vectors,
    master_matrices,
    master_vectors,
    first_matrices,
    first_vectors,
    second_matrices,
    second_vectors,
):
    row_count, model_width = tokens.shape
    ff_width = (matrices.shape[1] - 4 * model_width) // 2
    head_count = HEADS
    head_width = model_width // head_count
    factor = head_width ** (-0.5)
    group_size = lax.axis_size("ctx") * lax.axis_size("shard")
    group_rank = lax.axis_index("ctx") * lax.axis_size("shard") + lax.axis_index("shard")
    seq_length = row_count * group_size
    first_row = group_rank * row_count
    start_list = picture_starts[0]
    slopes = jnp.exp2(-8.0 * (jnp.arange(head_count, dtype=jnp.float32) + 1.0) / head_count)
    block_rows = math.gcd(seq_length, 512)
    block_count = seq_length // block_rows
    w_qkv = matrices[:, : 3 * model_width]
    w_proj = matrices[:, 3 * model_width : 4 * model_width]
    w_up = matrices[:, 4 * model_width : 4 * model_width + ff_width]
    w_down = matrices[:, 4 * model_width + ff_width :]
    inputs = tokens.astype(jnp.float32)
    vector_rows = vectors.astype(jnp.float32)
    up_bias = vector_rows[8:].reshape(ff_width)
    normed, inverse_std = layer_norm(inputs)
    hidden = (normed * vector_rows[0] + vector_rows[1]).astype(jnp.bfloat16)
    projected = jnp.dot(hidden, w_qkv, preferred_element_type=jnp.float32)
    queries = (projected[:, :model_width] + vector_rows[2]).astype(jnp.bfloat16)
    kv_bias = jnp.concatenate([jnp.zeros((model_width,), jnp.float32), vector_rows[3]])
    kv_local = (projected[:, model_width:] + kv_bias).astype(jnp.bfloat16)
    gathered = lax.all_gather(kv_local, ("ctx", "shard"), axis=0, tiled=True)
    query_index = first_row + jnp.arange(row_count, dtype=jnp.int32)
    query_heads = queries.reshape(row_count, head_count, head_width)

    def key_block(index):
        piece = lax.dynamic_slice_in_dim(gathered, index * block_rows, block_rows, 0)
        key_heads = piece[:, :model_width].reshape(block_rows, head_count, head_width)
        value_heads = piece[:, model_width:].reshape(block_rows, head_count, head_width)
        key_index = index * block_rows + jnp.arange(block_rows, dtype=jnp.int32)
        logits, visible = block_scores(
            query_heads, query_index, key_heads, key_index, start_list, slopes, factor
        )
        return (logits, visible, key_heads, value_heads)

    def running_total(index, carry):
        highest, total = carry
        logits, visible, key_heads, value_heads = key_block(index)
        masked = jnp.where(visible, logits, NEGATIVE)
        updated = jnp.maximum(highest, jnp.max(masked, axis=2))
        weights = jnp.where(visible, jnp.exp(logits - updated[:, :, None]), 0.0)
        return (updated, total * jnp.exp(highest - updated) + jnp.sum(weights, axis=2))

    start_high = jnp.full((head_count, row_count), NEGATIVE, jnp.float32)
    start_total = jnp.zeros((head_count, row_count), jnp.float32)
    highest, total = lax.fori_loop(0, block_count, running_total, (start_high, start_total))
    log_total = highest + jnp.log(total)

    def weighted_sum(index, accum):
        logits, visible, key_heads, value_heads = key_block(index)
        probs = jnp.where(visible, jnp.exp(logits - log_total[:, :, None]), 0.0).astype(
            jnp.bfloat16
        )
        return accum + jnp.einsum(
            "hqk,khd->qhd", probs, value_heads, preferred_element_type=jnp.float32
        )

    attended = lax.fori_loop(
        0, block_count, weighted_sum, jnp.zeros((row_count, head_count, head_width), jnp.float32)
    )
    attended_low = attended.reshape(row_count, model_width).astype(jnp.bfloat16)
    middle = (
        inputs + jnp.dot(attended_low, w_proj, preferred_element_type=jnp.float32) + vector_rows[4]
    )
    normed_two, inverse_two = layer_norm(middle)
    hidden_two = (normed_two * vector_rows[5] + vector_rows[6]).astype(jnp.bfloat16)
    pre_act = jnp.dot(hidden_two, w_up, preferred_element_type=jnp.float32) + up_bias
    act_low = activate(pre_act).astype(jnp.bfloat16)
    down_out = lax.dot_general(
        act_low, w_down, (((1,), (1,)), ((), ())), preferred_element_type=jnp.float32
    )
    layer_output = (middle + down_out + vector_rows[7]).astype(jnp.bfloat16)
    upstream = cotangent.astype(jnp.float32)
    grad_act = jnp.dot(cotangent, w_down, preferred_element_type=jnp.float32)
    gelu_value, gelu_pull = jax.vjp(activate, pre_act)
    grad_pre = gelu_pull(grad_act)[0].astype(jnp.bfloat16)
    grad_up_w = lax.dot_general(
        hidden_two, grad_pre, (((0,), (0,)), ((), ())), preferred_element_type=jnp.float32
    )
    grad_down_w = lax.dot_general(
        cotangent, act_low, (((0,), (0,)), ((), ())), preferred_element_type=jnp.float32
    )
    grad_two = lax.dot_general(
        grad_pre, w_up, (((1,), (1,)), ((), ())), preferred_element_type=jnp.float32
    )
    grad_mid = upstream + norm_backward(grad_two, vector_rows[5], normed_two, inverse_two)
    grad_mid_low = grad_mid.astype(jnp.bfloat16)
    grad_proj = lax.dot_general(
        attended_low, grad_mid_low, (((0,), (0,)), ((), ())), preferred_element_type=jnp.float32
    )
    grad_out = lax.dot_general(
        grad_mid_low, w_proj, (((1,), (1,)), ((), ())), preferred_element_type=jnp.float32
    ).astype(jnp.bfloat16)
    grad_heads = grad_out.reshape(row_count, head_count, head_width)
    delta = jnp.sum(grad_heads.astype(jnp.float32) * attended, axis=2).T

    def score_grads(index):
        logits, visible, key_heads, value_heads = key_block(index)
        probs = jnp.where(visible, jnp.exp(logits - log_total[:, :, None]), 0.0)
        product = jnp.einsum(
            "qhd,khd->hqk", grad_heads, value_heads, preferred_element_type=jnp.float32
        )
        grad_logits = (probs * (product - delta[:, :, None])).astype(jnp.bfloat16)
        return (probs, grad_logits, key_heads)

    def both_grads(index, carry):
        accum, key_terms = carry
        probs, grad_logits, key_heads = score_grads(index)
        accum = (
            accum
            + jnp.einsum("hqk,khd->qhd", grad_logits, key_heads, preferred_element_type=jnp.float32)
            * factor
        )
        grad_key = (
            jnp.einsum("hqk,qhd->khd", grad_logits, query_heads, preferred_element_type=jnp.float32)
            * factor
        )
        grad_value = jnp.einsum(
            "hqk,qhd->khd",
            probs.astype(jnp.bfloat16),
            grad_heads,
            preferred_element_type=jnp.float32,
        )
        term = jnp.concatenate(
            [
                grad_key.reshape(block_rows, model_width),
                grad_value.reshape(block_rows, model_width),
            ],
            axis=1,
        )
        return (accum, lax.dynamic_update_slice_in_dim(key_terms, term, index * block_rows, 0))

    grad_query, key_terms = lax.fori_loop(
        0,
        block_count,
        both_grads,
        (
            jnp.zeros((row_count, head_count, head_width), jnp.float32),
            jnp.zeros((seq_length, 2 * model_width), jnp.float32),
        ),
    )
    own_key_grads = lax.psum_scatter(key_terms, ("ctx", "shard"), scatter_dimension=0, tiled=True)
    grad_qkv = jnp.concatenate(
        [grad_query.reshape(row_count, model_width), own_key_grads], axis=1
    ).astype(jnp.bfloat16)
    grad_qkv_weights = lax.dot_general(
        hidden, grad_qkv, (((0,), (0,)), ((), ())), preferred_element_type=jnp.float32
    )
    grad_hidden = lax.dot_general(
        grad_qkv, w_qkv, (((1,), (1,)), ((), ())), preferred_element_type=jnp.float32
    )
    query_bias_grad = jnp.sum(grad_qkv[:, :model_width].astype(jnp.float32), axis=0)
    value_bias_grad = jnp.sum(grad_qkv[:, 2 * model_width :].astype(jnp.float32), axis=0)
    grad_vectors = jnp.concatenate(
        [
            jnp.stack(
                [
                    jnp.sum(grad_hidden * normed, axis=0),
                    jnp.sum(grad_hidden, axis=0),
                    query_bias_grad,
                    value_bias_grad,
                    jnp.sum(grad_mid, axis=0),
                    jnp.sum(grad_two * normed_two, axis=0),
                    jnp.sum(grad_two, axis=0),
                    jnp.sum(upstream, axis=0),
                ]
            ),
            jnp.sum(grad_pre.astype(jnp.float32), axis=0).reshape(
                ff_width // model_width, model_width
            ),
        ],
        axis=0,
    )
    token_grads = grad_mid + norm_backward(grad_hidden, vector_rows[0], normed, inverse_std)
    grad_matrix = jnp.concatenate([grad_qkv_weights, grad_proj, grad_up_w, grad_down_w], axis=1)
    shard_count = lax.axis_size("shard")
    replicas = lax.axis_size("dp") * lax.axis_size("ctx")
    part_matrix, part_vec = (
        lax.psum_scatter(
            regroup(grad_matrix, 0, replicas, shard_count), "shard", scatter_dimension=0, tiled=True
        ),
        lax.psum_scatter(
            regroup(grad_vectors, 1, replicas, shard_count),
            "shard",
            scatter_dimension=1,
            tiled=True,
        ),
    )
    part_matrix, part_vec = (
        lax.psum_scatter(part_matrix, ("dp", "ctx"), scatter_dimension=0, tiled=True),
        lax.psum_scatter(part_vec, ("dp", "ctx"), scatter_dimension=1, tiled=True),
    )
    root = (row_count * lax.axis_size("dp") * group_size) ** (-0.5)
    correction = 1.0 - BETA**STEP
    moment_w, variance_w, updated_w = adam_update(
        master_matrices, first_matrices, second_matrices, part_matrix * root, correction, DECAY_RATE
    )
    moment_v, variance_v, updated_v = adam_update(
        master_vectors, first_vectors, second_vectors, part_vec * root, correction, 0.0
    )
    copied_w, copied_v = (
        lax.all_gather(updated_w.astype(jnp.bfloat16), "shard", axis=0, tiled=True),
        lax.all_gather(updated_v.astype(jnp.bfloat16), "shard", axis=1, tiled=True),
    )
    return (
        layer_output,
        token_grads,
        moment_w,
        moment_v,
        variance_w,
        variance_v,
        updated_w,
        updated_v,
        copied_w,
        copied_v,
    )


BLOCK = 256
EXTRA = 1
f32 = jnp.float32
bf16 = jnp.bfloat16
NT = (((1,), (1,)), ((), ()))
GELU_SCALE = math.sqrt(2.0 / math.pi)
GELU_CUBE = 0.044715


def split3(value):
    high = value.astype(bf16).astype(f32)
    rest = value - high
    middle = rest.astype(bf16).astype(f32)
    low = (rest - middle).astype(bf16).astype(f32)
    return high, middle, low


def positions(index, starts_ref, count):
    result = index
    for b in range(count):
        result = result - jnp.clip(index - starts_ref[0, b], 0, PIC - 1)
    return result.astype(f32)


def limits(index, starts_ref, count):
    result = index + 1
    for b in range(count):
        start = starts_ref[0, b]
        result = jnp.where((index >= start) & (index < start + PIC), start + PIC, result)
    return result


def head_lanes(shape, h, width):
    lane = lax.broadcasted_iota(jnp.int32, shape, 1)
    inside = (lane < width) if h == 0 else (lane >= width)
    return inside, lane - width if h == 0 else lane


def pick(spare, values):
    out = jnp.zeros(spare.shape, f32)
    for e, value in enumerate(values):
        out = jnp.where(spare == e, value, out)
    return out


def smem():
    return pl.BlockSpec(memory_space=pltpu.SMEM)


def vmem():
    return pl.BlockSpec(memory_space=pltpu.VMEM)


def hbm():
    return pl.BlockSpec(memory_space=pl.ANY)


def params(mebibytes):
    return pltpu.CompilerParams(vmem_limit_bytes=mebibytes * 2**20)


def cost(microseconds):
    return pl.CostEstimate(
        flops=int(microseconds * 1.0e9), bytes_accessed=0, transcendentals=0
    )


def start_all(copies):
    for copy in copies:
        copy.start()
    return copies


def wait_all(copies):
    for copy in copies:
        copy.wait()


def pattern_kernel(width, count, starts_ref, slopes_ref, out_ref):
    lanes = out_ref.shape[2]
    step = pl.program_id(0)
    index = lax.broadcasted_iota(jnp.int32, (BLOCK, lanes), 0) + step * BLOCK
    pos = positions(index, starts_ref, count)
    for h in range(2):
        _, spare = head_lanes((BLOCK, lanes), h, width)
        parts = split3(pos * slopes_ref[h])
        out_ref[h] = pick(spare, parts + (1.0, 1.0, 1.0)).astype(bf16)


def key_pattern(starts, slopes, seq, lanes):
    return pl.pallas_call(
        functools.partial(pattern_kernel, lanes // 2, starts.shape[1]),
        grid=(seq // BLOCK,),
        out_shape=jax.ShapeDtypeStruct((2, seq, lanes), bf16),
        in_specs=[smem()] * 2,
        out_specs=pl.BlockSpec((2, BLOCK, lanes), lambda i: (0, i, 0)),
        compiler_params=params(40),
        cost_estimate=cost(3),
        name="key_pattern",
    )(starts, slopes)


def forward_kernel(width, tile, count, rank_ref, starts_ref, slopes_ref, *refs):
    blocks = refs[:8]
    matrices_ref, vectors_ref, pattern_in = refs[8:11]
    att_out, wide_out, q_out, k_out, v_out, all_out = refs[11 + EXTRA : 17 + EXTRA]
    hid, wts, vecs, pattern, qa, ka, va, att, wide, best_ref, acc_ref = refs[17 + EXTRA : 28 + EXTRA]
    in_sems, w_sems, hid_sems, out_sems = refs[28 + EXTRA :]
    seq, lanes = wide.shape
    model = hid.shape[1]
    rank = rank_ref[0]
    factor = width**-0.5
    w_copies = []
    for part in range(3):
        columns = pl.ds(pl.multiple_of(part * model + rank * lanes, lanes), lanes)
        w_copies.append(
            pltpu.make_async_copy(
                matrices_ref.at[:, columns],
                wts.at[:, part * lanes : (part + 1) * lanes],
                w_sems.at[part],
            )
        )
    w_copies.append(pltpu.make_async_copy(vectors_ref, vecs, w_sems.at[3]))
    start_all(w_copies)
    in_copies = start_all(
        [
            pltpu.make_async_copy(
                blocks[k], hid.at[k * BLOCK : (k + 1) * BLOCK], in_sems.at[k]
            )
            for k in range(8)
        ]
    )
    pattern_copy = pltpu.make_async_copy(pattern_in, pattern, w_sems.at[4])
    pattern_copy.start()
    wait_all(w_copies)
    bias = vecs[:, pl.ds(pl.multiple_of(rank * lanes, lanes), lanes)].astype(f32)
    out_copies = []
    ones = []
    for h in range(2):
        inside, spare = head_lanes((BLOCK, lanes), h, width)
        ones.append((inside, jnp.where(spare < 3, 1.0, 0.0)))
    for pair in range(4):
        first = 2 * pair
        for k in (first, first + 1):
            in_copies[k].wait()
            rows = slice(k * BLOCK, (k + 1) * BLOCK)
            copy = pltpu.make_async_copy(hid.at[rows], all_out.at[rows], hid_sems.at[k])
            copy.start()
            out_copies.append(copy)
        value = jnp.dot(
            hid[first * BLOCK : (first + 2) * BLOCK, :], wts[...], preferred_element_type=f32
        )
        if pair == 0:
            pattern_copy.wait()
        for k in (first, first + 1):
            local = slice((k - first) * BLOCK, (k - first + 1) * BLOCK)
            dst = pl.ds(pl.multiple_of((k ^ rank) * BLOCK, BLOCK), BLOCK)
            q = (value[local, 0:lanes] + bias[2:3]).astype(bf16).astype(f32) * factor
            key = value[local, lanes : 2 * lanes]
            v = value[local, 2 * lanes : 3 * lanes] + bias[3:4]
            for h in range(2):
                inside, spare_ones = ones[h]
                qa[h, dst, :] = jnp.where(inside, q, spare_ones).astype(bf16)
                ka[h, dst, :] = jnp.where(inside, key, pattern[h, dst, :].astype(f32)).astype(bf16)
                va[h, dst, :] = jnp.where(inside, v, spare_ones).astype(bf16)
    out_copies += start_all(
        [
            pltpu.make_async_copy(ka, k_out, out_sems.at[0]),
            pltpu.make_async_copy(va, v_out, out_sems.at[1]),
        ]
    )

    def scores(h, queries, keys):
        return lax.dot_general(
            qa[h, queries, :], ka[h, keys, :], NT, preferred_element_type=f32
        )

    def mask(first_row, first_column, shape):
        rows = lax.broadcasted_iota(jnp.int32, (shape[0], 1), 0) + first_row
        columns = lax.broadcasted_iota(jnp.int32, shape, 1) + first_column
        return columns < limits(rows, starts_ref, count)

    def raise_best(h, local, value):
        best = best_ref[h, local, :]
        for c in range(value.shape[1] // lanes):
            best = jnp.maximum(best, value[:, c * lanes : (c + 1) * lanes])
        best_ref[h, local, :] = best

    def add_mixed(h, local, value, keys):
        acc_ref[h, local, :] += jnp.dot(
            value.astype(bf16), va[h, keys, :], preferred_element_type=f32
        )

    def with_shift(h, rows, shift):
        inside, spare = head_lanes((tile, lanes), h, width)
        parts = split3(-jnp.broadcast_to(shift, (tile, lanes)))
        value = qa[h, rows, :].astype(f32)
        for e in range(3):
            value = jnp.where(spare == 3 + e, parts[e], value)
        qa[h, rows, :] = value.astype(bf16)

    for i in range(seq // tile):
        base = i * tile
        end = base + tile
        rows = slice(base, end)
        whole = slice(0, tile)
        edges = [(rows, rows, whole)]
        if end < seq:
            edges.append((slice(end - PIC, end), slice(end, end + PIC), slice(tile - PIC, tile)))
        best_ref[...] = jnp.full(best_ref.shape, NEGATIVE, f32)
        acc_ref[...] = jnp.zeros(acc_ref.shape, f32)

        def find(j, carry):
            keys = pl.ds(pl.multiple_of(j * tile, tile), tile)
            for h in range(2):
                raise_best(h, whole, scores(h, rows, keys))
            return carry

        if i > 0:
            lax.fori_loop(0, i, find, 0)
        for queries, keys, local in edges:
            seen = mask(
                queries.start, keys.start, (queries.stop - queries.start, keys.stop - keys.start)
            )
            for h in range(2):
                raise_best(h, local, jnp.where(seen, scores(h, queries, keys), NEGATIVE))
        best = [jnp.max(best_ref[h], axis=1, keepdims=True) for h in range(2)]
        for h in range(2):
            with_shift(h, rows, best[h])

        def mix(j, carry):
            keys = pl.ds(pl.multiple_of(j * tile, tile), tile)
            for h in range(2):
                add_mixed(h, whole, jnp.exp(scores(h, rows, keys)), keys)
            return carry

        if i > 0:
            lax.fori_loop(0, i, mix, 0)
        for queries, keys, local in edges:
            seen = mask(
                queries.start, keys.start, (queries.stop - queries.start, keys.stop - keys.start)
            )
            for h in range(2):
                add_mixed(
                    h, local, jnp.where(seen, jnp.exp(scores(h, queries, keys)), 0.0), keys
                )
        outs = []
        for h in range(2):
            acc = acc_ref[h]
            column = width if h == 0 else 0
            total = acc[:, column : column + 1]
            outs.append(acc / total)
            with_shift(h, rows, best[h] + jnp.log(total))
        inside, _ = head_lanes((tile, lanes), 0, width)
        out = jnp.where(inside, outs[0], outs[1])
        wide[rows, :] = out
        count_here = tile // BLOCK
        groups = slice(i * count_here, (i + 1) * count_here)
        att[groups] = out.astype(bf16).reshape(count_here, BLOCK, lanes)
        out_copies += start_all(
            [
                pltpu.make_async_copy(att.at[groups], att_out.at[groups], out_sems.at[2 + 3 * i]),
                pltpu.make_async_copy(wide.at[rows], wide_out.at[rows], out_sems.at[3 + 3 * i]),
                pltpu.make_async_copy(
                    qa.at[:, rows], q_out.at[:, rows], out_sems.at[4 + 3 * i]
                ),
            ]
        )
    wait_all(out_copies)


def attention_forward(blocks, matrices, vectors, pattern, rank, starts, slopes, extra, tile=512):
    rows, model = blocks[0].shape
    seq = 8 * rows
    lanes = model // 8
    heads = jax.ShapeDtypeStruct((2, seq, lanes), bf16)
    return pl.pallas_call(
        functools.partial(forward_kernel, lanes // 2, tile, starts.shape[1]),
        out_shape=(
            jax.ShapeDtypeStruct((8, rows, lanes), bf16),
            jax.ShapeDtypeStruct((seq, lanes), f32),
            heads,
            heads,
            heads,
            jax.ShapeDtypeStruct((seq, model), bf16),
        ),
        in_specs=[smem()] * 3 + [hbm()] * (11 + EXTRA),
        out_specs=(hbm(),) * 6,
        scratch_shapes=[
            pltpu.VMEM((seq, model), bf16),
            pltpu.VMEM((model, 3 * lanes), bf16),
            pltpu.VMEM(vectors.shape, bf16),
            pltpu.VMEM((2, seq, lanes), bf16),
            pltpu.VMEM((2, seq, lanes), bf16),
            pltpu.VMEM((2, seq, lanes), bf16),
            pltpu.VMEM((2, seq, lanes), bf16),
            pltpu.VMEM((8, rows, lanes), bf16),
            pltpu.VMEM((seq, lanes), f32),
            pltpu.VMEM((2, tile, lanes), f32),
            pltpu.VMEM((2, tile, lanes), f32),
            pltpu.SemaphoreType.DMA((8,)),
            pltpu.SemaphoreType.DMA((5,)),
            pltpu.SemaphoreType.DMA((8,)),
            pltpu.SemaphoreType.DMA((2 + 3 * (seq // tile),)),
        ],
        compiler_params=params(56),
        cost_estimate=cost(20),
        name="attention_forward",
    )(rank, starts, slopes, *blocks, matrices, vectors, pattern, extra)


def backward_kernel(width, tile, count, rank_ref, starts_ref, *refs):
    q_in, k_in, v_in, kt_in, wide_in, got_in = refs[:6]
    abs_out, rel_out, bias_out = refs[6 + EXTRA : 9 + EXTRA]
    qa, ka, va, kt, wide, grads, da, dq_ref, dk_ref, dv_ref = refs[9 + EXTRA : 19 + EXTRA]
    both_ref, bias_ref, in_sems, out_sems = refs[19 + EXTRA :]
    seq, lanes = wide.shape
    rank = rank_ref[0]
    factor = width**-0.5
    first = start_all(
        [
            pltpu.make_async_copy(wide_in, wide, in_sems.at[0]),
            pltpu.make_async_copy(got_in.at[:, :, 0:lanes], grads, in_sems.at[1]),
        ]
    )
    rest = start_all(
        [
            pltpu.make_async_copy(q_in, qa, in_sems.at[2]),
            pltpu.make_async_copy(k_in, ka, in_sems.at[3]),
            pltpu.make_async_copy(v_in, va, in_sems.at[4]),
            pltpu.make_async_copy(kt_in, kt, in_sems.at[5]),
        ]
    )
    wait_all(first)

    def prologue(t, carry):
        rows = pl.ds(pl.multiple_of(t * BLOCK, BLOCK), BLOCK)
        g = grads[t].astype(f32)
        product = g * wide[rows, :]
        for h in range(2):
            inside, spare = head_lanes((BLOCK, lanes), h, width)
            delta = jnp.sum(jnp.where(inside, product, 0.0), axis=1, keepdims=True)
            parts = split3(-jnp.broadcast_to(delta, (BLOCK, lanes)))
            da[h, rows, :] = jnp.where(inside, g, pick(spare, parts)).astype(bf16)
        return carry

    lax.fori_loop(0, seq // BLOCK, prologue, 0)
    dq_ref[...] = jnp.zeros(dq_ref.shape, f32)
    wait_all(rest)

    def pair(h, keys, queries, mask, local):
        logits = lax.dot_general(ka[h, keys, :], qa[h, queries, :], NT, preferred_element_type=f32)
        probs = jnp.exp(logits)
        if mask is not None:
            probs = jnp.where(mask(logits.shape), probs, 0.0)
        inner = lax.dot_general(va[h, keys, :], da[h, queries, :], NT, preferred_element_type=f32)
        grad = (probs * inner).astype(bf16)
        dv_ref[h, local, :] += jnp.dot(
            probs.astype(bf16), da[h, queries, :], preferred_element_type=f32
        )
        dk_ref[h, local, :] += jnp.dot(grad, qa[h, queries, :], preferred_element_type=f32)
        rows = slice(h * width, (h + 1) * width)
        dq_ref[rows, queries] += jnp.dot(kt[rows, keys], grad, preferred_element_type=f32)

    bias_ref[...] = jnp.zeros(bias_ref.shape, f32)
    out_copies = []

    def send(t, part, value):
        columns = slice(part * lanes, (part + 1) * lanes)
        rows = slice(t * BLOCK, (t + 1) * BLOCK)
        both_ref[rows, columns] = value
        bias_ref[:, columns] += jnp.sum(value.astype(f32), axis=0, keepdims=True)

    for j in range(seq // tile):
        base = j * tile
        dk_ref[...] = jnp.zeros(dk_ref.shape, f32)
        dv_ref[...] = jnp.zeros(dv_ref.shape, f32)

        def mask(first_key, first_query, shape):
            queries = lax.broadcasted_iota(jnp.int32, (1, shape[1]), 1) + first_query
            keys = lax.broadcasted_iota(jnp.int32, shape, 0) + first_key
            return keys < limits(queries, starts_ref, count)

        if base > 0:
            for h in range(2):
                pair(
                    h,
                    slice(base, base + PIC),
                    slice(base - PIC, base),
                    functools.partial(mask, base, base - PIC),
                    slice(0, PIC),
                )
        for h in range(2):
            pair(
                h,
                slice(base, base + tile),
                slice(base, base + tile),
                functools.partial(mask, base, base),
                slice(0, tile),
            )

        def full(i, carry, base=base):
            queries = pl.ds(pl.multiple_of(i * tile, tile), tile)
            for h in range(2):
                pair(h, slice(base, base + tile), queries, None, slice(0, tile))
            return carry

        if base + tile < seq:
            lax.fori_loop(j + 1, seq // tile, full, 0)
        inside, _ = head_lanes((BLOCK, lanes), 0, width)
        for t in range(tile // BLOCK):
            part = slice(t * BLOCK, (t + 1) * BLOCK)
            block = j * (tile // BLOCK) + t
            send(block, 1, jnp.where(inside, dk_ref[0, part, :], dk_ref[1, part, :]).astype(bf16))
            send(block, 2, jnp.where(inside, dv_ref[0, part, :], dv_ref[1, part, :]).astype(bf16))
    for t in range(seq // BLOCK):
        rows = slice(t * BLOCK, (t + 1) * BLOCK)
        send(t, 0, (dq_ref[:, rows].T * factor).astype(bf16))
        other = pl.ds(pl.multiple_of((t ^ rank) * BLOCK, BLOCK), BLOCK)
        out_copies += start_all(
            [
                pltpu.make_async_copy(both_ref.at[rows], abs_out.at[rows], out_sems.at[2 * t]),
                pltpu.make_async_copy(both_ref.at[rows], rel_out.at[other], out_sems.at[2 * t + 1]),
            ]
        )
    copy = pltpu.make_async_copy(bias_ref, bias_out, out_sems.at[2 * (seq // BLOCK)])
    copy.start()
    wait_all(out_copies + [copy])


def attention_backward(saved, wide, got, rank, starts, extra, tile=512):
    seq, lanes = wide.shape
    blocks = seq // BLOCK
    return pl.pallas_call(
        functools.partial(backward_kernel, lanes // 2, tile, starts.shape[1]),
        out_shape=(jax.ShapeDtypeStruct((seq, 3 * lanes), bf16),) * 2
        + (jax.ShapeDtypeStruct((1, 3 * lanes), f32),),
        in_specs=[smem()] * 2 + [hbm()] * (6 + EXTRA),
        out_specs=(hbm(),) * 3,
        scratch_shapes=[
            pltpu.VMEM((2, seq, lanes), bf16),
            pltpu.VMEM((2, seq, lanes), bf16),
            pltpu.VMEM((2, seq, lanes), bf16),
            pltpu.VMEM((lanes, seq), bf16),
            pltpu.VMEM((seq, lanes), f32),
            pltpu.VMEM((blocks, BLOCK, lanes), bf16),
            pltpu.VMEM((2, seq, lanes), bf16),
            pltpu.VMEM((lanes, seq), f32),
            pltpu.VMEM((2, tile, lanes), f32),
            pltpu.VMEM((2, tile, lanes), f32),
            pltpu.VMEM((seq, 3 * lanes), bf16),
            pltpu.VMEM((1, 3 * lanes), f32),
            pltpu.SemaphoreType.DMA((6,)),
            pltpu.SemaphoreType.DMA((2 * blocks + 1,)),
        ],
        compiler_params=params(56),
        cost_estimate=cost(21),
        name="attention_backward",
    )(rank, starts, *saved, wide, got, extra)


def normalize(value):
    centered = value - jnp.mean(value, axis=1, keepdims=True)
    inverse = lax.rsqrt(jnp.mean(centered * centered, axis=1, keepdims=True) + EPSILON)
    return centered * inverse, inverse


def whole(shape):
    return pl.BlockSpec(shape, lambda *_: (0,) * len(shape))


def gate(arrays, waits):
    count = len(arrays)
    return pl.pallas_call(
        lambda *refs: None,
        out_shape=tuple(jax.ShapeDtypeStruct(array.shape, array.dtype) for array in arrays),
        in_specs=[hbm()] * (count + len(waits)),
        out_specs=(hbm(),) * count,
        input_output_aliases={k: k for k in range(count)},
        cost_estimate=cost(1),
        name="gate",
    )(*arrays, *waits)


def norm_kernel(tokens_ref, vectors_ref, hidden_ref):
    vecs = vectors_ref[...].astype(f32)
    normed, _ = normalize(tokens_ref[...].astype(f32))
    hidden_ref[...] = (normed * vecs[0:1] + vecs[1:2]).astype(bf16)


def norm_one(tokens, vectors):
    rows, model = tokens.shape
    half = pl.BlockSpec((rows // 2, model), lambda i: (i, 0))
    return pl.pallas_call(
        norm_kernel,
        grid=(2,),
        out_shape=jax.ShapeDtypeStruct(tokens.shape, bf16),
        in_specs=[half, whole(vectors.shape)],
        out_specs=half,
        compiler_params=params(56),
        cost_estimate=cost(2),
        name="norm_one",
    )(tokens, vectors)


def project_kernel(
    heads_ref, tokens_ref, weights_ref, vectors_ref, extra_ref, attended_ref, middle_ref, hidden_ref
):
    lanes = heads_ref.shape[2]
    for g in range(heads_ref.shape[0]):
        attended_ref[:, g * lanes : (g + 1) * lanes] = heads_ref[g]
    vecs = vectors_ref[...].astype(f32)
    middle = (
        tokens_ref[...].astype(f32)
        + jnp.dot(attended_ref[...], weights_ref[...], preferred_element_type=f32)
        + vecs[4:5]
    )
    middle_ref[...] = middle
    normed, _ = normalize(middle)
    hidden_ref[...] = (normed * vecs[5:6] + vecs[6:7]).astype(bf16)


def project_norm(heads, tokens, matrices, vectors, extra):
    rows, model = tokens.shape
    return pl.pallas_call(
        project_kernel,
        grid=(1,),
        out_shape=(
            jax.ShapeDtypeStruct((rows, model), bf16),
            jax.ShapeDtypeStruct((rows, model), f32),
            jax.ShapeDtypeStruct((rows, model), bf16),
        ),
        in_specs=[
            whole(heads.shape),
            whole(tokens.shape),
            pl.BlockSpec((model, model), lambda i: (0, 3)),
            whole(vectors.shape),
            hbm(),
        ],
        out_specs=(whole((rows, model)),) * 3,
        compiler_params=params(40),
        cost_estimate=cost(3),
        name="project_norm",
    )(heads, tokens, matrices, vectors, extra)


def gelu_parts(pre):
    square = pre * pre
    half = 0.5 * (1.0 + jnp.tanh(GELU_SCALE * (pre + GELU_CUBE * square * pre)))
    act = pre * half
    slope = half + 2.0 * act * (1.0 - half) * (GELU_SCALE * (1.0 + 3.0 * GELU_CUBE * square))
    return act, slope


def norm_pull(grad, gain, normed, inverse):
    scaled = grad * gain
    return inverse * (
        scaled
        - jnp.mean(scaled, axis=1, keepdims=True)
        - normed * jnp.mean(scaled * normed, axis=1, keepdims=True)
    )


def feed_kernel(chunk, *refs):
    hidden_in, middle_in, cotangent_in, vectors_in, bias_in, matrices_in = refs[:6]
    layer_out, grad_mid_out, heads_out, sums_out = refs[6:10]
    hidden, middle, cotangent, vecs_ref, bias, up, down, proj = refs[10:18]
    layer, grad_mid_ref, heads, sums, down_acc, two_acc, in_sems, w_sems, out_sems = refs[18:]
    model = hidden.shape[1]
    count = up.shape[0]
    first = start_all(
        [
            pltpu.make_async_copy(source, target, in_sems.at[k])
            for k, (source, target) in enumerate(
                ((hidden_in, hidden), (cotangent_in, cotangent), (bias_in, bias))
            )
        ]
    )
    weights = []
    for i in range(count):
        for part, ref in ((0, up), (1, down)):
            start = 4 * model + part * count * chunk + i * chunk
            weights.append(
                pltpu.make_async_copy(
                    matrices_in.at[:, start : start + chunk], ref.at[i], w_sems.at[2 * i + part]
                )
            )
    start_all(weights)
    rest = start_all(
        [
            pltpu.make_async_copy(middle_in, middle, in_sems.at[3]),
            pltpu.make_async_copy(vectors_in, vecs_ref, in_sems.at[4]),
            pltpu.make_async_copy(
                matrices_in.at[:, 3 * model : 4 * model], proj, in_sems.at[5]
            ),
        ]
    )
    wait_all(first)
    for i in range(count):
        weights[2 * i].wait()
        pre = jnp.dot(hidden[...], up[i], preferred_element_type=f32)
        pre = pre + bias[:, i * chunk : (i + 1) * chunk]
        weights[2 * i + 1].wait()
        grad_act = jnp.dot(cotangent[...], down[i], preferred_element_type=f32)
        act, slope = gelu_parts(pre)
        grad_pre = (grad_act * slope).astype(bf16)
        down_part = lax.dot_general(act.astype(bf16), down[i], NT, preferred_element_type=f32)
        two_part = lax.dot_general(grad_pre, up[i], NT, preferred_element_type=f32)
        if i == 0:
            down_acc[...] = down_part
            two_acc[...] = two_part
        else:
            down_acc[...] += down_part
            two_acc[...] += two_part
    wait_all(rest)
    vecs = vecs_ref[...].astype(f32)
    grad_two = two_acc[...]
    mid = middle[...]
    normed, inverse = normalize(mid)
    upstream = cotangent[...].astype(f32)
    grad_mid = upstream + norm_pull(grad_two, vecs[5:6], normed, inverse)
    low = grad_mid.astype(bf16)
    grads = lax.dot_general(low, proj[...], NT, preferred_element_type=f32).astype(bf16)
    groups, _, double = heads.shape
    lanes = double // 2
    for g in range(groups):
        heads[g, :, 0:lanes] = grads[:, g * lanes : (g + 1) * lanes]
        heads[g, :, lanes:double] = low[:, g * lanes : (g + 1) * lanes]
    out_copies = [pltpu.make_async_copy(heads, heads_out, out_sems.at[0])]
    out_copies[0].start()
    grad_mid_ref[...] = grad_mid
    layer[...] = (mid + down_acc[...] + vecs[7:8]).astype(bf16)
    rows = [grad_mid, grad_two * normed, grad_two, upstream]
    for k, value in enumerate(rows):
        sums[k : k + 1, :] = jnp.sum(value, axis=0, keepdims=True)
    out_copies += start_all(
        [
            pltpu.make_async_copy(layer, layer_out, out_sems.at[1]),
            pltpu.make_async_copy(grad_mid_ref, grad_mid_out, out_sems.at[2]),
            pltpu.make_async_copy(sums, sums_out, out_sems.at[3]),
        ]
    )
    wait_all(out_copies)


def feed_forward(hidden, up_bias, middle, cotangent, vectors, matrices, chunk=1024):
    rows, model = hidden.shape
    ff_width = up_bias.shape[1]
    count = ff_width // chunk
    outs = (
        jax.ShapeDtypeStruct((rows, model), bf16),
        jax.ShapeDtypeStruct((rows, model), f32),
        jax.ShapeDtypeStruct((8, rows, model // 4), bf16),
        jax.ShapeDtypeStruct((4, model), f32),
    )
    return pl.pallas_call(
        functools.partial(feed_kernel, chunk),
        out_shape=outs,
        in_specs=[hbm()] * 6,
        out_specs=(hbm(),) * 4,
        scratch_shapes=[
            pltpu.VMEM((rows, model), bf16),
            pltpu.VMEM((rows, model), f32),
            pltpu.VMEM((rows, model), bf16),
            pltpu.VMEM(vectors.shape, bf16),
            pltpu.VMEM((1, ff_width), f32),
            pltpu.VMEM((count, model, chunk), bf16),
            pltpu.VMEM((count, model, chunk), bf16),
            pltpu.VMEM((model, model), bf16),
        ]
        + [pltpu.VMEM(out.shape, out.dtype) for out in outs]
        + [
            pltpu.VMEM((rows, model), f32),
            pltpu.VMEM((rows, model), f32),
            pltpu.SemaphoreType.DMA((6,)),
            pltpu.SemaphoreType.DMA((2 * count,)),
            pltpu.SemaphoreType.DMA((4,)),
        ],
        compiler_params=params(40),
        cost_estimate=cost(14),
        name="feed_forward",
    )(hidden, middle, cotangent, vectors, up_bias, matrices)


def units_kernel(rank_ref, *refs):
    blocks, (cotangent_in, bias_in, matrices_in) = refs[:4], refs[4:7]
    outs = refs[7 + EXTRA : 14 + EXTRA]
    hidden, cotangent, bias, up, down, act_ref, grad_ref, sums = refs[14 + EXTRA : 22 + EXTRA]
    w_sems, in_sems, out_sems = refs[22 + EXTRA :]
    seq, model = hidden.shape
    units = up.shape[1]
    half = units // 2
    rank = rank_ref[0]
    chip = rank // 2
    first = pl.multiple_of(chip * units, units)
    copies = [pltpu.make_async_copy(bias_in.at[:, pl.ds(first, units)], bias, w_sems.at[0])]
    for part, ref in ((0, up), (1, down)):
        source = pl.ds(pl.multiple_of((4 + 4 * part) * model + first, units), units)
        copies.append(
            pltpu.make_async_copy(matrices_in.at[:, source], ref, w_sems.at[1 + part])
        )
    start_all(copies)
    loads = []
    for i, k in enumerate((0, 4, 2, 6)):
        target = slice(i * BLOCK, (i + 1) * BLOCK)
        source = pl.ds(pl.multiple_of((rank ^ k) * BLOCK, BLOCK), BLOCK)
        loads += start_all(
            [
                pltpu.make_async_copy(blocks[i], hidden.at[target], in_sems.at[2 * i]),
                pltpu.make_async_copy(
                    cotangent_in.at[source], cotangent.at[target], in_sems.at[2 * i + 1]
                ),
            ]
        )
    wait_all(copies)
    sums[...] = jnp.zeros(sums.shape, f32)
    own = pl.multiple_of((rank % 2) * half, half)
    other = pl.multiple_of((1 - rank % 2) * half, half)
    out_copies = []
    for part in range(2):
        wait_all(loads[4 * part : 4 * part + 4])
        rows = slice(part * 2 * BLOCK, (part + 1) * 2 * BLOCK)
        pre = jnp.dot(hidden[rows, :], up[...], preferred_element_type=f32) + bias[...]
        act, slope = gelu_parts(pre)
        grad_act = jnp.dot(cotangent[rows, :], down[...], preferred_element_type=f32)
        act_ref[rows, :] = act.astype(bf16)
        grad_pre = (grad_act * slope).astype(bf16)
        grad_ref[rows, :] = grad_pre
        sums[...] += jnp.sum(grad_pre.astype(f32), axis=0, keepdims=True)
        pieces = []
        for source, targets in ((act_ref, outs[0:2]), (grad_ref, outs[2:4])):
            for lane, target in zip((other, own), targets):
                pieces.append((source.at[rows, pl.ds(lane, half)], target.at[rows]))
        for source, target in ((hidden, outs[4]), (cotangent, outs[5])):
            pieces.append((source.at[rows], target.at[rows]))
        out_copies += start_all(
            [
                pltpu.make_async_copy(source, target, out_sems.at[part * 6 + n])
                for n, (source, target) in enumerate(pieces)
            ]
        )
    copy = pltpu.make_async_copy(sums, outs[6], w_sems.at[0])
    copy.start()
    wait_all(out_copies + [copy])


def chip_units(rank, blocks, cotangent, up_bias, matrices, extra):
    rows, model = blocks[0].shape
    seq = 4 * rows
    units = up_bias.shape[1] // 4
    part = jax.ShapeDtypeStruct((seq, units // 2), bf16)
    full = jax.ShapeDtypeStruct((seq, model), bf16)
    return pl.pallas_call(
        units_kernel,
        out_shape=(part,) * 4 + (full,) * 2 + (jax.ShapeDtypeStruct((1, units), f32),),
        in_specs=[smem()] + [hbm()] * (7 + EXTRA),
        out_specs=(hbm(),) * 7,
        scratch_shapes=[
            pltpu.VMEM((seq, model), bf16),
            pltpu.VMEM((seq, model), bf16),
            pltpu.VMEM((1, units), f32),
            pltpu.VMEM((model, units), bf16),
            pltpu.VMEM((model, units), bf16),
            pltpu.VMEM((seq, units), bf16),
            pltpu.VMEM((seq, units), bf16),
            pltpu.VMEM((1, units), f32),
            pltpu.SemaphoreType.DMA((3,)),
            pltpu.SemaphoreType.DMA((8,)),
            pltpu.SemaphoreType.DMA((12,)),
        ],
        compiler_params=params(56),
        cost_estimate=cost(10),
        name="chip_units",
    )(rank, *blocks, cotangent, up_bias, matrices, extra)


def final_kernel(
    heads_ref, weights_ref, tokens_ref, grad_mid_ref, vectors_ref, *refs
):
    out_ref, sums_ref, acc_ref, lhs = refs[-4:]
    step = pl.program_id(0)
    lanes = heads_ref.shape[2] // 3

    @pl.when(step == 0)
    def _():
        acc_ref[...] = jnp.zeros(acc_ref.shape, f32)

    source = pl.ds(pl.multiple_of(step * lanes, lanes), lanes)
    for g in range(heads_ref.shape[0]):
        lhs[:, g * lanes : (g + 1) * lanes] = heads_ref[g, :, source]
    acc_ref[...] += lax.dot_general(lhs[...], weights_ref[...], NT, preferred_element_type=f32)

    @pl.when(step == pl.num_programs(0) - 1)
    def _():
        vecs = vectors_ref[...].astype(f32)
        grad = acc_ref[...]
        normed, inverse = normalize(tokens_ref[...].astype(f32))
        out_ref[...] = grad_mid_ref[...] + norm_pull(grad, vecs[0:1], normed, inverse)
        sums_ref[0:1, :] = jnp.sum(grad * normed, axis=0, keepdims=True)
        sums_ref[1:2, :] = jnp.sum(grad, axis=0, keepdims=True)


def token_gradient(heads, matrices, tokens, grad_mid, vectors, extras):
    rows, model = tokens.shape
    return pl.pallas_call(
        final_kernel,
        grid=(3,),
        out_shape=(
            jax.ShapeDtypeStruct((rows, model), f32),
            jax.ShapeDtypeStruct((2, model), f32),
        ),
        in_specs=[
            whole(heads.shape),
            pl.BlockSpec((model, model), lambda i: (0, i)),
            whole((rows, model)),
            whole((rows, model)),
            whole(vectors.shape),
        ]
        + [hbm()] * len(extras),
        out_specs=(whole((rows, model)), whole((2, model))),
        scratch_shapes=[pltpu.VMEM((rows, model), f32), pltpu.VMEM((rows, model), bf16)],
        compiler_params=params(40),
        cost_estimate=cost(6),
        name="token_gradient",
    )(heads, matrices, tokens, grad_mid, vectors, *extras)


def vector_pieces_kernel(rank_ref, one_ref, bias_ref, two_ref, units_ref, out_ref):
    rank = rank_ref[0]
    lanes = out_ref.shape[2]
    out_ref[...] = jnp.zeros(out_ref.shape, f32)
    copies = out_ref.shape[0] // 8
    for b in range(8):
        columns = slice(b * lanes, (b + 1) * lanes)
        for c in range(copies):
            out_ref[copies * b + c, 0:2, :] = one_ref[:, columns]
            out_ref[copies * b + c, 4:8, :] = two_ref[:, columns]
            out_ref[copies * b + c, pl.ds(8 + rank // 2, 1), :] = units_ref[:, columns]
    for c in range(copies):
        out_ref[copies * rank + c, 2:3, :] = bias_ref[:, 0:lanes]
        out_ref[copies * rank + c, 3:4, :] = bias_ref[:, 2 * lanes : 3 * lanes]


def vector_pieces(rank, one, bias, two, units, devices):
    lanes = one.shape[1] // 8
    return pl.pallas_call(
        vector_pieces_kernel,
        grid=(1,),
        out_shape=jax.ShapeDtypeStruct((devices, 16, lanes), f32),
        in_specs=[smem(), whole(one.shape), whole(bias.shape), whole(two.shape), whole(units.shape)],
        out_specs=whole((devices, 16, lanes)),
        compiler_params=params(40),
        cost_estimate=cost(1),
        name="vector_pieces",
    )(rank, one, bias, two, units)


def adam(master, first, second, gradient, decay_rate):
    correction = 1.0 - BETA**STEP
    moment = BETA * first + (1.0 - BETA) * gradient
    variance = BETA * second + (1.0 - BETA) * gradient * gradient
    direction = moment / correction / (jnp.sqrt(variance / correction) + ADAM_EPSILON)
    return moment, variance, master - RATE * (direction + decay_rate * master)


def vector_update_kernel(root, shard_ref, got_ref, states_ref, *refs):
    outs, copied_ref = refs[:3], refs[3]
    lanes = got_ref.shape[2]
    rows, own = outs[0].shape
    gradient = jnp.sum(got_ref[...], axis=0) * root
    shard = shard_ref[0]
    columns = lax.broadcasted_iota(jnp.int32, (16, lanes), 1) // own
    total = jnp.zeros((16, lanes), f32)
    for k in range(4):
        other = shard ^ k
        shifted = pltpu.roll(gradient, lax.rem(lanes - other * own, lanes), 1)[:rows, :own]
        values = adam(*[states_ref[k, n] for n in range(3)], shifted, 0.0)
        if k == 0:
            for ref, value in zip(outs, values):
                ref[...] = value
        wide = jnp.concatenate([values[2], jnp.zeros((rows, lanes - own), f32)], axis=1)
        wide = jnp.concatenate([wide, jnp.zeros((16 - rows, lanes), f32)], axis=0)
        total = jnp.where(columns == other, pltpu.roll(wide, other * own, 1), total)
    copied_ref[...] = total[:rows].astype(bf16)


def vector_update(shard, got, states, root):
    _, _, rows, own = states.shape
    lanes = got.shape[2]
    mine = jax.ShapeDtypeStruct((rows, own), f32)
    return pl.pallas_call(
        functools.partial(vector_update_kernel, root),
        grid=(1,),
        out_shape=(mine, mine, mine, jax.ShapeDtypeStruct((rows, lanes), bf16)),
        in_specs=[smem(), whole(got.shape), whole(states.shape)],
        out_specs=(whole((rows, own)),) * 3 + (whole((rows, lanes)),),
        compiler_params=params(40),
        cost_estimate=cost(1),
        name="vector_update",
    )(shard, got, states)


def update_kernel(root, got_ref, *refs):
    states, outs = refs[:3], refs[-5:-2]
    copied_ref, gradient_ref = refs[-2:]
    lanes = got_ref.shape[2]
    for g in range(got_ref.shape[0]):
        gradient_ref[:, g * lanes : (g + 1) * lanes] = got_ref[g].astype(f32)
    values = adam(*[ref[...] for ref in states], gradient_ref[...] * root, DECAY_RATE)
    for ref, value in zip(outs, values):
        ref[...] = value
    copied_ref[...] = values[2].astype(bf16)


def matrix_update(got, states, previous, extra, first, parts, root, name):
    groups, rows, packed = got.shape
    lanes = packed // parts
    block = groups * lanes
    total = states[0].shape[1]
    start = first // block
    state = pl.BlockSpec((rows, block), lambda i: (0, start + i))
    return pl.pallas_call(
        functools.partial(update_kernel, root),
        grid=(parts,),
        out_shape=(jax.ShapeDtypeStruct((rows, total), f32),) * 3
        + (jax.ShapeDtypeStruct((rows, parts * block), bf16),),
        in_specs=[pl.BlockSpec((groups, rows, lanes), lambda i: (0, 0, i))]
        + [state] * 3
        + [hbm()] * (len(previous) + 1),
        out_specs=(state,) * 3 + (pl.BlockSpec((rows, block), lambda i: (0, i)),),
        scratch_shapes=[pltpu.VMEM((rows, block), f32)],
        input_output_aliases={4 + k: k for k in range(len(previous))},
        compiler_params=params(56),
        cost_estimate=cost(4),
        name=name,
    )(got, *states, *previous, extra)


def place_kernel(shard_ref, *refs):
    out_ref = refs[-1]
    rows = refs[0].shape[0]
    for k in range(4):
        place = pl.multiple_of((shard_ref[0] ^ k) * rows, rows)
        out_ref[pl.ds(place, rows), :] = refs[k][...]


def place_copies(shard, pieces, previous, first, total, name):
    rows, columns = pieces[0].shape
    block = 2048
    return pl.pallas_call(
        place_kernel,
        grid=(columns // block,),
        out_shape=jax.ShapeDtypeStruct((4 * rows, total), bf16),
        in_specs=[smem()]
        + [pl.BlockSpec((rows, block), lambda i: (0, i))] * 4
        + [hbm()] * len(previous),
        out_specs=pl.BlockSpec((4 * rows, block), lambda i: (0, first // block + i)),
        input_output_aliases={5: 0} if previous else {},
        compiler_params=params(40),
        cost_estimate=cost(2),
        name=name,
    )(shard, *pieces, *previous)


def fits_sequence_plan(mesh):
    return mesh.shape["dp"] == 4 and mesh.shape["ctx"] == 2 and mesh.shape["shard"] == 4


EVERY = ("dp", "ctx", "shard")
SEQUENCE = ("ctx", "shard")


def swap(array, axis, bit):
    count = lax.axis_size(axis)
    return lax.ppermute(array, axis, [(i, i ^ bit) for i in range(count)])


def gather_blocks(block, ready):
    over_ctx = swap(block, "ctx", 1)
    over_y = swap(block, "shard", 2)
    over_core = swap(block, "shard", 1)
    even = (lax.axis_index("shard") % 2 == 0) & ready
    relay = jnp.where(even, over_ctx, over_y)
    opposite = lax.ppermute(relay, SEQUENCE, [(i, i ^ (4 if i % 2 else 2)) for i in range(8)])
    ctx_core = swap(over_ctx, "shard", 1)
    y_core = swap(over_y, "shard", 1)
    opposite_core = swap(opposite, "shard", 1)
    return relay, [
        block, over_core, over_y, y_core, over_ctx, ctx_core, opposite, opposite_core
    ]


def gather_same_core(block):
    over_ctx = swap(block, "ctx", 1)
    over_y = swap(block, "shard", 2)
    opposite = lax.ppermute(block, SEQUENCE, [(i, i ^ 6) for i in range(8)])
    return [block, over_ctx, over_y, opposite]


def gather_rows(array):
    return lax.all_gather(array, SEQUENCE, axis=0, tiled=True)


def exchange(array, axes=SEQUENCE):
    return lax.all_to_all(array, axes, 0, 0, tiled=True)


def dot_tn(left, right):
    return lax.dot_general(left, right, (((0,), (0,)), ((), ())), preferred_element_type=f32)


def dot_nt(left, right):
    return lax.dot_general(left, right, NT, preferred_element_type=f32)


def dot_nn(left, right):
    return jnp.dot(left, right, preferred_element_type=f32)


def row_block(array, index):
    rows = array.shape[0] // 4
    return lax.dynamic_slice_in_dim(array, index % 4 * rows, rows, 0)


def shift_dp(array, distance):
    return lax.ppermute(array, "dp", [(i, (i + distance) % 4) for i in range(4)])


def sum_over_dp(total, depth):
    result = row_block(total, depth)
    for k in range(1, 4):
        result += shift_dp(row_block(total, depth + k).astype(bf16), k).astype(f32)
    return result.astype(bf16)


def gather_shards(array):
    over_core = swap(array, "shard", 1)
    over_y = swap(array, "shard", 2)
    return [array, over_core, over_y, swap(over_y, "shard", 1)]


def sequence_shards(
    tokens,
    cotangent,
    picture_starts,
    matrices,
    vectors,
    master_matrices,
    master_vectors,
    first_matrices,
    first_vectors,
    second_matrices,
    second_vectors,
):
    row_count, width = tokens.shape
    ff_width = (matrices.shape[1] - 4 * width) // 2
    group = 8
    shard = lax.axis_index("shard")
    rank = lax.axis_index("ctx") * 4 + shard
    depth = lax.axis_index("dp")
    lanes = width // group
    units = ff_width // group
    own_rows = master_matrices.shape[0]
    seq = group * row_count
    head = rank * 2 + jnp.arange(2)
    slopes = jnp.exp2(-8.0 * (head.astype(f32) + 1.0) / HEADS)
    rank_array = rank.astype(jnp.int32).reshape(1)
    shard_array = shard.astype(jnp.int32).reshape(1)
    vector_rows = vectors.astype(f32)
    up_bias = vector_rows[8:].reshape(1, ff_width)

    hidden = norm_one(tokens, vectors)
    with jax.named_scope("prepare"):
        pattern = key_pattern(picture_starts, slopes, seq, lanes)
    with jax.named_scope("gather_hidden"):
        ready = pattern[0, 0, lanes // 2 + 3] == 1.0
        relay, hidden_blocks = gather_blocks(hidden, ready)
    with jax.named_scope("gather_cotangent"):
        zero = relay[0, 0] * 0
        cotangent_late = cotangent + zero
        cotangent_all = gather_rows(cotangent_late)
    attended_heads, attended_wide, *saved, hidden_all = attention_forward(
        hidden_blocks,
        matrices,
        vectors,
        pattern,
        rank_array,
        picture_starts,
        slopes,
        cotangent_late,
    )
    with jax.named_scope("attended_exchange"):
        attended_got = exchange(attended_heads)
    with jax.named_scope("gather_attended"):
        attended_all = gather_rows(attended_heads).reshape(group, seq, lanes)
    with jax.named_scope("transpose_keys"):
        half = lanes // 2
        keys_low = saved[1]
        keys_transposed = jnp.concatenate(
            [keys_low[0, :, :half], keys_low[1, :, half:]], axis=1
        ).T
    attended, middle, hidden_two = project_norm(
        attended_got, tokens, matrices, vectors, keys_transposed
    )
    with jax.named_scope("gather_hidden_two"):
        hidden_two_blocks = gather_same_core(hidden_two)
    layer_output, grad_mid, grad_out, sums_two = feed_forward(
        hidden_two, up_bias, middle, cotangent, vectors, matrices
    )
    with jax.named_scope("grad_attended_exchange"):
        grad_got = exchange(grad_out)
    act_other, act_own, grad_other, grad_own, hidden_rows, cotangent_rows, unit_sums = chip_units(
        rank_array, hidden_two_blocks, cotangent_all, up_bias, matrices, grad_out
    )
    with jax.named_scope("gather_states"):
        states_own = jnp.stack([master_vectors, first_vectors, second_vectors])
        states_own, act_other, act_own, grad_other, grad_own = gate(
            [states_own, act_other, act_own, grad_other, grad_own], [grad_got]
        )
        states = jnp.stack(gather_shards(states_own))
    with jax.named_scope("grad_feed"):
        other_up = swap(dot_tn(hidden_rows, grad_other).astype(bf16), "shard", 1)
        other_down = swap(dot_tn(cotangent_rows, act_other).astype(bf16), "shard", 1)
        early_up = (dot_tn(hidden_rows, grad_own) + other_up.astype(f32)).astype(bf16)
        early_down = (dot_tn(cotangent_rows, act_own) + other_down.astype(f32)).astype(bf16)
        early = jnp.concatenate([early_up, early_down], axis=1)
        early_sum = lax.psum_scatter(early, "dp", scatter_dimension=0, tiled=True)
    grad_abs, grad_rel, bias_sums = attention_backward(
        (*saved, keys_transposed), attended_wide, grad_got, rank_array, picture_starts, early
    )
    with jax.named_scope("grad_qkv_exchange"):
        grad_tokens = exchange(grad_abs.reshape(group, row_count, 3 * lanes))
    with jax.named_scope("grad_late"):
        grad_mid_columns = grad_got[:, :, lanes:].reshape(seq, lanes)
        grad_proj = lax.dot_general(
            attended_all,
            grad_mid_columns,
            (((1,), (0,)), ((), ())),
            preferred_element_type=f32,
        ).reshape(width, lanes)
        late = jnp.concatenate([dot_tn(hidden_all, grad_rel), grad_proj], axis=1)
        late_sum = sum_over_dp(late, depth)
    with jax.named_scope("early_rows"):
        (early_sum,) = gate([early_sum], [grad_tokens])
        early_got = exchange(early_sum.reshape(group, own_rows, 2 * units))
    token_grads, sums_one = token_gradient(
        grad_tokens, matrices, tokens, grad_mid, vectors, [late_sum]
    )
    with jax.named_scope("late_rows"):
        (late_sum,) = gate([late_sum], [early_got, sums_one])
        late_got = exchange(late_sum.reshape(group, own_rows, 4 * lanes))
    root = (row_count * lax.axis_size("dp") * group) ** (-0.5)
    matrix_states = (master_matrices, first_matrices, second_matrices)
    *early_states, early_copy = matrix_update(
        early_got, matrix_states, (), token_grads, 4 * width, 2, root, "early_update"
    )
    with jax.named_scope("early_copies"):
        early_copied = gather_shards(early_copy)
    with jax.named_scope("grad_vectors"):
        pieces = vector_pieces(rank_array, sums_one, bias_sums, sums_two, unit_sums, 32)
        (pieces,) = gate([pieces], [late_got])
        vectors_got = exchange(pieces, EVERY)
    moment_w, variance_w, updated_w, late_copy = matrix_update(
        late_got, matrix_states, early_states, early_copy, 0, 4, root, "late_update"
    )
    with jax.named_scope("late_copies"):
        late_copied = gather_shards(late_copy)
    total = matrices.shape[1]
    copied_w = place_copies(shard_array, early_copied, (), 4 * width, total, "place_early")
    copied_w = place_copies(shard_array, late_copied, (copied_w,), 0, total, "place_late")
    moment_v, variance_v, updated_v, copied_v = vector_update(
        shard_array, vectors_got, states, root
    )
    return (
        layer_output,
        token_grads,
        moment_w,
        moment_v,
        variance_w,
        variance_v,
        updated_w,
        updated_v,
        copied_w,
        copied_v,
    )


def solution(mesh):
    in_specs = (
        P(("dp", "ctx", "shard"), None),
        P(("dp", "ctx", "shard"), None),
        P("dp", None),
        P(),
        P(),
        P(("dp", "ctx", "shard"), None),
        P(None, ("dp", "ctx", "shard")),
        P(("dp", "ctx", "shard"), None),
        P(None, ("dp", "ctx", "shard")),
        P(("dp", "ctx", "shard"), None),
        P(None, ("dp", "ctx", "shard")),
    )
    out_specs = (
        P(("dp", "ctx", "shard"), None),
        P(("dp", "ctx", "shard"), None),
        P(("dp", "ctx", "shard"), None),
        P(None, ("dp", "ctx", "shard")),
        P(("dp", "ctx", "shard"), None),
        P(None, ("dp", "ctx", "shard")),
        P(("dp", "ctx", "shard"), None),
        P(None, ("dp", "ctx", "shard")),
        P(("dp", "ctx"), None),
        P(None, ("dp", "ctx")),
    )
    body = sequence_shards if fits_sequence_plan(mesh) else general_shards
    return jax.shard_map(body, mesh=mesh, in_specs=in_specs, out_specs=out_specs, check_vma=False)
```

```python
import functools
import math

import jax
import jax.numpy as jnp
from jax import lax
from jax.experimental import pallas as pl
from jax.experimental.pallas import tpu as pltpu
from jax.sharding import PartitionSpec as P

HEADS = 16
PIC = 256
STEP = 2


EPSILON = 1e-05
NEGATIVE = -1e30
BETA = 0.5
RATE = 0.03
DECAY_RATE = 0.1
ADAM_EPSILON = 1e-08


def token_tags(index, start_list, block_len):
    after = index[:, None] - start_list[None, :]
    inside = (after >= 0) & (after < block_len)
    offsets = jnp.sum(jnp.clip(after, 0, block_len - 1), axis=1)
    number = jnp.arange(1, start_list.shape[0] + 1, dtype=jnp.int32)
    picture = jnp.sum(jnp.where(inside, number[None, :], 0), axis=1) - 1
    return (index - offsets, picture)


def block_scores(query_heads, query_index, key_heads, key_index, start_list, slopes, factor):
    query_pos, query_pic = token_tags(query_index, start_list, PIC)
    key_pos, key_pic = token_tags(key_index, start_list, PIC)
    raw = jnp.einsum("qhd,khd->hqk", query_heads, key_heads, preferred_element_type=jnp.float32)
    distance = (query_pos[:, None] - key_pos[None, :]).astype(jnp.float32)
    logits = raw * factor - slopes[:, None, None] * distance[None, :, :]
    same = (query_pic[:, None] == key_pic[None, :]) & (query_pic[:, None] >= 0)
    visible = (key_index[None, :] <= query_index[:, None]) | same
    return (logits, visible[None, :, :])


def layer_norm(inputs):
    centered = inputs - jnp.mean(inputs, axis=1, keepdims=True)
    inverse_std = lax.rsqrt(jnp.mean(centered * centered, axis=1, keepdims=True) + EPSILON)
    return (centered * inverse_std, inverse_std)


def norm_backward(grad_normed, gain, normed, inverse_std):
    scaled = grad_normed * gain
    return inverse_std * (
        scaled
        - jnp.mean(scaled, axis=1, keepdims=True)
        - normed * jnp.mean(scaled * normed, axis=1, keepdims=True)
    )


def activate(value):
    return jax.nn.gelu(value, approximate=True)


def regroup(array, dim, outer, inner):
    shape = array.shape
    split = array.reshape(
        shape[:dim] + (outer, inner, shape[dim] // (outer * inner)) + shape[dim + 1 :]
    )
    return jnp.swapaxes(split, dim, dim + 1).reshape(shape)


def adam_update(master, first, second, gradient, correction, decay_rate):
    moment = BETA * first + (1.0 - BETA) * gradient
    variance = BETA * second + (1.0 - BETA) * gradient * gradient
    direction = moment / correction / (jnp.sqrt(variance / correction) + ADAM_EPSILON)
    return (moment, variance, master - RATE * (direction + decay_rate * master))


def general_shards(
    tokens,
    cotangent,
    picture_starts,
    matrices,
    vectors,
    master_matrices,
    master_vectors,
    first_matrices,
    first_vectors,
    second_matrices,
    second_vectors,
):
    row_count, model_width = tokens.shape
    ff_width = (matrices.shape[1] - 4 * model_width) // 2
    head_count = HEADS
    head_width = model_width // head_count
    factor = head_width ** (-0.5)
    group_size = lax.axis_size("ctx") * lax.axis_size("shard")
    group_rank = lax.axis_index("ctx") * lax.axis_size("shard") + lax.axis_index("shard")
    seq_length = row_count * group_size
    first_row = group_rank * row_count
    start_list = picture_starts[0]
    slopes = jnp.exp2(-8.0 * (jnp.arange(head_count, dtype=jnp.float32) + 1.0) / head_count)
    block_rows = math.gcd(seq_length, 512)
    block_count = seq_length // block_rows
    w_qkv = matrices[:, : 3 * model_width]
    w_proj = matrices[:, 3 * model_width : 4 * model_width]
    w_up = matrices[:, 4 * model_width : 4 * model_width + ff_width]
    w_down = matrices[:, 4 * model_width + ff_width :]
    inputs = tokens.astype(jnp.float32)
    vector_rows = vectors.astype(jnp.float32)
    up_bias = vector_rows[8:].reshape(ff_width)
    normed, inverse_std = layer_norm(inputs)
    hidden = (normed * vector_rows[0] + vector_rows[1]).astype(jnp.bfloat16)
    projected = jnp.dot(hidden, w_qkv, preferred_element_type=jnp.float32)
    queries = (projected[:, :model_width] + vector_rows[2]).astype(jnp.bfloat16)
    kv_bias = jnp.concatenate([jnp.zeros((model_width,), jnp.float32), vector_rows[3]])
    kv_local = (projected[:, model_width:] + kv_bias).astype(jnp.bfloat16)
    gathered = lax.all_gather(kv_local, ("ctx", "shard"), axis=0, tiled=True)
    query_index = first_row + jnp.arange(row_count, dtype=jnp.int32)
    query_heads = queries.reshape(row_count, head_count, head_width)

    def key_block(index):
        piece = lax.dynamic_slice_in_dim(gathered, index * block_rows, block_rows, 0)
        key_heads = piece[:, :model_width].reshape(block_rows, head_count, head_width)
        value_heads = piece[:, model_width:].reshape(block_rows, head_count, head_width)
        key_index = index * block_rows + jnp.arange(block_rows, dtype=jnp.int32)
        logits, visible = block_scores(
            query_heads, query_index, key_heads, key_index, start_list, slopes, factor
        )
        return (logits, visible, key_heads, value_heads)

    def running_total(index, carry):
        highest, total = carry
        logits, visible, key_heads, value_heads = key_block(index)
        masked = jnp.where(visible, logits, NEGATIVE)
        updated = jnp.maximum(highest, jnp.max(masked, axis=2))
        weights = jnp.where(visible, jnp.exp(logits - updated[:, :, None]), 0.0)
        return (updated, total * jnp.exp(highest - updated) + jnp.sum(weights, axis=2))

    start_high = jnp.full((head_count, row_count), NEGATIVE, jnp.float32)
    start_total = jnp.zeros((head_count, row_count), jnp.float32)
    highest, total = lax.fori_loop(0, block_count, running_total, (start_high, start_total))
    log_total = highest + jnp.log(total)

    def weighted_sum(index, accum):
        logits, visible, key_heads, value_heads = key_block(index)
        probs = jnp.where(visible, jnp.exp(logits - log_total[:, :, None]), 0.0).astype(
            jnp.bfloat16
        )
        return accum + jnp.einsum(
            "hqk,khd->qhd", probs, value_heads, preferred_element_type=jnp.float32
        )

    attended = lax.fori_loop(
        0, block_count, weighted_sum, jnp.zeros((row_count, head_count, head_width), jnp.float32)
    )
    attended_low = attended.reshape(row_count, model_width).astype(jnp.bfloat16)
    middle = (
        inputs + jnp.dot(attended_low, w_proj, preferred_element_type=jnp.float32) + vector_rows[4]
    )
    normed_two, inverse_two = layer_norm(middle)
    hidden_two = (normed_two * vector_rows[5] + vector_rows[6]).astype(jnp.bfloat16)
    pre_act = jnp.dot(hidden_two, w_up, preferred_element_type=jnp.float32) + up_bias
    act_low = activate(pre_act).astype(jnp.bfloat16)
    down_out = lax.dot_general(
        act_low, w_down, (((1,), (1,)), ((), ())), preferred_element_type=jnp.float32
    )
    layer_output = (middle + down_out + vector_rows[7]).astype(jnp.bfloat16)
    upstream = cotangent.astype(jnp.float32)
    grad_act = jnp.dot(cotangent, w_down, preferred_element_type=jnp.float32)
    gelu_value, gelu_pull = jax.vjp(activate, pre_act)
    grad_pre = gelu_pull(grad_act)[0].astype(jnp.bfloat16)
    grad_up_w = lax.dot_general(
        hidden_two, grad_pre, (((0,), (0,)), ((), ())), preferred_element_type=jnp.float32
    )
    grad_down_w = lax.dot_general(
        cotangent, act_low, (((0,), (0,)), ((), ())), preferred_element_type=jnp.float32
    )
    grad_two = lax.dot_general(
        grad_pre, w_up, (((1,), (1,)), ((), ())), preferred_element_type=jnp.float32
    )
    grad_mid = upstream + norm_backward(grad_two, vector_rows[5], normed_two, inverse_two)
    grad_mid_low = grad_mid.astype(jnp.bfloat16)
    grad_proj = lax.dot_general(
        attended_low, grad_mid_low, (((0,), (0,)), ((), ())), preferred_element_type=jnp.float32
    )
    grad_out = lax.dot_general(
        grad_mid_low, w_proj, (((1,), (1,)), ((), ())), preferred_element_type=jnp.float32
    ).astype(jnp.bfloat16)
    grad_heads = grad_out.reshape(row_count, head_count, head_width)
    delta = jnp.sum(grad_heads.astype(jnp.float32) * attended, axis=2).T

    def score_grads(index):
        logits, visible, key_heads, value_heads = key_block(index)
        probs = jnp.where(visible, jnp.exp(logits - log_total[:, :, None]), 0.0)
        product = jnp.einsum(
            "qhd,khd->hqk", grad_heads, value_heads, preferred_element_type=jnp.float32
        )
        grad_logits = (probs * (product - delta[:, :, None])).astype(jnp.bfloat16)
        return (probs, grad_logits, key_heads)

    def both_grads(index, carry):
        accum, key_terms = carry
        probs, grad_logits, key_heads = score_grads(index)
        accum = (
            accum
            + jnp.einsum("hqk,khd->qhd", grad_logits, key_heads, preferred_element_type=jnp.float32)
            * factor
        )
        grad_key = (
            jnp.einsum("hqk,qhd->khd", grad_logits, query_heads, preferred_element_type=jnp.float32)
            * factor
        )
        grad_value = jnp.einsum(
            "hqk,qhd->khd",
            probs.astype(jnp.bfloat16),
            grad_heads,
            preferred_element_type=jnp.float32,
        )
        term = jnp.concatenate(
            [
                grad_key.reshape(block_rows, model_width),
                grad_value.reshape(block_rows, model_width),
            ],
            axis=1,
        )
        return (accum, lax.dynamic_update_slice_in_dim(key_terms, term, index * block_rows, 0))

    grad_query, key_terms = lax.fori_loop(
        0,
        block_count,
        both_grads,
        (
            jnp.zeros((row_count, head_count, head_width), jnp.float32),
            jnp.zeros((seq_length, 2 * model_width), jnp.float32),
        ),
    )
    own_key_grads = lax.psum_scatter(key_terms, ("ctx", "shard"), scatter_dimension=0, tiled=True)
    grad_qkv = jnp.concatenate(
        [grad_query.reshape(row_count, model_width), own_key_grads], axis=1
    ).astype(jnp.bfloat16)
    grad_qkv_weights = lax.dot_general(
        hidden, grad_qkv, (((0,), (0,)), ((), ())), preferred_element_type=jnp.float32
    )
    grad_hidden = lax.dot_general(
        grad_qkv, w_qkv, (((1,), (1,)), ((), ())), preferred_element_type=jnp.float32
    )
    query_bias_grad = jnp.sum(grad_qkv[:, :model_width].astype(jnp.float32), axis=0)
    value_bias_grad = jnp.sum(grad_qkv[:, 2 * model_width :].astype(jnp.float32), axis=0)
    grad_vectors = jnp.concatenate(
        [
            jnp.stack(
                [
                    jnp.sum(grad_hidden * normed, axis=0),
                    jnp.sum(grad_hidden, axis=0),
                    query_bias_grad,
                    value_bias_grad,
                    jnp.sum(grad_mid, axis=0),
                    jnp.sum(grad_two * normed_two, axis=0),
                    jnp.sum(grad_two, axis=0),
                    jnp.sum(upstream, axis=0),
                ]
            ),
            jnp.sum(grad_pre.astype(jnp.float32), axis=0).reshape(
                ff_width // model_width, model_width
            ),
        ],
        axis=0,
    )
    token_grads = grad_mid + norm_backward(grad_hidden, vector_rows[0], normed, inverse_std)
    grad_matrix = jnp.concatenate([grad_qkv_weights, grad_proj, grad_up_w, grad_down_w], axis=1)
    shard_count = lax.axis_size("shard")
    replicas = lax.axis_size("dp") * lax.axis_size("ctx")
    part_matrix, part_vec = (
        lax.psum_scatter(
            regroup(grad_matrix, 0, replicas, shard_count), "shard", scatter_dimension=0, tiled=True
        ),
        lax.psum_scatter(
            regroup(grad_vectors, 1, replicas, shard_count),
            "shard",
            scatter_dimension=1,
            tiled=True,
        ),
    )
    part_matrix, part_vec = (
        lax.psum_scatter(part_matrix, ("dp", "ctx"), scatter_dimension=0, tiled=True),
        lax.psum_scatter(part_vec, ("dp", "ctx"), scatter_dimension=1, tiled=True),
    )
    root = (row_count * lax.axis_size("dp") * group_size) ** (-0.5)
    correction = 1.0 - BETA**STEP
    moment_w, variance_w, updated_w = adam_update(
        master_matrices, first_matrices, second_matrices, part_matrix * root, correction, DECAY_RATE
    )
    moment_v, variance_v, updated_v = adam_update(
        master_vectors, first_vectors, second_vectors, part_vec * root, correction, 0.0
    )
    copied_w, copied_v = (
        lax.all_gather(updated_w.astype(jnp.bfloat16), "shard", axis=0, tiled=True),
        lax.all_gather(updated_v.astype(jnp.bfloat16), "shard", axis=1, tiled=True),
    )
    return (
        layer_output,
        token_grads,
        moment_w,
        moment_v,
        variance_w,
        variance_v,
        updated_w,
        updated_v,
        copied_w,
        copied_v,
    )


BLOCK = 256
EXTRA = 1
f32 = jnp.float32
bf16 = jnp.bfloat16
NT = (((1,), (1,)), ((), ()))
GELU_SCALE = math.sqrt(2.0 / math.pi)
GELU_CUBE = 0.044715


def split3(value):
    high = value.astype(bf16).astype(f32)
    rest = value - high
    middle = rest.astype(bf16).astype(f32)
    low = (rest - middle).astype(bf16).astype(f32)
    return high, middle, low


def positions(index, starts_ref, count):
    result = index
    for b in range(count):
        result = result - jnp.clip(index - starts_ref[0, b], 0, PIC - 1)
    return result.astype(f32)


def limits(index, starts_ref, count):
    result = index + 1
    for b in range(count):
        start = starts_ref[0, b]
        result = jnp.where((index >= start) & (index < start + PIC), start + PIC, result)
    return result


def head_lanes(shape, h, width):
    lane = lax.broadcasted_iota(jnp.int32, shape, 1)
    inside = (lane < width) if h == 0 else (lane >= width)
    return inside, lane - width if h == 0 else lane


def pick(spare, values):
    out = jnp.zeros(spare.shape, f32)
    for e, value in enumerate(values):
        out = jnp.where(spare == e, value, out)
    return out


def smem():
    return pl.BlockSpec(memory_space=pltpu.SMEM)


def vmem():
    return pl.BlockSpec(memory_space=pltpu.VMEM)


def anywhere():
    return pl.BlockSpec(memory_space=pl.ANY)


def hbm():
    return pl.BlockSpec(memory_space=pltpu.HBM)


def params(mebibytes):
    return pltpu.CompilerParams(vmem_limit_bytes=mebibytes * 2**20)


def cost(microseconds):
    return pl.CostEstimate(
        flops=int(microseconds * 1.0e9), bytes_accessed=0, transcendentals=0
    )


def start_all(copies):
    for copy in copies:
        copy.start()
    return copies


def wait_all(copies):
    for copy in copies:
        copy.wait()


def pattern_kernel(width, count, starts_ref, slopes_ref, out_ref):
    lanes = out_ref.shape[2]
    step = pl.program_id(0)
    index = lax.broadcasted_iota(jnp.int32, (BLOCK, lanes), 0) + step * BLOCK
    pos = positions(index, starts_ref, count)
    for h in range(2):
        _, spare = head_lanes((BLOCK, lanes), h, width)
        parts = split3(pos * slopes_ref[h])
        out_ref[h] = pick(spare, parts + (1.0, 1.0, 1.0)).astype(bf16)


def key_pattern(starts, slopes, seq, lanes):
    return pl.pallas_call(
        functools.partial(pattern_kernel, lanes // 2, starts.shape[1]),
        grid=(seq // BLOCK,),
        out_shape=jax.ShapeDtypeStruct((2, seq, lanes), bf16),
        in_specs=[smem()] * 2,
        out_specs=pl.BlockSpec((2, BLOCK, lanes), lambda i: (0, i, 0)),
        compiler_params=params(40),
        cost_estimate=cost(3),
        name="key_pattern",
    )(starts, slopes)


def forward_kernel(width, tile, count, rank_ref, starts_ref, slopes_ref, *refs):
    blocks = refs[:8]
    matrices_ref, vectors_ref, pattern_in = refs[8:11]
    att_out, wide_out, q_out, k_out, v_out, all_out = refs[11 + EXTRA : 17 + EXTRA]
    hid, wts, vecs, pattern, qa, ka, va, att, wide, best_ref, acc_ref = refs[17 + EXTRA : 28 + EXTRA]
    in_sems, w_sems, hid_sems, out_sems = refs[28 + EXTRA :]
    seq, lanes = wide.shape
    model = hid.shape[1]
    rank = rank_ref[0]
    factor = width**-0.5
    w_copies = []
    for part in range(3):
        columns = pl.ds(pl.multiple_of(part * model + rank * lanes, lanes), lanes)
        w_copies.append(
            pltpu.make_async_copy(
                matrices_ref.at[:, columns],
                wts.at[:, part * lanes : (part + 1) * lanes],
                w_sems.at[part],
            )
        )
    w_copies.append(pltpu.make_async_copy(vectors_ref, vecs, w_sems.at[3]))
    start_all(w_copies)
    in_copies = start_all(
        [
            pltpu.make_async_copy(
                blocks[k], hid.at[k * BLOCK : (k + 1) * BLOCK], in_sems.at[k]
            )
            for k in range(8)
        ]
    )
    pattern_copy = pltpu.make_async_copy(pattern_in, pattern, w_sems.at[4])
    pattern_copy.start()
    wait_all(w_copies)
    gains = vecs[...].astype(f32)
    bias = vecs[:, pl.ds(pl.multiple_of(rank * lanes, lanes), lanes)].astype(f32)
    out_copies = []
    ones = []
    for h in range(2):
        inside, spare = head_lanes((BLOCK, lanes), h, width)
        ones.append((inside, jnp.where(spare < 3, 1.0, 0.0)))
    for pair in range(4):
        first = 2 * pair
        for k in (first, first + 1):
            in_copies[k].wait()
        both = slice(first * BLOCK, (first + 2) * BLOCK)
        normed, _ = normalize(hid[both, :].astype(f32))
        hid[both, :] = (normed * gains[0:1] + gains[1:2]).astype(bf16)
        for k in (first, first + 1):
            rows = slice(k * BLOCK, (k + 1) * BLOCK)
            dst = pl.ds(pl.multiple_of((k ^ rank) * BLOCK, BLOCK), BLOCK)
            copy = pltpu.make_async_copy(hid.at[rows], all_out.at[dst], hid_sems.at[k])
            copy.start()
            out_copies.append(copy)
        value = jnp.dot(hid[both, :], wts[...], preferred_element_type=f32)
        if pair == 0:
            pattern_copy.wait()
        for k in (first, first + 1):
            local = slice((k - first) * BLOCK, (k - first + 1) * BLOCK)
            dst = pl.ds(pl.multiple_of((k ^ rank) * BLOCK, BLOCK), BLOCK)
            q = (value[local, 0:lanes] + bias[2:3]).astype(bf16).astype(f32) * factor
            key = value[local, lanes : 2 * lanes]
            v = value[local, 2 * lanes : 3 * lanes] + bias[3:4]
            for h in range(2):
                inside, spare_ones = ones[h]
                qa[h, dst, :] = jnp.where(inside, q, spare_ones).astype(bf16)
                ka[h, dst, :] = jnp.where(inside, key, pattern[h, dst, :].astype(f32)).astype(bf16)
                va[h, dst, :] = jnp.where(inside, v, spare_ones).astype(bf16)
    out_copies += start_all(
        [
            pltpu.make_async_copy(ka, k_out, out_sems.at[0]),
            pltpu.make_async_copy(va, v_out, out_sems.at[1]),
        ]
    )

    def scores(h, queries, keys):
        return lax.dot_general(
            qa[h, queries, :], ka[h, keys, :], NT, preferred_element_type=f32
        )

    def mask(first_row, first_column, shape):
        rows = lax.broadcasted_iota(jnp.int32, (shape[0], 1), 0) + first_row
        columns = lax.broadcasted_iota(jnp.int32, shape, 1) + first_column
        return columns < limits(rows, starts_ref, count)

    def raise_best(h, local, value):
        best = best_ref[h, local, :]
        for c in range(value.shape[1] // lanes):
            best = jnp.maximum(best, value[:, c * lanes : (c + 1) * lanes])
        best_ref[h, local, :] = best

    def add_mixed(h, local, value, keys):
        acc_ref[h, local, :] += jnp.dot(
            value.astype(bf16), va[h, keys, :], preferred_element_type=f32
        )

    def with_shift(h, rows, shift):
        inside, spare = head_lanes((tile, lanes), h, width)
        parts = split3(-jnp.broadcast_to(shift, (tile, lanes)))
        value = qa[h, rows, :].astype(f32)
        for e in range(3):
            value = jnp.where(spare == 3 + e, parts[e], value)
        qa[h, rows, :] = value.astype(bf16)

    for i in range(seq // tile):
        base = i * tile
        end = base + tile
        rows = slice(base, end)
        whole = slice(0, tile)
        edges = [(rows, rows, whole)]
        if end < seq:
            edges.append((slice(end - PIC, end), slice(end, end + PIC), slice(tile - PIC, tile)))
        best_ref[...] = jnp.full(best_ref.shape, NEGATIVE, f32)
        acc_ref[...] = jnp.zeros(acc_ref.shape, f32)

        def find(j, carry):
            keys = pl.ds(pl.multiple_of(j * tile, tile), tile)
            for h in range(2):
                raise_best(h, whole, scores(h, rows, keys))
            return carry

        if i > 0:
            lax.fori_loop(0, i, find, 0)
        for queries, keys, local in edges:
            seen = mask(
                queries.start, keys.start, (queries.stop - queries.start, keys.stop - keys.start)
            )
            for h in range(2):
                raise_best(h, local, jnp.where(seen, scores(h, queries, keys), NEGATIVE))
        best = [jnp.max(best_ref[h], axis=1, keepdims=True) for h in range(2)]
        for h in range(2):
            with_shift(h, rows, best[h])

        def mix(j, carry):
            keys = pl.ds(pl.multiple_of(j * tile, tile), tile)
            for h in range(2):
                add_mixed(h, whole, jnp.exp(scores(h, rows, keys)), keys)
            return carry

        if i > 0:
            lax.fori_loop(0, i, mix, 0)
        for queries, keys, local in edges:
            seen = mask(
                queries.start, keys.start, (queries.stop - queries.start, keys.stop - keys.start)
            )
            for h in range(2):
                add_mixed(
                    h, local, jnp.where(seen, jnp.exp(scores(h, queries, keys)), 0.0), keys
                )
        outs = []
        for h in range(2):
            acc = acc_ref[h]
            column = width if h == 0 else 0
            total = acc[:, column : column + 1]
            outs.append(acc / total)
            with_shift(h, rows, best[h] + jnp.log(total))
        inside, _ = head_lanes((tile, lanes), 0, width)
        out = jnp.where(inside, outs[0], outs[1])
        wide[rows, :] = out
        count_here = tile // BLOCK
        groups = slice(i * count_here, (i + 1) * count_here)
        att[groups] = out.astype(bf16).reshape(count_here, BLOCK, lanes)
        out_copies += start_all(
            [
                pltpu.make_async_copy(att.at[groups], att_out.at[groups], out_sems.at[2 + 3 * i]),
                pltpu.make_async_copy(wide.at[rows], wide_out.at[rows], out_sems.at[3 + 3 * i]),
                pltpu.make_async_copy(
                    qa.at[:, rows], q_out.at[:, rows], out_sems.at[4 + 3 * i]
                ),
            ]
        )
    wait_all(out_copies)


def attention_forward(blocks, matrices, vectors, pattern, rank, starts, slopes, extra, tile=512):
    rows, model = blocks[0].shape
    seq = 8 * rows
    lanes = model // 8
    heads = jax.ShapeDtypeStruct((2, seq, lanes), bf16)
    return pl.pallas_call(
        functools.partial(forward_kernel, lanes // 2, tile, starts.shape[1]),
        out_shape=(
            jax.ShapeDtypeStruct((8, rows, lanes), bf16),
            jax.ShapeDtypeStruct((seq, lanes), f32),
            heads,
            heads,
            heads,
            jax.ShapeDtypeStruct((seq, model), bf16),
        ),
        in_specs=[smem()] * 3 + [hbm()] * 11 + [anywhere()] * EXTRA,
        out_specs=(hbm(),) * 6,
        scratch_shapes=[
            pltpu.VMEM((seq, model), bf16),
            pltpu.VMEM((model, 3 * lanes), bf16),
            pltpu.VMEM(vectors.shape, bf16),
            pltpu.VMEM((2, seq, lanes), bf16),
            pltpu.VMEM((2, seq, lanes), bf16),
            pltpu.VMEM((2, seq, lanes), bf16),
            pltpu.VMEM((2, seq, lanes), bf16),
            pltpu.VMEM((8, rows, lanes), bf16),
            pltpu.VMEM((seq, lanes), f32),
            pltpu.VMEM((2, tile, lanes), f32),
            pltpu.VMEM((2, tile, lanes), f32),
            pltpu.SemaphoreType.DMA((8,)),
            pltpu.SemaphoreType.DMA((5,)),
            pltpu.SemaphoreType.DMA((8,)),
            pltpu.SemaphoreType.DMA((2 + 3 * (seq // tile),)),
        ],
        compiler_params=params(56),
        cost_estimate=cost(20),
        name="attention_forward",
    )(rank, starts, slopes, *blocks, matrices, vectors, pattern, extra)


def backward_kernel(waits, width, tile, count, starts_ref, *refs):
    q_in, k_in, v_in, kt_in, wide_in, got_in = refs[:6]
    abs_out, rel_out, bias_out, mid_out = refs[6 + waits : 10 + waits]
    qa, ka, va, kt, wide, grads, mid, da, dq_ref, dk_ref, dv_ref = refs[10 + waits : 21 + waits]
    both_ref, flip_ref, mid_flip, bias_ref, in_sems, out_sems = refs[21 + waits :]
    seq, lanes = wide.shape
    factor = width**-0.5
    first = start_all(
        [
            pltpu.make_async_copy(wide_in, wide, in_sems.at[0]),
            pltpu.make_async_copy(got_in.at[:, :, 0:lanes], grads, in_sems.at[1]),
        ]
    )
    rest = start_all(
        [
            pltpu.make_async_copy(q_in, qa, in_sems.at[2]),
            pltpu.make_async_copy(k_in, ka, in_sems.at[3]),
            pltpu.make_async_copy(v_in, va, in_sems.at[4]),
            pltpu.make_async_copy(kt_in, kt, in_sems.at[5]),
            pltpu.make_async_copy(got_in.at[:, :, lanes : 2 * lanes], mid, in_sems.at[6]),
        ]
    )
    wait_all(first)

    def prologue(t, carry):
        rows = pl.ds(pl.multiple_of(t * BLOCK, BLOCK), BLOCK)
        g = grads[t].astype(f32)
        product = g * wide[rows, :]
        for h in range(2):
            inside, spare = head_lanes((BLOCK, lanes), h, width)
            delta = jnp.sum(jnp.where(inside, product, 0.0), axis=1, keepdims=True)
            parts = split3(-jnp.broadcast_to(delta, (BLOCK, lanes)))
            da[h, rows, :] = jnp.where(inside, g, pick(spare, parts)).astype(bf16)
        return carry

    lax.fori_loop(0, seq // BLOCK, prologue, 0)
    dq_ref[...] = jnp.zeros(dq_ref.shape, f32)
    wait_all(rest)

    def pair(h, keys, queries, mask, local):
        logits = lax.dot_general(ka[h, keys, :], qa[h, queries, :], NT, preferred_element_type=f32)
        probs = jnp.exp(logits)
        if mask is not None:
            probs = jnp.where(mask(logits.shape), probs, 0.0)
        inner = lax.dot_general(va[h, keys, :], da[h, queries, :], NT, preferred_element_type=f32)
        grad = (probs * inner).astype(bf16)
        dv_ref[h, local, :] += jnp.dot(
            probs.astype(bf16), da[h, queries, :], preferred_element_type=f32
        )
        dk_ref[h, local, :] += jnp.dot(grad, qa[h, queries, :], preferred_element_type=f32)
        rows = slice(h * width, (h + 1) * width)
        dq_ref[rows, queries] += jnp.dot(kt[rows, keys], grad, preferred_element_type=f32)

    bias_ref[...] = jnp.zeros(bias_ref.shape, f32)
    out_copies = []

    def send(t, part, value, flipped):
        columns = slice(part * lanes, (part + 1) * lanes)
        rows = slice(t * BLOCK, (t + 1) * BLOCK)
        both_ref[rows, columns] = value.astype(bf16)
        flip_ref[columns, rows] = flipped.astype(bf16)
        bias_ref[:, columns] += jnp.sum(value.astype(bf16).astype(f32), axis=0, keepdims=True)

    for j in range(seq // tile):
        base = j * tile
        dk_ref[...] = jnp.zeros(dk_ref.shape, f32)
        dv_ref[...] = jnp.zeros(dv_ref.shape, f32)

        def mask(first_key, first_query, shape):
            queries = lax.broadcasted_iota(jnp.int32, (1, shape[1]), 1) + first_query
            keys = lax.broadcasted_iota(jnp.int32, shape, 0) + first_key
            return keys < limits(queries, starts_ref, count)

        if base > 0:
            for h in range(2):
                pair(
                    h,
                    slice(base, base + PIC),
                    slice(base - PIC, base),
                    functools.partial(mask, base, base - PIC),
                    slice(0, PIC),
                )
        for h in range(2):
            pair(
                h,
                slice(base, base + tile),
                slice(base, base + tile),
                functools.partial(mask, base, base),
                slice(0, tile),
            )

        def full(i, carry, base=base):
            queries = pl.ds(pl.multiple_of(i * tile, tile), tile)
            for h in range(2):
                pair(h, slice(base, base + tile), queries, None, slice(0, tile))
            return carry

        if base + tile < seq:
            lax.fori_loop(j + 1, seq // tile, full, 0)
        inside, _ = head_lanes((BLOCK, lanes), 0, width)
        for t in range(tile // BLOCK):
            part = slice(t * BLOCK, (t + 1) * BLOCK)
            block = j * (tile // BLOCK) + t
            dk = jnp.where(inside, dk_ref[0, part, :], dk_ref[1, part, :])
            dv = jnp.where(inside, dv_ref[0, part, :], dv_ref[1, part, :])
            send(block, 1, dk, dk.T)
            send(block, 2, dv, dv.T)
    for t in range(seq // BLOCK):
        rows = slice(t * BLOCK, (t + 1) * BLOCK)
        dq = dq_ref[:, rows] * factor
        send(t, 0, dq.T, dq)
        mid_flip[:, rows] = mid[t].astype(f32).T.astype(bf16)
        out_copies += start_all(
            [
                pltpu.make_async_copy(both_ref.at[rows], abs_out.at[rows], out_sems.at[2 * t]),
                pltpu.make_async_copy(
                    flip_ref.at[:, rows], rel_out.at[:, rows], out_sems.at[2 * t + 1]
                ),
            ]
        )
    out_copies += start_all(
        [
            pltpu.make_async_copy(bias_ref, bias_out, out_sems.at[2 * (seq // BLOCK)]),
            pltpu.make_async_copy(mid_flip, mid_out, out_sems.at[2 * (seq // BLOCK) + 1]),
        ]
    )
    wait_all(out_copies)


def attention_backward(saved, wide, got, starts, extras, tile=512):
    seq, lanes = wide.shape
    blocks = seq // BLOCK
    return pl.pallas_call(
        functools.partial(backward_kernel, len(extras), lanes // 2, tile, starts.shape[1]),
        out_shape=(
            jax.ShapeDtypeStruct((seq, 3 * lanes), bf16),
            jax.ShapeDtypeStruct((3 * lanes, seq), bf16),
            jax.ShapeDtypeStruct((1, 3 * lanes), f32),
            jax.ShapeDtypeStruct((lanes, seq), bf16),
        ),
        in_specs=[smem()] + [hbm()] * 6 + [anywhere()] * len(extras),
        out_specs=(hbm(),) * 4,
        scratch_shapes=[
            pltpu.VMEM((2, seq, lanes), bf16),
            pltpu.VMEM((2, seq, lanes), bf16),
            pltpu.VMEM((2, seq, lanes), bf16),
            pltpu.VMEM((lanes, seq), bf16),
            pltpu.VMEM((seq, lanes), f32),
            pltpu.VMEM((blocks, BLOCK, lanes), bf16),
            pltpu.VMEM((blocks, BLOCK, lanes), bf16),
            pltpu.VMEM((2, seq, lanes), bf16),
            pltpu.VMEM((lanes, seq), f32),
            pltpu.VMEM((2, tile, lanes), f32),
            pltpu.VMEM((2, tile, lanes), f32),
            pltpu.VMEM((seq, 3 * lanes), bf16),
            pltpu.VMEM((3 * lanes, seq), bf16),
            pltpu.VMEM((lanes, seq), bf16),
            pltpu.VMEM((1, 3 * lanes), f32),
            pltpu.SemaphoreType.DMA((7,)),
            pltpu.SemaphoreType.DMA((2 * blocks + 2,)),
        ],
        compiler_params=params(56),
        cost_estimate=cost(21),
        name="attention_backward",
    )(starts, *saved, wide, got, *extras)


def normalize(value):
    centered = value - jnp.mean(value, axis=1, keepdims=True)
    inverse = lax.rsqrt(jnp.mean(centered * centered, axis=1, keepdims=True) + EPSILON)
    return centered * inverse, inverse


def whole(shape):
    return pl.BlockSpec(shape, lambda *_: (0,) * len(shape))


def gate(arrays, waits):
    count = len(arrays)
    return pl.pallas_call(
        lambda *refs: None,
        out_shape=tuple(jax.ShapeDtypeStruct(array.shape, array.dtype) for array in arrays),
        in_specs=[anywhere()] * (count + len(waits)),
        out_specs=(anywhere(),) * count,
        input_output_aliases={k: k for k in range(count)},
        cost_estimate=cost(1),
        name="gate",
    )(*arrays, *waits)


def project_kernel(
    heads_ref, tokens_ref, weights_ref, vectors_ref, extra_ref, middle_ref, hidden_ref, flag_ref, attended_ref
):
    flag_ref[0] = 1
    lanes = heads_ref.shape[2]
    for g in range(heads_ref.shape[0]):
        attended_ref[:, g * lanes : (g + 1) * lanes] = heads_ref[g]
    vecs = vectors_ref[...].astype(f32)
    middle = (
        tokens_ref[...].astype(f32)
        + jnp.dot(attended_ref[...], weights_ref[...], preferred_element_type=f32)
        + vecs[4:5]
    )
    middle_ref[...] = middle
    normed, _ = normalize(middle)
    hidden_ref[...] = (normed * vecs[5:6] + vecs[6:7]).astype(bf16)


def project_norm(heads, tokens, matrices, vectors, extra):
    rows, model = tokens.shape
    return pl.pallas_call(
        project_kernel,
        grid=(1,),
        out_shape=(
            jax.ShapeDtypeStruct((rows, model), f32),
            jax.ShapeDtypeStruct((rows, model), bf16),
            jax.ShapeDtypeStruct((1,), jnp.int32),
        ),
        in_specs=[
            whole(heads.shape),
            whole(tokens.shape),
            pl.BlockSpec((model, model), lambda i: (0, 3)),
            whole(vectors.shape),
            anywhere(),
        ],
        out_specs=(whole((rows, model)),) * 2 + (smem(),),
        scratch_shapes=[pltpu.VMEM((rows, model), bf16)],
        compiler_params=params(40),
        cost_estimate=cost(3),
        name="project_norm",
    )(heads, tokens, matrices, vectors, extra)


def gelu_parts(pre):
    square = pre * pre
    half = 0.5 * (1.0 + jnp.tanh(GELU_SCALE * (pre + GELU_CUBE * square * pre)))
    act = pre * half
    slope = half + 2.0 * act * (1.0 - half) * (GELU_SCALE * (1.0 + 3.0 * GELU_CUBE * square))
    return act, slope


def norm_pull(grad, gain, normed, inverse):
    scaled = grad * gain
    return inverse * (
        scaled
        - jnp.mean(scaled, axis=1, keepdims=True)
        - normed * jnp.mean(scaled * normed, axis=1, keepdims=True)
    )


def feed_kernel(chunk, *refs):
    hidden_in, middle_in, cotangent_in, vectors_in, bias_in, matrices_in = refs[:6]
    layer_out, grad_mid_out, heads_out, sums_out = refs[6:10]
    hidden, middle, cotangent, vecs_ref, bias, up, down, proj = refs[10:18]
    layer, grad_mid_ref, heads, sums, down_acc, two_acc, in_sems, w_sems, out_sems = refs[18:]
    model = hidden.shape[1]
    count = up.shape[0]
    first = start_all(
        [
            pltpu.make_async_copy(source, target, in_sems.at[k])
            for k, (source, target) in enumerate(
                ((hidden_in, hidden), (cotangent_in, cotangent), (bias_in, bias))
            )
        ]
    )
    weights = []
    for i in range(count):
        for part, ref in ((0, up), (1, down)):
            start = 4 * model + part * count * chunk + i * chunk
            weights.append(
                pltpu.make_async_copy(
                    matrices_in.at[:, start : start + chunk], ref.at[i], w_sems.at[2 * i + part]
                )
            )
    start_all(weights)
    rest = start_all(
        [
            pltpu.make_async_copy(middle_in, middle, in_sems.at[3]),
            pltpu.make_async_copy(vectors_in, vecs_ref, in_sems.at[4]),
            pltpu.make_async_copy(
                matrices_in.at[:, 3 * model : 4 * model], proj, in_sems.at[5]
            ),
        ]
    )
    wait_all(first)
    for i in range(count):
        weights[2 * i].wait()
        pre = jnp.dot(hidden[...], up[i], preferred_element_type=f32)
        pre = pre + bias[:, i * chunk : (i + 1) * chunk]
        weights[2 * i + 1].wait()
        grad_act = jnp.dot(cotangent[...], down[i], preferred_element_type=f32)
        act, slope = gelu_parts(pre)
        grad_pre = (grad_act * slope).astype(bf16)
        down_part = lax.dot_general(act.astype(bf16), down[i], NT, preferred_element_type=f32)
        two_part = lax.dot_general(grad_pre, up[i], NT, preferred_element_type=f32)
        if i == 0:
            down_acc[...] = down_part
            two_acc[...] = two_part
        else:
            down_acc[...] += down_part
            two_acc[...] += two_part
    wait_all(rest)
    vecs = vecs_ref[...].astype(f32)
    grad_two = two_acc[...]
    mid = middle[...]
    normed, inverse = normalize(mid)
    upstream = cotangent[...].astype(f32)
    grad_mid = upstream + norm_pull(grad_two, vecs[5:6], normed, inverse)
    low = grad_mid.astype(bf16)
    grads = lax.dot_general(low, proj[...], NT, preferred_element_type=f32).astype(bf16)
    groups, _, double = heads.shape
    lanes = double // 2
    for g in range(groups):
        heads[g, :, 0:lanes] = grads[:, g * lanes : (g + 1) * lanes]
        heads[g, :, lanes:double] = low[:, g * lanes : (g + 1) * lanes]
    out_copies = [pltpu.make_async_copy(heads, heads_out, out_sems.at[0])]
    out_copies[0].start()
    grad_mid_ref[...] = grad_mid
    layer[...] = (mid + down_acc[...] + vecs[7:8]).astype(bf16)
    rows = [grad_mid, grad_two * normed, grad_two, upstream]
    for k, value in enumerate(rows):
        sums[k : k + 1, :] = jnp.sum(value, axis=0, keepdims=True)
    out_copies += start_all(
        [
            pltpu.make_async_copy(layer, layer_out, out_sems.at[1]),
            pltpu.make_async_copy(grad_mid_ref, grad_mid_out, out_sems.at[2]),
            pltpu.make_async_copy(sums, sums_out, out_sems.at[3]),
        ]
    )
    wait_all(out_copies)


def feed_forward(hidden, up_bias, middle, cotangent, vectors, matrices, chunk=1024):
    rows, model = hidden.shape
    ff_width = up_bias.shape[1]
    count = ff_width // chunk
    outs = (
        jax.ShapeDtypeStruct((rows, model), bf16),
        jax.ShapeDtypeStruct((rows, model), f32),
        jax.ShapeDtypeStruct((8, rows, model // 4), bf16),
        jax.ShapeDtypeStruct((4, model), f32),
    )
    return pl.pallas_call(
        functools.partial(feed_kernel, chunk),
        out_shape=outs,
        in_specs=[hbm()] * 6,
        out_specs=(hbm(),) * 4,
        scratch_shapes=[
            pltpu.VMEM((rows, model), bf16),
            pltpu.VMEM((rows, model), f32),
            pltpu.VMEM((rows, model), bf16),
            pltpu.VMEM(vectors.shape, bf16),
            pltpu.VMEM((1, ff_width), f32),
            pltpu.VMEM((count, model, chunk), bf16),
            pltpu.VMEM((count, model, chunk), bf16),
            pltpu.VMEM((model, model), bf16),
        ]
        + [pltpu.VMEM(out.shape, out.dtype) for out in outs]
        + [
            pltpu.VMEM((rows, model), f32),
            pltpu.VMEM((rows, model), f32),
            pltpu.SemaphoreType.DMA((6,)),
            pltpu.SemaphoreType.DMA((2 * count,)),
            pltpu.SemaphoreType.DMA((4,)),
        ],
        compiler_params=params(40),
        cost_estimate=cost(14),
        name="feed_forward",
    )(hidden, middle, cotangent, vectors, up_bias, matrices)


def units_kernel(waits, rank_ref, *refs):
    blocks, heads = refs[:8], refs[8:16]
    cotangent_in, bias_in, matrices_in, vectors_in = refs[16:20]
    early_out, sums_out, attended_out = refs[20 + waits : 23 + waits]
    tokens, attended, hidden, cotangent, proj, vecs_ref = refs[23 + waits : 29 + waits]
    bias, up, down, act_ref, grad_ref, low, sums = refs[29 + waits : 36 + waits]
    w_sems, in_sems, head_sems, out_sems = refs[36 + waits :]
    seq, model = hidden.shape
    units = up.shape[1]
    lanes = model // 8
    rank = rank_ref[0]
    first = pl.multiple_of(rank * units, units)
    copies = [
        pltpu.make_async_copy(bias_in.at[:, pl.ds(first, units)], bias, w_sems.at[0]),
        pltpu.make_async_copy(vectors_in, vecs_ref, w_sems.at[1]),
        pltpu.make_async_copy(matrices_in.at[:, 3 * model : 4 * model], proj, w_sems.at[2]),
    ]
    start_all(copies)
    loads = []
    for k in range(8):
        columns = pl.ds(pl.multiple_of((rank ^ k) * lanes, lanes), lanes)
        loads.append(
            pltpu.make_async_copy(heads[k], attended.at[:, :, columns], head_sems.at[k])
        )
    for k in range(8):
        rows = pl.ds(pl.multiple_of((rank ^ k) * BLOCK, BLOCK), BLOCK)
        loads.append(pltpu.make_async_copy(blocks[k], tokens.at[rows], in_sems.at[k]))
    start_all(loads)
    weights = []
    for part, ref in ((0, up), (1, down)):
        source = pl.ds(pl.multiple_of((4 + 4 * part) * model + first, units), units)
        weights.append(
            pltpu.make_async_copy(matrices_in.at[:, source], ref, w_sems.at[3 + part])
        )
    weights.append(pltpu.make_async_copy(cotangent_in, cotangent, w_sems.at[5]))
    start_all(weights)
    wait_all(copies + loads)
    out_copies = [pltpu.make_async_copy(attended, attended_out, w_sems.at[6])]
    out_copies[0].start()
    vecs = vecs_ref[...].astype(f32)
    sums[...] = jnp.zeros(sums.shape, f32)
    for part in range(4):
        rows = slice(part * 2 * BLOCK, (part + 1) * 2 * BLOCK)
        heads_here = attended[2 * part : 2 * part + 2].reshape(2 * BLOCK, model)
        middle = (
            tokens[rows, :].astype(f32)
            + jnp.dot(heads_here, proj[...], preferred_element_type=f32)
            + vecs[4:5]
        )
        normed, _ = normalize(middle)
        hidden[rows, :] = (normed * vecs[5:6] + vecs[6:7]).astype(bf16)
        if part == 0:
            wait_all(weights)
        pre = jnp.dot(hidden[rows, :], up[...], preferred_element_type=f32) + bias[...]
        act, slope = gelu_parts(pre)
        grad_act = jnp.dot(cotangent[rows, :], down[...], preferred_element_type=f32)
        grad_pre = grad_act * slope
        act_ref[:, rows] = act.T.astype(bf16)
        grad_ref[:, rows] = grad_pre.T.astype(bf16)
        sums[...] += jnp.sum(grad_pre.astype(bf16).astype(f32), axis=0, keepdims=True)
    quarter = model // 4
    copy = pltpu.make_async_copy(sums, sums_out, w_sems.at[0])
    copy.start()
    out_copies.append(copy)
    for block in range(4):
        columns = slice(block * quarter, (block + 1) * quarter)
        for n, (left, right) in enumerate(((grad_ref, hidden), (act_ref, cotangent))):
            low[block, n * units : (n + 1) * units, :] = jnp.dot(
                left[...], right[:, columns], preferred_element_type=f32
            ).astype(bf16)
        copy = pltpu.make_async_copy(low.at[block], early_out.at[block], out_sems.at[block])
        copy.start()
        out_copies.append(copy)
    wait_all(out_copies)


def own_units(rank, blocks, heads, cotangent, up_bias, matrices, vectors, extras):
    rows, model = blocks[0].shape
    seq = 8 * rows
    units = up_bias.shape[1] // 8
    attended = (8, rows, model)
    return pl.pallas_call(
        functools.partial(units_kernel, len(extras)),
        out_shape=(
            jax.ShapeDtypeStruct((4, 2 * units, model // 4), bf16),
            jax.ShapeDtypeStruct((1, units), f32),
            jax.ShapeDtypeStruct(attended, bf16),
        ),
        in_specs=[smem()] + [hbm()] * 20 + [anywhere()] * len(extras),
        out_specs=(hbm(),) * 3,
        scratch_shapes=[
            pltpu.VMEM((seq, model), bf16),
            pltpu.VMEM(attended, bf16),
            pltpu.VMEM((seq, model), bf16),
            pltpu.VMEM((seq, model), bf16),
            pltpu.VMEM((model, model), bf16),
            pltpu.VMEM(vectors.shape, bf16),
            pltpu.VMEM((1, units), f32),
            pltpu.VMEM((model, units), bf16),
            pltpu.VMEM((model, units), bf16),
            pltpu.VMEM((units, seq), bf16),
            pltpu.VMEM((units, seq), bf16),
            pltpu.VMEM((4, 2 * units, model // 4), bf16),
            pltpu.VMEM((1, units), f32),
            pltpu.SemaphoreType.DMA((7,)),
            pltpu.SemaphoreType.DMA((8,)),
            pltpu.SemaphoreType.DMA((8,)),
            pltpu.SemaphoreType.DMA((4,)),
        ],
        compiler_params=params(56),
        cost_estimate=cost(1),
        name="own_units",
    )(rank, *blocks, *heads, cotangent, up_bias, matrices, vectors, *extras)


def late_kernel(depth_ref, grads_in, hidden_in, mid_in, attended_in, *refs):
    outs = refs[:4]
    grads, hidden, mid, attended, total, low, in_sems, out_sems = refs[4:]
    columns, model = total.shape
    quarter = model // 4
    first = grads.shape[0]
    copies = start_all(
        [
            pltpu.make_async_copy(source, target, in_sems.at[n])
            for n, (source, target) in enumerate(
                (
                    (mid_in, mid),
                    (attended_in, attended),
                    (grads_in, grads),
                    (hidden_in, hidden),
                )
            )
        ]
    )
    wait_all(copies[:2])
    total[first:, :] = jnp.dot(mid[...], attended[...], preferred_element_type=f32)
    wait_all(copies[2:])
    total[:first, :] = jnp.dot(grads[...], hidden[...], preferred_element_type=f32)
    depth = depth_ref[0]
    near = depth ^ 1
    out_copies = []
    for n, (block, target) in enumerate(
        ((3 - near, outs[0]), (near, outs[1]), (3 - depth, outs[2]), (depth, outs[3]))
    ):
        lane = pl.ds(pl.multiple_of(block * quarter, quarter), quarter)
        if n < 2:
            low[n] = total[:, lane].astype(bf16)
            copy = pltpu.make_async_copy(low.at[n], target, out_sems.at[n])
        else:
            copy = pltpu.make_async_copy(total.at[:, lane], target, out_sems.at[n])
        copy.start()
        out_copies.append(copy)
    wait_all(out_copies)


def late_weights(depth, grads, hidden, mid, attended):
    seq, model = hidden.shape
    columns = grads.shape[0] + mid.shape[0]
    quarter = model // 4
    return pl.pallas_call(
        late_kernel,
        out_shape=(jax.ShapeDtypeStruct((columns, quarter), bf16),) * 2
        + (jax.ShapeDtypeStruct((columns, quarter), f32),) * 2,
        in_specs=[smem()] + [hbm()] * 4,
        out_specs=(hbm(),) * 4,
        scratch_shapes=[
            pltpu.VMEM(grads.shape, bf16),
            pltpu.VMEM(hidden.shape, bf16),
            pltpu.VMEM(mid.shape, bf16),
            pltpu.VMEM(attended.shape, bf16),
            pltpu.VMEM((columns, model), f32),
            pltpu.VMEM((2, columns, quarter), bf16),
            pltpu.SemaphoreType.DMA((4,)),
            pltpu.SemaphoreType.DMA((4,)),
        ],
        compiler_params=params(56),
        cost_estimate=cost(5),
        name="late_weights",
    )(depth, grads, hidden, mid, attended)


def flip_kernel(in_ref, out_ref):
    out_ref[...] = in_ref[0].astype(f32).T.astype(bf16)


def flip(array):
    _, columns, rows = array.shape
    return pl.pallas_call(
        flip_kernel,
        grid=(1,),
        out_shape=jax.ShapeDtypeStruct((rows, columns), bf16),
        in_specs=[whole(array.shape)],
        out_specs=whole((rows, columns)),
        compiler_params=params(40),
        cost_estimate=cost(0.1),
        name="flip",
    )(array)


def final_kernel(
    heads_ref, weights_ref, tokens_ref, grad_mid_ref, vectors_ref, *refs
):
    out_ref, sums_ref, acc_ref, lhs = refs[-4:]
    step = pl.program_id(0)
    lanes = heads_ref.shape[2] // 3

    @pl.when(step == 0)
    def _():
        acc_ref[...] = jnp.zeros(acc_ref.shape, f32)

    source = pl.ds(pl.multiple_of(step * lanes, lanes), lanes)
    for g in range(heads_ref.shape[0]):
        lhs[:, g * lanes : (g + 1) * lanes] = heads_ref[g, :, source]
    acc_ref[...] += lax.dot_general(lhs[...], weights_ref[...], NT, preferred_element_type=f32)

    @pl.when(step == pl.num_programs(0) - 1)
    def _():
        vecs = vectors_ref[...].astype(f32)
        grad = acc_ref[...]
        normed, inverse = normalize(tokens_ref[...].astype(f32))
        out_ref[...] = grad_mid_ref[...] + norm_pull(grad, vecs[0:1], normed, inverse)
        sums_ref[0:1, :] = jnp.sum(grad * normed, axis=0, keepdims=True)
        sums_ref[1:2, :] = jnp.sum(grad, axis=0, keepdims=True)


def token_gradient(heads, matrices, tokens, grad_mid, vectors, extras):
    rows, model = tokens.shape
    return pl.pallas_call(
        final_kernel,
        grid=(3,),
        out_shape=(
            jax.ShapeDtypeStruct((rows, model), f32),
            jax.ShapeDtypeStruct((2, model), f32),
        ),
        in_specs=[
            whole(heads.shape),
            pl.BlockSpec((model, model), lambda i: (0, i)),
            whole((rows, model)),
            whole((rows, model)),
            whole(vectors.shape),
        ]
        + [anywhere()] * len(extras),
        out_specs=(whole((rows, model)), whole((2, model))),
        scratch_shapes=[pltpu.VMEM((rows, model), f32), pltpu.VMEM((rows, model), bf16)],
        compiler_params=params(56),
        cost_estimate=cost(6),
        name="token_gradient",
    )(heads, matrices, tokens, grad_mid, vectors, *extras)


def vector_pieces_kernel(rank_ref, one_ref, bias_ref, two_ref, units_ref, *refs):
    states, out_ref = refs[:3], refs[3]
    rank = rank_ref[0]
    lanes = out_ref.shape[2]
    out_ref[...] = jnp.zeros(out_ref.shape, f32)
    copies = out_ref.shape[0] // 8
    for b in range(8):
        columns = slice(b * lanes, (b + 1) * lanes)
        for c in range(copies):
            out_ref[copies * b + c, 0:2, :] = one_ref[:, columns]
            out_ref[copies * b + c, 4:8, :] = two_ref[:, columns]
    rows, own = states[0].shape
    packed = jnp.concatenate(
        [ref[...] for ref in states] + [jnp.zeros((rows, lanes - 3 * own), f32)], axis=1
    )
    for b in range(out_ref.shape[0]):
        out_ref[b, 12 : 12 + rows, :] = packed
    for c in range(copies):
        out_ref[copies * rank + c, 2:3, :] = bias_ref[:, 0:lanes]
        out_ref[copies * rank + c, 3:4, :] = bias_ref[:, 2 * lanes : 3 * lanes]
    pieces = units_ref.shape[1] // lanes
    for n in range(pieces):
        place = rank * pieces + n
        for c in range(copies):
            out_ref[copies * (place % 8) + c, pl.ds(8 + place // 8, 1), :] = units_ref[
                :, n * lanes : (n + 1) * lanes
            ]


def vector_pieces(rank, one, bias, two, units, states, devices):
    lanes = one.shape[1] // 8
    return pl.pallas_call(
        vector_pieces_kernel,
        grid=(1,),
        out_shape=jax.ShapeDtypeStruct((devices, 24, lanes), f32),
        in_specs=[smem(), whole(one.shape), whole(bias.shape), whole(two.shape), whole(units.shape)]
        + [whole(state.shape) for state in states],
        out_specs=whole((devices, 24, lanes)),
        compiler_params=params(40),
        cost_estimate=cost(1),
        name="vector_pieces",
    )(rank, one, bias, two, units, *states)


def adam(master, first, second, gradient, decay_rate):
    correction = 1.0 - BETA**STEP
    moment = BETA * first + (1.0 - BETA) * gradient
    variance = BETA * second + (1.0 - BETA) * gradient * gradient
    direction = moment / correction / (jnp.sqrt(variance / correction) + ADAM_EPSILON)
    return moment, variance, master - RATE * (direction + decay_rate * master)


def vector_update_kernel(root, place_ref, got_ref, *refs):
    outs, copied_ref = refs[:3], refs[3]
    lanes = got_ref.shape[2]
    rows, own = outs[0].shape
    gradient = jnp.sum(got_ref[:, :16, :], axis=0) * root
    shard = place_ref[0] % 4
    first = place_ref[0] - shard
    columns = lax.broadcasted_iota(jnp.int32, (16, lanes), 1) // own
    total = jnp.zeros((16, lanes), f32)
    for k in range(4):
        other = shard ^ k
        shifted = pltpu.roll(gradient, lax.rem(lanes - other * own, lanes), 1)[:rows, :own]
        packed = got_ref[first + other, 12 : 12 + rows, :]
        states = [packed[:, n * own : (n + 1) * own] for n in range(3)]
        values = adam(*states, shifted, 0.0)
        if k == 0:
            for ref, value in zip(outs, values):
                ref[...] = value
        wide = jnp.concatenate([values[2], jnp.zeros((rows, lanes - own), f32)], axis=1)
        wide = jnp.concatenate([wide, jnp.zeros((16 - rows, lanes), f32)], axis=0)
        total = jnp.where(columns == other, pltpu.roll(wide, other * own, 1), total)
    copied_ref[...] = total[:rows].astype(bf16)


def vector_update(place, got, rows, own, root):
    lanes = got.shape[2]
    mine = jax.ShapeDtypeStruct((rows, own), f32)
    return pl.pallas_call(
        functools.partial(vector_update_kernel, root),
        grid=(1,),
        out_shape=(mine, mine, mine, jax.ShapeDtypeStruct((rows, lanes), bf16)),
        in_specs=[smem(), whole(got.shape)],
        out_specs=(whole((rows, own)),) * 3 + (whole((rows, lanes)),),
        compiler_params=params(40),
        cost_estimate=cost(1),
        name="vector_update",
    )(place, got)


def update_kernel(root, got_ref, *refs):
    states, outs = refs[:3], refs[-5:-2]
    copied_ref, gradient_ref = refs[-2:]
    lanes = got_ref.shape[2]
    for g in range(got_ref.shape[0]):
        gradient_ref[:, g * lanes : (g + 1) * lanes] = got_ref[g].astype(f32)
    values = adam(*[ref[...] for ref in states], gradient_ref[...] * root, DECAY_RATE)
    for ref, value in zip(outs, values):
        ref[...] = value
    copied_ref[...] = values[2].astype(bf16)


def matrix_update(got, states, previous, extra, first, parts, root, name):
    groups, rows, packed = got.shape
    lanes = packed // parts
    block = groups * lanes
    total = states[0].shape[1]
    start = first // block
    state = pl.BlockSpec((rows, block), lambda i: (0, start + i))
    return pl.pallas_call(
        functools.partial(update_kernel, root),
        grid=(parts,),
        out_shape=(jax.ShapeDtypeStruct((rows, total), f32),) * 3
        + (jax.ShapeDtypeStruct((rows, parts * block), bf16),),
        in_specs=[pl.BlockSpec((groups, rows, lanes), lambda i: (0, 0, i))]
        + [state] * 3
        + [anywhere()] * (len(previous) + 1),
        out_specs=(state,) * 3 + (pl.BlockSpec((rows, block), lambda i: (0, i)),),
        scratch_shapes=[pltpu.VMEM((rows, block), f32)],
        input_output_aliases={4 + k: k for k in range(len(previous))},
        compiler_params=params(56),
        cost_estimate=cost(0.1),
        name=name,
    )(got, *states, *previous, extra)


def place_kernel(shard_ref, *refs):
    out_ref = refs[-1]
    rows = refs[0].shape[0]
    for k in range(4):
        place = pl.multiple_of((shard_ref[0] ^ k) * rows, rows)
        out_ref[pl.ds(place, rows), :] = refs[k][...]


def place_copies(shard, pieces, previous, first, total, name):
    rows, columns = pieces[0].shape
    block = 2048
    return pl.pallas_call(
        place_kernel,
        grid=(columns // block,),
        out_shape=jax.ShapeDtypeStruct((4 * rows, total), bf16),
        in_specs=[smem()]
        + [pl.BlockSpec((rows, block), lambda i: (0, i))] * 4
        + [anywhere()] * len(previous),
        out_specs=pl.BlockSpec((4 * rows, block), lambda i: (0, first // block + i)),
        input_output_aliases={5: 0} if previous else {},
        compiler_params=params(40),
        cost_estimate=cost(2),
        name=name,
    )(shard, *pieces, *previous)


def fits_sequence_plan(mesh):
    return mesh.shape["dp"] == 4 and mesh.shape["ctx"] == 2 and mesh.shape["shard"] == 4


EVERY = ("dp", "ctx", "shard")
SEQUENCE = ("ctx", "shard")


def swap(array, axis, bit):
    count = lax.axis_size(axis)
    return lax.ppermute(array, axis, [(i, i ^ bit) for i in range(count)])


def gather_blocks(block, ready=True):
    over_ctx = swap(block, "ctx", 1)
    over_y = swap(block, "shard", 2)
    over_core = swap(block, "shard", 1)
    even = (lax.axis_index("shard") % 2 == 0) & ready
    relay = jnp.where(even, over_ctx, over_y)
    opposite = lax.ppermute(relay, SEQUENCE, [(i, i ^ (4 if i % 2 else 2)) for i in range(8)])
    ctx_core = swap(over_ctx, "shard", 1)
    y_core = swap(over_y, "shard", 1)
    opposite_core = swap(opposite, "shard", 1)
    return relay, [
        block, over_core, over_y, y_core, over_ctx, ctx_core, opposite, opposite_core
    ]


def gather_rows(array):
    return lax.all_gather(array, SEQUENCE, axis=0, tiled=True)


def exchange(array, axes=SEQUENCE):
    return lax.all_to_all(array, axes, 0, 0, tiled=True)


def dot_tn(left, right):
    return lax.dot_general(left, right, (((0,), (0,)), ((), ())), preferred_element_type=f32)


def dot_nt(left, right):
    return lax.dot_general(left, right, NT, preferred_element_type=f32)


def dot_nn(left, right):
    return jnp.dot(left, right, preferred_element_type=f32)


def shift_dp(array, distance):
    return lax.ppermute(array, "dp", [(i, (i + distance) % 4) for i in range(4)])


def gather_shards(array):
    over_core = swap(array, "shard", 1)
    over_y = swap(array, "shard", 2)
    return [array, over_core, over_y, swap(over_y, "shard", 1)]


def sequence_shards(
    tokens,
    cotangent,
    picture_starts,
    matrices,
    vectors,
    master_matrices,
    master_vectors,
    first_matrices,
    first_vectors,
    second_matrices,
    second_vectors,
):
    row_count, width = tokens.shape
    ff_width = (matrices.shape[1] - 4 * width) // 2
    group = 8
    shard = lax.axis_index("shard")
    rank = lax.axis_index("ctx") * 4 + shard
    depth = lax.axis_index("dp")
    lanes = width // group
    units = ff_width // group
    own_rows = master_matrices.shape[0]
    seq = group * row_count
    head = rank * 2 + jnp.arange(2)
    slopes = jnp.exp2(-8.0 * (head.astype(f32) + 1.0) / HEADS)
    rank_array = rank.astype(jnp.int32).reshape(1)
    shard_array = shard.astype(jnp.int32).reshape(1)
    vector_rows = vectors.astype(f32)
    up_bias = vector_rows[8:].reshape(1, ff_width)

    with jax.named_scope("prepare"):
        pattern = key_pattern(picture_starts, slopes, seq, lanes)
    with jax.named_scope("gather_tokens"):
        ready = pattern[0, 0, lanes // 2 + 3] == 1.0
        passed, token_blocks = gather_blocks(tokens, ready)
    with jax.named_scope("gather_cotangent"):
        zero = passed[0, 0] * 0
        cotangent_late = cotangent + zero
        cotangent_all = gather_rows(cotangent_late)
    attended_heads, attended_wide, *saved, hidden_all = attention_forward(
        token_blocks,
        matrices,
        vectors,
        pattern,
        rank_array,
        picture_starts,
        slopes,
        cotangent_late,
    )
    with jax.named_scope("attended_exchange"):
        attended_got = exchange(attended_heads)
    with jax.named_scope("transpose_keys"):
        half = lanes // 2
        keys_low = saved[1]
        keys_transposed = jnp.concatenate(
            [keys_low[0, :, :half], keys_low[1, :, half:]], axis=1
        ).T
    middle, hidden_two, flag = project_norm(
        attended_got, tokens, matrices, vectors, keys_transposed
    )
    with jax.named_scope("gather_attended"):
        _, head_blocks = gather_blocks(attended_heads, flag[0] == 1)
    layer_output, grad_mid, grad_out, sums_two = feed_forward(
        hidden_two, up_bias, middle, cotangent, vectors, matrices
    )
    with jax.named_scope("grad_attended_exchange"):
        grad_got = exchange(grad_out)
    early, unit_sums, attended_all = own_units(
        rank_array,
        token_blocks,
        head_blocks,
        cotangent_all,
        up_bias,
        matrices,
        vectors,
        [grad_out],
    )
    with jax.named_scope("grad_feed"):
        (early,) = gate([early], [grad_got])
        early_sum = flip(lax.psum_scatter(early, "dp", scatter_dimension=0, tiled=True))
    grad_abs, grad_flipped, bias_sums, mid_flipped = attention_backward(
        (*saved, keys_transposed), attended_wide, grad_got, picture_starts, [early]
    )
    with jax.named_scope("grad_qkv_exchange"):
        grad_tokens = exchange(grad_abs.reshape(group, row_count, 3 * lanes))
    with jax.named_scope("grad_late"):
        near_far, near, relay, late_own = late_weights(
            depth.astype(jnp.int32).reshape(1), grad_flipped, hidden_all, mid_flipped, attended_all.reshape(seq, width)
        )
        beside = [(i, i ^ 1) for i in range(4)]
        relay = (relay + lax.ppermute(near_far, "dp", beside).astype(f32)).astype(bf16)
        near = lax.ppermute(near, "dp", beside)
        far = lax.ppermute(relay, "dp", [(i, 3 - i) for i in range(4)])
        late_sum = (late_own + near.astype(f32) + far.astype(f32)).T.astype(bf16)
    with jax.named_scope("early_rows"):
        (early_sum,) = gate([early_sum], [grad_tokens, relay])
        early_got = exchange(early_sum.reshape(group, own_rows, 2 * units))
    token_grads, sums_one = token_gradient(
        grad_tokens, matrices, tokens, grad_mid, vectors, [relay]
    )
    with jax.named_scope("late_rows"):
        (late_sum,) = gate([late_sum], [early_got, sums_one])
        late_got = exchange(late_sum.reshape(group, own_rows, 4 * lanes))
    root = (row_count * lax.axis_size("dp") * group) ** (-0.5)
    matrix_states = (master_matrices, first_matrices, second_matrices)
    *early_states, early_copy = matrix_update(
        early_got, matrix_states, (), token_grads, 4 * width, 2, root, "early_update"
    )
    total = matrices.shape[1]
    with jax.named_scope("early_copies"):
        early_copied = gather_shards(early_copy)
    copied_w = place_copies(shard_array, early_copied, (), 4 * width, total, "place_early")
    moment_w, variance_w, updated_w, late_copy = matrix_update(
        late_got, matrix_states, early_states, early_copy, 0, 4, root, "late_update"
    )
    with jax.named_scope("grad_vectors"):
        vector_states = (master_vectors, first_vectors, second_vectors)
        pieces = vector_pieces(rank_array, sums_one, bias_sums, sums_two, unit_sums, vector_states, 32)
        (pieces,) = gate([pieces], [late_copy, copied_w])
        vectors_got = exchange(pieces, EVERY)
    with jax.named_scope("late_copies"):
        late_copied = gather_shards(late_copy)
    copied_w = place_copies(shard_array, late_copied, (copied_w,), 0, total, "place_late")
    moment_v, variance_v, updated_v, copied_v = vector_update(
        (depth * group + rank).astype(jnp.int32).reshape(1),
        vectors_got,
        *master_vectors.shape,
        root,
    )
    return (
        layer_output,
        token_grads,
        moment_w,
        moment_v,
        variance_w,
        variance_v,
        updated_w,
        updated_v,
        copied_w,
        copied_v,
    )


def solution(mesh):
    in_specs = (
        P(("dp", "ctx", "shard"), None),
        P(("dp", "ctx", "shard"), None),
        P("dp", None),
        P(),
        P(),
        P(("dp", "ctx", "shard"), None),
        P(None, ("dp", "ctx", "shard")),
        P(("dp", "ctx", "shard"), None),
        P(None, ("dp", "ctx", "shard")),
        P(("dp", "ctx", "shard"), None),
        P(None, ("dp", "ctx", "shard")),
    )
    out_specs = (
        P(("dp", "ctx", "shard"), None),
        P(("dp", "ctx", "shard"), None),
        P(("dp", "ctx", "shard"), None),
        P(None, ("dp", "ctx", "shard")),
        P(("dp", "ctx", "shard"), None),
        P(None, ("dp", "ctx", "shard")),
        P(("dp", "ctx", "shard"), None),
        P(None, ("dp", "ctx", "shard")),
        P(("dp", "ctx"), None),
        P(None, ("dp", "ctx")),
    )
    body = sequence_shards if fits_sequence_plan(mesh) else general_shards
    return jax.shard_map(body, mesh=mesh, in_specs=in_specs, out_specs=out_specs, check_vma=False)
```

```python
import functools
import math

import jax
import jax.numpy as jnp
from jax import lax
from jax.experimental import pallas as pl
from jax.experimental.pallas import tpu as pltpu
from jax.sharding import PartitionSpec as P

HEADS = 16
PIC = 256
STEP = 2


EPSILON = 1e-05
NEGATIVE = -1e30
BETA = 0.5
RATE = 0.03
DECAY_RATE = 0.1
ADAM_EPSILON = 1e-08


def token_tags(index, start_list, block_len):
    after = index[:, None] - start_list[None, :]
    inside = (after >= 0) & (after < block_len)
    offsets = jnp.sum(jnp.clip(after, 0, block_len - 1), axis=1)
    number = jnp.arange(1, start_list.shape[0] + 1, dtype=jnp.int32)
    picture = jnp.sum(jnp.where(inside, number[None, :], 0), axis=1) - 1
    return (index - offsets, picture)


def block_scores(query_heads, query_index, key_heads, key_index, start_list, slopes, factor):
    query_pos, query_pic = token_tags(query_index, start_list, PIC)
    key_pos, key_pic = token_tags(key_index, start_list, PIC)
    raw = jnp.einsum("qhd,khd->hqk", query_heads, key_heads, preferred_element_type=jnp.float32)
    distance = (query_pos[:, None] - key_pos[None, :]).astype(jnp.float32)
    logits = raw * factor - slopes[:, None, None] * distance[None, :, :]
    same = (query_pic[:, None] == key_pic[None, :]) & (query_pic[:, None] >= 0)
    visible = (key_index[None, :] <= query_index[:, None]) | same
    return (logits, visible[None, :, :])


def layer_norm(inputs):
    centered = inputs - jnp.mean(inputs, axis=1, keepdims=True)
    inverse_std = lax.rsqrt(jnp.mean(centered * centered, axis=1, keepdims=True) + EPSILON)
    return (centered * inverse_std, inverse_std)


def norm_backward(grad_normed, gain, normed, inverse_std):
    scaled = grad_normed * gain
    return inverse_std * (
        scaled
        - jnp.mean(scaled, axis=1, keepdims=True)
        - normed * jnp.mean(scaled * normed, axis=1, keepdims=True)
    )


def activate(value):
    return jax.nn.gelu(value, approximate=True)


def regroup(array, dim, outer, inner):
    shape = array.shape
    split = array.reshape(
        shape[:dim] + (outer, inner, shape[dim] // (outer * inner)) + shape[dim + 1 :]
    )
    return jnp.swapaxes(split, dim, dim + 1).reshape(shape)


def adam_update(master, first, second, gradient, correction, decay_rate):
    moment = BETA * first + (1.0 - BETA) * gradient
    variance = BETA * second + (1.0 - BETA) * gradient * gradient
    direction = moment / correction / (jnp.sqrt(variance / correction) + ADAM_EPSILON)
    return (moment, variance, master - RATE * (direction + decay_rate * master))


def general_shards(
    tokens,
    cotangent,
    picture_starts,
    matrices,
    vectors,
    master_matrices,
    master_vectors,
    first_matrices,
    first_vectors,
    second_matrices,
    second_vectors,
):
    row_count, model_width = tokens.shape
    ff_width = (matrices.shape[1] - 4 * model_width) // 2
    head_count = HEADS
    head_width = model_width // head_count
    factor = head_width ** (-0.5)
    group_size = lax.axis_size("ctx") * lax.axis_size("shard")
    group_rank = lax.axis_index("ctx") * lax.axis_size("shard") + lax.axis_index("shard")
    seq_length = row_count * group_size
    first_row = group_rank * row_count
    start_list = picture_starts[0]
    slopes = jnp.exp2(-8.0 * (jnp.arange(head_count, dtype=jnp.float32) + 1.0) / head_count)
    block_rows = math.gcd(seq_length, 512)
    block_count = seq_length // block_rows
    w_qkv = matrices[:, : 3 * model_width]
    w_proj = matrices[:, 3 * model_width : 4 * model_width]
    w_up = matrices[:, 4 * model_width : 4 * model_width + ff_width]
    w_down = matrices[:, 4 * model_width + ff_width :]
    inputs = tokens.astype(jnp.float32)
    vector_rows = vectors.astype(jnp.float32)
    up_bias = vector_rows[8:].reshape(ff_width)
    normed, inverse_std = layer_norm(inputs)
    hidden = (normed * vector_rows[0] + vector_rows[1]).astype(jnp.bfloat16)
    projected = jnp.dot(hidden, w_qkv, preferred_element_type=jnp.float32)
    queries = (projected[:, :model_width] + vector_rows[2]).astype(jnp.bfloat16)
    kv_bias = jnp.concatenate([jnp.zeros((model_width,), jnp.float32), vector_rows[3]])
    kv_local = (projected[:, model_width:] + kv_bias).astype(jnp.bfloat16)
    gathered = lax.all_gather(kv_local, ("ctx", "shard"), axis=0, tiled=True)
    query_index = first_row + jnp.arange(row_count, dtype=jnp.int32)
    query_heads = queries.reshape(row_count, head_count, head_width)

    def key_block(index):
        piece = lax.dynamic_slice_in_dim(gathered, index * block_rows, block_rows, 0)
        key_heads = piece[:, :model_width].reshape(block_rows, head_count, head_width)
        value_heads = piece[:, model_width:].reshape(block_rows, head_count, head_width)
        key_index = index * block_rows + jnp.arange(block_rows, dtype=jnp.int32)
        logits, visible = block_scores(
            query_heads, query_index, key_heads, key_index, start_list, slopes, factor
        )
        return (logits, visible, key_heads, value_heads)

    def running_total(index, carry):
        highest, total = carry
        logits, visible, key_heads, value_heads = key_block(index)
        masked = jnp.where(visible, logits, NEGATIVE)
        updated = jnp.maximum(highest, jnp.max(masked, axis=2))
        weights = jnp.where(visible, jnp.exp(logits - updated[:, :, None]), 0.0)
        return (updated, total * jnp.exp(highest - updated) + jnp.sum(weights, axis=2))

    start_high = jnp.full((head_count, row_count), NEGATIVE, jnp.float32)
    start_total = jnp.zeros((head_count, row_count), jnp.float32)
    highest, total = lax.fori_loop(0, block_count, running_total, (start_high, start_total))
    log_total = highest + jnp.log(total)

    def weighted_sum(index, accum):
        logits, visible, key_heads, value_heads = key_block(index)
        probs = jnp.where(visible, jnp.exp(logits - log_total[:, :, None]), 0.0).astype(
            jnp.bfloat16
        )
        return accum + jnp.einsum(
            "hqk,khd->qhd", probs, value_heads, preferred_element_type=jnp.float32
        )

    attended = lax.fori_loop(
        0, block_count, weighted_sum, jnp.zeros((row_count, head_count, head_width), jnp.float32)
    )
    attended_low = attended.reshape(row_count, model_width).astype(jnp.bfloat16)
    middle = (
        inputs + jnp.dot(attended_low, w_proj, preferred_element_type=jnp.float32) + vector_rows[4]
    )
    normed_two, inverse_two = layer_norm(middle)
    hidden_two = (normed_two * vector_rows[5] + vector_rows[6]).astype(jnp.bfloat16)
    pre_act = jnp.dot(hidden_two, w_up, preferred_element_type=jnp.float32) + up_bias
    act_low = activate(pre_act).astype(jnp.bfloat16)
    down_out = lax.dot_general(
        act_low, w_down, (((1,), (1,)), ((), ())), preferred_element_type=jnp.float32
    )
    layer_output = (middle + down_out + vector_rows[7]).astype(jnp.bfloat16)
    upstream = cotangent.astype(jnp.float32)
    grad_act = jnp.dot(cotangent, w_down, preferred_element_type=jnp.float32)
    gelu_value, gelu_pull = jax.vjp(activate, pre_act)
    grad_pre = gelu_pull(grad_act)[0].astype(jnp.bfloat16)
    grad_up_w = lax.dot_general(
        hidden_two, grad_pre, (((0,), (0,)), ((), ())), preferred_element_type=jnp.float32
    )
    grad_down_w = lax.dot_general(
        cotangent, act_low, (((0,), (0,)), ((), ())), preferred_element_type=jnp.float32
    )
    grad_two = lax.dot_general(
        grad_pre, w_up, (((1,), (1,)), ((), ())), preferred_element_type=jnp.float32
    )
    grad_mid = upstream + norm_backward(grad_two, vector_rows[5], normed_two, inverse_two)
    grad_mid_low = grad_mid.astype(jnp.bfloat16)
    grad_proj = lax.dot_general(
        attended_low, grad_mid_low, (((0,), (0,)), ((), ())), preferred_element_type=jnp.float32
    )
    grad_out = lax.dot_general(
        grad_mid_low, w_proj, (((1,), (1,)), ((), ())), preferred_element_type=jnp.float32
    ).astype(jnp.bfloat16)
    grad_heads = grad_out.reshape(row_count, head_count, head_width)
    delta = jnp.sum(grad_heads.astype(jnp.float32) * attended, axis=2).T

    def score_grads(index):
        logits, visible, key_heads, value_heads = key_block(index)
        probs = jnp.where(visible, jnp.exp(logits - log_total[:, :, None]), 0.0)
        product = jnp.einsum(
            "qhd,khd->hqk", grad_heads, value_heads, preferred_element_type=jnp.float32
        )
        grad_logits = (probs * (product - delta[:, :, None])).astype(jnp.bfloat16)
        return (probs, grad_logits, key_heads)

    def both_grads(index, carry):
        accum, key_terms = carry
        probs, grad_logits, key_heads = score_grads(index)
        accum = (
            accum
            + jnp.einsum("hqk,khd->qhd", grad_logits, key_heads, preferred_element_type=jnp.float32)
            * factor
        )
        grad_key = (
            jnp.einsum("hqk,qhd->khd", grad_logits, query_heads, preferred_element_type=jnp.float32)
            * factor
        )
        grad_value = jnp.einsum(
            "hqk,qhd->khd",
            probs.astype(jnp.bfloat16),
            grad_heads,
            preferred_element_type=jnp.float32,
        )
        term = jnp.concatenate(
            [
                grad_key.reshape(block_rows, model_width),
                grad_value.reshape(block_rows, model_width),
            ],
            axis=1,
        )
        return (accum, lax.dynamic_update_slice_in_dim(key_terms, term, index * block_rows, 0))

    grad_query, key_terms = lax.fori_loop(
        0,
        block_count,
        both_grads,
        (
            jnp.zeros((row_count, head_count, head_width), jnp.float32),
            jnp.zeros((seq_length, 2 * model_width), jnp.float32),
        ),
    )
    own_key_grads = lax.psum_scatter(key_terms, ("ctx", "shard"), scatter_dimension=0, tiled=True)
    grad_qkv = jnp.concatenate(
        [grad_query.reshape(row_count, model_width), own_key_grads], axis=1
    ).astype(jnp.bfloat16)
    grad_qkv_weights = lax.dot_general(
        hidden, grad_qkv, (((0,), (0,)), ((), ())), preferred_element_type=jnp.float32
    )
    grad_hidden = lax.dot_general(
        grad_qkv, w_qkv, (((1,), (1,)), ((), ())), preferred_element_type=jnp.float32
    )
    query_bias_grad = jnp.sum(grad_qkv[:, :model_width].astype(jnp.float32), axis=0)
    value_bias_grad = jnp.sum(grad_qkv[:, 2 * model_width :].astype(jnp.float32), axis=0)
    grad_vectors = jnp.concatenate(
        [
            jnp.stack(
                [
                    jnp.sum(grad_hidden * normed, axis=0),
                    jnp.sum(grad_hidden, axis=0),
                    query_bias_grad,
                    value_bias_grad,
                    jnp.sum(grad_mid, axis=0),
                    jnp.sum(grad_two * normed_two, axis=0),
                    jnp.sum(grad_two, axis=0),
                    jnp.sum(upstream, axis=0),
                ]
            ),
            jnp.sum(grad_pre.astype(jnp.float32), axis=0).reshape(
                ff_width // model_width, model_width
            ),
        ],
        axis=0,
    )
    token_grads = grad_mid + norm_backward(grad_hidden, vector_rows[0], normed, inverse_std)
    grad_matrix = jnp.concatenate([grad_qkv_weights, grad_proj, grad_up_w, grad_down_w], axis=1)
    shard_count = lax.axis_size("shard")
    replicas = lax.axis_size("dp") * lax.axis_size("ctx")
    part_matrix, part_vec = (
        lax.psum_scatter(
            regroup(grad_matrix, 0, replicas, shard_count), "shard", scatter_dimension=0, tiled=True
        ),
        lax.psum_scatter(
            regroup(grad_vectors, 1, replicas, shard_count),
            "shard",
            scatter_dimension=1,
            tiled=True,
        ),
    )
    part_matrix, part_vec = (
        lax.psum_scatter(part_matrix, ("dp", "ctx"), scatter_dimension=0, tiled=True),
        lax.psum_scatter(part_vec, ("dp", "ctx"), scatter_dimension=1, tiled=True),
    )
    root = (row_count * lax.axis_size("dp") * group_size) ** (-0.5)
    correction = 1.0 - BETA**STEP
    moment_w, variance_w, updated_w = adam_update(
        master_matrices, first_matrices, second_matrices, part_matrix * root, correction, DECAY_RATE
    )
    moment_v, variance_v, updated_v = adam_update(
        master_vectors, first_vectors, second_vectors, part_vec * root, correction, 0.0
    )
    copied_w, copied_v = (
        lax.all_gather(updated_w.astype(jnp.bfloat16), "shard", axis=0, tiled=True),
        lax.all_gather(updated_v.astype(jnp.bfloat16), "shard", axis=1, tiled=True),
    )
    return (
        layer_output,
        token_grads,
        moment_w,
        moment_v,
        variance_w,
        variance_v,
        updated_w,
        updated_v,
        copied_w,
        copied_v,
    )


BLOCK = 256
EXTRA = 1
f32 = jnp.float32
bf16 = jnp.bfloat16
NT = (((1,), (1,)), ((), ()))
GELU_SCALE = math.sqrt(2.0 / math.pi)
GELU_CUBE = 0.044715


def split3(value):
    high = value.astype(bf16).astype(f32)
    rest = value - high
    middle = rest.astype(bf16).astype(f32)
    low = (rest - middle).astype(bf16).astype(f32)
    return high, middle, low


def positions(index, starts_ref, count):
    result = index
    for b in range(count):
        result = result - jnp.clip(index - starts_ref[0, b], 0, PIC - 1)
    return result.astype(f32)


def limits(index, starts_ref, count):
    result = index + 1
    for b in range(count):
        start = starts_ref[0, b]
        result = jnp.where((index >= start) & (index < start + PIC), start + PIC, result)
    return result


def head_lanes(shape, h, width):
    lane = lax.broadcasted_iota(jnp.int32, shape, 1)
    inside = (lane < width) if h == 0 else (lane >= width)
    return inside, lane - width if h == 0 else lane


def pick(spare, values):
    out = jnp.zeros(spare.shape, f32)
    for e, value in enumerate(values):
        out = jnp.where(spare == e, value, out)
    return out


def smem():
    return pl.BlockSpec(memory_space=pltpu.SMEM)


def vmem():
    return pl.BlockSpec(memory_space=pltpu.VMEM)


def anywhere():
    return pl.BlockSpec(memory_space=pl.ANY)


def hbm():
    return pl.BlockSpec(memory_space=pltpu.HBM)


def params(mebibytes):
    return pltpu.CompilerParams(vmem_limit_bytes=mebibytes * 2**20)


def cost(microseconds):
    return pl.CostEstimate(
        flops=int(microseconds * 1.0e9), bytes_accessed=0, transcendentals=0
    )


def start_all(copies):
    for copy in copies:
        copy.start()
    return copies


def wait_all(copies):
    for copy in copies:
        copy.wait()


def pattern_kernel(width, count, starts_ref, slopes_ref, out_ref):
    lanes = out_ref.shape[2]
    step = pl.program_id(0)
    index = lax.broadcasted_iota(jnp.int32, (BLOCK, lanes), 0) + step * BLOCK
    pos = positions(index, starts_ref, count)
    for h in range(2):
        _, spare = head_lanes((BLOCK, lanes), h, width)
        parts = split3(pos * slopes_ref[h])
        out_ref[h] = pick(spare, parts + (1.0, 1.0, 1.0)).astype(bf16)


def key_pattern(starts, slopes, seq, lanes):
    return pl.pallas_call(
        functools.partial(pattern_kernel, lanes // 2, starts.shape[1]),
        grid=(seq // BLOCK,),
        out_shape=jax.ShapeDtypeStruct((2, seq, lanes), bf16),
        in_specs=[smem()] * 2,
        out_specs=pl.BlockSpec((2, BLOCK, lanes), lambda i: (0, i, 0)),
        compiler_params=params(40),
        cost_estimate=cost(3),
        name="key_pattern",
    )(starts, slopes)


def forward_kernel(width, tile, count, rank_ref, starts_ref, slopes_ref, *refs):
    blocks = refs[:8]
    matrices_ref, vectors_ref, pattern_in = refs[8:11]
    att_out, wide_out, q_out, k_out, v_out, all_out = refs[11 + EXTRA : 17 + EXTRA]
    hid, wts, vecs, pattern, qa, ka, va, att, wide = refs[17 + EXTRA : 26 + EXTRA]
    in_sems, w_sems, hid_sems, out_sems = refs[26 + EXTRA :]
    seq, lanes = wide.shape
    model = hid.shape[1]
    rank = rank_ref[0]
    factor = width**-0.5
    w_copies = []
    for part in range(3):
        columns = pl.ds(pl.multiple_of(part * model + rank * lanes, lanes), lanes)
        w_copies.append(
            pltpu.make_async_copy(
                matrices_ref.at[:, columns],
                wts.at[:, part * lanes : (part + 1) * lanes],
                w_sems.at[part],
            )
        )
    w_copies.append(pltpu.make_async_copy(vectors_ref, vecs, w_sems.at[3]))
    start_all(w_copies)
    in_copies = start_all(
        [
            pltpu.make_async_copy(
                blocks[k], hid.at[k * BLOCK : (k + 1) * BLOCK], in_sems.at[k]
            )
            for k in range(8)
        ]
    )
    pattern_copy = pltpu.make_async_copy(pattern_in, pattern, w_sems.at[4])
    pattern_copy.start()
    wait_all(w_copies)
    gains = vecs[...].astype(f32)
    bias = vecs[:, pl.ds(pl.multiple_of(rank * lanes, lanes), lanes)].astype(f32)
    out_copies = []
    ones = []
    for h in range(2):
        inside, spare = head_lanes((BLOCK, lanes), h, width)
        ones.append((inside, jnp.where(spare < 3, 1.0, 0.0)))
    for pair in range(4):
        first = 2 * pair
        for k in (first, first + 1):
            in_copies[k].wait()
        both = slice(first * BLOCK, (first + 2) * BLOCK)
        normed, _ = normalize(hid[both, :].astype(f32))
        hid[both, :] = (normed * gains[0:1] + gains[1:2]).astype(bf16)
        for k in (first, first + 1):
            rows = slice(k * BLOCK, (k + 1) * BLOCK)
            dst = pl.ds(pl.multiple_of((k ^ rank) * BLOCK, BLOCK), BLOCK)
            copy = pltpu.make_async_copy(hid.at[rows], all_out.at[dst], hid_sems.at[k])
            copy.start()
            out_copies.append(copy)
        value = jnp.dot(hid[both, :], wts[...], preferred_element_type=f32)
        if pair == 0:
            pattern_copy.wait()
        for k in (first, first + 1):
            local = slice((k - first) * BLOCK, (k - first + 1) * BLOCK)
            dst = pl.ds(pl.multiple_of((k ^ rank) * BLOCK, BLOCK), BLOCK)
            q = (value[local, 0:lanes] + bias[2:3]).astype(bf16).astype(f32) * factor
            key = value[local, lanes : 2 * lanes]
            v = value[local, 2 * lanes : 3 * lanes] + bias[3:4]
            for h in range(2):
                inside, spare_ones = ones[h]
                qa[h, dst, :] = jnp.where(inside, q, spare_ones).astype(bf16)
                ka[h, dst, :] = jnp.where(inside, key, pattern[h, dst, :].astype(f32)).astype(bf16)
                va[h, dst, :] = jnp.where(inside, v, spare_ones).astype(bf16)
    out_copies += start_all(
        [
            pltpu.make_async_copy(ka, k_out, out_sems.at[0]),
            pltpu.make_async_copy(va, v_out, out_sems.at[1]),
        ]
    )

    def scores(h, queries, keys):
        return lax.dot_general(
            qa[h, queries, :], ka[h, keys, :], NT, preferred_element_type=f32
        )

    def mask(first_row, first_column, shape):
        rows = lax.broadcasted_iota(jnp.int32, (shape[0], 1), 0) + first_row
        columns = lax.broadcasted_iota(jnp.int32, shape, 1) + first_column
        return columns < limits(rows, starts_ref, count)

    def lane_best(value):
        best = value[:, :lanes]
        for c in range(1, value.shape[1] // lanes):
            best = jnp.maximum(best, value[:, c * lanes : (c + 1) * lanes])
        return best

    def with_shift(h, rows, shift):
        inside, spare = head_lanes((tile, lanes), h, width)
        parts = split3(-jnp.broadcast_to(shift, (tile, lanes)))
        value = qa[h, rows, :].astype(f32)
        for e in range(3):
            value = jnp.where(spare == 3 + e, parts[e], value)
        qa[h, rows, :] = value.astype(bf16)

    for i in range(seq // tile):
        base = i * tile
        end = base + tile
        rows = slice(base, end)
        tail = slice(end - PIC, end)
        over = slice(end, end + PIC)
        seen = mask(base, base, (tile, tile))
        if end < seq:
            seen_over = mask(end - PIC, end, (PIC, PIC))
        best = []
        kept = []
        for h in range(2):
            diagonal = jnp.where(seen, scores(h, rows, rows), NEGATIVE)
            top = lane_best(diagonal)
            below = []
            for j in range(i):
                below.append(scores(h, rows, slice(j * tile, (j + 1) * tile)))
                top = jnp.maximum(top, lane_best(below[-1]))
            beyond = None
            if end < seq:
                beyond = jnp.where(seen_over, scores(h, tail, over), NEGATIVE)
                low = jnp.maximum(top[tile - PIC :], lane_best(beyond))
                top = jnp.concatenate([top[: tile - PIC], low], axis=0)
            best.append(jnp.max(top, axis=1, keepdims=True))
            kept.append((below, diagonal, beyond))
        sums = []
        for h in range(2):
            below, diagonal, beyond = kept[h]
            weights = [jnp.exp(value - best[h]).astype(bf16) for value in below]
            weights.append(jnp.exp(diagonal - best[h]).astype(bf16))
            acc = jnp.dot(
                jnp.concatenate(weights, axis=1), va[h, :end, :], preferred_element_type=f32
            )
            if end < seq:
                beyond = jnp.exp(beyond - best[h][tile - PIC :])
                low = acc[tile - PIC :] + jnp.dot(
                    beyond.astype(bf16), va[h, over, :], preferred_element_type=f32
                )
                acc = jnp.concatenate([acc[: tile - PIC], low], axis=0)
            sums.append(acc)
        outs = []
        for h in range(2):
            acc = sums[h]
            column = width if h == 0 else 0
            total = acc[:, column : column + 1]
            outs.append(acc / total)
            with_shift(h, rows, best[h] + jnp.log(total))
        inside, _ = head_lanes((tile, lanes), 0, width)
        out = jnp.where(inside, outs[0], outs[1])
        wide[rows, :] = out
        count_here = tile // BLOCK
        groups = slice(i * count_here, (i + 1) * count_here)
        att[groups] = out.astype(bf16).reshape(count_here, BLOCK, lanes)
        out_copies += start_all(
            [
                pltpu.make_async_copy(att.at[groups], att_out.at[groups], out_sems.at[2 + 3 * i]),
                pltpu.make_async_copy(wide.at[rows], wide_out.at[rows], out_sems.at[3 + 3 * i]),
                pltpu.make_async_copy(
                    qa.at[:, rows], q_out.at[:, rows], out_sems.at[4 + 3 * i]
                ),
            ]
        )
    wait_all(out_copies)


def attention_forward(blocks, matrices, vectors, pattern, rank, starts, slopes, extra, tile=512):
    rows, model = blocks[0].shape
    seq = 8 * rows
    lanes = model // 8
    heads = jax.ShapeDtypeStruct((2, seq, lanes), bf16)
    return pl.pallas_call(
        functools.partial(forward_kernel, lanes // 2, tile, starts.shape[1]),
        out_shape=(
            jax.ShapeDtypeStruct((8, rows, lanes), bf16),
            jax.ShapeDtypeStruct((seq, lanes), f32),
            heads,
            heads,
            heads,
            jax.ShapeDtypeStruct((seq, model), bf16),
        ),
        in_specs=[smem()] * 3 + [hbm()] * 11 + [anywhere()] * EXTRA,
        out_specs=(hbm(),) * 6,
        scratch_shapes=[
            pltpu.VMEM((seq, model), bf16),
            pltpu.VMEM((model, 3 * lanes), bf16),
            pltpu.VMEM(vectors.shape, bf16),
            pltpu.VMEM((2, seq, lanes), bf16),
            pltpu.VMEM((2, seq, lanes), bf16),
            pltpu.VMEM((2, seq, lanes), bf16),
            pltpu.VMEM((2, seq, lanes), bf16),
            pltpu.VMEM((8, rows, lanes), bf16),
            pltpu.VMEM((seq, lanes), f32),
            pltpu.SemaphoreType.DMA((8,)),
            pltpu.SemaphoreType.DMA((5,)),
            pltpu.SemaphoreType.DMA((8,)),
            pltpu.SemaphoreType.DMA((2 + 3 * (seq // tile),)),
        ],
        compiler_params=params(56),
        cost_estimate=cost(20),
        name="attention_forward",
    )(rank, starts, slopes, *blocks, matrices, vectors, pattern, extra)


def backward_kernel(waits, width, tile, count, starts_ref, *refs):
    q_in, k_in, v_in, kt_in, wide_in, got_in = refs[:6]
    abs_out, rel_out, bias_out, mid_out = refs[6 + waits : 10 + waits]
    qa, ka, va, kt, wide, grads, mid, da, dq_ref, dk_ref, dv_ref = refs[10 + waits : 21 + waits]
    both_ref, flip_ref, mid_flip, bias_ref, in_sems, out_sems = refs[21 + waits :]
    seq, lanes = wide.shape
    factor = width**-0.5
    first = start_all(
        [
            pltpu.make_async_copy(wide_in, wide, in_sems.at[0]),
            pltpu.make_async_copy(got_in.at[:, :, 0:lanes], grads, in_sems.at[1]),
        ]
    )
    rest = start_all(
        [
            pltpu.make_async_copy(q_in, qa, in_sems.at[2]),
            pltpu.make_async_copy(k_in, ka, in_sems.at[3]),
            pltpu.make_async_copy(v_in, va, in_sems.at[4]),
            pltpu.make_async_copy(kt_in, kt, in_sems.at[5]),
            pltpu.make_async_copy(got_in.at[:, :, lanes : 2 * lanes], mid, in_sems.at[6]),
        ]
    )
    wait_all(first)

    def prologue(t, carry):
        rows = pl.ds(pl.multiple_of(t * BLOCK, BLOCK), BLOCK)
        g = grads[t].astype(f32)
        product = g * wide[rows, :]
        for h in range(2):
            inside, spare = head_lanes((BLOCK, lanes), h, width)
            delta = jnp.sum(jnp.where(inside, product, 0.0), axis=1, keepdims=True)
            parts = split3(-jnp.broadcast_to(delta, (BLOCK, lanes)))
            da[h, rows, :] = jnp.where(inside, g, pick(spare, parts)).astype(bf16)
        return carry

    lax.fori_loop(0, seq // BLOCK, prologue, 0)
    dq_ref[...] = jnp.zeros(dq_ref.shape, f32)
    wait_all(rest)

    def pair(h, keys, queries, mask, local):
        logits = lax.dot_general(ka[h, keys, :], qa[h, queries, :], NT, preferred_element_type=f32)
        probs = jnp.exp(logits)
        if mask is not None:
            probs = jnp.where(mask(logits.shape), probs, 0.0)
        inner = lax.dot_general(va[h, keys, :], da[h, queries, :], NT, preferred_element_type=f32)
        grad = (probs * inner).astype(bf16)
        dv_ref[h, local, :] += jnp.dot(
            probs.astype(bf16), da[h, queries, :], preferred_element_type=f32
        )
        dk_ref[h, local, :] += jnp.dot(grad, qa[h, queries, :], preferred_element_type=f32)
        rows = slice(h * width, (h + 1) * width)
        dq_ref[rows, queries] += jnp.dot(kt[rows, keys], grad, preferred_element_type=f32)

    bias_ref[...] = jnp.zeros(bias_ref.shape, f32)
    out_copies = []

    def send(t, part, value, flipped):
        columns = slice(part * lanes, (part + 1) * lanes)
        rows = slice(t * BLOCK, (t + 1) * BLOCK)
        both_ref[rows, columns] = value.astype(bf16)
        flip_ref[columns, rows] = flipped.astype(bf16)
        bias_ref[:, columns] += jnp.sum(value.astype(bf16).astype(f32), axis=0, keepdims=True)

    for j in range(seq // tile):
        base = j * tile
        dk_ref[...] = jnp.zeros(dk_ref.shape, f32)
        dv_ref[...] = jnp.zeros(dv_ref.shape, f32)

        def mask(first_key, first_query, shape):
            queries = lax.broadcasted_iota(jnp.int32, (1, shape[1]), 1) + first_query
            keys = lax.broadcasted_iota(jnp.int32, shape, 0) + first_key
            return keys < limits(queries, starts_ref, count)

        if base > 0:
            for h in range(2):
                pair(
                    h,
                    slice(base, base + PIC),
                    slice(base - PIC, base),
                    functools.partial(mask, base, base - PIC),
                    slice(0, PIC),
                )
        for h in range(2):
            pair(
                h,
                slice(base, base + tile),
                slice(base, base + tile),
                functools.partial(mask, base, base),
                slice(0, tile),
            )

        def full(i, base=base):
            queries = slice(i * tile, (i + 1) * tile)
            for h in range(2):
                pair(h, slice(base, base + tile), queries, None, slice(0, tile))

        if base + tile < seq:
            for i in range(j + 1, seq // tile):
                full(i)
        inside, _ = head_lanes((BLOCK, lanes), 0, width)
        for t in range(tile // BLOCK):
            part = slice(t * BLOCK, (t + 1) * BLOCK)
            block = j * (tile // BLOCK) + t
            dk = jnp.where(inside, dk_ref[0, part, :], dk_ref[1, part, :])
            dv = jnp.where(inside, dv_ref[0, part, :], dv_ref[1, part, :])
            send(block, 1, dk, dk.T)
            send(block, 2, dv, dv.T)
    for t in range(seq // BLOCK):
        rows = slice(t * BLOCK, (t + 1) * BLOCK)
        dq = dq_ref[:, rows] * factor
        send(t, 0, dq.T, dq)
        mid_flip[:, rows] = mid[t].astype(f32).T.astype(bf16)
        out_copies += start_all(
            [
                pltpu.make_async_copy(both_ref.at[rows], abs_out.at[rows], out_sems.at[2 * t]),
                pltpu.make_async_copy(
                    flip_ref.at[:, rows], rel_out.at[:, rows], out_sems.at[2 * t + 1]
                ),
            ]
        )
    out_copies += start_all(
        [
            pltpu.make_async_copy(bias_ref, bias_out, out_sems.at[2 * (seq // BLOCK)]),
            pltpu.make_async_copy(mid_flip, mid_out, out_sems.at[2 * (seq // BLOCK) + 1]),
        ]
    )
    wait_all(out_copies)


def attention_backward(saved, wide, got, starts, extras, tile=512):
    seq, lanes = wide.shape
    blocks = seq // BLOCK
    return pl.pallas_call(
        functools.partial(backward_kernel, len(extras), lanes // 2, tile, starts.shape[1]),
        out_shape=(
            jax.ShapeDtypeStruct((seq, 3 * lanes), bf16),
            jax.ShapeDtypeStruct((3 * lanes, seq), bf16),
            jax.ShapeDtypeStruct((1, 3 * lanes), f32),
            jax.ShapeDtypeStruct((lanes, seq), bf16),
        ),
        in_specs=[smem()] + [hbm()] * 6 + [anywhere()] * len(extras),
        out_specs=(hbm(),) * 4,
        scratch_shapes=[
            pltpu.VMEM((2, seq, lanes), bf16),
            pltpu.VMEM((2, seq, lanes), bf16),
            pltpu.VMEM((2, seq, lanes), bf16),
            pltpu.VMEM((lanes, seq), bf16),
            pltpu.VMEM((seq, lanes), f32),
            pltpu.VMEM((blocks, BLOCK, lanes), bf16),
            pltpu.VMEM((blocks, BLOCK, lanes), bf16),
            pltpu.VMEM((2, seq, lanes), bf16),
            pltpu.VMEM((lanes, seq), f32),
            pltpu.VMEM((2, tile, lanes), f32),
            pltpu.VMEM((2, tile, lanes), f32),
            pltpu.VMEM((seq, 3 * lanes), bf16),
            pltpu.VMEM((3 * lanes, seq), bf16),
            pltpu.VMEM((lanes, seq), bf16),
            pltpu.VMEM((1, 3 * lanes), f32),
            pltpu.SemaphoreType.DMA((7,)),
            pltpu.SemaphoreType.DMA((2 * blocks + 2,)),
        ],
        compiler_params=params(56),
        cost_estimate=cost(21),
        name="attention_backward",
    )(starts, *saved, wide, got, *extras)


def normalize(value):
    centered = value - jnp.mean(value, axis=1, keepdims=True)
    inverse = lax.rsqrt(jnp.mean(centered * centered, axis=1, keepdims=True) + EPSILON)
    return centered * inverse, inverse


def whole(shape):
    return pl.BlockSpec(shape, lambda *_: (0,) * len(shape))


def gate(arrays, waits):
    count = len(arrays)
    return pl.pallas_call(
        lambda *refs: None,
        out_shape=tuple(jax.ShapeDtypeStruct(array.shape, array.dtype) for array in arrays),
        in_specs=[anywhere()] * (count + len(waits)),
        out_specs=(anywhere(),) * count,
        input_output_aliases={k: k for k in range(count)},
        cost_estimate=cost(1),
        name="gate",
    )(*arrays, *waits)


def project_kernel(
    heads_ref, tokens_ref, weights_ref, vectors_ref, extra_ref, middle_ref, hidden_ref, attended_ref
):
    lanes = heads_ref.shape[2]
    for g in range(heads_ref.shape[0]):
        attended_ref[:, g * lanes : (g + 1) * lanes] = heads_ref[g]
    vecs = vectors_ref[...].astype(f32)
    middle = (
        tokens_ref[...].astype(f32)
        + jnp.dot(attended_ref[...], weights_ref[...], preferred_element_type=f32)
        + vecs[4:5]
    )
    middle_ref[...] = middle
    normed, _ = normalize(middle)
    hidden_ref[...] = (normed * vecs[5:6] + vecs[6:7]).astype(bf16)


def project_norm(heads, tokens, matrices, vectors, extra):
    rows, model = tokens.shape
    return pl.pallas_call(
        project_kernel,
        grid=(1,),
        out_shape=(
            jax.ShapeDtypeStruct((rows, model), f32),
            jax.ShapeDtypeStruct((rows, model), bf16),
        ),
        in_specs=[
            whole(heads.shape),
            whole(tokens.shape),
            pl.BlockSpec((model, model), lambda i: (0, 3)),
            whole(vectors.shape),
            anywhere(),
        ],
        out_specs=(whole((rows, model)),) * 2,
        scratch_shapes=[pltpu.VMEM((rows, model), bf16)],
        compiler_params=params(40),
        cost_estimate=cost(3),
        name="project_norm",
    )(heads, tokens, matrices, vectors, extra)


def gelu_parts(pre):
    square = pre * pre
    half = 0.5 * (1.0 + jnp.tanh(GELU_SCALE * (pre + GELU_CUBE * square * pre)))
    act = pre * half
    slope = half + 2.0 * act * (1.0 - half) * (GELU_SCALE * (1.0 + 3.0 * GELU_CUBE * square))
    return act, slope


def norm_pull(grad, gain, normed, inverse):
    scaled = grad * gain
    return inverse * (
        scaled
        - jnp.mean(scaled, axis=1, keepdims=True)
        - normed * jnp.mean(scaled * normed, axis=1, keepdims=True)
    )


def feed_kernel(chunk, *refs):
    hidden_in, middle_in, cotangent_in, vectors_in, bias_in, matrices_in = refs[:6]
    layer_out, grad_mid_out, heads_out, sums_out = refs[6:10]
    hidden, middle, cotangent, vecs_ref, bias, up, down, proj = refs[10:18]
    layer, grad_mid_ref, heads, sums, down_acc, two_acc, in_sems, w_sems, out_sems = refs[18:]
    model = hidden.shape[1]
    count = up.shape[0]
    first = start_all(
        [
            pltpu.make_async_copy(source, target, in_sems.at[k])
            for k, (source, target) in enumerate(
                ((hidden_in, hidden), (cotangent_in, cotangent), (bias_in, bias))
            )
        ]
    )
    weights = []
    for i in range(count):
        for part, ref in ((0, up), (1, down)):
            start = 4 * model + part * count * chunk + i * chunk
            weights.append(
                pltpu.make_async_copy(
                    matrices_in.at[:, start : start + chunk], ref.at[i], w_sems.at[2 * i + part]
                )
            )
    start_all(weights)
    rest = start_all(
        [
            pltpu.make_async_copy(middle_in, middle, in_sems.at[3]),
            pltpu.make_async_copy(vectors_in, vecs_ref, in_sems.at[4]),
            pltpu.make_async_copy(
                matrices_in.at[:, 3 * model : 4 * model], proj, in_sems.at[5]
            ),
        ]
    )
    wait_all(first)
    for i in range(count):
        weights[2 * i].wait()
        pre = jnp.dot(hidden[...], up[i], preferred_element_type=f32)
        pre = pre + bias[:, i * chunk : (i + 1) * chunk]
        weights[2 * i + 1].wait()
        grad_act = jnp.dot(cotangent[...], down[i], preferred_element_type=f32)
        act, slope = gelu_parts(pre)
        grad_pre = (grad_act * slope).astype(bf16)
        down_part = lax.dot_general(act.astype(bf16), down[i], NT, preferred_element_type=f32)
        two_part = lax.dot_general(grad_pre, up[i], NT, preferred_element_type=f32)
        if i == 0:
            down_acc[...] = down_part
            two_acc[...] = two_part
        else:
            down_acc[...] += down_part
            two_acc[...] += two_part
    wait_all(rest)
    vecs = vecs_ref[...].astype(f32)
    grad_two = two_acc[...]
    mid = middle[...]
    normed, inverse = normalize(mid)
    upstream = cotangent[...].astype(f32)
    grad_mid = upstream + norm_pull(grad_two, vecs[5:6], normed, inverse)
    low = grad_mid.astype(bf16)
    grads = lax.dot_general(low, proj[...], NT, preferred_element_type=f32).astype(bf16)
    groups, _, double = heads.shape
    lanes = double // 2
    for g in range(groups):
        heads[g, :, 0:lanes] = grads[:, g * lanes : (g + 1) * lanes]
        heads[g, :, lanes:double] = low[:, g * lanes : (g + 1) * lanes]
    out_copies = [pltpu.make_async_copy(heads, heads_out, out_sems.at[0])]
    out_copies[0].start()
    grad_mid_ref[...] = grad_mid
    layer[...] = (mid + down_acc[...] + vecs[7:8]).astype(bf16)
    rows = [grad_mid, grad_two * normed, grad_two, upstream]
    for k, value in enumerate(rows):
        sums[k : k + 1, :] = jnp.sum(value, axis=0, keepdims=True)
    out_copies += start_all(
        [
            pltpu.make_async_copy(layer, layer_out, out_sems.at[1]),
            pltpu.make_async_copy(grad_mid_ref, grad_mid_out, out_sems.at[2]),
            pltpu.make_async_copy(sums, sums_out, out_sems.at[3]),
        ]
    )
    wait_all(out_copies)


def feed_forward(hidden, up_bias, middle, cotangent, vectors, matrices, chunk=1024):
    rows, model = hidden.shape
    ff_width = up_bias.shape[1]
    count = ff_width // chunk
    outs = (
        jax.ShapeDtypeStruct((rows, model), bf16),
        jax.ShapeDtypeStruct((rows, model), f32),
        jax.ShapeDtypeStruct((8, rows, model // 4), bf16),
        jax.ShapeDtypeStruct((4, model), f32),
    )
    return pl.pallas_call(
        functools.partial(feed_kernel, chunk),
        out_shape=outs,
        in_specs=[hbm()] * 6,
        out_specs=(hbm(),) * 4,
        scratch_shapes=[
            pltpu.VMEM((rows, model), bf16),
            pltpu.VMEM((rows, model), f32),
            pltpu.VMEM((rows, model), bf16),
            pltpu.VMEM(vectors.shape, bf16),
            pltpu.VMEM((1, ff_width), f32),
            pltpu.VMEM((count, model, chunk), bf16),
            pltpu.VMEM((count, model, chunk), bf16),
            pltpu.VMEM((model, model), bf16),
        ]
        + [pltpu.VMEM(out.shape, out.dtype) for out in outs]
        + [
            pltpu.VMEM((rows, model), f32),
            pltpu.VMEM((rows, model), f32),
            pltpu.SemaphoreType.DMA((6,)),
            pltpu.SemaphoreType.DMA((2 * count,)),
            pltpu.SemaphoreType.DMA((4,)),
        ],
        compiler_params=params(40),
        cost_estimate=cost(14),
        name="feed_forward",
    )(hidden, middle, cotangent, vectors, up_bias, matrices)


def units_kernel(waits, rank_ref, *refs):
    blocks, heads = refs[:8], refs[8:16]
    cotangent_in, bias_in, matrices_in, vectors_in = refs[16:20]
    early_out, sums_out, attended_out = refs[20 + waits : 23 + waits]
    tokens, attended, hidden, cotangent, proj, vecs_ref = refs[23 + waits : 29 + waits]
    bias, up, down, act_ref, grad_ref, low, sums, grad_act = refs[29 + waits : 37 + waits]
    w_sems, in_sems, head_sems, out_sems = refs[37 + waits :]
    seq, model = hidden.shape
    units = up.shape[1]
    lanes = model // 8
    rank = rank_ref[0]
    first = pl.multiple_of(rank * units, units)
    weights = []
    for part, ref in ((1, down), (0, up)):
        source = pl.ds(pl.multiple_of((4 + 4 * part) * model + first, units), units)
        weights.append(
            pltpu.make_async_copy(matrices_in.at[:, source], ref, w_sems.at[3 + part])
        )
    early_copies = [pltpu.make_async_copy(cotangent_in, cotangent, w_sems.at[5]), weights[0]]
    start_all(early_copies)
    copies = [
        pltpu.make_async_copy(bias_in.at[:, pl.ds(first, units)], bias, w_sems.at[0]),
        pltpu.make_async_copy(vectors_in, vecs_ref, w_sems.at[1]),
        pltpu.make_async_copy(matrices_in.at[:, 3 * model : 4 * model], proj, w_sems.at[2]),
    ]
    start_all(copies)
    loads = []
    for k in range(8):
        columns = pl.ds(pl.multiple_of((rank ^ k) * lanes, lanes), lanes)
        loads.append(
            pltpu.make_async_copy(heads[k], attended.at[:, :, columns], head_sems.at[k])
        )
    for k in range(8):
        rows = pl.ds(pl.multiple_of((rank ^ k) * BLOCK, BLOCK), BLOCK)
        loads.append(pltpu.make_async_copy(blocks[k], tokens.at[rows], in_sems.at[k]))
    start_all(loads)
    weights[1].start()
    wait_all(early_copies)
    grad_act[...] = jnp.dot(cotangent[...], down[...], preferred_element_type=f32)
    wait_all(copies + loads)
    out_copies = [pltpu.make_async_copy(attended, attended_out, w_sems.at[6])]
    out_copies[0].start()
    vecs = vecs_ref[...].astype(f32)
    sums[...] = jnp.zeros(sums.shape, f32)
    for part in range(4):
        rows = slice(part * 2 * BLOCK, (part + 1) * 2 * BLOCK)
        heads_here = attended[2 * part : 2 * part + 2].reshape(2 * BLOCK, model)
        middle = (
            tokens[rows, :].astype(f32)
            + jnp.dot(heads_here, proj[...], preferred_element_type=f32)
            + vecs[4:5]
        )
        normed, _ = normalize(middle)
        hidden[rows, :] = (normed * vecs[5:6] + vecs[6:7]).astype(bf16)
        if part == 0:
            weights[1].wait()
        pre = jnp.dot(hidden[rows, :], up[...], preferred_element_type=f32) + bias[...]
        act, slope = gelu_parts(pre)
        grad_pre = grad_act[rows, :] * slope
        act_ref[:, rows] = act.T.astype(bf16)
        grad_ref[:, rows] = grad_pre.T.astype(bf16)
        sums[...] += jnp.sum(grad_pre.astype(bf16).astype(f32), axis=0, keepdims=True)
    quarter = model // 4
    copy = pltpu.make_async_copy(sums, sums_out, w_sems.at[0])
    copy.start()
    out_copies.append(copy)
    for block in range(4):
        columns = slice(block * quarter, (block + 1) * quarter)
        for n, (left, right) in enumerate(((grad_ref, hidden), (act_ref, cotangent))):
            low[block, n * units : (n + 1) * units, :] = jnp.dot(
                left[...], right[:, columns], preferred_element_type=f32
            ).astype(bf16)
        copy = pltpu.make_async_copy(low.at[block], early_out.at[block], out_sems.at[block])
        copy.start()
        out_copies.append(copy)
    wait_all(out_copies)


def own_units(rank, blocks, heads, cotangent, up_bias, matrices, vectors, extras):
    rows, model = blocks[0].shape
    seq = 8 * rows
    units = up_bias.shape[1] // 8
    attended = (8, rows, model)
    return pl.pallas_call(
        functools.partial(units_kernel, len(extras)),
        out_shape=(
            jax.ShapeDtypeStruct((4, 2 * units, model // 4), bf16),
            jax.ShapeDtypeStruct((1, units), f32),
            jax.ShapeDtypeStruct(attended, bf16),
        ),
        in_specs=[smem()] + [hbm()] * 20 + [anywhere()] * len(extras),
        out_specs=(hbm(),) * 3,
        scratch_shapes=[
            pltpu.VMEM((seq, model), bf16),
            pltpu.VMEM(attended, bf16),
            pltpu.VMEM((seq, model), bf16),
            pltpu.VMEM((seq, model), bf16),
            pltpu.VMEM((model, model), bf16),
            pltpu.VMEM(vectors.shape, bf16),
            pltpu.VMEM((1, units), f32),
            pltpu.VMEM((model, units), bf16),
            pltpu.VMEM((model, units), bf16),
            pltpu.VMEM((units, seq), bf16),
            pltpu.VMEM((units, seq), bf16),
            pltpu.VMEM((4, 2 * units, model // 4), bf16),
            pltpu.VMEM((1, units), f32),
            pltpu.VMEM((seq, units), f32),
            pltpu.SemaphoreType.DMA((7,)),
            pltpu.SemaphoreType.DMA((8,)),
            pltpu.SemaphoreType.DMA((8,)),
            pltpu.SemaphoreType.DMA((4,)),
        ],
        compiler_params=params(56),
        cost_estimate=cost(1),
        name="own_units",
    )(rank, *blocks, *heads, cotangent, up_bias, matrices, vectors, *extras)


def late_kernel(depth_ref, grads_in, hidden_in, mid_in, attended_in, *refs):
    outs = refs[:4]
    grads, hidden, mid, attended, total, low, in_sems, out_sems = refs[4:]
    columns, model = total.shape
    quarter = model // 4
    first = grads.shape[0]
    copies = start_all(
        [
            pltpu.make_async_copy(source, target, in_sems.at[n])
            for n, (source, target) in enumerate(
                (
                    (mid_in, mid),
                    (attended_in, attended),
                    (grads_in, grads),
                    (hidden_in, hidden),
                )
            )
        ]
    )
    wait_all(copies[:2])
    total[first:, :] = jnp.dot(mid[...], attended[...], preferred_element_type=f32)
    wait_all(copies[2:])
    total[:first, :] = jnp.dot(grads[...], hidden[...], preferred_element_type=f32)
    depth = depth_ref[0]
    near = depth ^ 1
    out_copies = []
    for n, (block, target) in enumerate(
        ((3 - near, outs[0]), (near, outs[1]), (3 - depth, outs[2]), (depth, outs[3]))
    ):
        lane = pl.ds(pl.multiple_of(block * quarter, quarter), quarter)
        if n < 2:
            low[n] = total[:, lane].astype(bf16)
            copy = pltpu.make_async_copy(low.at[n], target, out_sems.at[n])
        else:
            copy = pltpu.make_async_copy(total.at[:, lane], target, out_sems.at[n])
        copy.start()
        out_copies.append(copy)
    wait_all(out_copies)


def late_weights(depth, grads, hidden, mid, attended):
    seq, model = hidden.shape
    columns = grads.shape[0] + mid.shape[0]
    quarter = model // 4
    return pl.pallas_call(
        late_kernel,
        out_shape=(jax.ShapeDtypeStruct((columns, quarter), bf16),) * 2
        + (jax.ShapeDtypeStruct((columns, quarter), f32),) * 2,
        in_specs=[smem()] + [hbm()] * 4,
        out_specs=(hbm(),) * 4,
        scratch_shapes=[
            pltpu.VMEM(grads.shape, bf16),
            pltpu.VMEM(hidden.shape, bf16),
            pltpu.VMEM(mid.shape, bf16),
            pltpu.VMEM(attended.shape, bf16),
            pltpu.VMEM((columns, model), f32),
            pltpu.VMEM((2, columns, quarter), bf16),
            pltpu.SemaphoreType.DMA((4,)),
            pltpu.SemaphoreType.DMA((4,)),
        ],
        compiler_params=params(56),
        cost_estimate=cost(5),
        name="late_weights",
    )(depth, grads, hidden, mid, attended)


def flip_kernel(in_ref, out_ref):
    out_ref[...] = in_ref[0].astype(f32).T.astype(bf16)


def flip(array):
    _, columns, rows = array.shape
    return pl.pallas_call(
        flip_kernel,
        grid=(1,),
        out_shape=jax.ShapeDtypeStruct((rows, columns), bf16),
        in_specs=[whole(array.shape)],
        out_specs=whole((rows, columns)),
        compiler_params=params(40),
        cost_estimate=cost(0.1),
        name="flip",
    )(array)


def final_kernel(
    heads_ref, weights_ref, tokens_ref, grad_mid_ref, vectors_ref, *refs
):
    out_ref, sums_ref, acc_ref, lhs = refs[-4:]
    step = pl.program_id(0)
    lanes = heads_ref.shape[2] // 3

    @pl.when(step == 0)
    def _():
        acc_ref[...] = jnp.zeros(acc_ref.shape, f32)

    source = pl.ds(pl.multiple_of(step * lanes, lanes), lanes)
    for g in range(heads_ref.shape[0]):
        lhs[:, g * lanes : (g + 1) * lanes] = heads_ref[g, :, source]
    acc_ref[...] += lax.dot_general(lhs[...], weights_ref[...], NT, preferred_element_type=f32)

    @pl.when(step == pl.num_programs(0) - 1)
    def _():
        vecs = vectors_ref[...].astype(f32)
        grad = acc_ref[...]
        normed, inverse = normalize(tokens_ref[...].astype(f32))
        out_ref[...] = grad_mid_ref[...] + norm_pull(grad, vecs[0:1], normed, inverse)
        sums_ref[0:1, :] = jnp.sum(grad * normed, axis=0, keepdims=True)
        sums_ref[1:2, :] = jnp.sum(grad, axis=0, keepdims=True)


def token_gradient(heads, matrices, tokens, grad_mid, vectors, extras):
    rows, model = tokens.shape
    return pl.pallas_call(
        final_kernel,
        grid=(3,),
        out_shape=(
            jax.ShapeDtypeStruct((rows, model), f32),
            jax.ShapeDtypeStruct((2, model), f32),
        ),
        in_specs=[
            whole(heads.shape),
            pl.BlockSpec((model, model), lambda i: (0, i)),
            whole((rows, model)),
            whole((rows, model)),
            whole(vectors.shape),
        ]
        + [anywhere()] * len(extras),
        out_specs=(whole((rows, model)), whole((2, model))),
        scratch_shapes=[pltpu.VMEM((rows, model), f32), pltpu.VMEM((rows, model), bf16)],
        compiler_params=params(56),
        cost_estimate=cost(6),
        name="token_gradient",
    )(heads, matrices, tokens, grad_mid, vectors, *extras)


def vector_pieces_kernel(rank_ref, one_ref, bias_ref, two_ref, units_ref, *refs):
    states, out_ref = refs[:3], refs[3]
    rank = rank_ref[0]
    lanes = out_ref.shape[2]
    out_ref[...] = jnp.zeros(out_ref.shape, f32)
    copies = out_ref.shape[0] // 8
    for b in range(8):
        columns = slice(b * lanes, (b + 1) * lanes)
        for c in range(copies):
            out_ref[copies * b + c, 0:2, :] = one_ref[:, columns]
            out_ref[copies * b + c, 4:8, :] = two_ref[:, columns]
    rows, own = states[0].shape
    packed = jnp.concatenate(
        [ref[...] for ref in states] + [jnp.zeros((rows, lanes - 3 * own), f32)], axis=1
    )
    for b in range(out_ref.shape[0]):
        out_ref[b, 12 : 12 + rows, :] = packed
    for c in range(copies):
        out_ref[copies * rank + c, 2:3, :] = bias_ref[:, 0:lanes]
        out_ref[copies * rank + c, 3:4, :] = bias_ref[:, 2 * lanes : 3 * lanes]
    pieces = units_ref.shape[1] // lanes
    for n in range(pieces):
        place = rank * pieces + n
        for c in range(copies):
            out_ref[copies * (place % 8) + c, pl.ds(8 + place // 8, 1), :] = units_ref[
                :, n * lanes : (n + 1) * lanes
            ]


def vector_pieces(rank, one, bias, two, units, states, devices):
    lanes = one.shape[1] // 8
    return pl.pallas_call(
        vector_pieces_kernel,
        grid=(1,),
        out_shape=jax.ShapeDtypeStruct((devices, 24, lanes), f32),
        in_specs=[smem(), whole(one.shape), whole(bias.shape), whole(two.shape), whole(units.shape)]
        + [whole(state.shape) for state in states],
        out_specs=whole((devices, 24, lanes)),
        compiler_params=params(40),
        cost_estimate=cost(1),
        name="vector_pieces",
    )(rank, one, bias, two, units, *states)


def adam(master, first, second, gradient, decay_rate):
    correction = 1.0 - BETA**STEP
    moment = BETA * first + (1.0 - BETA) * gradient
    variance = BETA * second + (1.0 - BETA) * gradient * gradient
    direction = moment / correction / (jnp.sqrt(variance / correction) + ADAM_EPSILON)
    return moment, variance, master - RATE * (direction + decay_rate * master)


def vector_update_kernel(root, place_ref, got_ref, *refs):
    outs, copied_ref = refs[:3], refs[3]
    lanes = got_ref.shape[2]
    rows, own = outs[0].shape
    gradient = jnp.sum(got_ref[:, :16, :], axis=0) * root
    shard = place_ref[0] % 4
    first = place_ref[0] - shard
    columns = lax.broadcasted_iota(jnp.int32, (16, lanes), 1) // own
    total = jnp.zeros((16, lanes), f32)
    for k in range(4):
        other = shard ^ k
        shifted = pltpu.roll(gradient, lax.rem(lanes - other * own, lanes), 1)[:rows, :own]
        packed = got_ref[first + other, 12 : 12 + rows, :]
        states = [packed[:, n * own : (n + 1) * own] for n in range(3)]
        values = adam(*states, shifted, 0.0)
        if k == 0:
            for ref, value in zip(outs, values):
                ref[...] = value
        wide = jnp.concatenate([values[2], jnp.zeros((rows, lanes - own), f32)], axis=1)
        wide = jnp.concatenate([wide, jnp.zeros((16 - rows, lanes), f32)], axis=0)
        total = jnp.where(columns == other, pltpu.roll(wide, other * own, 1), total)
    copied_ref[...] = total[:rows].astype(bf16)


def vector_update(place, got, rows, own, root):
    lanes = got.shape[2]
    mine = jax.ShapeDtypeStruct((rows, own), f32)
    return pl.pallas_call(
        functools.partial(vector_update_kernel, root),
        grid=(1,),
        out_shape=(mine, mine, mine, jax.ShapeDtypeStruct((rows, lanes), bf16)),
        in_specs=[smem(), whole(got.shape)],
        out_specs=(whole((rows, own)),) * 3 + (whole((rows, lanes)),),
        compiler_params=params(40),
        cost_estimate=cost(1),
        name="vector_update",
    )(place, got)


def update_kernel(root, got_ref, *refs):
    states, outs = refs[:3], refs[-5:-2]
    copied_ref, gradient_ref = refs[-2:]
    lanes = got_ref.shape[2]
    for g in range(got_ref.shape[0]):
        gradient_ref[:, g * lanes : (g + 1) * lanes] = got_ref[g].astype(f32)
    values = adam(*[ref[...] for ref in states], gradient_ref[...] * root, DECAY_RATE)
    for ref, value in zip(outs, values):
        ref[...] = value
    copied_ref[...] = values[2].astype(bf16)


def matrix_update(got, states, previous, extras, first, parts, root, name):
    groups, rows, packed = got.shape
    lanes = packed // parts
    block = groups * lanes
    total = states[0].shape[1]
    start = first // block
    state = pl.BlockSpec((rows, block), lambda i: (0, start + i))
    return pl.pallas_call(
        functools.partial(update_kernel, root),
        grid=(parts,),
        out_shape=(jax.ShapeDtypeStruct((rows, total), f32),) * 3
        + (jax.ShapeDtypeStruct((rows, parts * block), bf16),),
        in_specs=[pl.BlockSpec((groups, rows, lanes), lambda i: (0, 0, i))]
        + [state] * 3
        + [anywhere()] * (len(previous) + len(extras)),
        out_specs=(state,) * 3 + (pl.BlockSpec((rows, block), lambda i: (0, i)),),
        scratch_shapes=[pltpu.VMEM((rows, block), f32)],
        input_output_aliases={4 + k: k for k in range(len(previous))},
        compiler_params=params(56),
        cost_estimate=cost(4),
        name=name,
    )(got, *states, *previous, *extras)


def place_kernel(late_blocks, shard_ref, *refs):
    out_ref = refs[-1]
    rows = refs[0].shape[0]
    for first, chosen in ((0, pl.program_id(0) < late_blocks), (4, pl.program_id(0) >= late_blocks)):

        @pl.when(chosen)
        def _(first=first):
            for k in range(4):
                place = pl.multiple_of((shard_ref[0] ^ k) * rows, rows)
                out_ref[pl.ds(place, rows), :] = refs[first + k][...]


def place_copies(shard, late, early):
    rows = late[0].shape[0]
    block = 2048
    count = late[0].shape[1] // block
    total = count * block + early[0].shape[1]
    return pl.pallas_call(
        functools.partial(place_kernel, count),
        grid=(total // block,),
        out_shape=jax.ShapeDtypeStruct((4 * rows, total), bf16),
        in_specs=[smem()]
        + [pl.BlockSpec((rows, block), lambda i: (0, jnp.minimum(i, count - 1)))] * 4
        + [pl.BlockSpec((rows, block), lambda i: (0, jnp.maximum(i - count, 0)))] * 4,
        out_specs=pl.BlockSpec((4 * rows, block), lambda i: (0, i)),
        compiler_params=params(40),
        cost_estimate=cost(2),
        name="place_copies",
    )(shard, *late, *early)


def fits_sequence_plan(mesh):
    return mesh.shape["dp"] == 4 and mesh.shape["ctx"] == 2 and mesh.shape["shard"] == 4


EVERY = ("dp", "ctx", "shard")
SEQUENCE = ("ctx", "shard")


def swap(array, axis, bit):
    count = lax.axis_size(axis)
    return lax.ppermute(array, axis, [(i, i ^ bit) for i in range(count)])


def gather_blocks(block, ready=True):
    over_ctx = swap(block, "ctx", 1)
    over_y = swap(block, "shard", 2)
    over_core = swap(block, "shard", 1)
    even = (lax.axis_index("shard") % 2 == 0) & ready
    relay = jnp.where(even, over_ctx, over_y)
    opposite = lax.ppermute(relay, SEQUENCE, [(i, i ^ (4 if i % 2 else 2)) for i in range(8)])
    ctx_core = swap(over_ctx, "shard", 1)
    y_core = swap(over_y, "shard", 1)
    opposite_core = swap(opposite, "shard", 1)
    return relay, [
        block, over_core, over_y, y_core, over_ctx, ctx_core, opposite, opposite_core
    ]


def gather_direct(block):
    straight = [
        block,
        swap(block, "shard", 2),
        swap(block, "ctx", 1),
        lax.ppermute(block, SEQUENCE, [(i, i ^ 6) for i in range(8)]),
    ]
    return [array for first in straight for array in (first, swap(first, "shard", 1))]


def gather_rows(array):
    return lax.all_gather(array, SEQUENCE, axis=0, tiled=True)


def exchange(array, axes=SEQUENCE):
    return lax.all_to_all(array, axes, 0, 0, tiled=True)


def dot_tn(left, right):
    return lax.dot_general(left, right, (((0,), (0,)), ((), ())), preferred_element_type=f32)


def dot_nt(left, right):
    return lax.dot_general(left, right, NT, preferred_element_type=f32)


def dot_nn(left, right):
    return jnp.dot(left, right, preferred_element_type=f32)


def shift_dp(array, distance):
    return lax.ppermute(array, "dp", [(i, (i + distance) % 4) for i in range(4)])


def gather_shards(array):
    over_core = swap(array, "shard", 1)
    over_y = swap(array, "shard", 2)
    return [array, over_core, over_y, swap(over_y, "shard", 1)]


def sequence_shards(
    tokens,
    cotangent,
    picture_starts,
    matrices,
    vectors,
    master_matrices,
    master_vectors,
    first_matrices,
    first_vectors,
    second_matrices,
    second_vectors,
):
    row_count, width = tokens.shape
    ff_width = (matrices.shape[1] - 4 * width) // 2
    group = 8
    shard = lax.axis_index("shard")
    rank = lax.axis_index("ctx") * 4 + shard
    depth = lax.axis_index("dp")
    lanes = width // group
    units = ff_width // group
    own_rows = master_matrices.shape[0]
    seq = group * row_count
    head = rank * 2 + jnp.arange(2)
    slopes = jnp.exp2(-8.0 * (head.astype(f32) + 1.0) / HEADS)
    rank_array = rank.astype(jnp.int32).reshape(1)
    shard_array = shard.astype(jnp.int32).reshape(1)
    vector_rows = vectors.astype(f32)
    up_bias = vector_rows[8:].reshape(1, ff_width)

    with jax.named_scope("prepare"):
        pattern = key_pattern(picture_starts, slopes, seq, lanes)
    with jax.named_scope("gather_tokens"):
        ready = pattern[0, 0, lanes // 2 + 3] == 1.0
        passed, token_blocks = gather_blocks(tokens, ready)
    with jax.named_scope("gather_cotangent"):
        zero = passed[0, 0] * 0
        cotangent_late = cotangent + zero
        cotangent_all = gather_rows(cotangent_late)
    attended_heads, attended_wide, *saved, hidden_all = attention_forward(
        token_blocks,
        matrices,
        vectors,
        pattern,
        rank_array,
        picture_starts,
        slopes,
        cotangent_late,
    )
    with jax.named_scope("attended_exchange"):
        attended_got = exchange(attended_heads)
    with jax.named_scope("transpose_keys"):
        half = lanes // 2
        keys_low = saved[1]
        keys_transposed = jnp.concatenate(
            [keys_low[0, :, :half], keys_low[1, :, half:]], axis=1
        ).T
    middle, hidden_two = project_norm(
        attended_got, tokens, matrices, vectors, keys_transposed
    )
    with jax.named_scope("gather_attended"):
        head_blocks = gather_direct(attended_heads)
    layer_output, grad_mid, grad_out, sums_two = feed_forward(
        hidden_two, up_bias, middle, cotangent, vectors, matrices
    )
    with jax.named_scope("grad_attended_exchange"):
        grad_got = exchange(grad_out)
    early, unit_sums, attended_all = own_units(
        rank_array,
        token_blocks,
        head_blocks,
        cotangent_all,
        up_bias,
        matrices,
        vectors,
        [grad_out],
    )
    with jax.named_scope("grad_feed"):
        (early,) = gate([early], [grad_got])
        early_sum = flip(lax.psum_scatter(early, "dp", scatter_dimension=0, tiled=True))
    grad_abs, grad_flipped, bias_sums, mid_flipped = attention_backward(
        (*saved, keys_transposed), attended_wide, grad_got, picture_starts, [early]
    )
    with jax.named_scope("grad_qkv_exchange"):
        grad_tokens = exchange(grad_abs.reshape(group, row_count, 3 * lanes))
    with jax.named_scope("grad_late"):
        near_far, near, relay, late_own = late_weights(
            depth.astype(jnp.int32).reshape(1), grad_flipped, hidden_all, mid_flipped, attended_all.reshape(seq, width)
        )
        beside = [(i, i ^ 1) for i in range(4)]
        near_far = lax.ppermute(near_far, "dp", beside)
        near = lax.ppermute(near, "dp", beside)
    with jax.named_scope("early_rows"):
        (early_sum,) = gate([early_sum], [grad_tokens, late_own])
        early_got = exchange(early_sum.reshape(group, own_rows, 2 * units))
    with jax.named_scope("grad_late"):
        near_far, near = gate([near_far, near], [early_sum])
        relay = (relay + near_far.astype(f32)).astype(bf16)
        far = lax.ppermute(relay, "dp", [(i, 3 - i) for i in range(4)])
    with jax.named_scope("late_rows"):
        late_sum = (late_own + near.astype(f32) + far.astype(f32)).T.astype(bf16)
        (late_sum,) = gate([late_sum], [early_got])
        late_got = exchange(late_sum.reshape(group, own_rows, 4 * lanes))
    root = (row_count * lax.axis_size("dp") * group) ** (-0.5)
    matrix_states = (master_matrices, first_matrices, second_matrices)
    *early_states, early_copy = matrix_update(
        early_got, matrix_states, (), [late_sum], 4 * width, 2, root, "early_update"
    )
    with jax.named_scope("early_copies"):
        early_copied = gather_shards(early_copy)
    token_grads, sums_one = token_gradient(
        grad_tokens, matrices, tokens, grad_mid, vectors, [early_copy]
    )
    with jax.named_scope("grad_vectors"):
        vector_states = (master_vectors, first_vectors, second_vectors)
        pieces = vector_pieces(
            rank_array, sums_one, bias_sums, sums_two, unit_sums, vector_states, 32
        )
        (pieces,) = gate([pieces], [late_got])
        vectors_got = exchange(pieces, EVERY)
    moment_w, variance_w, updated_w, late_copy = matrix_update(
        late_got,
        matrix_states,
        early_states,
        [early_copied[2], pieces],
        0,
        4,
        root,
        "late_update",
    )
    with jax.named_scope("late_copies"):
        late_copied = gather_shards(late_copy)
    copied_w = place_copies(shard_array, late_copied, early_copied)
    moment_v, variance_v, updated_v, copied_v = vector_update(
        (depth * group + rank).astype(jnp.int32).reshape(1),
        vectors_got,
        *master_vectors.shape,
        root,
    )
    return (
        layer_output,
        token_grads,
        moment_w,
        moment_v,
        variance_w,
        variance_v,
        updated_w,
        updated_v,
        copied_w,
        copied_v,
    )


def solution(mesh):
    in_specs = (
        P(("dp", "ctx", "shard"), None),
        P(("dp", "ctx", "shard"), None),
        P("dp", None),
        P(),
        P(),
        P(("dp", "ctx", "shard"), None),
        P(None, ("dp", "ctx", "shard")),
        P(("dp", "ctx", "shard"), None),
        P(None, ("dp", "ctx", "shard")),
        P(("dp", "ctx", "shard"), None),
        P(None, ("dp", "ctx", "shard")),
    )
    out_specs = (
        P(("dp", "ctx", "shard"), None),
        P(("dp", "ctx", "shard"), None),
        P(("dp", "ctx", "shard"), None),
        P(None, ("dp", "ctx", "shard")),
        P(("dp", "ctx", "shard"), None),
        P(None, ("dp", "ctx", "shard")),
        P(("dp", "ctx", "shard"), None),
        P(None, ("dp", "ctx", "shard")),
        P(("dp", "ctx"), None),
        P(None, ("dp", "ctx")),
    )
    body = sequence_shards if fits_sequence_plan(mesh) else general_shards
    return jax.shard_map(body, mesh=mesh, in_specs=in_specs, out_specs=out_specs, check_vma=False)
```

```python
import functools
import math

import jax
import jax.numpy as jnp
from jax import lax
from jax.experimental import pallas as pl
from jax.experimental.pallas import tpu as pltpu
from jax.sharding import PartitionSpec as P

HEADS = 16
PIC = 256
STEP = 2


EPSILON = 1e-05
NEGATIVE = -1e30
BETA = 0.5
RATE = 0.03
DECAY_RATE = 0.1
ADAM_EPSILON = 1e-08


def token_tags(index, start_list, block_len):
    after = index[:, None] - start_list[None, :]
    inside = (after >= 0) & (after < block_len)
    offsets = jnp.sum(jnp.clip(after, 0, block_len - 1), axis=1)
    number = jnp.arange(1, start_list.shape[0] + 1, dtype=jnp.int32)
    picture = jnp.sum(jnp.where(inside, number[None, :], 0), axis=1) - 1
    return (index - offsets, picture)


def block_scores(query_heads, query_index, key_heads, key_index, start_list, slopes, factor):
    query_pos, query_pic = token_tags(query_index, start_list, PIC)
    key_pos, key_pic = token_tags(key_index, start_list, PIC)
    raw = jnp.einsum("qhd,khd->hqk", query_heads, key_heads, preferred_element_type=jnp.float32)
    distance = (query_pos[:, None] - key_pos[None, :]).astype(jnp.float32)
    logits = raw * factor - slopes[:, None, None] * distance[None, :, :]
    same = (query_pic[:, None] == key_pic[None, :]) & (query_pic[:, None] >= 0)
    visible = (key_index[None, :] <= query_index[:, None]) | same
    return (logits, visible[None, :, :])


def layer_norm(inputs):
    centered = inputs - jnp.mean(inputs, axis=1, keepdims=True)
    inverse_std = lax.rsqrt(jnp.mean(centered * centered, axis=1, keepdims=True) + EPSILON)
    return (centered * inverse_std, inverse_std)


def norm_backward(grad_normed, gain, normed, inverse_std):
    scaled = grad_normed * gain
    return inverse_std * (
        scaled
        - jnp.mean(scaled, axis=1, keepdims=True)
        - normed * jnp.mean(scaled * normed, axis=1, keepdims=True)
    )


def activate(value):
    return jax.nn.gelu(value, approximate=True)


def regroup(array, dim, outer, inner):
    shape = array.shape
    split = array.reshape(
        shape[:dim] + (outer, inner, shape[dim] // (outer * inner)) + shape[dim + 1 :]
    )
    return jnp.swapaxes(split, dim, dim + 1).reshape(shape)


def adam_update(master, first, second, gradient, correction, decay_rate):
    moment = BETA * first + (1.0 - BETA) * gradient
    variance = BETA * second + (1.0 - BETA) * gradient * gradient
    direction = moment / correction / (jnp.sqrt(variance / correction) + ADAM_EPSILON)
    return (moment, variance, master - RATE * (direction + decay_rate * master))


def general_shards(
    tokens,
    cotangent,
    picture_starts,
    matrices,
    vectors,
    master_matrices,
    master_vectors,
    first_matrices,
    first_vectors,
    second_matrices,
    second_vectors,
):
    row_count, model_width = tokens.shape
    ff_width = (matrices.shape[1] - 4 * model_width) // 2
    head_count = HEADS
    head_width = model_width // head_count
    factor = head_width ** (-0.5)
    group_size = lax.axis_size("ctx") * lax.axis_size("shard")
    group_rank = lax.axis_index("ctx") * lax.axis_size("shard") + lax.axis_index("shard")
    seq_length = row_count * group_size
    first_row = group_rank * row_count
    start_list = picture_starts[0]
    slopes = jnp.exp2(-8.0 * (jnp.arange(head_count, dtype=jnp.float32) + 1.0) / head_count)
    block_rows = math.gcd(seq_length, 512)
    block_count = seq_length // block_rows
    w_qkv = matrices[:, : 3 * model_width]
    w_proj = matrices[:, 3 * model_width : 4 * model_width]
    w_up = matrices[:, 4 * model_width : 4 * model_width + ff_width]
    w_down = matrices[:, 4 * model_width + ff_width :]
    inputs = tokens.astype(jnp.float32)
    vector_rows = vectors.astype(jnp.float32)
    up_bias = vector_rows[8:].reshape(ff_width)
    normed, inverse_std = layer_norm(inputs)
    hidden = (normed * vector_rows[0] + vector_rows[1]).astype(jnp.bfloat16)
    projected = jnp.dot(hidden, w_qkv, preferred_element_type=jnp.float32)
    queries = (projected[:, :model_width] + vector_rows[2]).astype(jnp.bfloat16)
    kv_bias = jnp.concatenate([jnp.zeros((model_width,), jnp.float32), vector_rows[3]])
    kv_local = (projected[:, model_width:] + kv_bias).astype(jnp.bfloat16)
    gathered = lax.all_gather(kv_local, ("ctx", "shard"), axis=0, tiled=True)
    query_index = first_row + jnp.arange(row_count, dtype=jnp.int32)
    query_heads = queries.reshape(row_count, head_count, head_width)

    def key_block(index):
        piece = lax.dynamic_slice_in_dim(gathered, index * block_rows, block_rows, 0)
        key_heads = piece[:, :model_width].reshape(block_rows, head_count, head_width)
        value_heads = piece[:, model_width:].reshape(block_rows, head_count, head_width)
        key_index = index * block_rows + jnp.arange(block_rows, dtype=jnp.int32)
        logits, visible = block_scores(
            query_heads, query_index, key_heads, key_index, start_list, slopes, factor
        )
        return (logits, visible, key_heads, value_heads)

    def running_total(index, carry):
        highest, total = carry
        logits, visible, key_heads, value_heads = key_block(index)
        masked = jnp.where(visible, logits, NEGATIVE)
        updated = jnp.maximum(highest, jnp.max(masked, axis=2))
        weights = jnp.where(visible, jnp.exp(logits - updated[:, :, None]), 0.0)
        return (updated, total * jnp.exp(highest - updated) + jnp.sum(weights, axis=2))

    start_high = jnp.full((head_count, row_count), NEGATIVE, jnp.float32)
    start_total = jnp.zeros((head_count, row_count), jnp.float32)
    highest, total = lax.fori_loop(0, block_count, running_total, (start_high, start_total))
    log_total = highest + jnp.log(total)

    def weighted_sum(index, accum):
        logits, visible, key_heads, value_heads = key_block(index)
        probs = jnp.where(visible, jnp.exp(logits - log_total[:, :, None]), 0.0).astype(
            jnp.bfloat16
        )
        return accum + jnp.einsum(
            "hqk,khd->qhd", probs, value_heads, preferred_element_type=jnp.float32
        )

    attended = lax.fori_loop(
        0, block_count, weighted_sum, jnp.zeros((row_count, head_count, head_width), jnp.float32)
    )
    attended_low = attended.reshape(row_count, model_width).astype(jnp.bfloat16)
    middle = (
        inputs + jnp.dot(attended_low, w_proj, preferred_element_type=jnp.float32) + vector_rows[4]
    )
    normed_two, inverse_two = layer_norm(middle)
    hidden_two = (normed_two * vector_rows[5] + vector_rows[6]).astype(jnp.bfloat16)
    pre_act = jnp.dot(hidden_two, w_up, preferred_element_type=jnp.float32) + up_bias
    act_low = activate(pre_act).astype(jnp.bfloat16)
    down_out = lax.dot_general(
        act_low, w_down, (((1,), (1,)), ((), ())), preferred_element_type=jnp.float32
    )
    layer_output = (middle + down_out + vector_rows[7]).astype(jnp.bfloat16)
    upstream = cotangent.astype(jnp.float32)
    grad_act = jnp.dot(cotangent, w_down, preferred_element_type=jnp.float32)
    gelu_value, gelu_pull = jax.vjp(activate, pre_act)
    grad_pre = gelu_pull(grad_act)[0].astype(jnp.bfloat16)
    grad_up_w = lax.dot_general(
        hidden_two, grad_pre, (((0,), (0,)), ((), ())), preferred_element_type=jnp.float32
    )
    grad_down_w = lax.dot_general(
        cotangent, act_low, (((0,), (0,)), ((), ())), preferred_element_type=jnp.float32
    )
    grad_two = lax.dot_general(
        grad_pre, w_up, (((1,), (1,)), ((), ())), preferred_element_type=jnp.float32
    )
    grad_mid = upstream + norm_backward(grad_two, vector_rows[5], normed_two, inverse_two)
    grad_mid_low = grad_mid.astype(jnp.bfloat16)
    grad_proj = lax.dot_general(
        attended_low, grad_mid_low, (((0,), (0,)), ((), ())), preferred_element_type=jnp.float32
    )
    grad_out = lax.dot_general(
        grad_mid_low, w_proj, (((1,), (1,)), ((), ())), preferred_element_type=jnp.float32
    ).astype(jnp.bfloat16)
    grad_heads = grad_out.reshape(row_count, head_count, head_width)
    delta = jnp.sum(grad_heads.astype(jnp.float32) * attended, axis=2).T

    def score_grads(index):
        logits, visible, key_heads, value_heads = key_block(index)
        probs = jnp.where(visible, jnp.exp(logits - log_total[:, :, None]), 0.0)
        product = jnp.einsum(
            "qhd,khd->hqk", grad_heads, value_heads, preferred_element_type=jnp.float32
        )
        grad_logits = (probs * (product - delta[:, :, None])).astype(jnp.bfloat16)
        return (probs, grad_logits, key_heads)

    def both_grads(index, carry):
        accum, key_terms = carry
        probs, grad_logits, key_heads = score_grads(index)
        accum = (
            accum
            + jnp.einsum("hqk,khd->qhd", grad_logits, key_heads, preferred_element_type=jnp.float32)
            * factor
        )
        grad_key = (
            jnp.einsum("hqk,qhd->khd", grad_logits, query_heads, preferred_element_type=jnp.float32)
            * factor
        )
        grad_value = jnp.einsum(
            "hqk,qhd->khd",
            probs.astype(jnp.bfloat16),
            grad_heads,
            preferred_element_type=jnp.float32,
        )
        term = jnp.concatenate(
            [
                grad_key.reshape(block_rows, model_width),
                grad_value.reshape(block_rows, model_width),
            ],
            axis=1,
        )
        return (accum, lax.dynamic_update_slice_in_dim(key_terms, term, index * block_rows, 0))

    grad_query, key_terms = lax.fori_loop(
        0,
        block_count,
        both_grads,
        (
            jnp.zeros((row_count, head_count, head_width), jnp.float32),
            jnp.zeros((seq_length, 2 * model_width), jnp.float32),
        ),
    )
    own_key_grads = lax.psum_scatter(key_terms, ("ctx", "shard"), scatter_dimension=0, tiled=True)
    grad_qkv = jnp.concatenate(
        [grad_query.reshape(row_count, model_width), own_key_grads], axis=1
    ).astype(jnp.bfloat16)
    grad_qkv_weights = lax.dot_general(
        hidden, grad_qkv, (((0,), (0,)), ((), ())), preferred_element_type=jnp.float32
    )
    grad_hidden = lax.dot_general(
        grad_qkv, w_qkv, (((1,), (1,)), ((), ())), preferred_element_type=jnp.float32
    )
    query_bias_grad = jnp.sum(grad_qkv[:, :model_width].astype(jnp.float32), axis=0)
    value_bias_grad = jnp.sum(grad_qkv[:, 2 * model_width :].astype(jnp.float32), axis=0)
    grad_vectors = jnp.concatenate(
        [
            jnp.stack(
                [
                    jnp.sum(grad_hidden * normed, axis=0),
                    jnp.sum(grad_hidden, axis=0),
                    query_bias_grad,
                    value_bias_grad,
                    jnp.sum(grad_mid, axis=0),
                    jnp.sum(grad_two * normed_two, axis=0),
                    jnp.sum(grad_two, axis=0),
                    jnp.sum(upstream, axis=0),
                ]
            ),
            jnp.sum(grad_pre.astype(jnp.float32), axis=0).reshape(
                ff_width // model_width, model_width
            ),
        ],
        axis=0,
    )
    token_grads = grad_mid + norm_backward(grad_hidden, vector_rows[0], normed, inverse_std)
    grad_matrix = jnp.concatenate([grad_qkv_weights, grad_proj, grad_up_w, grad_down_w], axis=1)
    shard_count = lax.axis_size("shard")
    replicas = lax.axis_size("dp") * lax.axis_size("ctx")
    part_matrix, part_vec = (
        lax.psum_scatter(
            regroup(grad_matrix, 0, replicas, shard_count), "shard", scatter_dimension=0, tiled=True
        ),
        lax.psum_scatter(
            regroup(grad_vectors, 1, replicas, shard_count),
            "shard",
            scatter_dimension=1,
            tiled=True,
        ),
    )
    part_matrix, part_vec = (
        lax.psum_scatter(part_matrix, ("dp", "ctx"), scatter_dimension=0, tiled=True),
        lax.psum_scatter(part_vec, ("dp", "ctx"), scatter_dimension=1, tiled=True),
    )
    root = (row_count * lax.axis_size("dp") * group_size) ** (-0.5)
    correction = 1.0 - BETA**STEP
    moment_w, variance_w, updated_w = adam_update(
        master_matrices, first_matrices, second_matrices, part_matrix * root, correction, DECAY_RATE
    )
    moment_v, variance_v, updated_v = adam_update(
        master_vectors, first_vectors, second_vectors, part_vec * root, correction, 0.0
    )
    copied_w, copied_v = (
        lax.all_gather(updated_w.astype(jnp.bfloat16), "shard", axis=0, tiled=True),
        lax.all_gather(updated_v.astype(jnp.bfloat16), "shard", axis=1, tiled=True),
    )
    return (
        layer_output,
        token_grads,
        moment_w,
        moment_v,
        variance_w,
        variance_v,
        updated_w,
        updated_v,
        copied_w,
        copied_v,
    )


BLOCK = 256
EXTRA = 1
f32 = jnp.float32
bf16 = jnp.bfloat16
NT = (((1,), (1,)), ((), ()))
GELU_SCALE = math.sqrt(2.0 / math.pi)
GELU_CUBE = 0.044715


def split3(value):
    high = value.astype(bf16).astype(f32)
    rest = value - high
    middle = rest.astype(bf16).astype(f32)
    low = (rest - middle).astype(bf16).astype(f32)
    return high, middle, low


def positions(index, starts_ref, count):
    result = index
    for b in range(count):
        result = result - jnp.clip(index - starts_ref[0, b], 0, PIC - 1)
    return result.astype(f32)


def limits(index, starts_ref, count):
    result = index + 1
    for b in range(count):
        start = starts_ref[0, b]
        result = jnp.where((index >= start) & (index < start + PIC), start + PIC, result)
    return result


def head_lanes(shape, h, width):
    lane = lax.broadcasted_iota(jnp.int32, shape, 1)
    inside = (lane < width) if h == 0 else (lane >= width)
    return inside, lane - width if h == 0 else lane


def pick(spare, values):
    out = jnp.zeros(spare.shape, f32)
    for e, value in enumerate(values):
        out = jnp.where(spare == e, value, out)
    return out


def smem():
    return pl.BlockSpec(memory_space=pltpu.SMEM)


def vmem():
    return pl.BlockSpec(memory_space=pltpu.VMEM)


def anywhere():
    return pl.BlockSpec(memory_space=pl.ANY)


def hbm():
    return pl.BlockSpec(memory_space=pltpu.HBM)


def params(mebibytes):
    return pltpu.CompilerParams(vmem_limit_bytes=mebibytes * 2**20)


def cost(microseconds):
    return pl.CostEstimate(
        flops=int(microseconds * 1.0e9), bytes_accessed=0, transcendentals=0
    )


def start_all(copies):
    for copy in copies:
        copy.start()
    return copies


def wait_all(copies):
    for copy in copies:
        copy.wait()


def pattern_kernel(width, count, starts_ref, slopes_ref, out_ref):
    lanes = out_ref.shape[2]
    step = pl.program_id(0)
    index = lax.broadcasted_iota(jnp.int32, (BLOCK, lanes), 0) + step * BLOCK
    pos = positions(index, starts_ref, count)
    for h in range(2):
        _, spare = head_lanes((BLOCK, lanes), h, width)
        parts = split3(pos * slopes_ref[h])
        out_ref[h] = pick(spare, parts + (1.0, 1.0, 1.0)).astype(bf16)


def key_pattern(starts, slopes, seq, lanes):
    return pl.pallas_call(
        functools.partial(pattern_kernel, lanes // 2, starts.shape[1]),
        grid=(seq // BLOCK,),
        out_shape=jax.ShapeDtypeStruct((2, seq, lanes), bf16),
        in_specs=[smem()] * 2,
        out_specs=pl.BlockSpec((2, BLOCK, lanes), lambda i: (0, i, 0)),
        compiler_params=params(40),
        cost_estimate=cost(3),
        name="key_pattern",
    )(starts, slopes)


def forward_kernel(width, tile, count, rank_ref, starts_ref, slopes_ref, *refs):
    blocks = refs[:8]
    matrices_ref, vectors_ref, pattern_in = refs[8:11]
    att_out, wide_out, q_out, k_out, v_out, all_out = refs[11 + EXTRA : 17 + EXTRA]
    hid, wts, vecs, pattern, qa, ka, va, att, wide = refs[17 + EXTRA : 26 + EXTRA]
    in_sems, w_sems, hid_sems, out_sems = refs[26 + EXTRA :]
    seq, lanes = wide.shape
    model = hid.shape[1]
    rank = rank_ref[0]
    factor = width**-0.5
    w_copies = []
    for part in range(3):
        columns = pl.ds(pl.multiple_of(part * model + rank * lanes, lanes), lanes)
        w_copies.append(
            pltpu.make_async_copy(
                matrices_ref.at[:, columns],
                wts.at[:, part * lanes : (part + 1) * lanes],
                w_sems.at[part],
            )
        )
    w_copies.append(pltpu.make_async_copy(vectors_ref, vecs, w_sems.at[3]))
    start_all(w_copies)
    in_copies = start_all(
        [
            pltpu.make_async_copy(
                blocks[k], hid.at[k * BLOCK : (k + 1) * BLOCK], in_sems.at[k]
            )
            for k in range(8)
        ]
    )
    pattern_copy = pltpu.make_async_copy(pattern_in, pattern, w_sems.at[4])
    pattern_copy.start()
    wait_all(w_copies)
    gains = vecs[...].astype(f32)
    bias = vecs[:, pl.ds(pl.multiple_of(rank * lanes, lanes), lanes)].astype(f32)
    out_copies = []
    ones = []
    for h in range(2):
        inside, spare = head_lanes((BLOCK, lanes), h, width)
        ones.append((inside, jnp.where(spare < 3, 1.0, 0.0)))
    for pair in range(4):
        first = 2 * pair
        for k in (first, first + 1):
            in_copies[k].wait()
        both = slice(first * BLOCK, (first + 2) * BLOCK)
        normed, _ = normalize(hid[both, :].astype(f32))
        hid[both, :] = (normed * gains[0:1] + gains[1:2]).astype(bf16)
        for k in (first, first + 1):
            rows = slice(k * BLOCK, (k + 1) * BLOCK)
            dst = pl.ds(pl.multiple_of((k ^ rank) * BLOCK, BLOCK), BLOCK)
            copy = pltpu.make_async_copy(hid.at[rows], all_out.at[dst], hid_sems.at[k])
            copy.start()
            out_copies.append(copy)
        value = jnp.dot(hid[both, :], wts[...], preferred_element_type=f32)
        if pair == 0:
            pattern_copy.wait()
        for k in (first, first + 1):
            local = slice((k - first) * BLOCK, (k - first + 1) * BLOCK)
            dst = pl.ds(pl.multiple_of((k ^ rank) * BLOCK, BLOCK), BLOCK)
            q = (value[local, 0:lanes] + bias[2:3]).astype(bf16).astype(f32) * factor
            key = value[local, lanes : 2 * lanes]
            v = value[local, 2 * lanes : 3 * lanes] + bias[3:4]
            for h in range(2):
                inside, spare_ones = ones[h]
                qa[h, dst, :] = jnp.where(inside, q, spare_ones).astype(bf16)
                ka[h, dst, :] = jnp.where(inside, key, pattern[h, dst, :].astype(f32)).astype(bf16)
                va[h, dst, :] = jnp.where(inside, v, spare_ones).astype(bf16)
    out_copies += start_all(
        [
            pltpu.make_async_copy(ka, k_out, out_sems.at[0]),
            pltpu.make_async_copy(va, v_out, out_sems.at[1]),
        ]
    )

    def scores(h, queries, keys):
        return lax.dot_general(
            qa[h, queries, :], ka[h, keys, :], NT, preferred_element_type=f32
        )

    def mask(first_row, first_column, shape):
        rows = lax.broadcasted_iota(jnp.int32, (shape[0], 1), 0) + first_row
        columns = lax.broadcasted_iota(jnp.int32, shape, 1) + first_column
        return columns < limits(rows, starts_ref, count)

    def lane_best(value):
        best = value[:, :lanes]
        for c in range(1, value.shape[1] // lanes):
            best = jnp.maximum(best, value[:, c * lanes : (c + 1) * lanes])
        return best

    def with_shift(h, rows, shift):
        inside, spare = head_lanes((tile, lanes), h, width)
        parts = split3(-jnp.broadcast_to(shift, (tile, lanes)))
        value = qa[h, rows, :].astype(f32)
        for e in range(3):
            value = jnp.where(spare == 3 + e, parts[e], value)
        qa[h, rows, :] = value.astype(bf16)

    for i in range(seq // tile):
        base = i * tile
        end = base + tile
        rows = slice(base, end)
        tail = slice(end - PIC, end)
        over = slice(end, end + PIC)
        seen = mask(base, base, (tile, tile))
        if end < seq:
            seen_over = mask(end - PIC, end, (PIC, PIC))
        best = []
        kept = []
        for h in range(2):
            diagonal = jnp.where(seen, scores(h, rows, rows), NEGATIVE)
            top = lane_best(diagonal)
            below = []
            for j in range(i):
                below.append(scores(h, rows, slice(j * tile, (j + 1) * tile)))
                top = jnp.maximum(top, lane_best(below[-1]))
            beyond = None
            if end < seq:
                beyond = jnp.where(seen_over, scores(h, tail, over), NEGATIVE)
                low = jnp.maximum(top[tile - PIC :], lane_best(beyond))
                top = jnp.concatenate([top[: tile - PIC], low], axis=0)
            best.append(jnp.max(top, axis=1, keepdims=True))
            kept.append((below, diagonal, beyond))
        sums = []
        for h in range(2):
            below, diagonal, beyond = kept[h]
            weights = [jnp.exp(value - best[h]).astype(bf16) for value in below]
            weights.append(jnp.exp(diagonal - best[h]).astype(bf16))
            acc = jnp.dot(
                jnp.concatenate(weights, axis=1), va[h, :end, :], preferred_element_type=f32
            )
            if end < seq:
                beyond = jnp.exp(beyond - best[h][tile - PIC :])
                low = acc[tile - PIC :] + jnp.dot(
                    beyond.astype(bf16), va[h, over, :], preferred_element_type=f32
                )
                acc = jnp.concatenate([acc[: tile - PIC], low], axis=0)
            sums.append(acc)
        outs = []
        for h in range(2):
            acc = sums[h]
            column = width if h == 0 else 0
            total = acc[:, column : column + 1]
            outs.append(acc / total)
            with_shift(h, rows, best[h] + jnp.log(total))
        inside, _ = head_lanes((tile, lanes), 0, width)
        out = jnp.where(inside, outs[0], outs[1])
        wide[rows, :] = out
        count_here = tile // BLOCK
        groups = slice(i * count_here, (i + 1) * count_here)
        att[groups] = out.astype(bf16).reshape(count_here, BLOCK, lanes)
        out_copies += start_all(
            [
                pltpu.make_async_copy(att.at[groups], att_out.at[groups], out_sems.at[2 + 3 * i]),
                pltpu.make_async_copy(wide.at[rows], wide_out.at[rows], out_sems.at[3 + 3 * i]),
                pltpu.make_async_copy(
                    qa.at[:, rows], q_out.at[:, rows], out_sems.at[4 + 3 * i]
                ),
            ]
        )
    wait_all(out_copies)


def attention_forward(blocks, matrices, vectors, pattern, rank, starts, slopes, extra, tile=512):
    rows, model = blocks[0].shape
    seq = 8 * rows
    lanes = model // 8
    heads = jax.ShapeDtypeStruct((2, seq, lanes), bf16)
    return pl.pallas_call(
        functools.partial(forward_kernel, lanes // 2, tile, starts.shape[1]),
        out_shape=(
            jax.ShapeDtypeStruct((8, rows, lanes), bf16),
            jax.ShapeDtypeStruct((seq, lanes), f32),
            heads,
            heads,
            heads,
            jax.ShapeDtypeStruct((seq, model), bf16),
        ),
        in_specs=[smem()] * 3 + [hbm()] * 11 + [anywhere()] * EXTRA,
        out_specs=(hbm(),) * 6,
        scratch_shapes=[
            pltpu.VMEM((seq, model), bf16),
            pltpu.VMEM((model, 3 * lanes), bf16),
            pltpu.VMEM(vectors.shape, bf16),
            pltpu.VMEM((2, seq, lanes), bf16),
            pltpu.VMEM((2, seq, lanes), bf16),
            pltpu.VMEM((2, seq, lanes), bf16),
            pltpu.VMEM((2, seq, lanes), bf16),
            pltpu.VMEM((8, rows, lanes), bf16),
            pltpu.VMEM((seq, lanes), f32),
            pltpu.SemaphoreType.DMA((8,)),
            pltpu.SemaphoreType.DMA((5,)),
            pltpu.SemaphoreType.DMA((8,)),
            pltpu.SemaphoreType.DMA((2 + 3 * (seq // tile),)),
        ],
        compiler_params=params(56),
        cost_estimate=cost(20),
        name="attention_forward",
    )(rank, starts, slopes, *blocks, matrices, vectors, pattern, extra)


def backward_kernel(waits, width, tile, count, starts_ref, *refs):
    q_in, k_in, v_in, kt_in, wide_in, got_in = refs[:6]
    abs_out, rel_out, bias_out, mid_out = refs[6 + waits : 10 + waits]
    qa, ka, va, kt, wide, grads, mid, da, dq_ref, dk_ref, dv_ref = refs[10 + waits : 21 + waits]
    both_ref, flip_ref, mid_flip, bias_ref, in_sems, out_sems = refs[21 + waits :]
    seq, lanes = wide.shape
    factor = width**-0.5
    first = start_all(
        [
            pltpu.make_async_copy(wide_in, wide, in_sems.at[0]),
            pltpu.make_async_copy(got_in.at[:, :, 0:lanes], grads, in_sems.at[1]),
        ]
    )
    rest = start_all(
        [
            pltpu.make_async_copy(q_in, qa, in_sems.at[2]),
            pltpu.make_async_copy(k_in, ka, in_sems.at[3]),
            pltpu.make_async_copy(v_in, va, in_sems.at[4]),
            pltpu.make_async_copy(kt_in, kt, in_sems.at[5]),
            pltpu.make_async_copy(got_in.at[:, :, lanes : 2 * lanes], mid, in_sems.at[6]),
        ]
    )
    wait_all(first)

    def prologue(t, carry):
        rows = pl.ds(pl.multiple_of(t * BLOCK, BLOCK), BLOCK)
        g = grads[t].astype(f32)
        product = g * wide[rows, :]
        for h in range(2):
            inside, spare = head_lanes((BLOCK, lanes), h, width)
            delta = jnp.sum(jnp.where(inside, product, 0.0), axis=1, keepdims=True)
            parts = split3(-jnp.broadcast_to(delta, (BLOCK, lanes)))
            da[h, rows, :] = jnp.where(inside, g, pick(spare, parts)).astype(bf16)
        return carry

    lax.fori_loop(0, seq // BLOCK, prologue, 0)
    dq_ref[...] = jnp.zeros(dq_ref.shape, f32)
    wait_all(rest)

    def pair(h, keys, queries, mask, local):
        logits = lax.dot_general(ka[h, keys, :], qa[h, queries, :], NT, preferred_element_type=f32)
        probs = jnp.exp(logits)
        if mask is not None:
            probs = jnp.where(mask(logits.shape), probs, 0.0)
        inner = lax.dot_general(va[h, keys, :], da[h, queries, :], NT, preferred_element_type=f32)
        grad = (probs * inner).astype(bf16)
        dv_ref[h, local, :] += jnp.dot(
            probs.astype(bf16), da[h, queries, :], preferred_element_type=f32
        )
        dk_ref[h, local, :] += jnp.dot(grad, qa[h, queries, :], preferred_element_type=f32)
        rows = slice(h * width, (h + 1) * width)
        dq_ref[rows, queries] += jnp.dot(kt[rows, keys], grad, preferred_element_type=f32)

    bias_ref[...] = jnp.zeros(bias_ref.shape, f32)
    out_copies = []

    def send(t, part, value, flipped):
        columns = slice(part * lanes, (part + 1) * lanes)
        rows = slice(t * BLOCK, (t + 1) * BLOCK)
        both_ref[rows, columns] = value.astype(bf16)
        flip_ref[columns, rows] = flipped.astype(bf16)
        bias_ref[:, columns] += jnp.sum(value.astype(bf16).astype(f32), axis=0, keepdims=True)

    for j in range(seq // tile):
        base = j * tile
        dk_ref[...] = jnp.zeros(dk_ref.shape, f32)
        dv_ref[...] = jnp.zeros(dv_ref.shape, f32)

        def mask(first_key, first_query, shape):
            queries = lax.broadcasted_iota(jnp.int32, (1, shape[1]), 1) + first_query
            keys = lax.broadcasted_iota(jnp.int32, shape, 0) + first_key
            return keys < limits(queries, starts_ref, count)

        if base > 0:
            for h in range(2):
                pair(
                    h,
                    slice(base, base + PIC),
                    slice(base - PIC, base),
                    functools.partial(mask, base, base - PIC),
                    slice(0, PIC),
                )
        for h in range(2):
            pair(
                h,
                slice(base, base + tile),
                slice(base, base + tile),
                functools.partial(mask, base, base),
                slice(0, tile),
            )

        def full(i, base=base):
            queries = slice(i * tile, (i + 1) * tile)
            for h in range(2):
                pair(h, slice(base, base + tile), queries, None, slice(0, tile))

        if base + tile < seq:
            for i in range(j + 1, seq // tile):
                full(i)
        inside, _ = head_lanes((BLOCK, lanes), 0, width)
        for t in range(tile // BLOCK):
            part = slice(t * BLOCK, (t + 1) * BLOCK)
            block = j * (tile // BLOCK) + t
            dk = jnp.where(inside, dk_ref[0, part, :], dk_ref[1, part, :])
            dv = jnp.where(inside, dv_ref[0, part, :], dv_ref[1, part, :])
            send(block, 1, dk, dk.T)
            send(block, 2, dv, dv.T)
    for t in range(seq // BLOCK):
        rows = slice(t * BLOCK, (t + 1) * BLOCK)
        dq = dq_ref[:, rows] * factor
        send(t, 0, dq.T, dq)
        mid_flip[:, rows] = mid[t].astype(f32).T.astype(bf16)
        out_copies += start_all(
            [
                pltpu.make_async_copy(both_ref.at[rows], abs_out.at[rows], out_sems.at[2 * t]),
                pltpu.make_async_copy(
                    flip_ref.at[:, rows], rel_out.at[:, rows], out_sems.at[2 * t + 1]
                ),
            ]
        )
    out_copies += start_all(
        [
            pltpu.make_async_copy(bias_ref, bias_out, out_sems.at[2 * (seq // BLOCK)]),
            pltpu.make_async_copy(mid_flip, mid_out, out_sems.at[2 * (seq // BLOCK) + 1]),
        ]
    )
    wait_all(out_copies)


def attention_backward(saved, wide, got, starts, extras, tile=512):
    seq, lanes = wide.shape
    blocks = seq // BLOCK
    return pl.pallas_call(
        functools.partial(backward_kernel, len(extras), lanes // 2, tile, starts.shape[1]),
        out_shape=(
            jax.ShapeDtypeStruct((seq, 3 * lanes), bf16),
            jax.ShapeDtypeStruct((3 * lanes, seq), bf16),
            jax.ShapeDtypeStruct((1, 3 * lanes), f32),
            jax.ShapeDtypeStruct((lanes, seq), bf16),
        ),
        in_specs=[smem()] + [hbm()] * 6 + [anywhere()] * len(extras),
        out_specs=(hbm(),) * 4,
        scratch_shapes=[
            pltpu.VMEM((2, seq, lanes), bf16),
            pltpu.VMEM((2, seq, lanes), bf16),
            pltpu.VMEM((2, seq, lanes), bf16),
            pltpu.VMEM((lanes, seq), bf16),
            pltpu.VMEM((seq, lanes), f32),
            pltpu.VMEM((blocks, BLOCK, lanes), bf16),
            pltpu.VMEM((blocks, BLOCK, lanes), bf16),
            pltpu.VMEM((2, seq, lanes), bf16),
            pltpu.VMEM((lanes, seq), f32),
            pltpu.VMEM((2, tile, lanes), f32),
            pltpu.VMEM((2, tile, lanes), f32),
            pltpu.VMEM((seq, 3 * lanes), bf16),
            pltpu.VMEM((3 * lanes, seq), bf16),
            pltpu.VMEM((lanes, seq), bf16),
            pltpu.VMEM((1, 3 * lanes), f32),
            pltpu.SemaphoreType.DMA((7,)),
            pltpu.SemaphoreType.DMA((2 * blocks + 2,)),
        ],
        compiler_params=params(56),
        cost_estimate=cost(21),
        name="attention_backward",
    )(starts, *saved, wide, got, *extras)


def normalize(value):
    centered = value - jnp.mean(value, axis=1, keepdims=True)
    inverse = lax.rsqrt(jnp.mean(centered * centered, axis=1, keepdims=True) + EPSILON)
    return centered * inverse, inverse


def whole(shape):
    return pl.BlockSpec(shape, lambda *_: (0,) * len(shape))


def gate(arrays, waits):
    count = len(arrays)
    return pl.pallas_call(
        lambda *refs: None,
        out_shape=tuple(jax.ShapeDtypeStruct(array.shape, array.dtype) for array in arrays),
        in_specs=[anywhere()] * (count + len(waits)),
        out_specs=(anywhere(),) * count,
        input_output_aliases={k: k for k in range(count)},
        cost_estimate=cost(1),
        name="gate",
    )(*arrays, *waits)


def project_kernel(
    heads_ref, tokens_ref, weights_ref, vectors_ref, extra_ref, middle_ref, hidden_ref, attended_ref
):
    lanes = heads_ref.shape[2]
    for g in range(heads_ref.shape[0]):
        attended_ref[:, g * lanes : (g + 1) * lanes] = heads_ref[g]
    vecs = vectors_ref[...].astype(f32)
    middle = (
        tokens_ref[...].astype(f32)
        + jnp.dot(attended_ref[...], weights_ref[...], preferred_element_type=f32)
        + vecs[4:5]
    )
    middle_ref[...] = middle
    normed, _ = normalize(middle)
    hidden_ref[...] = (normed * vecs[5:6] + vecs[6:7]).astype(bf16)


def project_norm(heads, tokens, matrices, vectors, extra):
    rows, model = tokens.shape
    return pl.pallas_call(
        project_kernel,
        grid=(1,),
        out_shape=(
            jax.ShapeDtypeStruct((rows, model), f32),
            jax.ShapeDtypeStruct((rows, model), bf16),
        ),
        in_specs=[
            whole(heads.shape),
            whole(tokens.shape),
            pl.BlockSpec((model, model), lambda i: (0, 3)),
            whole(vectors.shape),
            anywhere(),
        ],
        out_specs=(whole((rows, model)),) * 2,
        scratch_shapes=[pltpu.VMEM((rows, model), bf16)],
        compiler_params=params(40),
        cost_estimate=cost(3),
        name="project_norm",
    )(heads, tokens, matrices, vectors, extra)


def gelu_parts(pre):
    square = pre * pre
    half = 0.5 * (1.0 + jnp.tanh(GELU_SCALE * (pre + GELU_CUBE * square * pre)))
    act = pre * half
    slope = half + 2.0 * act * (1.0 - half) * (GELU_SCALE * (1.0 + 3.0 * GELU_CUBE * square))
    return act, slope


def norm_pull(grad, gain, normed, inverse):
    scaled = grad * gain
    return inverse * (
        scaled
        - jnp.mean(scaled, axis=1, keepdims=True)
        - normed * jnp.mean(scaled * normed, axis=1, keepdims=True)
    )


def feed_kernel(chunk, *refs):
    hidden_in, middle_in, cotangent_in, vectors_in, bias_in, matrices_in = refs[:6]
    layer_out, grad_mid_out, heads_out, sums_out = refs[6:10]
    hidden, middle, cotangent, vecs_ref, bias, up, down, proj = refs[10:18]
    layer, grad_mid_ref, heads, sums, down_acc, two_acc, in_sems, w_sems, out_sems = refs[18:]
    model = hidden.shape[1]
    count = up.shape[0]
    first = start_all(
        [
            pltpu.make_async_copy(source, target, in_sems.at[k])
            for k, (source, target) in enumerate(
                ((hidden_in, hidden), (cotangent_in, cotangent), (bias_in, bias))
            )
        ]
    )
    weights = []
    for i in range(count):
        for part, ref in ((0, up), (1, down)):
            start = 4 * model + part * count * chunk + i * chunk
            weights.append(
                pltpu.make_async_copy(
                    matrices_in.at[:, start : start + chunk], ref.at[i], w_sems.at[2 * i + part]
                )
            )
    start_all(weights)
    rest = start_all(
        [
            pltpu.make_async_copy(middle_in, middle, in_sems.at[3]),
            pltpu.make_async_copy(vectors_in, vecs_ref, in_sems.at[4]),
            pltpu.make_async_copy(
                matrices_in.at[:, 3 * model : 4 * model], proj, in_sems.at[5]
            ),
        ]
    )
    wait_all(first)
    for i in range(count):
        weights[2 * i].wait()
        pre = jnp.dot(hidden[...], up[i], preferred_element_type=f32)
        pre = pre + bias[:, i * chunk : (i + 1) * chunk]
        weights[2 * i + 1].wait()
        grad_act = jnp.dot(cotangent[...], down[i], preferred_element_type=f32)
        act, slope = gelu_parts(pre)
        grad_pre = (grad_act * slope).astype(bf16)
        down_part = lax.dot_general(act.astype(bf16), down[i], NT, preferred_element_type=f32)
        two_part = lax.dot_general(grad_pre, up[i], NT, preferred_element_type=f32)
        if i == 0:
            down_acc[...] = down_part
            two_acc[...] = two_part
        else:
            down_acc[...] += down_part
            two_acc[...] += two_part
    wait_all(rest)
    vecs = vecs_ref[...].astype(f32)
    grad_two = two_acc[...]
    mid = middle[...]
    normed, inverse = normalize(mid)
    upstream = cotangent[...].astype(f32)
    grad_mid = upstream + norm_pull(grad_two, vecs[5:6], normed, inverse)
    low = grad_mid.astype(bf16)
    grads = lax.dot_general(low, proj[...], NT, preferred_element_type=f32).astype(bf16)
    groups, _, double = heads.shape
    lanes = double // 2
    for g in range(groups):
        heads[g, :, 0:lanes] = grads[:, g * lanes : (g + 1) * lanes]
        heads[g, :, lanes:double] = low[:, g * lanes : (g + 1) * lanes]
    out_copies = [pltpu.make_async_copy(heads, heads_out, out_sems.at[0])]
    out_copies[0].start()
    grad_mid_ref[...] = grad_mid
    layer[...] = (mid + down_acc[...] + vecs[7:8]).astype(bf16)
    rows = [grad_mid, grad_two * normed, grad_two, upstream]
    for k, value in enumerate(rows):
        sums[k : k + 1, :] = jnp.sum(value, axis=0, keepdims=True)
    out_copies += start_all(
        [
            pltpu.make_async_copy(layer, layer_out, out_sems.at[1]),
            pltpu.make_async_copy(grad_mid_ref, grad_mid_out, out_sems.at[2]),
            pltpu.make_async_copy(sums, sums_out, out_sems.at[3]),
        ]
    )
    wait_all(out_copies)


def feed_forward(hidden, up_bias, middle, cotangent, vectors, matrices, chunk=1024):
    rows, model = hidden.shape
    ff_width = up_bias.shape[1]
    count = ff_width // chunk
    outs = (
        jax.ShapeDtypeStruct((rows, model), bf16),
        jax.ShapeDtypeStruct((rows, model), f32),
        jax.ShapeDtypeStruct((8, rows, model // 4), bf16),
        jax.ShapeDtypeStruct((4, model), f32),
    )
    return pl.pallas_call(
        functools.partial(feed_kernel, chunk),
        out_shape=outs,
        in_specs=[hbm()] * 6,
        out_specs=(hbm(),) * 4,
        scratch_shapes=[
            pltpu.VMEM((rows, model), bf16),
            pltpu.VMEM((rows, model), f32),
            pltpu.VMEM((rows, model), bf16),
            pltpu.VMEM(vectors.shape, bf16),
            pltpu.VMEM((1, ff_width), f32),
            pltpu.VMEM((count, model, chunk), bf16),
            pltpu.VMEM((count, model, chunk), bf16),
            pltpu.VMEM((model, model), bf16),
        ]
        + [pltpu.VMEM(out.shape, out.dtype) for out in outs]
        + [
            pltpu.VMEM((rows, model), f32),
            pltpu.VMEM((rows, model), f32),
            pltpu.SemaphoreType.DMA((6,)),
            pltpu.SemaphoreType.DMA((2 * count,)),
            pltpu.SemaphoreType.DMA((4,)),
        ],
        compiler_params=params(40),
        cost_estimate=cost(14),
        name="feed_forward",
    )(hidden, middle, cotangent, vectors, up_bias, matrices)


def units_kernel(waits, rank_ref, *refs):
    blocks, heads = refs[:8], refs[8:16]
    cotangent_in, bias_in, matrices_in, vectors_in = refs[16:20]
    early_out, sums_out, attended_out = refs[20 + waits : 23 + waits]
    tokens, attended, hidden, cotangent, proj, vecs_ref = refs[23 + waits : 29 + waits]
    bias, up, down, act_ref, grad_ref, low, sums, grad_act = refs[29 + waits : 37 + waits]
    w_sems, in_sems, head_sems, out_sems = refs[37 + waits :]
    seq, model = hidden.shape
    units = up.shape[1]
    lanes = model // 8
    rank = rank_ref[0]
    first = pl.multiple_of(rank * units, units)
    weights = []
    for part, ref in ((1, down), (0, up)):
        source = pl.ds(pl.multiple_of((4 + 4 * part) * model + first, units), units)
        weights.append(
            pltpu.make_async_copy(matrices_in.at[:, source], ref, w_sems.at[3 + part])
        )
    early_copies = [pltpu.make_async_copy(cotangent_in, cotangent, w_sems.at[5]), weights[0]]
    start_all(early_copies)
    copies = [
        pltpu.make_async_copy(bias_in.at[:, pl.ds(first, units)], bias, w_sems.at[0]),
        pltpu.make_async_copy(vectors_in, vecs_ref, w_sems.at[1]),
        pltpu.make_async_copy(matrices_in.at[:, 3 * model : 4 * model], proj, w_sems.at[2]),
    ]
    start_all(copies)
    loads = []
    for k in range(8):
        columns = pl.ds(pl.multiple_of((rank ^ k) * lanes, lanes), lanes)
        loads.append(
            pltpu.make_async_copy(heads[k], attended.at[:, :, columns], head_sems.at[k])
        )
    for k in range(8):
        rows = pl.ds(pl.multiple_of((rank ^ k) * BLOCK, BLOCK), BLOCK)
        loads.append(pltpu.make_async_copy(blocks[k], tokens.at[rows], in_sems.at[k]))
    start_all(loads)
    weights[1].start()
    wait_all(early_copies)
    grad_act[...] = jnp.dot(cotangent[...], down[...], preferred_element_type=f32)
    wait_all(copies + loads)
    out_copies = [pltpu.make_async_copy(attended, attended_out, w_sems.at[6])]
    out_copies[0].start()
    vecs = vecs_ref[...].astype(f32)
    sums[...] = jnp.zeros(sums.shape, f32)
    for part in range(4):
        rows = slice(part * 2 * BLOCK, (part + 1) * 2 * BLOCK)
        heads_here = attended[2 * part : 2 * part + 2].reshape(2 * BLOCK, model)
        middle = (
            tokens[rows, :].astype(f32)
            + jnp.dot(heads_here, proj[...], preferred_element_type=f32)
            + vecs[4:5]
        )
        normed, _ = normalize(middle)
        hidden[rows, :] = (normed * vecs[5:6] + vecs[6:7]).astype(bf16)
        if part == 0:
            weights[1].wait()
        pre = jnp.dot(hidden[rows, :], up[...], preferred_element_type=f32) + bias[...]
        act, slope = gelu_parts(pre)
        grad_pre = grad_act[rows, :] * slope
        act_ref[:, rows] = act.T.astype(bf16)
        grad_ref[:, rows] = grad_pre.T.astype(bf16)
        sums[...] += jnp.sum(grad_pre.astype(bf16).astype(f32), axis=0, keepdims=True)
    quarter = model // 4
    copy = pltpu.make_async_copy(sums, sums_out, w_sems.at[0])
    copy.start()
    out_copies.append(copy)
    for block in range(4):
        columns = slice(block * quarter, (block + 1) * quarter)
        for n, (left, right) in enumerate(((grad_ref, hidden), (act_ref, cotangent))):
            low[block, n * units : (n + 1) * units, :] = jnp.dot(
                left[...], right[:, columns], preferred_element_type=f32
            ).astype(bf16)
        copy = pltpu.make_async_copy(low.at[block], early_out.at[block], out_sems.at[block])
        copy.start()
        out_copies.append(copy)
    wait_all(out_copies)


def own_units(rank, blocks, heads, cotangent, up_bias, matrices, vectors, extras):
    rows, model = blocks[0].shape
    seq = 8 * rows
    units = up_bias.shape[1] // 8
    attended = (8, rows, model)
    return pl.pallas_call(
        functools.partial(units_kernel, len(extras)),
        out_shape=(
            jax.ShapeDtypeStruct((4, 2 * units, model // 4), bf16),
            jax.ShapeDtypeStruct((1, units), f32),
            jax.ShapeDtypeStruct(attended, bf16),
        ),
        in_specs=[smem()] + [hbm()] * 20 + [anywhere()] * len(extras),
        out_specs=(hbm(),) * 3,
        scratch_shapes=[
            pltpu.VMEM((seq, model), bf16),
            pltpu.VMEM(attended, bf16),
            pltpu.VMEM((seq, model), bf16),
            pltpu.VMEM((seq, model), bf16),
            pltpu.VMEM((model, model), bf16),
            pltpu.VMEM(vectors.shape, bf16),
            pltpu.VMEM((1, units), f32),
            pltpu.VMEM((model, units), bf16),
            pltpu.VMEM((model, units), bf16),
            pltpu.VMEM((units, seq), bf16),
            pltpu.VMEM((units, seq), bf16),
            pltpu.VMEM((4, 2 * units, model // 4), bf16),
            pltpu.VMEM((1, units), f32),
            pltpu.VMEM((seq, units), f32),
            pltpu.SemaphoreType.DMA((7,)),
            pltpu.SemaphoreType.DMA((8,)),
            pltpu.SemaphoreType.DMA((8,)),
            pltpu.SemaphoreType.DMA((4,)),
        ],
        compiler_params=params(56),
        cost_estimate=cost(1),
        name="own_units",
    )(rank, *blocks, *heads, cotangent, up_bias, matrices, vectors, *extras)


def late_kernel(depth_ref, grads_in, hidden_in, mid_in, attended_in, *refs):
    outs = refs[:4]
    grads, hidden, mid, attended, total, low, in_sems, out_sems = refs[4:]
    columns, model = total.shape
    quarter = model // 4
    first = grads.shape[0]
    copies = start_all(
        [
            pltpu.make_async_copy(source, target, in_sems.at[n])
            for n, (source, target) in enumerate(
                (
                    (mid_in, mid),
                    (attended_in, attended),
                    (grads_in, grads),
                    (hidden_in, hidden),
                )
            )
        ]
    )
    wait_all(copies[:2])
    total[first:, :] = jnp.dot(mid[...], attended[...], preferred_element_type=f32)
    wait_all(copies[2:])
    total[:first, :] = jnp.dot(grads[...], hidden[...], preferred_element_type=f32)
    depth = depth_ref[0]
    near = depth ^ 1
    out_copies = []
    for n, (block, target) in enumerate(
        ((3 - near, outs[0]), (near, outs[1]), (3 - depth, outs[2]), (depth, outs[3]))
    ):
        lane = pl.ds(pl.multiple_of(block * quarter, quarter), quarter)
        if n < 2:
            low[n] = total[:, lane].astype(bf16)
            copy = pltpu.make_async_copy(low.at[n], target, out_sems.at[n])
        else:
            copy = pltpu.make_async_copy(total.at[:, lane], target, out_sems.at[n])
        copy.start()
        out_copies.append(copy)
    wait_all(out_copies)


def late_weights(depth, grads, hidden, mid, attended):
    seq, model = hidden.shape
    columns = grads.shape[0] + mid.shape[0]
    quarter = model // 4
    return pl.pallas_call(
        late_kernel,
        out_shape=(jax.ShapeDtypeStruct((columns, quarter), bf16),) * 2
        + (jax.ShapeDtypeStruct((columns, quarter), f32),) * 2,
        in_specs=[smem()] + [hbm()] * 4,
        out_specs=(hbm(),) * 4,
        scratch_shapes=[
            pltpu.VMEM(grads.shape, bf16),
            pltpu.VMEM(hidden.shape, bf16),
            pltpu.VMEM(mid.shape, bf16),
            pltpu.VMEM(attended.shape, bf16),
            pltpu.VMEM((columns, model), f32),
            pltpu.VMEM((2, columns, quarter), bf16),
            pltpu.SemaphoreType.DMA((4,)),
            pltpu.SemaphoreType.DMA((4,)),
        ],
        compiler_params=params(56),
        cost_estimate=cost(5),
        name="late_weights",
    )(depth, grads, hidden, mid, attended)


def flip_kernel(parts, *refs):
    total = refs[0][...].reshape(refs[0].shape[-2:]).astype(f32)
    for ref in refs[1:parts]:
        total = total + ref[...].astype(f32)
    refs[-1][...] = total.T.astype(bf16)


def flip_sum(arrays, waits, name):
    columns, rows = arrays[0].shape[-2:]
    return pl.pallas_call(
        functools.partial(flip_kernel, len(arrays)),
        grid=(1,),
        out_shape=jax.ShapeDtypeStruct((rows, columns), bf16),
        in_specs=[whole(array.shape) for array in arrays] + [anywhere()] * len(waits),
        out_specs=whole((rows, columns)),
        compiler_params=params(56),
        cost_estimate=cost(0.1),
        name=name,
    )(*arrays, *waits)


def final_kernel(
    heads_ref, weights_ref, tokens_ref, grad_mid_ref, vectors_ref, *refs
):
    out_ref, sums_ref, acc_ref, lhs = refs[-4:]
    step = pl.program_id(0)
    lanes = heads_ref.shape[2] // 3

    @pl.when(step == 0)
    def _():
        acc_ref[...] = jnp.zeros(acc_ref.shape, f32)

    source = pl.ds(pl.multiple_of(step * lanes, lanes), lanes)
    for g in range(heads_ref.shape[0]):
        lhs[:, g * lanes : (g + 1) * lanes] = heads_ref[g, :, source]
    acc_ref[...] += lax.dot_general(lhs[...], weights_ref[...], NT, preferred_element_type=f32)

    @pl.when(step == pl.num_programs(0) - 1)
    def _():
        vecs = vectors_ref[...].astype(f32)
        grad = acc_ref[...]
        normed, inverse = normalize(tokens_ref[...].astype(f32))
        out_ref[...] = grad_mid_ref[...] + norm_pull(grad, vecs[0:1], normed, inverse)
        sums_ref[0:1, :] = jnp.sum(grad * normed, axis=0, keepdims=True)
        sums_ref[1:2, :] = jnp.sum(grad, axis=0, keepdims=True)


def token_gradient(heads, matrices, tokens, grad_mid, vectors, extras):
    rows, model = tokens.shape
    return pl.pallas_call(
        final_kernel,
        grid=(3,),
        out_shape=(
            jax.ShapeDtypeStruct((rows, model), f32),
            jax.ShapeDtypeStruct((2, model), f32),
        ),
        in_specs=[
            whole(heads.shape),
            pl.BlockSpec((model, model), lambda i: (0, i)),
            whole((rows, model)),
            whole((rows, model)),
            whole(vectors.shape),
        ]
        + [anywhere()] * len(extras),
        out_specs=(whole((rows, model)), whole((2, model))),
        scratch_shapes=[pltpu.VMEM((rows, model), f32), pltpu.VMEM((rows, model), bf16)],
        compiler_params=params(56),
        cost_estimate=cost(6),
        name="token_gradient",
    )(heads, matrices, tokens, grad_mid, vectors, *extras)


def vector_pieces_kernel(rank_ref, one_ref, bias_ref, two_ref, units_ref, *refs):
    states, out_ref = refs[:3], refs[-1]
    rank = rank_ref[0]
    lanes = out_ref.shape[2]
    out_ref[...] = jnp.zeros(out_ref.shape, f32)
    copies = out_ref.shape[0] // 8
    for b in range(8):
        columns = slice(b * lanes, (b + 1) * lanes)
        for c in range(copies):
            out_ref[copies * b + c, 0:2, :] = one_ref[:, columns]
            out_ref[copies * b + c, 4:8, :] = two_ref[:, columns]
    rows, own = states[0].shape
    packed = jnp.concatenate(
        [ref[...] for ref in states] + [jnp.zeros((rows, lanes - 3 * own), f32)], axis=1
    )
    for b in range(out_ref.shape[0]):
        out_ref[b, 12 : 12 + rows, :] = packed
    for c in range(copies):
        out_ref[copies * rank + c, 2:3, :] = bias_ref[:, 0:lanes]
        out_ref[copies * rank + c, 3:4, :] = bias_ref[:, 2 * lanes : 3 * lanes]
    pieces = units_ref.shape[1] // lanes
    for n in range(pieces):
        place = rank * pieces + n
        for c in range(copies):
            out_ref[copies * (place % 8) + c, pl.ds(8 + place // 8, 1), :] = units_ref[
                :, n * lanes : (n + 1) * lanes
            ]


def vector_pieces(rank, one, bias, two, units, states, devices, waits):
    lanes = one.shape[1] // 8
    return pl.pallas_call(
        vector_pieces_kernel,
        grid=(1,),
        out_shape=jax.ShapeDtypeStruct((devices, 24, lanes), f32),
        in_specs=[smem(), whole(one.shape), whole(bias.shape), whole(two.shape), whole(units.shape)]
        + [whole(state.shape) for state in states]
        + [anywhere()] * len(waits),
        out_specs=whole((devices, 24, lanes)),
        compiler_params=params(40),
        cost_estimate=cost(1),
        name="vector_pieces",
    )(rank, one, bias, two, units, *states, *waits)


def adam(master, first, second, gradient, decay_rate):
    correction = 1.0 - BETA**STEP
    moment = BETA * first + (1.0 - BETA) * gradient
    variance = BETA * second + (1.0 - BETA) * gradient * gradient
    direction = moment / correction / (jnp.sqrt(variance / correction) + ADAM_EPSILON)
    return moment, variance, master - RATE * (direction + decay_rate * master)


def vector_update_kernel(root, place_ref, got_ref, *refs):
    outs, copied_ref = refs[-4:-1], refs[-1]
    lanes = got_ref.shape[2]
    rows, own = outs[0].shape
    gradient = jnp.sum(got_ref[:, :16, :], axis=0) * root
    shard = place_ref[0] % 4
    first = place_ref[0] - shard
    columns = lax.broadcasted_iota(jnp.int32, (16, lanes), 1) // own
    total = jnp.zeros((16, lanes), f32)
    for k in range(4):
        other = shard ^ k
        shifted = pltpu.roll(gradient, lax.rem(lanes - other * own, lanes), 1)[:rows, :own]
        packed = got_ref[first + other, 12 : 12 + rows, :]
        states = [packed[:, n * own : (n + 1) * own] for n in range(3)]
        values = adam(*states, shifted, 0.0)
        if k == 0:
            for ref, value in zip(outs, values):
                ref[...] = value
        wide = jnp.concatenate([values[2], jnp.zeros((rows, lanes - own), f32)], axis=1)
        wide = jnp.concatenate([wide, jnp.zeros((16 - rows, lanes), f32)], axis=0)
        total = jnp.where(columns == other, pltpu.roll(wide, other * own, 1), total)
    copied_ref[...] = total[:rows].astype(bf16)


def vector_update(place, got, rows, own, root, extras):
    lanes = got.shape[2]
    mine = jax.ShapeDtypeStruct((rows, own), f32)
    return pl.pallas_call(
        functools.partial(vector_update_kernel, root),
        grid=(1,),
        out_shape=(mine, mine, mine, jax.ShapeDtypeStruct((rows, lanes), bf16)),
        in_specs=[smem(), whole(got.shape)] + [anywhere()] * len(extras),
        out_specs=(whole((rows, own)),) * 3 + (whole((rows, lanes)),),
        compiler_params=params(40),
        cost_estimate=cost(1),
        name="vector_update",
    )(place, got, *extras)


def update_kernel(root, got_ref, *refs):
    states, outs = refs[:3], refs[-5:-2]
    copied_ref, gradient_ref = refs[-2:]
    lanes = got_ref.shape[2]
    for g in range(got_ref.shape[0]):
        gradient_ref[:, g * lanes : (g + 1) * lanes] = got_ref[g].astype(f32)
    values = adam(*[ref[...] for ref in states], gradient_ref[...] * root, DECAY_RATE)
    for ref, value in zip(outs, values):
        ref[...] = value
    copied_ref[...] = values[2].astype(bf16)


def matrix_update(got, states, previous, extras, first, parts, root, name):
    groups, rows, packed = got.shape
    lanes = packed // parts
    block = groups * lanes
    total = states[0].shape[1]
    start = first // block
    state = pl.BlockSpec((rows, block), lambda i: (0, start + i))
    return pl.pallas_call(
        functools.partial(update_kernel, root),
        grid=(parts,),
        out_shape=(jax.ShapeDtypeStruct((rows, total), f32),) * 3
        + (jax.ShapeDtypeStruct((rows, parts * block), bf16),),
        in_specs=[pl.BlockSpec((groups, rows, lanes), lambda i: (0, 0, i))]
        + [state] * 3
        + [anywhere()] * (len(previous) + len(extras)),
        out_specs=(state,) * 3 + (pl.BlockSpec((rows, block), lambda i: (0, i)),),
        scratch_shapes=[pltpu.VMEM((rows, block), f32)],
        input_output_aliases={4 + k: k for k in range(len(previous))},
        compiler_params=params(56),
        cost_estimate=cost(4),
        name=name,
    )(got, *states, *previous, *extras)


def place_kernel(late_blocks, shard_ref, *refs):
    out_ref = refs[-1]
    rows = refs[0].shape[0]
    for first, chosen in ((0, pl.program_id(0) < late_blocks), (4, pl.program_id(0) >= late_blocks)):

        @pl.when(chosen)
        def _(first=first):
            for k in range(4):
                place = pl.multiple_of((shard_ref[0] ^ k) * rows, rows)
                out_ref[pl.ds(place, rows), :] = refs[first + k][...]


def place_copies(shard, late, early):
    rows = late[0].shape[0]
    block = 2048
    count = late[0].shape[1] // block
    total = count * block + early[0].shape[1]
    return pl.pallas_call(
        functools.partial(place_kernel, count),
        grid=(total // block,),
        out_shape=jax.ShapeDtypeStruct((4 * rows, total), bf16),
        in_specs=[smem()]
        + [pl.BlockSpec((rows, block), lambda i: (0, jnp.minimum(i, count - 1)))] * 4
        + [pl.BlockSpec((rows, block), lambda i: (0, jnp.maximum(i - count, 0)))] * 4,
        out_specs=pl.BlockSpec((4 * rows, block), lambda i: (0, i)),
        compiler_params=params(40),
        cost_estimate=cost(2),
        name="place_copies",
    )(shard, *late, *early)


def fits_sequence_plan(mesh):
    return mesh.shape["dp"] == 4 and mesh.shape["ctx"] == 2 and mesh.shape["shard"] == 4


EVERY = ("dp", "ctx", "shard")
SEQUENCE = ("ctx", "shard")


def swap(array, axis, bit):
    count = lax.axis_size(axis)
    return lax.ppermute(array, axis, [(i, i ^ bit) for i in range(count)])


def gather_blocks(block, ready=True):
    over_ctx = swap(block, "ctx", 1)
    over_y = swap(block, "shard", 2)
    over_core = swap(block, "shard", 1)
    even = (lax.axis_index("shard") % 2 == 0) & ready
    relay = jnp.where(even, over_ctx, over_y)
    opposite = lax.ppermute(relay, SEQUENCE, [(i, i ^ (4 if i % 2 else 2)) for i in range(8)])
    ctx_core = swap(over_ctx, "shard", 1)
    y_core = swap(over_y, "shard", 1)
    opposite_core = swap(opposite, "shard", 1)
    return relay, [
        block, over_core, over_y, y_core, over_ctx, ctx_core, opposite, opposite_core
    ]


def gather_direct(block):
    straight = [
        block,
        swap(block, "shard", 2),
        swap(block, "ctx", 1),
        lax.ppermute(block, SEQUENCE, [(i, i ^ 6) for i in range(8)]),
    ]
    return [array for first in straight for array in (first, swap(first, "shard", 1))]


def gather_rows(array):
    return lax.all_gather(array, SEQUENCE, axis=0, tiled=True)


def exchange(array, axes=SEQUENCE):
    return lax.all_to_all(array, axes, 0, 0, tiled=True)


def dot_tn(left, right):
    return lax.dot_general(left, right, (((0,), (0,)), ((), ())), preferred_element_type=f32)


def dot_nt(left, right):
    return lax.dot_general(left, right, NT, preferred_element_type=f32)


def dot_nn(left, right):
    return jnp.dot(left, right, preferred_element_type=f32)


def shift_dp(array, distance):
    return lax.ppermute(array, "dp", [(i, (i + distance) % 4) for i in range(4)])


def gather_shards(array):
    over_core = swap(array, "shard", 1)
    over_y = swap(array, "shard", 2)
    return [array, over_core, over_y, swap(over_y, "shard", 1)]


def sequence_shards(
    tokens,
    cotangent,
    picture_starts,
    matrices,
    vectors,
    master_matrices,
    master_vectors,
    first_matrices,
    first_vectors,
    second_matrices,
    second_vectors,
):
    row_count, width = tokens.shape
    ff_width = (matrices.shape[1] - 4 * width) // 2
    group = 8
    shard = lax.axis_index("shard")
    rank = lax.axis_index("ctx") * 4 + shard
    depth = lax.axis_index("dp")
    lanes = width // group
    units = ff_width // group
    own_rows = master_matrices.shape[0]
    seq = group * row_count
    head = rank * 2 + jnp.arange(2)
    slopes = jnp.exp2(-8.0 * (head.astype(f32) + 1.0) / HEADS)
    rank_array = rank.astype(jnp.int32).reshape(1)
    shard_array = shard.astype(jnp.int32).reshape(1)
    vector_rows = vectors.astype(f32)
    up_bias = vector_rows[8:].reshape(1, ff_width)

    with jax.named_scope("prepare"):
        pattern = key_pattern(picture_starts, slopes, seq, lanes)
    with jax.named_scope("gather_tokens"):
        ready = pattern[0, 0, lanes // 2 + 3] == 1.0
        passed, token_blocks = gather_blocks(tokens, ready)
    with jax.named_scope("gather_cotangent"):
        zero = passed[0, 0] * 0
        cotangent_late = cotangent + zero
        cotangent_all = gather_rows(cotangent_late)
    attended_heads, attended_wide, *saved, hidden_all = attention_forward(
        token_blocks,
        matrices,
        vectors,
        pattern,
        rank_array,
        picture_starts,
        slopes,
        cotangent_late,
    )
    with jax.named_scope("attended_exchange"):
        attended_got = exchange(attended_heads)
    with jax.named_scope("transpose_keys"):
        half = lanes // 2
        keys_low = saved[1]
        keys_transposed = jnp.concatenate(
            [keys_low[0, :, :half], keys_low[1, :, half:]], axis=1
        ).T
    middle, hidden_two = project_norm(
        attended_got, tokens, matrices, vectors, keys_transposed
    )
    with jax.named_scope("gather_attended"):
        head_blocks = gather_direct(attended_heads)
    layer_output, grad_mid, grad_out, sums_two = feed_forward(
        hidden_two, up_bias, middle, cotangent, vectors, matrices
    )
    with jax.named_scope("grad_attended_exchange"):
        grad_got = exchange(grad_out)
    early, unit_sums, attended_all = own_units(
        rank_array,
        token_blocks,
        head_blocks,
        cotangent_all,
        up_bias,
        matrices,
        vectors,
        [grad_out],
    )
    with jax.named_scope("grad_feed"):
        (early,) = gate([early], [grad_got])
        early_sum = lax.psum_scatter(early, "dp", scatter_dimension=0, tiled=True)
    grad_abs, grad_flipped, bias_sums, mid_flipped = attention_backward(
        (*saved, keys_transposed), attended_wide, grad_got, picture_starts, [early]
    )
    with jax.named_scope("grad_qkv_exchange"):
        grad_tokens = exchange(grad_abs.reshape(group, row_count, 3 * lanes))
    with jax.named_scope("grad_late"):
        near_far, near, relay, late_own = late_weights(
            depth.astype(jnp.int32).reshape(1), grad_flipped, hidden_all, mid_flipped, attended_all.reshape(seq, width)
        )
        beside = [(i, i ^ 1) for i in range(4)]
        relay = (relay + lax.ppermute(near_far, "dp", beside).astype(f32)).astype(bf16)
        near = lax.ppermute(near, "dp", beside)
        far = lax.ppermute(relay, "dp", [(i, 3 - i) for i in range(4)])
    with jax.named_scope("early_rows"):
        early_sum = flip_sum([early_sum], [grad_tokens, relay], "early_rows")
        early_got = exchange(early_sum.reshape(group, own_rows, 2 * units))
    token_grads, sums_one = token_gradient(
        grad_tokens, matrices, tokens, grad_mid, vectors, [early_sum]
    )
    with jax.named_scope("late_rows"):
        late_sum = flip_sum([late_own, near, far], [early_got, sums_one], "late_rows")
        late_got = exchange(late_sum.reshape(group, own_rows, 4 * lanes))
    root = (row_count * lax.axis_size("dp") * group) ** (-0.5)
    matrix_states = (master_matrices, first_matrices, second_matrices)
    *early_states, early_copy = matrix_update(
        early_got, matrix_states, (), [late_got], 4 * width, 2, root, "early_update"
    )
    with jax.named_scope("early_copies"):
        early_copied = gather_shards(early_copy)
    moment_w, variance_w, updated_w, late_copy = matrix_update(
        late_got,
        matrix_states,
        early_states,
        [],
        0,
        4,
        root,
        "late_update",
    )
    with jax.named_scope("grad_vectors"):
        vector_states = (master_vectors, first_vectors, second_vectors)
        pieces = vector_pieces(
            rank_array, sums_one, bias_sums, sums_two, unit_sums, vector_states, 32, [late_copy]
        )
        vectors_got = exchange(pieces, EVERY)
    with jax.named_scope("late_copies"):
        late_copied = gather_shards(late_copy)
    copied_w = place_copies(shard_array, late_copied, early_copied)
    moment_v, variance_v, updated_v, copied_v = vector_update(
        (depth * group + rank).astype(jnp.int32).reshape(1),
        vectors_got,
        *master_vectors.shape,
        root,
        [early_copied[3]],
    )
    return (
        layer_output,
        token_grads,
        moment_w,
        moment_v,
        variance_w,
        variance_v,
        updated_w,
        updated_v,
        copied_w,
        copied_v,
    )


def solution(mesh):
    in_specs = (
        P(("dp", "ctx", "shard"), None),
        P(("dp", "ctx", "shard"), None),
        P("dp", None),
        P(),
        P(),
        P(("dp", "ctx", "shard"), None),
        P(None, ("dp", "ctx", "shard")),
        P(("dp", "ctx", "shard"), None),
        P(None, ("dp", "ctx", "shard")),
        P(("dp", "ctx", "shard"), None),
        P(None, ("dp", "ctx", "shard")),
    )
    out_specs = (
        P(("dp", "ctx", "shard"), None),
        P(("dp", "ctx", "shard"), None),
        P(("dp", "ctx", "shard"), None),
        P(None, ("dp", "ctx", "shard")),
        P(("dp", "ctx", "shard"), None),
        P(None, ("dp", "ctx", "shard")),
        P(("dp", "ctx", "shard"), None),
        P(None, ("dp", "ctx", "shard")),
        P(("dp", "ctx"), None),
        P(None, ("dp", "ctx")),
    )
    body = sequence_shards if fits_sequence_plan(mesh) else general_shards
    return jax.shard_map(body, mesh=mesh, in_specs=in_specs, out_specs=out_specs, check_vma=False)
```

```python
import functools
import math

import jax
import jax.numpy as jnp
from jax import lax
from jax.experimental import pallas as pl
from jax.experimental.pallas import tpu as pltpu
from jax.sharding import PartitionSpec as P

HEADS = 16
PIC = 256
STEP = 2


EPSILON = 1e-05
NEGATIVE = -1e30
BETA = 0.5
RATE = 0.03
DECAY_RATE = 0.1
ADAM_EPSILON = 1e-08


def token_tags(index, start_list, block_len):
    after = index[:, None] - start_list[None, :]
    inside = (after >= 0) & (after < block_len)
    offsets = jnp.sum(jnp.clip(after, 0, block_len - 1), axis=1)
    number = jnp.arange(1, start_list.shape[0] + 1, dtype=jnp.int32)
    picture = jnp.sum(jnp.where(inside, number[None, :], 0), axis=1) - 1
    return (index - offsets, picture)


def block_scores(query_heads, query_index, key_heads, key_index, start_list, slopes, factor):
    query_pos, query_pic = token_tags(query_index, start_list, PIC)
    key_pos, key_pic = token_tags(key_index, start_list, PIC)
    raw = jnp.einsum("qhd,khd->hqk", query_heads, key_heads, preferred_element_type=jnp.float32)
    distance = (query_pos[:, None] - key_pos[None, :]).astype(jnp.float32)
    logits = raw * factor - slopes[:, None, None] * distance[None, :, :]
    same = (query_pic[:, None] == key_pic[None, :]) & (query_pic[:, None] >= 0)
    visible = (key_index[None, :] <= query_index[:, None]) | same
    return (logits, visible[None, :, :])


def layer_norm(inputs):
    centered = inputs - jnp.mean(inputs, axis=1, keepdims=True)
    inverse_std = lax.rsqrt(jnp.mean(centered * centered, axis=1, keepdims=True) + EPSILON)
    return (centered * inverse_std, inverse_std)


def norm_backward(grad_normed, gain, normed, inverse_std):
    scaled = grad_normed * gain
    return inverse_std * (
        scaled
        - jnp.mean(scaled, axis=1, keepdims=True)
        - normed * jnp.mean(scaled * normed, axis=1, keepdims=True)
    )


def activate(value):
    return jax.nn.gelu(value, approximate=True)


def regroup(array, dim, outer, inner):
    shape = array.shape
    split = array.reshape(
        shape[:dim] + (outer, inner, shape[dim] // (outer * inner)) + shape[dim + 1 :]
    )
    return jnp.swapaxes(split, dim, dim + 1).reshape(shape)


def adam_update(master, first, second, gradient, correction, decay_rate):
    moment = BETA * first + (1.0 - BETA) * gradient
    variance = BETA * second + (1.0 - BETA) * gradient * gradient
    direction = moment / correction / (jnp.sqrt(variance / correction) + ADAM_EPSILON)
    return (moment, variance, master - RATE * (direction + decay_rate * master))


def general_shards(
    tokens,
    cotangent,
    picture_starts,
    matrices,
    vectors,
    master_matrices,
    master_vectors,
    first_matrices,
    first_vectors,
    second_matrices,
    second_vectors,
):
    row_count, model_width = tokens.shape
    ff_width = (matrices.shape[1] - 4 * model_width) // 2
    head_count = HEADS
    head_width = model_width // head_count
    factor = head_width ** (-0.5)
    group_size = lax.axis_size("ctx") * lax.axis_size("shard")
    group_rank = lax.axis_index("ctx") * lax.axis_size("shard") + lax.axis_index("shard")
    seq_length = row_count * group_size
    first_row = group_rank * row_count
    start_list = picture_starts[0]
    slopes = jnp.exp2(-8.0 * (jnp.arange(head_count, dtype=jnp.float32) + 1.0) / head_count)
    block_rows = math.gcd(seq_length, 512)
    block_count = seq_length // block_rows
    w_qkv = matrices[:, : 3 * model_width]
    w_proj = matrices[:, 3 * model_width : 4 * model_width]
    w_up = matrices[:, 4 * model_width : 4 * model_width + ff_width]
    w_down = matrices[:, 4 * model_width + ff_width :]
    inputs = tokens.astype(jnp.float32)
    vector_rows = vectors.astype(jnp.float32)
    up_bias = vector_rows[8:].reshape(ff_width)
    normed, inverse_std = layer_norm(inputs)
    hidden = (normed * vector_rows[0] + vector_rows[1]).astype(jnp.bfloat16)
    projected = jnp.dot(hidden, w_qkv, preferred_element_type=jnp.float32)
    queries = (projected[:, :model_width] + vector_rows[2]).astype(jnp.bfloat16)
    kv_bias = jnp.concatenate([jnp.zeros((model_width,), jnp.float32), vector_rows[3]])
    kv_local = (projected[:, model_width:] + kv_bias).astype(jnp.bfloat16)
    gathered = lax.all_gather(kv_local, ("ctx", "shard"), axis=0, tiled=True)
    query_index = first_row + jnp.arange(row_count, dtype=jnp.int32)
    query_heads = queries.reshape(row_count, head_count, head_width)

    def key_block(index):
        piece = lax.dynamic_slice_in_dim(gathered, index * block_rows, block_rows, 0)
        key_heads = piece[:, :model_width].reshape(block_rows, head_count, head_width)
        value_heads = piece[:, model_width:].reshape(block_rows, head_count, head_width)
        key_index = index * block_rows + jnp.arange(block_rows, dtype=jnp.int32)
        logits, visible = block_scores(
            query_heads, query_index, key_heads, key_index, start_list, slopes, factor
        )
        return (logits, visible, key_heads, value_heads)

    def running_total(index, carry):
        highest, total = carry
        logits, visible, key_heads, value_heads = key_block(index)
        masked = jnp.where(visible, logits, NEGATIVE)
        updated = jnp.maximum(highest, jnp.max(masked, axis=2))
        weights = jnp.where(visible, jnp.exp(logits - updated[:, :, None]), 0.0)
        return (updated, total * jnp.exp(highest - updated) + jnp.sum(weights, axis=2))

    start_high = jnp.full((head_count, row_count), NEGATIVE, jnp.float32)
    start_total = jnp.zeros((head_count, row_count), jnp.float32)
    highest, total = lax.fori_loop(0, block_count, running_total, (start_high, start_total))
    log_total = highest + jnp.log(total)

    def weighted_sum(index, accum):
        logits, visible, key_heads, value_heads = key_block(index)
        probs = jnp.where(visible, jnp.exp(logits - log_total[:, :, None]), 0.0).astype(
            jnp.bfloat16
        )
        return accum + jnp.einsum(
            "hqk,khd->qhd", probs, value_heads, preferred_element_type=jnp.float32
        )

    attended = lax.fori_loop(
        0, block_count, weighted_sum, jnp.zeros((row_count, head_count, head_width), jnp.float32)
    )
    attended_low = attended.reshape(row_count, model_width).astype(jnp.bfloat16)
    middle = (
        inputs + jnp.dot(attended_low, w_proj, preferred_element_type=jnp.float32) + vector_rows[4]
    )
    normed_two, inverse_two = layer_norm(middle)
    hidden_two = (normed_two * vector_rows[5] + vector_rows[6]).astype(jnp.bfloat16)
    pre_act = jnp.dot(hidden_two, w_up, preferred_element_type=jnp.float32) + up_bias
    act_low = activate(pre_act).astype(jnp.bfloat16)
    down_out = lax.dot_general(
        act_low, w_down, (((1,), (1,)), ((), ())), preferred_element_type=jnp.float32
    )
    layer_output = (middle + down_out + vector_rows[7]).astype(jnp.bfloat16)
    upstream = cotangent.astype(jnp.float32)
    grad_act = jnp.dot(cotangent, w_down, preferred_element_type=jnp.float32)
    gelu_value, gelu_pull = jax.vjp(activate, pre_act)
    grad_pre = gelu_pull(grad_act)[0].astype(jnp.bfloat16)
    grad_up_w = lax.dot_general(
        hidden_two, grad_pre, (((0,), (0,)), ((), ())), preferred_element_type=jnp.float32
    )
    grad_down_w = lax.dot_general(
        cotangent, act_low, (((0,), (0,)), ((), ())), preferred_element_type=jnp.float32
    )
    grad_two = lax.dot_general(
        grad_pre, w_up, (((1,), (1,)), ((), ())), preferred_element_type=jnp.float32
    )
    grad_mid = upstream + norm_backward(grad_two, vector_rows[5], normed_two, inverse_two)
    grad_mid_low = grad_mid.astype(jnp.bfloat16)
    grad_proj = lax.dot_general(
        attended_low, grad_mid_low, (((0,), (0,)), ((), ())), preferred_element_type=jnp.float32
    )
    grad_out = lax.dot_general(
        grad_mid_low, w_proj, (((1,), (1,)), ((), ())), preferred_element_type=jnp.float32
    ).astype(jnp.bfloat16)
    grad_heads = grad_out.reshape(row_count, head_count, head_width)
    delta = jnp.sum(grad_heads.astype(jnp.float32) * attended, axis=2).T

    def score_grads(index):
        logits, visible, key_heads, value_heads = key_block(index)
        probs = jnp.where(visible, jnp.exp(logits - log_total[:, :, None]), 0.0)
        product = jnp.einsum(
            "qhd,khd->hqk", grad_heads, value_heads, preferred_element_type=jnp.float32
        )
        grad_logits = (probs * (product - delta[:, :, None])).astype(jnp.bfloat16)
        return (probs, grad_logits, key_heads)

    def both_grads(index, carry):
        accum, key_terms = carry
        probs, grad_logits, key_heads = score_grads(index)
        accum = (
            accum
            + jnp.einsum("hqk,khd->qhd", grad_logits, key_heads, preferred_element_type=jnp.float32)
            * factor
        )
        grad_key = (
            jnp.einsum("hqk,qhd->khd", grad_logits, query_heads, preferred_element_type=jnp.float32)
            * factor
        )
        grad_value = jnp.einsum(
            "hqk,qhd->khd",
            probs.astype(jnp.bfloat16),
            grad_heads,
            preferred_element_type=jnp.float32,
        )
        term = jnp.concatenate(
            [
                grad_key.reshape(block_rows, model_width),
                grad_value.reshape(block_rows, model_width),
            ],
            axis=1,
        )
        return (accum, lax.dynamic_update_slice_in_dim(key_terms, term, index * block_rows, 0))

    grad_query, key_terms = lax.fori_loop(
        0,
        block_count,
        both_grads,
        (
            jnp.zeros((row_count, head_count, head_width), jnp.float32),
            jnp.zeros((seq_length, 2 * model_width), jnp.float32),
        ),
    )
    own_key_grads = lax.psum_scatter(key_terms, ("ctx", "shard"), scatter_dimension=0, tiled=True)
    grad_qkv = jnp.concatenate(
        [grad_query.reshape(row_count, model_width), own_key_grads], axis=1
    ).astype(jnp.bfloat16)
    grad_qkv_weights = lax.dot_general(
        hidden, grad_qkv, (((0,), (0,)), ((), ())), preferred_element_type=jnp.float32
    )
    grad_hidden = lax.dot_general(
        grad_qkv, w_qkv, (((1,), (1,)), ((), ())), preferred_element_type=jnp.float32
    )
    query_bias_grad = jnp.sum(grad_qkv[:, :model_width].astype(jnp.float32), axis=0)
    value_bias_grad = jnp.sum(grad_qkv[:, 2 * model_width :].astype(jnp.float32), axis=0)
    grad_vectors = jnp.concatenate(
        [
            jnp.stack(
                [
                    jnp.sum(grad_hidden * normed, axis=0),
                    jnp.sum(grad_hidden, axis=0),
                    query_bias_grad,
                    value_bias_grad,
                    jnp.sum(grad_mid, axis=0),
                    jnp.sum(grad_two * normed_two, axis=0),
                    jnp.sum(grad_two, axis=0),
                    jnp.sum(upstream, axis=0),
                ]
            ),
            jnp.sum(grad_pre.astype(jnp.float32), axis=0).reshape(
                ff_width // model_width, model_width
            ),
        ],
        axis=0,
    )
    token_grads = grad_mid + norm_backward(grad_hidden, vector_rows[0], normed, inverse_std)
    grad_matrix = jnp.concatenate([grad_qkv_weights, grad_proj, grad_up_w, grad_down_w], axis=1)
    shard_count = lax.axis_size("shard")
    replicas = lax.axis_size("dp") * lax.axis_size("ctx")
    part_matrix, part_vec = (
        lax.psum_scatter(
            regroup(grad_matrix, 0, replicas, shard_count), "shard", scatter_dimension=0, tiled=True
        ),
        lax.psum_scatter(
            regroup(grad_vectors, 1, replicas, shard_count),
            "shard",
            scatter_dimension=1,
            tiled=True,
        ),
    )
    part_matrix, part_vec = (
        lax.psum_scatter(part_matrix, ("dp", "ctx"), scatter_dimension=0, tiled=True),
        lax.psum_scatter(part_vec, ("dp", "ctx"), scatter_dimension=1, tiled=True),
    )
    root = (row_count * lax.axis_size("dp") * group_size) ** (-0.5)
    correction = 1.0 - BETA**STEP
    moment_w, variance_w, updated_w = adam_update(
        master_matrices, first_matrices, second_matrices, part_matrix * root, correction, DECAY_RATE
    )
    moment_v, variance_v, updated_v = adam_update(
        master_vectors, first_vectors, second_vectors, part_vec * root, correction, 0.0
    )
    copied_w, copied_v = (
        lax.all_gather(updated_w.astype(jnp.bfloat16), "shard", axis=0, tiled=True),
        lax.all_gather(updated_v.astype(jnp.bfloat16), "shard", axis=1, tiled=True),
    )
    return (
        layer_output,
        token_grads,
        moment_w,
        moment_v,
        variance_w,
        variance_v,
        updated_w,
        updated_v,
        copied_w,
        copied_v,
    )


BLOCK = 256
EXTRA = 1
f32 = jnp.float32
bf16 = jnp.bfloat16
NT = (((1,), (1,)), ((), ()))
GELU_SCALE = math.sqrt(2.0 / math.pi)
GELU_CUBE = 0.044715


def split3(value):
    high = value.astype(bf16).astype(f32)
    rest = value - high
    middle = rest.astype(bf16).astype(f32)
    low = (rest - middle).astype(bf16).astype(f32)
    return high, middle, low


def positions(index, starts_ref, count):
    result = index
    for b in range(count):
        result = result - jnp.clip(index - starts_ref[0, b], 0, PIC - 1)
    return result.astype(f32)


def limits(index, starts_ref, count):
    result = index + 1
    for b in range(count):
        start = starts_ref[0, b]
        result = jnp.where((index >= start) & (index < start + PIC), start + PIC, result)
    return result


def head_lanes(shape, h, width):
    lane = lax.broadcasted_iota(jnp.int32, shape, 1)
    inside = (lane < width) if h == 0 else (lane >= width)
    return inside, lane - width if h == 0 else lane


def pick(spare, values):
    out = jnp.zeros(spare.shape, f32)
    for e, value in enumerate(values):
        out = jnp.where(spare == e, value, out)
    return out


def smem():
    return pl.BlockSpec(memory_space=pltpu.SMEM)


def vmem():
    return pl.BlockSpec(memory_space=pltpu.VMEM)


def anywhere():
    return pl.BlockSpec(memory_space=pl.ANY)


def hbm():
    return pl.BlockSpec(memory_space=pltpu.HBM)


def params(mebibytes):
    return pltpu.CompilerParams(vmem_limit_bytes=mebibytes * 2**20)


def cost(microseconds):
    return pl.CostEstimate(
        flops=int(microseconds * 1.0e9), bytes_accessed=0, transcendentals=0
    )


def start_all(copies):
    for copy in copies:
        copy.start()
    return copies


def wait_all(copies):
    for copy in copies:
        copy.wait()


def pattern_kernel(width, count, starts_ref, slopes_ref, out_ref):
    lanes = out_ref.shape[2]
    step = pl.program_id(0)
    index = lax.broadcasted_iota(jnp.int32, (BLOCK, lanes), 0) + step * BLOCK
    pos = positions(index, starts_ref, count)
    for h in range(2):
        _, spare = head_lanes((BLOCK, lanes), h, width)
        parts = split3(pos * slopes_ref[h])
        out_ref[h] = pick(spare, parts + (1.0, 1.0, 1.0)).astype(bf16)


def key_pattern(starts, slopes, seq, lanes):
    return pl.pallas_call(
        functools.partial(pattern_kernel, lanes // 2, starts.shape[1]),
        grid=(seq // BLOCK,),
        out_shape=jax.ShapeDtypeStruct((2, seq, lanes), bf16),
        in_specs=[smem()] * 2,
        out_specs=pl.BlockSpec((2, BLOCK, lanes), lambda i: (0, i, 0)),
        compiler_params=params(40),
        cost_estimate=cost(3),
        name="key_pattern",
    )(starts, slopes)


def forward_kernel(width, tile, count, rank_ref, starts_ref, slopes_ref, *refs):
    blocks = refs[:8]
    matrices_ref, vectors_ref, pattern_in = refs[8:11]
    att_out, wide_out, q_out, k_out, v_out, all_out = refs[11 + EXTRA : 17 + EXTRA]
    hid, wts, vecs, pattern, qa, ka, va, att, wide = refs[17 + EXTRA : 26 + EXTRA]
    in_sems, w_sems, hid_sems, out_sems = refs[26 + EXTRA :]
    seq, lanes = wide.shape
    model = hid.shape[1]
    rank = rank_ref[0]
    factor = width**-0.5
    w_copies = []
    for part in range(3):
        columns = pl.ds(pl.multiple_of(part * model + rank * lanes, lanes), lanes)
        w_copies.append(
            pltpu.make_async_copy(
                matrices_ref.at[:, columns],
                wts.at[:, part * lanes : (part + 1) * lanes],
                w_sems.at[part],
            )
        )
    w_copies.append(pltpu.make_async_copy(vectors_ref, vecs, w_sems.at[3]))
    start_all(w_copies)
    in_copies = start_all(
        [
            pltpu.make_async_copy(
                blocks[k], hid.at[k * BLOCK : (k + 1) * BLOCK], in_sems.at[k]
            )
            for k in range(8)
        ]
    )
    pattern_copy = pltpu.make_async_copy(pattern_in, pattern, w_sems.at[4])
    pattern_copy.start()
    wait_all(w_copies)
    gains = vecs[...].astype(f32)
    bias = vecs[:, pl.ds(pl.multiple_of(rank * lanes, lanes), lanes)].astype(f32)
    out_copies = []
    ones = []
    for h in range(2):
        inside, spare = head_lanes((BLOCK, lanes), h, width)
        ones.append((inside, jnp.where(spare < 3, 1.0, 0.0)))
    for pair in range(4):
        first = 2 * pair
        for k in (first, first + 1):
            in_copies[k].wait()
        both = slice(first * BLOCK, (first + 2) * BLOCK)
        normed, _ = normalize(hid[both, :].astype(f32))
        hid[both, :] = (normed * gains[0:1] + gains[1:2]).astype(bf16)
        for k in (first, first + 1):
            rows = slice(k * BLOCK, (k + 1) * BLOCK)
            dst = pl.ds(pl.multiple_of((k ^ rank) * BLOCK, BLOCK), BLOCK)
            copy = pltpu.make_async_copy(hid.at[rows], all_out.at[dst], hid_sems.at[k])
            copy.start()
            out_copies.append(copy)
        value = jnp.dot(hid[both, :], wts[...], preferred_element_type=f32)
        if pair == 0:
            pattern_copy.wait()
        for k in (first, first + 1):
            local = slice((k - first) * BLOCK, (k - first + 1) * BLOCK)
            dst = pl.ds(pl.multiple_of((k ^ rank) * BLOCK, BLOCK), BLOCK)
            q = (value[local, 0:lanes] + bias[2:3]).astype(bf16).astype(f32) * factor
            key = value[local, lanes : 2 * lanes]
            v = value[local, 2 * lanes : 3 * lanes] + bias[3:4]
            for h in range(2):
                inside, spare_ones = ones[h]
                qa[h, dst, :] = jnp.where(inside, q, spare_ones).astype(bf16)
                ka[h, dst, :] = jnp.where(inside, key, pattern[h, dst, :].astype(f32)).astype(bf16)
                va[h, dst, :] = jnp.where(inside, v, spare_ones).astype(bf16)
    out_copies += start_all(
        [
            pltpu.make_async_copy(ka, k_out, out_sems.at[0]),
            pltpu.make_async_copy(va, v_out, out_sems.at[1]),
        ]
    )

    def scores(h, queries, keys):
        return lax.dot_general(
            qa[h, queries, :], ka[h, keys, :], NT, preferred_element_type=f32
        )

    def mask(first_row, first_column, shape):
        rows = lax.broadcasted_iota(jnp.int32, (shape[0], 1), 0) + first_row
        columns = lax.broadcasted_iota(jnp.int32, shape, 1) + first_column
        return columns < limits(rows, starts_ref, count)

    def lane_best(value):
        best = value[:, :lanes]
        for c in range(1, value.shape[1] // lanes):
            best = jnp.maximum(best, value[:, c * lanes : (c + 1) * lanes])
        return best

    def with_shift(h, rows, shift):
        inside, spare = head_lanes((tile, lanes), h, width)
        parts = split3(-jnp.broadcast_to(shift, (tile, lanes)))
        value = qa[h, rows, :].astype(f32)
        for e in range(3):
            value = jnp.where(spare == 3 + e, parts[e], value)
        qa[h, rows, :] = value.astype(bf16)

    for i in range(seq // tile):
        base = i * tile
        end = base + tile
        rows = slice(base, end)
        tail = slice(end - PIC, end)
        over = slice(end, end + PIC)
        seen = mask(base, base, (tile, tile))
        if end < seq:
            seen_over = mask(end - PIC, end, (PIC, PIC))
        best = []
        kept = []
        for h in range(2):
            diagonal = jnp.where(seen, scores(h, rows, rows), NEGATIVE)
            top = lane_best(diagonal)
            below = []
            for j in range(i):
                below.append(scores(h, rows, slice(j * tile, (j + 1) * tile)))
                top = jnp.maximum(top, lane_best(below[-1]))
            beyond = None
            if end < seq:
                beyond = jnp.where(seen_over, scores(h, tail, over), NEGATIVE)
                low = jnp.maximum(top[tile - PIC :], lane_best(beyond))
                top = jnp.concatenate([top[: tile - PIC], low], axis=0)
            best.append(jnp.max(top, axis=1, keepdims=True))
            kept.append((below, diagonal, beyond))
        sums = []
        for h in range(2):
            below, diagonal, beyond = kept[h]
            weights = [jnp.exp(value - best[h]).astype(bf16) for value in below]
            weights.append(jnp.exp(diagonal - best[h]).astype(bf16))
            acc = jnp.dot(
                jnp.concatenate(weights, axis=1), va[h, :end, :], preferred_element_type=f32
            )
            if end < seq:
                beyond = jnp.exp(beyond - best[h][tile - PIC :])
                low = acc[tile - PIC :] + jnp.dot(
                    beyond.astype(bf16), va[h, over, :], preferred_element_type=f32
                )
                acc = jnp.concatenate([acc[: tile - PIC], low], axis=0)
            sums.append(acc)
        outs = []
        for h in range(2):
            acc = sums[h]
            column = width if h == 0 else 0
            total = acc[:, column : column + 1]
            outs.append(acc / total)
            with_shift(h, rows, best[h] + jnp.log(total))
        inside, _ = head_lanes((tile, lanes), 0, width)
        out = jnp.where(inside, outs[0], outs[1])
        wide[rows, :] = out
        count_here = tile // BLOCK
        groups = slice(i * count_here, (i + 1) * count_here)
        att[groups] = out.astype(bf16).reshape(count_here, BLOCK, lanes)
        out_copies += start_all(
            [
                pltpu.make_async_copy(att.at[groups], att_out.at[groups], out_sems.at[2 + 3 * i]),
                pltpu.make_async_copy(wide.at[rows], wide_out.at[rows], out_sems.at[3 + 3 * i]),
                pltpu.make_async_copy(
                    qa.at[:, rows], q_out.at[:, rows], out_sems.at[4 + 3 * i]
                ),
            ]
        )
    wait_all(out_copies)


def attention_forward(blocks, matrices, vectors, pattern, rank, starts, slopes, extra, tile=512):
    rows, model = blocks[0].shape
    seq = 8 * rows
    lanes = model // 8
    heads = jax.ShapeDtypeStruct((2, seq, lanes), bf16)
    return pl.pallas_call(
        functools.partial(forward_kernel, lanes // 2, tile, starts.shape[1]),
        out_shape=(
            jax.ShapeDtypeStruct((8, rows, lanes), bf16),
            jax.ShapeDtypeStruct((seq, lanes), f32),
            heads,
            heads,
            heads,
            jax.ShapeDtypeStruct((seq, model), bf16),
        ),
        in_specs=[smem()] * 3 + [hbm()] * 11 + [anywhere()] * EXTRA,
        out_specs=(hbm(),) * 6,
        scratch_shapes=[
            pltpu.VMEM((seq, model), bf16),
            pltpu.VMEM((model, 3 * lanes), bf16),
            pltpu.VMEM(vectors.shape, bf16),
            pltpu.VMEM((2, seq, lanes), bf16),
            pltpu.VMEM((2, seq, lanes), bf16),
            pltpu.VMEM((2, seq, lanes), bf16),
            pltpu.VMEM((2, seq, lanes), bf16),
            pltpu.VMEM((8, rows, lanes), bf16),
            pltpu.VMEM((seq, lanes), f32),
            pltpu.SemaphoreType.DMA((8,)),
            pltpu.SemaphoreType.DMA((5,)),
            pltpu.SemaphoreType.DMA((8,)),
            pltpu.SemaphoreType.DMA((2 + 3 * (seq // tile),)),
        ],
        compiler_params=params(56),
        cost_estimate=cost(20),
        name="attention_forward",
    )(rank, starts, slopes, *blocks, matrices, vectors, pattern, extra)


def backward_kernel(waits, width, tile, count, starts_ref, *refs):
    q_in, k_in, v_in, kt_in, wide_in, got_in = refs[:6]
    abs_out, rel_out, bias_out, mid_out = refs[6 + waits : 10 + waits]
    qa, ka, va, kt, wide, grads, mid, da, dq_ref, dk_ref, dv_ref = refs[10 + waits : 21 + waits]
    both_ref, flip_ref, mid_flip, bias_ref, in_sems, out_sems = refs[21 + waits :]
    seq, lanes = wide.shape
    factor = width**-0.5
    first = start_all(
        [
            pltpu.make_async_copy(wide_in, wide, in_sems.at[0]),
            pltpu.make_async_copy(got_in.at[:, :, 0:lanes], grads, in_sems.at[1]),
        ]
    )
    rest = start_all(
        [
            pltpu.make_async_copy(q_in, qa, in_sems.at[2]),
            pltpu.make_async_copy(k_in, ka, in_sems.at[3]),
            pltpu.make_async_copy(v_in, va, in_sems.at[4]),
            pltpu.make_async_copy(kt_in, kt, in_sems.at[5]),
            pltpu.make_async_copy(got_in.at[:, :, lanes : 2 * lanes], mid, in_sems.at[6]),
        ]
    )
    wait_all(first)

    def prologue(t, carry):
        rows = pl.ds(pl.multiple_of(t * BLOCK, BLOCK), BLOCK)
        g = grads[t].astype(f32)
        product = g * wide[rows, :]
        for h in range(2):
            inside, spare = head_lanes((BLOCK, lanes), h, width)
            delta = jnp.sum(jnp.where(inside, product, 0.0), axis=1, keepdims=True)
            parts = split3(-jnp.broadcast_to(delta, (BLOCK, lanes)))
            da[h, rows, :] = jnp.where(inside, g, pick(spare, parts)).astype(bf16)
        return carry

    lax.fori_loop(0, seq // BLOCK, prologue, 0)
    dq_ref[...] = jnp.zeros(dq_ref.shape, f32)
    wait_all(rest)

    def pair(h, keys, queries, mask, local):
        logits = lax.dot_general(ka[h, keys, :], qa[h, queries, :], NT, preferred_element_type=f32)
        probs = jnp.exp(logits)
        if mask is not None:
            probs = jnp.where(mask(logits.shape), probs, 0.0)
        inner = lax.dot_general(va[h, keys, :], da[h, queries, :], NT, preferred_element_type=f32)
        grad = (probs * inner).astype(bf16)
        dv_ref[h, local, :] += jnp.dot(
            probs.astype(bf16), da[h, queries, :], preferred_element_type=f32
        )
        dk_ref[h, local, :] += jnp.dot(grad, qa[h, queries, :], preferred_element_type=f32)
        rows = slice(h * width, (h + 1) * width)
        dq_ref[rows, queries] += jnp.dot(kt[rows, keys], grad, preferred_element_type=f32)

    bias_ref[...] = jnp.zeros(bias_ref.shape, f32)
    out_copies = []

    def send(t, part, value, flipped):
        columns = slice(part * lanes, (part + 1) * lanes)
        rows = slice(t * BLOCK, (t + 1) * BLOCK)
        both_ref[rows, columns] = value.astype(bf16)
        flip_ref[columns, rows] = flipped.astype(bf16)
        bias_ref[:, columns] += jnp.sum(value.astype(bf16).astype(f32), axis=0, keepdims=True)

    for j in range(seq // tile):
        base = j * tile
        dk_ref[...] = jnp.zeros(dk_ref.shape, f32)
        dv_ref[...] = jnp.zeros(dv_ref.shape, f32)

        def mask(first_key, first_query, shape):
            queries = lax.broadcasted_iota(jnp.int32, (1, shape[1]), 1) + first_query
            keys = lax.broadcasted_iota(jnp.int32, shape, 0) + first_key
            return keys < limits(queries, starts_ref, count)

        if base > 0:
            for h in range(2):
                pair(
                    h,
                    slice(base, base + PIC),
                    slice(base - PIC, base),
                    functools.partial(mask, base, base - PIC),
                    slice(0, PIC),
                )
        for h in range(2):
            pair(
                h,
                slice(base, base + tile),
                slice(base, base + tile),
                functools.partial(mask, base, base),
                slice(0, tile),
            )

        def full(i, base=base):
            queries = slice(i * tile, (i + 1) * tile)
            for h in range(2):
                pair(h, slice(base, base + tile), queries, None, slice(0, tile))

        if base + tile < seq:
            for i in range(j + 1, seq // tile):
                full(i)
        inside, _ = head_lanes((BLOCK, lanes), 0, width)
        for t in range(tile // BLOCK):
            part = slice(t * BLOCK, (t + 1) * BLOCK)
            block = j * (tile // BLOCK) + t
            dk = jnp.where(inside, dk_ref[0, part, :], dk_ref[1, part, :])
            dv = jnp.where(inside, dv_ref[0, part, :], dv_ref[1, part, :])
            send(block, 1, dk, dk.T)
            send(block, 2, dv, dv.T)
    for t in range(seq // BLOCK):
        rows = slice(t * BLOCK, (t + 1) * BLOCK)
        dq = dq_ref[:, rows] * factor
        send(t, 0, dq.T, dq)
        mid_flip[:, rows] = mid[t].astype(f32).T.astype(bf16)
        out_copies += start_all(
            [
                pltpu.make_async_copy(both_ref.at[rows], abs_out.at[rows], out_sems.at[2 * t]),
                pltpu.make_async_copy(
                    flip_ref.at[:, rows], rel_out.at[:, rows], out_sems.at[2 * t + 1]
                ),
            ]
        )
    out_copies += start_all(
        [
            pltpu.make_async_copy(bias_ref, bias_out, out_sems.at[2 * (seq // BLOCK)]),
            pltpu.make_async_copy(mid_flip, mid_out, out_sems.at[2 * (seq // BLOCK) + 1]),
        ]
    )
    wait_all(out_copies)


def attention_backward(saved, wide, got, starts, extras, tile=512):
    seq, lanes = wide.shape
    blocks = seq // BLOCK
    return pl.pallas_call(
        functools.partial(backward_kernel, len(extras), lanes // 2, tile, starts.shape[1]),
        out_shape=(
            jax.ShapeDtypeStruct((seq, 3 * lanes), bf16),
            jax.ShapeDtypeStruct((3 * lanes, seq), bf16),
            jax.ShapeDtypeStruct((1, 3 * lanes), f32),
            jax.ShapeDtypeStruct((lanes, seq), bf16),
        ),
        in_specs=[smem()] + [hbm()] * 6 + [anywhere()] * len(extras),
        out_specs=(hbm(),) * 4,
        scratch_shapes=[
            pltpu.VMEM((2, seq, lanes), bf16),
            pltpu.VMEM((2, seq, lanes), bf16),
            pltpu.VMEM((2, seq, lanes), bf16),
            pltpu.VMEM((lanes, seq), bf16),
            pltpu.VMEM((seq, lanes), f32),
            pltpu.VMEM((blocks, BLOCK, lanes), bf16),
            pltpu.VMEM((blocks, BLOCK, lanes), bf16),
            pltpu.VMEM((2, seq, lanes), bf16),
            pltpu.VMEM((lanes, seq), f32),
            pltpu.VMEM((2, tile, lanes), f32),
            pltpu.VMEM((2, tile, lanes), f32),
            pltpu.VMEM((seq, 3 * lanes), bf16),
            pltpu.VMEM((3 * lanes, seq), bf16),
            pltpu.VMEM((lanes, seq), bf16),
            pltpu.VMEM((1, 3 * lanes), f32),
            pltpu.SemaphoreType.DMA((7,)),
            pltpu.SemaphoreType.DMA((2 * blocks + 2,)),
        ],
        compiler_params=params(56),
        cost_estimate=cost(21),
        name="attention_backward",
    )(starts, *saved, wide, got, *extras)


def normalize(value):
    centered = value - jnp.mean(value, axis=1, keepdims=True)
    inverse = lax.rsqrt(jnp.mean(centered * centered, axis=1, keepdims=True) + EPSILON)
    return centered * inverse, inverse


def whole(shape):
    return pl.BlockSpec(shape, lambda *_: (0,) * len(shape))


def gate(arrays, waits):
    count = len(arrays)
    return pl.pallas_call(
        lambda *refs: None,
        out_shape=tuple(jax.ShapeDtypeStruct(array.shape, array.dtype) for array in arrays),
        in_specs=[anywhere()] * (count + len(waits)),
        out_specs=(anywhere(),) * count,
        input_output_aliases={k: k for k in range(count)},
        cost_estimate=cost(1),
        name="gate",
    )(*arrays, *waits)


def project_kernel(
    heads_ref, tokens_ref, weights_ref, vectors_ref, extra_ref, middle_ref, hidden_ref, attended_ref
):
    lanes = heads_ref.shape[2]
    for g in range(heads_ref.shape[0]):
        attended_ref[:, g * lanes : (g + 1) * lanes] = heads_ref[g]
    vecs = vectors_ref[...].astype(f32)
    middle = (
        tokens_ref[...].astype(f32)
        + jnp.dot(attended_ref[...], weights_ref[...], preferred_element_type=f32)
        + vecs[4:5]
    )
    middle_ref[...] = middle
    normed, _ = normalize(middle)
    hidden_ref[...] = (normed * vecs[5:6] + vecs[6:7]).astype(bf16)


def project_norm(heads, tokens, matrices, vectors, extra):
    rows, model = tokens.shape
    return pl.pallas_call(
        project_kernel,
        grid=(1,),
        out_shape=(
            jax.ShapeDtypeStruct((rows, model), f32),
            jax.ShapeDtypeStruct((rows, model), bf16),
        ),
        in_specs=[
            whole(heads.shape),
            whole(tokens.shape),
            pl.BlockSpec((model, model), lambda i: (0, 3)),
            whole(vectors.shape),
            anywhere(),
        ],
        out_specs=(whole((rows, model)),) * 2,
        scratch_shapes=[pltpu.VMEM((rows, model), bf16)],
        compiler_params=params(40),
        cost_estimate=cost(3),
        name="project_norm",
    )(heads, tokens, matrices, vectors, extra)


def gelu_parts(pre):
    square = pre * pre
    half = 0.5 * (1.0 + jnp.tanh(GELU_SCALE * (pre + GELU_CUBE * square * pre)))
    act = pre * half
    slope = half + 2.0 * act * (1.0 - half) * (GELU_SCALE * (1.0 + 3.0 * GELU_CUBE * square))
    return act, slope


def norm_pull(grad, gain, normed, inverse):
    scaled = grad * gain
    return inverse * (
        scaled
        - jnp.mean(scaled, axis=1, keepdims=True)
        - normed * jnp.mean(scaled * normed, axis=1, keepdims=True)
    )


def feed_kernel(chunk, *refs):
    hidden_in, middle_in, cotangent_in, vectors_in, bias_in, matrices_in = refs[:6]
    layer_out, grad_mid_out, heads_out, sums_out = refs[6:10]
    hidden, middle, cotangent, vecs_ref, bias, up, down, proj = refs[10:18]
    layer, grad_mid_ref, heads, sums, down_acc, two_acc, in_sems, w_sems, out_sems = refs[18:]
    model = hidden.shape[1]
    count = up.shape[0]
    first = start_all(
        [
            pltpu.make_async_copy(source, target, in_sems.at[k])
            for k, (source, target) in enumerate(
                ((hidden_in, hidden), (cotangent_in, cotangent), (bias_in, bias))
            )
        ]
    )
    weights = []
    for i in range(count):
        for part, ref in ((0, up), (1, down)):
            start = 4 * model + part * count * chunk + i * chunk
            weights.append(
                pltpu.make_async_copy(
                    matrices_in.at[:, start : start + chunk], ref.at[i], w_sems.at[2 * i + part]
                )
            )
    start_all(weights)
    rest = start_all(
        [
            pltpu.make_async_copy(middle_in, middle, in_sems.at[3]),
            pltpu.make_async_copy(vectors_in, vecs_ref, in_sems.at[4]),
            pltpu.make_async_copy(
                matrices_in.at[:, 3 * model : 4 * model], proj, in_sems.at[5]
            ),
        ]
    )
    wait_all(first)
    for i in range(count):
        weights[2 * i].wait()
        pre = jnp.dot(hidden[...], up[i], preferred_element_type=f32)
        pre = pre + bias[:, i * chunk : (i + 1) * chunk]
        weights[2 * i + 1].wait()
        grad_act = jnp.dot(cotangent[...], down[i], preferred_element_type=f32)
        act, slope = gelu_parts(pre)
        grad_pre = (grad_act * slope).astype(bf16)
        down_part = lax.dot_general(act.astype(bf16), down[i], NT, preferred_element_type=f32)
        two_part = lax.dot_general(grad_pre, up[i], NT, preferred_element_type=f32)
        if i == 0:
            down_acc[...] = down_part
            two_acc[...] = two_part
        else:
            down_acc[...] += down_part
            two_acc[...] += two_part
    wait_all(rest)
    vecs = vecs_ref[...].astype(f32)
    grad_two = two_acc[...]
    mid = middle[...]
    normed, inverse = normalize(mid)
    upstream = cotangent[...].astype(f32)
    grad_mid = upstream + norm_pull(grad_two, vecs[5:6], normed, inverse)
    low = grad_mid.astype(bf16)
    grads = lax.dot_general(low, proj[...], NT, preferred_element_type=f32).astype(bf16)
    groups, _, double = heads.shape
    lanes = double // 2
    for g in range(groups):
        heads[g, :, 0:lanes] = grads[:, g * lanes : (g + 1) * lanes]
        heads[g, :, lanes:double] = low[:, g * lanes : (g + 1) * lanes]
    out_copies = [pltpu.make_async_copy(heads, heads_out, out_sems.at[0])]
    out_copies[0].start()
    grad_mid_ref[...] = grad_mid
    layer[...] = (mid + down_acc[...] + vecs[7:8]).astype(bf16)
    rows = [grad_mid, grad_two * normed, grad_two, upstream]
    for k, value in enumerate(rows):
        sums[k : k + 1, :] = jnp.sum(value, axis=0, keepdims=True)
    out_copies += start_all(
        [
            pltpu.make_async_copy(layer, layer_out, out_sems.at[1]),
            pltpu.make_async_copy(grad_mid_ref, grad_mid_out, out_sems.at[2]),
            pltpu.make_async_copy(sums, sums_out, out_sems.at[3]),
        ]
    )
    wait_all(out_copies)


def feed_forward(hidden, up_bias, middle, cotangent, vectors, matrices, chunk=1024):
    rows, model = hidden.shape
    ff_width = up_bias.shape[1]
    count = ff_width // chunk
    outs = (
        jax.ShapeDtypeStruct((rows, model), bf16),
        jax.ShapeDtypeStruct((rows, model), f32),
        jax.ShapeDtypeStruct((8, rows, model // 4), bf16),
        jax.ShapeDtypeStruct((4, model), f32),
    )
    return pl.pallas_call(
        functools.partial(feed_kernel, chunk),
        out_shape=outs,
        in_specs=[hbm()] * 6,
        out_specs=(hbm(),) * 4,
        scratch_shapes=[
            pltpu.VMEM((rows, model), bf16),
            pltpu.VMEM((rows, model), f32),
            pltpu.VMEM((rows, model), bf16),
            pltpu.VMEM(vectors.shape, bf16),
            pltpu.VMEM((1, ff_width), f32),
            pltpu.VMEM((count, model, chunk), bf16),
            pltpu.VMEM((count, model, chunk), bf16),
            pltpu.VMEM((model, model), bf16),
        ]
        + [pltpu.VMEM(out.shape, out.dtype) for out in outs]
        + [
            pltpu.VMEM((rows, model), f32),
            pltpu.VMEM((rows, model), f32),
            pltpu.SemaphoreType.DMA((6,)),
            pltpu.SemaphoreType.DMA((2 * count,)),
            pltpu.SemaphoreType.DMA((4,)),
        ],
        compiler_params=params(40),
        cost_estimate=cost(14),
        name="feed_forward",
    )(hidden, middle, cotangent, vectors, up_bias, matrices)


def units_kernel(waits, rank_ref, *refs):
    blocks, heads = refs[:8], refs[8:16]
    cotangent_in, bias_in, matrices_in, vectors_in = refs[16:20]
    early_out, sums_out, attended_out = refs[20 + waits : 23 + waits]
    tokens, attended, hidden, cotangent, proj, vecs_ref = refs[23 + waits : 29 + waits]
    bias, up, down, act_ref, grad_ref, low, sums, grad_act = refs[29 + waits : 37 + waits]
    w_sems, c_sems, in_sems, head_sems, out_sems = refs[37 + waits :]
    seq, model = hidden.shape
    units = up.shape[1]
    lanes = model // 8
    rank = rank_ref[0]
    first = pl.multiple_of(rank * units, units)
    weights = []
    for part, ref in ((1, down), (0, up)):
        source = pl.ds(pl.multiple_of((4 + 4 * part) * model + first, units), units)
        weights.append(
            pltpu.make_async_copy(matrices_in.at[:, source], ref, w_sems.at[3 + part])
        )
    weights[0].start()
    pieces = [slice(n * 2 * BLOCK, (n + 1) * 2 * BLOCK) for n in range(4)]
    early_copies = start_all(
        [
            pltpu.make_async_copy(cotangent_in.at[piece], cotangent.at[piece], c_sems.at[n])
            for n, piece in enumerate(pieces)
        ]
    )
    copies = [
        pltpu.make_async_copy(bias_in.at[:, pl.ds(first, units)], bias, w_sems.at[0]),
        pltpu.make_async_copy(vectors_in, vecs_ref, w_sems.at[1]),
        pltpu.make_async_copy(matrices_in.at[:, 3 * model : 4 * model], proj, w_sems.at[2]),
    ]
    start_all(copies)
    loads = []
    for k in range(8):
        columns = pl.ds(pl.multiple_of((rank ^ k) * lanes, lanes), lanes)
        loads.append(
            pltpu.make_async_copy(heads[k], attended.at[:, :, columns], head_sems.at[k])
        )
    for k in range(8):
        rows = pl.ds(pl.multiple_of((rank ^ k) * BLOCK, BLOCK), BLOCK)
        loads.append(pltpu.make_async_copy(blocks[k], tokens.at[rows], in_sems.at[k]))
    start_all(loads)
    weights[1].start()
    weights[0].wait()
    for piece, copy in zip(pieces, early_copies):
        copy.wait()
        grad_act[piece, :] = jnp.dot(cotangent[piece, :], down[...], preferred_element_type=f32)
    wait_all(copies + loads)
    out_copies = [pltpu.make_async_copy(attended, attended_out, w_sems.at[6])]
    out_copies[0].start()
    vecs = vecs_ref[...].astype(f32)
    sums[...] = jnp.zeros(sums.shape, f32)
    for part in range(4):
        rows = slice(part * 2 * BLOCK, (part + 1) * 2 * BLOCK)
        heads_here = attended[2 * part : 2 * part + 2].reshape(2 * BLOCK, model)
        middle = (
            tokens[rows, :].astype(f32)
            + jnp.dot(heads_here, proj[...], preferred_element_type=f32)
            + vecs[4:5]
        )
        normed, _ = normalize(middle)
        hidden[rows, :] = (normed * vecs[5:6] + vecs[6:7]).astype(bf16)
        if part == 0:
            weights[1].wait()
        pre = jnp.dot(hidden[rows, :], up[...], preferred_element_type=f32) + bias[...]
        act, slope = gelu_parts(pre)
        grad_pre = grad_act[rows, :] * slope
        act_ref[:, rows] = act.T.astype(bf16)
        grad_ref[:, rows] = grad_pre.T.astype(bf16)
        sums[...] += jnp.sum(grad_pre.astype(bf16).astype(f32), axis=0, keepdims=True)
    quarter = model // 4
    copy = pltpu.make_async_copy(sums, sums_out, w_sems.at[0])
    copy.start()
    out_copies.append(copy)
    for block in range(4):
        columns = slice(block * quarter, (block + 1) * quarter)
        for n, (left, right) in enumerate(((grad_ref, hidden), (act_ref, cotangent))):
            value = jnp.dot(left[...], right[:, columns], preferred_element_type=f32)
            low[block, :, n * units : (n + 1) * units] = value.T.astype(bf16)
        copy = pltpu.make_async_copy(low.at[block], early_out.at[block], out_sems.at[block])
        copy.start()
        out_copies.append(copy)
    wait_all(out_copies)


def own_units(rank, blocks, heads, cotangent, up_bias, matrices, vectors, extras):
    rows, model = blocks[0].shape
    seq = 8 * rows
    units = up_bias.shape[1] // 8
    attended = (8, rows, model)
    return pl.pallas_call(
        functools.partial(units_kernel, len(extras)),
        out_shape=(
            jax.ShapeDtypeStruct((4, model // 4, 2 * units), bf16),
            jax.ShapeDtypeStruct((1, units), f32),
            jax.ShapeDtypeStruct(attended, bf16),
        ),
        in_specs=[smem()] + [hbm()] * 20 + [anywhere()] * len(extras),
        out_specs=(hbm(),) * 3,
        scratch_shapes=[
            pltpu.VMEM((seq, model), bf16),
            pltpu.VMEM(attended, bf16),
            pltpu.VMEM((seq, model), bf16),
            pltpu.VMEM((seq, model), bf16),
            pltpu.VMEM((model, model), bf16),
            pltpu.VMEM(vectors.shape, bf16),
            pltpu.VMEM((1, units), f32),
            pltpu.VMEM((model, units), bf16),
            pltpu.VMEM((model, units), bf16),
            pltpu.VMEM((units, seq), bf16),
            pltpu.VMEM((units, seq), bf16),
            pltpu.VMEM((4, model // 4, 2 * units), bf16),
            pltpu.VMEM((1, units), f32),
            pltpu.VMEM((seq, units), f32),
            pltpu.SemaphoreType.DMA((7,)),
            pltpu.SemaphoreType.DMA((4,)),
            pltpu.SemaphoreType.DMA((8,)),
            pltpu.SemaphoreType.DMA((8,)),
            pltpu.SemaphoreType.DMA((4,)),
        ],
        compiler_params=params(56),
        cost_estimate=cost(1),
        name="own_units",
    )(rank, *blocks, *heads, cotangent, up_bias, matrices, vectors, *extras)


def late_kernel(depth_ref, grads_in, hidden_in, mid_in, attended_in, *refs):
    outs = refs[:4]
    grads, hidden, mid, attended, total, low, in_sems, out_sems = refs[4:]
    columns, model = total.shape
    quarter = model // 4
    first = grads.shape[0]
    copies = start_all(
        [
            pltpu.make_async_copy(source, target, in_sems.at[n])
            for n, (source, target) in enumerate(
                (
                    (mid_in, mid),
                    (attended_in, attended),
                    (grads_in, grads),
                    (hidden_in, hidden),
                )
            )
        ]
    )
    wait_all(copies[:2])
    total[first:, :] = jnp.dot(mid[...], attended[...], preferred_element_type=f32)
    wait_all(copies[2:])
    total[:first, :] = jnp.dot(grads[...], hidden[...], preferred_element_type=f32)
    depth = depth_ref[0]
    near = depth ^ 1
    out_copies = []
    for n, (block, target) in enumerate(
        ((3 - near, outs[0]), (near, outs[1]), (3 - depth, outs[2]), (depth, outs[3]))
    ):
        lane = pl.ds(pl.multiple_of(block * quarter, quarter), quarter)
        if n < 2:
            low[n] = total[:, lane].astype(bf16)
            copy = pltpu.make_async_copy(low.at[n], target, out_sems.at[n])
        else:
            copy = pltpu.make_async_copy(total.at[:, lane], target, out_sems.at[n])
        copy.start()
        out_copies.append(copy)
    wait_all(out_copies)


def late_weights(depth, grads, hidden, mid, attended):
    seq, model = hidden.shape
    columns = grads.shape[0] + mid.shape[0]
    quarter = model // 4
    return pl.pallas_call(
        late_kernel,
        out_shape=(jax.ShapeDtypeStruct((columns, quarter), bf16),) * 2
        + (jax.ShapeDtypeStruct((columns, quarter), f32),) * 2,
        in_specs=[smem()] + [hbm()] * 4,
        out_specs=(hbm(),) * 4,
        scratch_shapes=[
            pltpu.VMEM(grads.shape, bf16),
            pltpu.VMEM(hidden.shape, bf16),
            pltpu.VMEM(mid.shape, bf16),
            pltpu.VMEM(attended.shape, bf16),
            pltpu.VMEM((columns, model), f32),
            pltpu.VMEM((2, columns, quarter), bf16),
            pltpu.SemaphoreType.DMA((4,)),
            pltpu.SemaphoreType.DMA((4,)),
        ],
        compiler_params=params(56),
        cost_estimate=cost(5),
        name="late_weights",
    )(depth, grads, hidden, mid, attended)


def flip_kernel(parts, *refs):
    total = refs[0][...].reshape(refs[0].shape[-2:]).astype(f32)
    for ref in refs[1:parts]:
        total = total + ref[...].astype(f32)
    refs[-1][...] = total.T.astype(bf16)


def flip_sum(arrays, waits, name):
    columns, rows = arrays[0].shape[-2:]
    return pl.pallas_call(
        functools.partial(flip_kernel, len(arrays)),
        grid=(1,),
        out_shape=jax.ShapeDtypeStruct((rows, columns), bf16),
        in_specs=[whole(array.shape) for array in arrays] + [anywhere()] * len(waits),
        out_specs=whole((rows, columns)),
        compiler_params=params(56),
        cost_estimate=cost(0.1),
        name=name,
    )(*arrays, *waits)


def final_kernel(
    heads_ref, weights_ref, tokens_ref, grad_mid_ref, vectors_ref, *refs
):
    out_ref, sums_ref, acc_ref, lhs = refs[-4:]
    step = pl.program_id(0)
    lanes = heads_ref.shape[2] // 3

    @pl.when(step == 0)
    def _():
        acc_ref[...] = jnp.zeros(acc_ref.shape, f32)

    source = pl.ds(pl.multiple_of(step * lanes, lanes), lanes)
    for g in range(heads_ref.shape[0]):
        lhs[:, g * lanes : (g + 1) * lanes] = heads_ref[g, :, source]
    acc_ref[...] += lax.dot_general(lhs[...], weights_ref[...], NT, preferred_element_type=f32)

    @pl.when(step == pl.num_programs(0) - 1)
    def _():
        vecs = vectors_ref[...].astype(f32)
        grad = acc_ref[...]
        normed, inverse = normalize(tokens_ref[...].astype(f32))
        out_ref[...] = grad_mid_ref[...] + norm_pull(grad, vecs[0:1], normed, inverse)
        sums_ref[0:1, :] = jnp.sum(grad * normed, axis=0, keepdims=True)
        sums_ref[1:2, :] = jnp.sum(grad, axis=0, keepdims=True)


def token_gradient(heads, matrices, tokens, grad_mid, vectors, extras):
    rows, model = tokens.shape
    return pl.pallas_call(
        final_kernel,
        grid=(3,),
        out_shape=(
            jax.ShapeDtypeStruct((rows, model), f32),
            jax.ShapeDtypeStruct((2, model), f32),
        ),
        in_specs=[
            whole(heads.shape),
            pl.BlockSpec((model, model), lambda i: (0, i)),
            whole((rows, model)),
            whole((rows, model)),
            whole(vectors.shape),
        ]
        + [anywhere()] * len(extras),
        out_specs=(whole((rows, model)), whole((2, model))),
        scratch_shapes=[pltpu.VMEM((rows, model), f32), pltpu.VMEM((rows, model), bf16)],
        compiler_params=params(56),
        cost_estimate=cost(6),
        name="token_gradient",
    )(heads, matrices, tokens, grad_mid, vectors, *extras)


def vector_pieces_kernel(rank_ref, one_ref, bias_ref, two_ref, units_ref, *refs):
    states, out_ref = refs[:3], refs[-1]
    rank = rank_ref[0]
    lanes = out_ref.shape[2]
    out_ref[...] = jnp.zeros(out_ref.shape, f32)
    copies = out_ref.shape[0] // 8
    for b in range(8):
        columns = slice(b * lanes, (b + 1) * lanes)
        for c in range(copies):
            out_ref[copies * b + c, 0:2, :] = one_ref[:, columns]
            out_ref[copies * b + c, 4:8, :] = two_ref[:, columns]
    rows, own = states[0].shape
    packed = jnp.concatenate(
        [ref[...] for ref in states] + [jnp.zeros((rows, lanes - 3 * own), f32)], axis=1
    )
    for b in range(out_ref.shape[0]):
        out_ref[b, 12 : 12 + rows, :] = packed
    for c in range(copies):
        out_ref[copies * rank + c, 2:3, :] = bias_ref[:, 0:lanes]
        out_ref[copies * rank + c, 3:4, :] = bias_ref[:, 2 * lanes : 3 * lanes]
    pieces = units_ref.shape[1] // lanes
    for n in range(pieces):
        place = rank * pieces + n
        for c in range(copies):
            out_ref[copies * (place % 8) + c, pl.ds(8 + place // 8, 1), :] = units_ref[
                :, n * lanes : (n + 1) * lanes
            ]


def vector_pieces(rank, one, bias, two, units, states, devices, waits):
    lanes = one.shape[1] // 8
    return pl.pallas_call(
        vector_pieces_kernel,
        grid=(1,),
        out_shape=jax.ShapeDtypeStruct((devices, 24, lanes), f32),
        in_specs=[smem(), whole(one.shape), whole(bias.shape), whole(two.shape), whole(units.shape)]
        + [whole(state.shape) for state in states]
        + [anywhere()] * len(waits),
        out_specs=whole((devices, 24, lanes)),
        compiler_params=params(40),
        cost_estimate=cost(0.01),
        name="vector_pieces",
    )(rank, one, bias, two, units, *states, *waits)


def adam(master, first, second, gradient, decay_rate):
    correction = 1.0 - BETA**STEP
    moment = BETA * first + (1.0 - BETA) * gradient
    variance = BETA * second + (1.0 - BETA) * gradient * gradient
    direction = moment / correction / (jnp.sqrt(variance / correction) + ADAM_EPSILON)
    return moment, variance, master - RATE * (direction + decay_rate * master)


def vector_update_kernel(root, place_ref, got_ref, *refs):
    outs, copied_ref = refs[-4:-1], refs[-1]
    lanes = got_ref.shape[2]
    rows, own = outs[0].shape
    gradient = jnp.sum(got_ref[:, :16, :], axis=0) * root
    shard = place_ref[0] % 4
    first = place_ref[0] - shard
    columns = lax.broadcasted_iota(jnp.int32, (16, lanes), 1) // own
    total = jnp.zeros((16, lanes), f32)
    for k in range(4):
        other = shard ^ k
        shifted = pltpu.roll(gradient, lax.rem(lanes - other * own, lanes), 1)[:rows, :own]
        packed = got_ref[first + other, 12 : 12 + rows, :]
        states = [packed[:, n * own : (n + 1) * own] for n in range(3)]
        values = adam(*states, shifted, 0.0)
        if k == 0:
            for ref, value in zip(outs, values):
                ref[...] = value
        wide = jnp.concatenate([values[2], jnp.zeros((rows, lanes - own), f32)], axis=1)
        wide = jnp.concatenate([wide, jnp.zeros((16 - rows, lanes), f32)], axis=0)
        total = jnp.where(columns == other, pltpu.roll(wide, other * own, 1), total)
    copied_ref[...] = total[:rows].astype(bf16)


def vector_update(place, got, rows, own, root, extras):
    lanes = got.shape[2]
    mine = jax.ShapeDtypeStruct((rows, own), f32)
    return pl.pallas_call(
        functools.partial(vector_update_kernel, root),
        grid=(1,),
        out_shape=(mine, mine, mine, jax.ShapeDtypeStruct((rows, lanes), bf16)),
        in_specs=[smem(), whole(got.shape)] + [anywhere()] * len(extras),
        out_specs=(whole((rows, own)),) * 3 + (whole((rows, lanes)),),
        compiler_params=params(40),
        cost_estimate=cost(0.01),
        name="vector_update",
    )(place, got, *extras)


def update_kernel(root, got_ref, *refs):
    states, outs = refs[:3], refs[-5:-2]
    copied_ref, gradient_ref = refs[-2:]
    lanes = got_ref.shape[2]
    for g in range(got_ref.shape[0]):
        gradient_ref[:, g * lanes : (g + 1) * lanes] = got_ref[g].astype(f32)
    values = adam(*[ref[...] for ref in states], gradient_ref[...] * root, DECAY_RATE)
    for ref, value in zip(outs, values):
        ref[...] = value
    copied_ref[...] = values[2].astype(bf16)


def matrix_update(got, states, previous, extras, first, parts, root, name):
    groups, rows, packed = got.shape
    lanes = packed // parts
    block = groups * lanes
    total = states[0].shape[1]
    start = first // block
    state = pl.BlockSpec((rows, block), lambda i: (0, start + i))
    return pl.pallas_call(
        functools.partial(update_kernel, root),
        grid=(parts,),
        out_shape=(jax.ShapeDtypeStruct((rows, total), f32),) * 3
        + (jax.ShapeDtypeStruct((rows, parts * block), bf16),),
        in_specs=[pl.BlockSpec((groups, rows, lanes), lambda i: (0, 0, i))]
        + [state] * 3
        + [anywhere()] * (len(previous) + len(extras)),
        out_specs=(state,) * 3 + (pl.BlockSpec((rows, block), lambda i: (0, i)),),
        scratch_shapes=[pltpu.VMEM((rows, block), f32)],
        input_output_aliases={4 + k: k for k in range(len(previous))},
        compiler_params=params(56),
        cost_estimate=cost(4),
        name=name,
    )(got, *states, *previous, *extras)


def place_kernel(late_blocks, shard_ref, *refs):
    out_ref = refs[-1]
    rows = refs[0].shape[0]
    for first, chosen in ((0, pl.program_id(0) < late_blocks), (4, pl.program_id(0) >= late_blocks)):

        @pl.when(chosen)
        def _(first=first):
            for k in range(4):
                place = pl.multiple_of((shard_ref[0] ^ k) * rows, rows)
                out_ref[pl.ds(place, rows), :] = refs[first + k][...]


def place_copies(shard, late, early):
    rows = late[0].shape[0]
    block = 2048
    count = late[0].shape[1] // block
    total = count * block + early[0].shape[1]
    return pl.pallas_call(
        functools.partial(place_kernel, count),
        grid=(total // block,),
        out_shape=jax.ShapeDtypeStruct((4 * rows, total), bf16),
        in_specs=[smem()]
        + [pl.BlockSpec((rows, block), lambda i: (0, jnp.minimum(i, count - 1)))] * 4
        + [pl.BlockSpec((rows, block), lambda i: (0, jnp.maximum(i - count, 0)))] * 4,
        out_specs=pl.BlockSpec((4 * rows, block), lambda i: (0, i)),
        compiler_params=params(40),
        cost_estimate=cost(0.01),
        name="place_copies",
    )(shard, *late, *early)


def fits_sequence_plan(mesh):
    return mesh.shape["dp"] == 4 and mesh.shape["ctx"] == 2 and mesh.shape["shard"] == 4


EVERY = ("dp", "ctx", "shard")
SEQUENCE = ("ctx", "shard")


def swap(array, axis, bit):
    count = lax.axis_size(axis)
    return lax.ppermute(array, axis, [(i, i ^ bit) for i in range(count)])


def gather_blocks(block, ready=True):
    over_ctx = swap(block, "ctx", 1)
    over_y = swap(block, "shard", 2)
    over_core = swap(block, "shard", 1)
    even = (lax.axis_index("shard") % 2 == 0) & ready
    relay = jnp.where(even, over_ctx, over_y)
    opposite = lax.ppermute(relay, SEQUENCE, [(i, i ^ (4 if i % 2 else 2)) for i in range(8)])
    ctx_core = swap(over_ctx, "shard", 1)
    y_core = swap(over_y, "shard", 1)
    opposite_core = swap(opposite, "shard", 1)
    return relay, [
        block, over_core, over_y, y_core, over_ctx, ctx_core, opposite, opposite_core
    ]


def gather_direct(block):
    straight = [
        block,
        swap(block, "shard", 2),
        swap(block, "ctx", 1),
        lax.ppermute(block, SEQUENCE, [(i, i ^ 6) for i in range(8)]),
    ]
    return [array for first in straight for array in (first, swap(first, "shard", 1))]


def gather_rows(array):
    return lax.all_gather(array, SEQUENCE, axis=0, tiled=True)


def exchange(array, axes=SEQUENCE):
    return lax.all_to_all(array, axes, 0, 0, tiled=True)


def dot_tn(left, right):
    return lax.dot_general(left, right, (((0,), (0,)), ((), ())), preferred_element_type=f32)


def dot_nt(left, right):
    return lax.dot_general(left, right, NT, preferred_element_type=f32)


def dot_nn(left, right):
    return jnp.dot(left, right, preferred_element_type=f32)


def shift_dp(array, distance):
    return lax.ppermute(array, "dp", [(i, (i + distance) % 4) for i in range(4)])


def gather_shards(array):
    over_core = swap(array, "shard", 1)
    over_y = swap(array, "shard", 2)
    return [array, over_core, over_y, swap(over_y, "shard", 1)]


def sequence_shards(
    tokens,
    cotangent,
    picture_starts,
    matrices,
    vectors,
    master_matrices,
    master_vectors,
    first_matrices,
    first_vectors,
    second_matrices,
    second_vectors,
):
    row_count, width = tokens.shape
    ff_width = (matrices.shape[1] - 4 * width) // 2
    group = 8
    shard = lax.axis_index("shard")
    rank = lax.axis_index("ctx") * 4 + shard
    depth = lax.axis_index("dp")
    lanes = width // group
    units = ff_width // group
    own_rows = master_matrices.shape[0]
    seq = group * row_count
    head = rank * 2 + jnp.arange(2)
    slopes = jnp.exp2(-8.0 * (head.astype(f32) + 1.0) / HEADS)
    rank_array = rank.astype(jnp.int32).reshape(1)
    shard_array = shard.astype(jnp.int32).reshape(1)
    vector_rows = vectors.astype(f32)
    up_bias = vector_rows[8:].reshape(1, ff_width)

    with jax.named_scope("prepare"):
        pattern = key_pattern(picture_starts, slopes, seq, lanes)
    with jax.named_scope("gather_tokens"):
        ready = pattern[0, 0, lanes // 2 + 3] == 1.0
        passed, token_blocks = gather_blocks(tokens, ready)
    with jax.named_scope("gather_cotangent"):
        zero = passed[0, 0] * 0
        cotangent_late = cotangent + zero
        cotangent_all = gather_rows(cotangent_late)
    attended_heads, attended_wide, *saved, hidden_all = attention_forward(
        token_blocks,
        matrices,
        vectors,
        pattern,
        rank_array,
        picture_starts,
        slopes,
        cotangent_late,
    )
    with jax.named_scope("attended_exchange"):
        attended_got = exchange(attended_heads)
    with jax.named_scope("transpose_keys"):
        half = lanes // 2
        keys_low = saved[1]
        keys_transposed = jnp.concatenate(
            [keys_low[0, :, :half], keys_low[1, :, half:]], axis=1
        ).T
    middle, hidden_two = project_norm(
        attended_got, tokens, matrices, vectors, keys_transposed
    )
    with jax.named_scope("gather_attended"):
        head_blocks = gather_direct(attended_heads)
    layer_output, grad_mid, grad_out, sums_two = feed_forward(
        hidden_two, up_bias, middle, cotangent, vectors, matrices
    )
    with jax.named_scope("grad_attended_exchange"):
        grad_got = exchange(grad_out)
    early, unit_sums, attended_all = own_units(
        rank_array,
        token_blocks,
        head_blocks,
        cotangent_all,
        up_bias,
        matrices,
        vectors,
        [grad_out],
    )
    with jax.named_scope("grad_feed"):
        (early,) = gate([early], [grad_got])
        early_sum = lax.psum_scatter(early, "dp", scatter_dimension=0, tiled=True)
    grad_abs, grad_flipped, bias_sums, mid_flipped = attention_backward(
        (*saved, keys_transposed), attended_wide, grad_got, picture_starts, [early]
    )
    with jax.named_scope("grad_qkv_exchange"):
        grad_tokens = exchange(grad_abs.reshape(group, row_count, 3 * lanes))
    with jax.named_scope("grad_late"):
        near_far, near, relay, late_own = late_weights(
            depth.astype(jnp.int32).reshape(1), grad_flipped, hidden_all, mid_flipped, attended_all.reshape(seq, width)
        )
        beside = [(i, i ^ 1) for i in range(4)]
        relay = (relay + lax.ppermute(near_far, "dp", beside).astype(f32)).astype(bf16)
        near = lax.ppermute(near, "dp", beside)
        far = lax.ppermute(relay, "dp", [(i, 3 - i) for i in range(4)])
    with jax.named_scope("early_rows"):
        (early_sum,) = gate([early_sum], [grad_tokens, relay])
        early_got = exchange(early_sum.reshape(group, own_rows, 2 * units))
    token_grads, sums_one = token_gradient(
        grad_tokens, matrices, tokens, grad_mid, vectors, [early_sum]
    )
    with jax.named_scope("late_rows"):
        late_sum = flip_sum([late_own, near, far], [early_got, sums_one], "late_rows")
        late_got = exchange(late_sum.reshape(group, own_rows, 4 * lanes))
    root = (row_count * lax.axis_size("dp") * group) ** (-0.5)
    matrix_states = (master_matrices, first_matrices, second_matrices)
    *early_states, early_copy = matrix_update(
        early_got, matrix_states, (), [late_got], 4 * width, 2, root, "early_update"
    )
    with jax.named_scope("early_copies"):
        early_copied = gather_shards(early_copy)
    moment_w, variance_w, updated_w, late_copy = matrix_update(
        late_got,
        matrix_states,
        early_states,
        [],
        0,
        4,
        root,
        "late_update",
    )
    with jax.named_scope("grad_vectors"):
        vector_states = (master_vectors, first_vectors, second_vectors)
        pieces = vector_pieces(
            rank_array, sums_one, bias_sums, sums_two, unit_sums, vector_states, 32, [late_copy]
        )
        vectors_got = exchange(pieces, EVERY)
    with jax.named_scope("late_copies"):
        late_copied = gather_shards(late_copy)
    copied_w = place_copies(shard_array, late_copied, early_copied)
    moment_v, variance_v, updated_v, copied_v = vector_update(
        (depth * group + rank).astype(jnp.int32).reshape(1),
        vectors_got,
        *master_vectors.shape,
        root,
        [early_copied[3]],
    )
    return (
        layer_output,
        token_grads,
        moment_w,
        moment_v,
        variance_w,
        variance_v,
        updated_w,
        updated_v,
        copied_w,
        copied_v,
    )


def solution(mesh):
    in_specs = (
        P(("dp", "ctx", "shard"), None),
        P(("dp", "ctx", "shard"), None),
        P("dp", None),
        P(),
        P(),
        P(("dp", "ctx", "shard"), None),
        P(None, ("dp", "ctx", "shard")),
        P(("dp", "ctx", "shard"), None),
        P(None, ("dp", "ctx", "shard")),
        P(("dp", "ctx", "shard"), None),
        P(None, ("dp", "ctx", "shard")),
    )
    out_specs = (
        P(("dp", "ctx", "shard"), None),
        P(("dp", "ctx", "shard"), None),
        P(("dp", "ctx", "shard"), None),
        P(None, ("dp", "ctx", "shard")),
        P(("dp", "ctx", "shard"), None),
        P(None, ("dp", "ctx", "shard")),
        P(("dp", "ctx", "shard"), None),
        P(None, ("dp", "ctx", "shard")),
        P(("dp", "ctx"), None),
        P(None, ("dp", "ctx")),
    )
    body = sequence_shards if fits_sequence_plan(mesh) else general_shards
    return jax.shard_map(body, mesh=mesh, in_specs=in_specs, out_specs=out_specs, check_vma=False)
```

```python
import functools
import math

import jax
import jax.numpy as jnp
from jax import lax
from jax.experimental import pallas as pl
from jax.experimental.pallas import tpu as pltpu
from jax.sharding import PartitionSpec as P

HEADS = 16
PIC = 256
STEP = 2


EPSILON = 1e-05
NEGATIVE = -1e30
BETA = 0.5
RATE = 0.03
DECAY_RATE = 0.1
ADAM_EPSILON = 1e-08


def token_tags(index, start_list, block_len):
    after = index[:, None] - start_list[None, :]
    inside = (after >= 0) & (after < block_len)
    offsets = jnp.sum(jnp.clip(after, 0, block_len - 1), axis=1)
    number = jnp.arange(1, start_list.shape[0] + 1, dtype=jnp.int32)
    picture = jnp.sum(jnp.where(inside, number[None, :], 0), axis=1) - 1
    return (index - offsets, picture)


def block_scores(query_heads, query_index, key_heads, key_index, start_list, slopes, factor):
    query_pos, query_pic = token_tags(query_index, start_list, PIC)
    key_pos, key_pic = token_tags(key_index, start_list, PIC)
    raw = jnp.einsum("qhd,khd->hqk", query_heads, key_heads, preferred_element_type=jnp.float32)
    distance = (query_pos[:, None] - key_pos[None, :]).astype(jnp.float32)
    logits = raw * factor - slopes[:, None, None] * distance[None, :, :]
    same = (query_pic[:, None] == key_pic[None, :]) & (query_pic[:, None] >= 0)
    visible = (key_index[None, :] <= query_index[:, None]) | same
    return (logits, visible[None, :, :])


def layer_norm(inputs):
    centered = inputs - jnp.mean(inputs, axis=1, keepdims=True)
    inverse_std = lax.rsqrt(jnp.mean(centered * centered, axis=1, keepdims=True) + EPSILON)
    return (centered * inverse_std, inverse_std)


def norm_backward(grad_normed, gain, normed, inverse_std):
    scaled = grad_normed * gain
    return inverse_std * (
        scaled
        - jnp.mean(scaled, axis=1, keepdims=True)
        - normed * jnp.mean(scaled * normed, axis=1, keepdims=True)
    )


def activate(value):
    return jax.nn.gelu(value, approximate=True)


def regroup(array, dim, outer, inner):
    shape = array.shape
    split = array.reshape(
        shape[:dim] + (outer, inner, shape[dim] // (outer * inner)) + shape[dim + 1 :]
    )
    return jnp.swapaxes(split, dim, dim + 1).reshape(shape)


def adam_update(master, first, second, gradient, correction, decay_rate):
    moment = BETA * first + (1.0 - BETA) * gradient
    variance = BETA * second + (1.0 - BETA) * gradient * gradient
    direction = moment / correction / (jnp.sqrt(variance / correction) + ADAM_EPSILON)
    return (moment, variance, master - RATE * (direction + decay_rate * master))


def general_shards(
    tokens,
    cotangent,
    picture_starts,
    matrices,
    vectors,
    master_matrices,
    master_vectors,
    first_matrices,
    first_vectors,
    second_matrices,
    second_vectors,
):
    row_count, model_width = tokens.shape
    ff_width = (matrices.shape[1] - 4 * model_width) // 2
    head_count = HEADS
    head_width = model_width // head_count
    factor = head_width ** (-0.5)
    group_size = lax.axis_size("ctx") * lax.axis_size("shard")
    group_rank = lax.axis_index("ctx") * lax.axis_size("shard") + lax.axis_index("shard")
    seq_length = row_count * group_size
    first_row = group_rank * row_count
    start_list = picture_starts[0]
    slopes = jnp.exp2(-8.0 * (jnp.arange(head_count, dtype=jnp.float32) + 1.0) / head_count)
    block_rows = math.gcd(seq_length, 512)
    block_count = seq_length // block_rows
    w_qkv = matrices[:, : 3 * model_width]
    w_proj = matrices[:, 3 * model_width : 4 * model_width]
    w_up = matrices[:, 4 * model_width : 4 * model_width + ff_width]
    w_down = matrices[:, 4 * model_width + ff_width :]
    inputs = tokens.astype(jnp.float32)
    vector_rows = vectors.astype(jnp.float32)
    up_bias = vector_rows[8:].reshape(ff_width)
    normed, inverse_std = layer_norm(inputs)
    hidden = (normed * vector_rows[0] + vector_rows[1]).astype(jnp.bfloat16)
    projected = jnp.dot(hidden, w_qkv, preferred_element_type=jnp.float32)
    queries = (projected[:, :model_width] + vector_rows[2]).astype(jnp.bfloat16)
    kv_bias = jnp.concatenate([jnp.zeros((model_width,), jnp.float32), vector_rows[3]])
    kv_local = (projected[:, model_width:] + kv_bias).astype(jnp.bfloat16)
    gathered = lax.all_gather(kv_local, ("ctx", "shard"), axis=0, tiled=True)
    query_index = first_row + jnp.arange(row_count, dtype=jnp.int32)
    query_heads = queries.reshape(row_count, head_count, head_width)

    def key_block(index):
        piece = lax.dynamic_slice_in_dim(gathered, index * block_rows, block_rows, 0)
        key_heads = piece[:, :model_width].reshape(block_rows, head_count, head_width)
        value_heads = piece[:, model_width:].reshape(block_rows, head_count, head_width)
        key_index = index * block_rows + jnp.arange(block_rows, dtype=jnp.int32)
        logits, visible = block_scores(
            query_heads, query_index, key_heads, key_index, start_list, slopes, factor
        )
        return (logits, visible, key_heads, value_heads)

    def running_total(index, carry):
        highest, total = carry
        logits, visible, key_heads, value_heads = key_block(index)
        masked = jnp.where(visible, logits, NEGATIVE)
        updated = jnp.maximum(highest, jnp.max(masked, axis=2))
        weights = jnp.where(visible, jnp.exp(logits - updated[:, :, None]), 0.0)
        return (updated, total * jnp.exp(highest - updated) + jnp.sum(weights, axis=2))

    start_high = jnp.full((head_count, row_count), NEGATIVE, jnp.float32)
    start_total = jnp.zeros((head_count, row_count), jnp.float32)
    highest, total = lax.fori_loop(0, block_count, running_total, (start_high, start_total))
    log_total = highest + jnp.log(total)

    def weighted_sum(index, accum):
        logits, visible, key_heads, value_heads = key_block(index)
        probs = jnp.where(visible, jnp.exp(logits - log_total[:, :, None]), 0.0).astype(
            jnp.bfloat16
        )
        return accum + jnp.einsum(
            "hqk,khd->qhd", probs, value_heads, preferred_element_type=jnp.float32
        )

    attended = lax.fori_loop(
        0, block_count, weighted_sum, jnp.zeros((row_count, head_count, head_width), jnp.float32)
    )
    attended_low = attended.reshape(row_count, model_width).astype(jnp.bfloat16)
    middle = (
        inputs + jnp.dot(attended_low, w_proj, preferred_element_type=jnp.float32) + vector_rows[4]
    )
    normed_two, inverse_two = layer_norm(middle)
    hidden_two = (normed_two * vector_rows[5] + vector_rows[6]).astype(jnp.bfloat16)
    pre_act = jnp.dot(hidden_two, w_up, preferred_element_type=jnp.float32) + up_bias
    act_low = activate(pre_act).astype(jnp.bfloat16)
    down_out = lax.dot_general(
        act_low, w_down, (((1,), (1,)), ((), ())), preferred_element_type=jnp.float32
    )
    layer_output = (middle + down_out + vector_rows[7]).astype(jnp.bfloat16)
    upstream = cotangent.astype(jnp.float32)
    grad_act = jnp.dot(cotangent, w_down, preferred_element_type=jnp.float32)
    gelu_value, gelu_pull = jax.vjp(activate, pre_act)
    grad_pre = gelu_pull(grad_act)[0].astype(jnp.bfloat16)
    grad_up_w = lax.dot_general(
        hidden_two, grad_pre, (((0,), (0,)), ((), ())), preferred_element_type=jnp.float32
    )
    grad_down_w = lax.dot_general(
        cotangent, act_low, (((0,), (0,)), ((), ())), preferred_element_type=jnp.float32
    )
    grad_two = lax.dot_general(
        grad_pre, w_up, (((1,), (1,)), ((), ())), preferred_element_type=jnp.float32
    )
    grad_mid = upstream + norm_backward(grad_two, vector_rows[5], normed_two, inverse_two)
    grad_mid_low = grad_mid.astype(jnp.bfloat16)
    grad_proj = lax.dot_general(
        attended_low, grad_mid_low, (((0,), (0,)), ((), ())), preferred_element_type=jnp.float32
    )
    grad_out = lax.dot_general(
        grad_mid_low, w_proj, (((1,), (1,)), ((), ())), preferred_element_type=jnp.float32
    ).astype(jnp.bfloat16)
    grad_heads = grad_out.reshape(row_count, head_count, head_width)
    delta = jnp.sum(grad_heads.astype(jnp.float32) * attended, axis=2).T

    def score_grads(index):
        logits, visible, key_heads, value_heads = key_block(index)
        probs = jnp.where(visible, jnp.exp(logits - log_total[:, :, None]), 0.0)
        product = jnp.einsum(
            "qhd,khd->hqk", grad_heads, value_heads, preferred_element_type=jnp.float32
        )
        grad_logits = (probs * (product - delta[:, :, None])).astype(jnp.bfloat16)
        return (probs, grad_logits, key_heads)

    def both_grads(index, carry):
        accum, key_terms = carry
        probs, grad_logits, key_heads = score_grads(index)
        accum = (
            accum
            + jnp.einsum("hqk,khd->qhd", grad_logits, key_heads, preferred_element_type=jnp.float32)
            * factor
        )
        grad_key = (
            jnp.einsum("hqk,qhd->khd", grad_logits, query_heads, preferred_element_type=jnp.float32)
            * factor
        )
        grad_value = jnp.einsum(
            "hqk,qhd->khd",
            probs.astype(jnp.bfloat16),
            grad_heads,
            preferred_element_type=jnp.float32,
        )
        term = jnp.concatenate(
            [
                grad_key.reshape(block_rows, model_width),
                grad_value.reshape(block_rows, model_width),
            ],
            axis=1,
        )
        return (accum, lax.dynamic_update_slice_in_dim(key_terms, term, index * block_rows, 0))

    grad_query, key_terms = lax.fori_loop(
        0,
        block_count,
        both_grads,
        (
            jnp.zeros((row_count, head_count, head_width), jnp.float32),
            jnp.zeros((seq_length, 2 * model_width), jnp.float32),
        ),
    )
    own_key_grads = lax.psum_scatter(key_terms, ("ctx", "shard"), scatter_dimension=0, tiled=True)
    grad_qkv = jnp.concatenate(
        [grad_query.reshape(row_count, model_width), own_key_grads], axis=1
    ).astype(jnp.bfloat16)
    grad_qkv_weights = lax.dot_general(
        hidden, grad_qkv, (((0,), (0,)), ((), ())), preferred_element_type=jnp.float32
    )
    grad_hidden = lax.dot_general(
        grad_qkv, w_qkv, (((1,), (1,)), ((), ())), preferred_element_type=jnp.float32
    )
    query_bias_grad = jnp.sum(grad_qkv[:, :model_width].astype(jnp.float32), axis=0)
    value_bias_grad = jnp.sum(grad_qkv[:, 2 * model_width :].astype(jnp.float32), axis=0)
    grad_vectors = jnp.concatenate(
        [
            jnp.stack(
                [
                    jnp.sum(grad_hidden * normed, axis=0),
                    jnp.sum(grad_hidden, axis=0),
                    query_bias_grad,
                    value_bias_grad,
                    jnp.sum(grad_mid, axis=0),
                    jnp.sum(grad_two * normed_two, axis=0),
                    jnp.sum(grad_two, axis=0),
                    jnp.sum(upstream, axis=0),
                ]
            ),
            jnp.sum(grad_pre.astype(jnp.float32), axis=0).reshape(
                ff_width // model_width, model_width
            ),
        ],
        axis=0,
    )
    token_grads = grad_mid + norm_backward(grad_hidden, vector_rows[0], normed, inverse_std)
    grad_matrix = jnp.concatenate([grad_qkv_weights, grad_proj, grad_up_w, grad_down_w], axis=1)
    shard_count = lax.axis_size("shard")
    replicas = lax.axis_size("dp") * lax.axis_size("ctx")
    part_matrix, part_vec = (
        lax.psum_scatter(
            regroup(grad_matrix, 0, replicas, shard_count), "shard", scatter_dimension=0, tiled=True
        ),
        lax.psum_scatter(
            regroup(grad_vectors, 1, replicas, shard_count),
            "shard",
            scatter_dimension=1,
            tiled=True,
        ),
    )
    part_matrix, part_vec = (
        lax.psum_scatter(part_matrix, ("dp", "ctx"), scatter_dimension=0, tiled=True),
        lax.psum_scatter(part_vec, ("dp", "ctx"), scatter_dimension=1, tiled=True),
    )
    root = (row_count * lax.axis_size("dp") * group_size) ** (-0.5)
    correction = 1.0 - BETA**STEP
    moment_w, variance_w, updated_w = adam_update(
        master_matrices, first_matrices, second_matrices, part_matrix * root, correction, DECAY_RATE
    )
    moment_v, variance_v, updated_v = adam_update(
        master_vectors, first_vectors, second_vectors, part_vec * root, correction, 0.0
    )
    copied_w, copied_v = (
        lax.all_gather(updated_w.astype(jnp.bfloat16), "shard", axis=0, tiled=True),
        lax.all_gather(updated_v.astype(jnp.bfloat16), "shard", axis=1, tiled=True),
    )
    return (
        layer_output,
        token_grads,
        moment_w,
        moment_v,
        variance_w,
        variance_v,
        updated_w,
        updated_v,
        copied_w,
        copied_v,
    )


BLOCK = 256
EXTRA = 1
f32 = jnp.float32
bf16 = jnp.bfloat16
NT = (((1,), (1,)), ((), ()))
GELU_SCALE = math.sqrt(2.0 / math.pi)
GELU_CUBE = 0.044715


def split3(value):
    high = value.astype(bf16).astype(f32)
    rest = value - high
    middle = rest.astype(bf16).astype(f32)
    low = (rest - middle).astype(bf16).astype(f32)
    return high, middle, low


def positions(index, starts_ref, count):
    result = index
    for b in range(count):
        result = result - jnp.clip(index - starts_ref[0, b], 0, PIC - 1)
    return result.astype(f32)


def limits(index, starts_ref, count):
    result = index + 1
    for b in range(count):
        start = starts_ref[0, b]
        result = jnp.where((index >= start) & (index < start + PIC), start + PIC, result)
    return result


def head_lanes(shape, h, width):
    lane = lax.broadcasted_iota(jnp.int32, shape, 1)
    inside = (lane < width) if h == 0 else (lane >= width)
    return inside, lane - width if h == 0 else lane


def pick(spare, values):
    out = jnp.zeros(spare.shape, f32)
    for e, value in enumerate(values):
        out = jnp.where(spare == e, value, out)
    return out


def smem():
    return pl.BlockSpec(memory_space=pltpu.SMEM)


def vmem():
    return pl.BlockSpec(memory_space=pltpu.VMEM)


def anywhere():
    return pl.BlockSpec(memory_space=pl.ANY)


def hbm():
    return pl.BlockSpec(memory_space=pltpu.HBM)


def params(mebibytes):
    return pltpu.CompilerParams(vmem_limit_bytes=mebibytes * 2**20)


def cost(microseconds):
    return pl.CostEstimate(
        flops=int(microseconds * 1.0e9), bytes_accessed=0, transcendentals=0
    )


def start_all(copies):
    for copy in copies:
        copy.start()
    return copies


def wait_all(copies):
    for copy in copies:
        copy.wait()


def pattern_kernel(width, count, starts_ref, slopes_ref, out_ref):
    lanes = out_ref.shape[2]
    step = pl.program_id(0)
    index = lax.broadcasted_iota(jnp.int32, (BLOCK, lanes), 0) + step * BLOCK
    pos = positions(index, starts_ref, count)
    for h in range(2):
        _, spare = head_lanes((BLOCK, lanes), h, width)
        parts = split3(pos * slopes_ref[h])
        out_ref[h] = pick(spare, parts + (1.0, 1.0, 1.0)).astype(bf16)


def key_pattern(starts, slopes, seq, lanes):
    return pl.pallas_call(
        functools.partial(pattern_kernel, lanes // 2, starts.shape[1]),
        grid=(seq // BLOCK,),
        out_shape=jax.ShapeDtypeStruct((2, seq, lanes), bf16),
        in_specs=[smem()] * 2,
        out_specs=pl.BlockSpec((2, BLOCK, lanes), lambda i: (0, i, 0)),
        compiler_params=params(40),
        cost_estimate=cost(3),
        name="key_pattern",
    )(starts, slopes)


def forward_kernel(width, tile, count, rank_ref, starts_ref, slopes_ref, *refs):
    blocks = refs[:8]
    matrices_ref, vectors_ref, pattern_in = refs[8:11]
    att_out, wide_out, q_out, k_out, v_out, all_out = refs[11 + EXTRA : 17 + EXTRA]
    hid, wts, vecs, pattern, qa, ka, va, att, wide = refs[17 + EXTRA : 26 + EXTRA]
    in_sems, w_sems, hid_sems, out_sems = refs[26 + EXTRA :]
    seq, lanes = wide.shape
    model = hid.shape[1]
    rank = rank_ref[0]
    factor = width**-0.5
    w_copies = []
    for part in range(3):
        columns = pl.ds(pl.multiple_of(part * model + rank * lanes, lanes), lanes)
        w_copies.append(
            pltpu.make_async_copy(
                matrices_ref.at[:, columns],
                wts.at[:, part * lanes : (part + 1) * lanes],
                w_sems.at[part],
            )
        )
    w_copies.append(pltpu.make_async_copy(vectors_ref, vecs, w_sems.at[3]))
    start_all(w_copies)
    in_copies = start_all(
        [
            pltpu.make_async_copy(
                blocks[k], hid.at[k * BLOCK : (k + 1) * BLOCK], in_sems.at[k]
            )
            for k in range(8)
        ]
    )
    pattern_copy = pltpu.make_async_copy(pattern_in, pattern, w_sems.at[4])
    pattern_copy.start()
    wait_all(w_copies)
    gains = vecs[...].astype(f32)
    bias = vecs[:, pl.ds(pl.multiple_of(rank * lanes, lanes), lanes)].astype(f32)
    out_copies = []
    ones = []
    for h in range(2):
        inside, spare = head_lanes((BLOCK, lanes), h, width)
        ones.append((inside, jnp.where(spare < 3, 1.0, 0.0)))
    for pair in range(4):
        first = 2 * pair
        for k in (first, first + 1):
            in_copies[k].wait()
        both = slice(first * BLOCK, (first + 2) * BLOCK)
        normed, _ = normalize(hid[both, :].astype(f32))
        hid[both, :] = (normed * gains[0:1] + gains[1:2]).astype(bf16)
        for k in (first, first + 1):
            rows = slice(k * BLOCK, (k + 1) * BLOCK)
            dst = pl.ds(pl.multiple_of((k ^ rank) * BLOCK, BLOCK), BLOCK)
            copy = pltpu.make_async_copy(hid.at[rows], all_out.at[dst], hid_sems.at[k])
            copy.start()
            out_copies.append(copy)
        value = jnp.dot(hid[both, :], wts[...], preferred_element_type=f32)
        if pair == 0:
            pattern_copy.wait()
        for k in (first, first + 1):
            local = slice((k - first) * BLOCK, (k - first + 1) * BLOCK)
            dst = pl.ds(pl.multiple_of((k ^ rank) * BLOCK, BLOCK), BLOCK)
            q = (value[local, 0:lanes] + bias[2:3]).astype(bf16).astype(f32) * factor
            key = value[local, lanes : 2 * lanes]
            v = value[local, 2 * lanes : 3 * lanes] + bias[3:4]
            for h in range(2):
                inside, spare_ones = ones[h]
                qa[h, dst, :] = jnp.where(inside, q, spare_ones).astype(bf16)
                ka[h, dst, :] = jnp.where(inside, key, pattern[h, dst, :].astype(f32)).astype(bf16)
                va[h, dst, :] = jnp.where(inside, v, spare_ones).astype(bf16)
    out_copies += start_all(
        [
            pltpu.make_async_copy(ka, k_out, out_sems.at[0]),
            pltpu.make_async_copy(va, v_out, out_sems.at[1]),
        ]
    )

    def scores(h, queries, keys):
        return lax.dot_general(
            qa[h, queries, :], ka[h, keys, :], NT, preferred_element_type=f32
        )

    def mask(first_row, first_column, shape):
        rows = lax.broadcasted_iota(jnp.int32, (shape[0], 1), 0) + first_row
        columns = lax.broadcasted_iota(jnp.int32, shape, 1) + first_column
        return columns < limits(rows, starts_ref, count)

    def lane_best(value):
        best = value[:, :lanes]
        for c in range(1, value.shape[1] // lanes):
            best = jnp.maximum(best, value[:, c * lanes : (c + 1) * lanes])
        return best

    def with_shift(h, rows, shift):
        inside, spare = head_lanes((tile, lanes), h, width)
        parts = split3(-jnp.broadcast_to(shift, (tile, lanes)))
        value = qa[h, rows, :].astype(f32)
        for e in range(3):
            value = jnp.where(spare == 3 + e, parts[e], value)
        qa[h, rows, :] = value.astype(bf16)

    for i in range(seq // tile):
        base = i * tile
        end = base + tile
        rows = slice(base, end)
        tail = slice(end - PIC, end)
        over = slice(end, end + PIC)
        seen = mask(base, base, (tile, tile))
        if end < seq:
            seen_over = mask(end - PIC, end, (PIC, PIC))
        best = []
        kept = []
        for h in range(2):
            diagonal = jnp.where(seen, scores(h, rows, rows), NEGATIVE)
            top = lane_best(diagonal)
            below = []
            for j in range(i):
                below.append(scores(h, rows, slice(j * tile, (j + 1) * tile)))
                top = jnp.maximum(top, lane_best(below[-1]))
            beyond = None
            if end < seq:
                beyond = jnp.where(seen_over, scores(h, tail, over), NEGATIVE)
                low = jnp.maximum(top[tile - PIC :], lane_best(beyond))
                top = jnp.concatenate([top[: tile - PIC], low], axis=0)
            best.append(jnp.max(top, axis=1, keepdims=True))
            kept.append((below, diagonal, beyond))
        sums = []
        for h in range(2):
            below, diagonal, beyond = kept[h]
            weights = [jnp.exp(value - best[h]).astype(bf16) for value in below]
            weights.append(jnp.exp(diagonal - best[h]).astype(bf16))
            acc = jnp.dot(
                jnp.concatenate(weights, axis=1), va[h, :end, :], preferred_element_type=f32
            )
            if end < seq:
                beyond = jnp.exp(beyond - best[h][tile - PIC :])
                low = acc[tile - PIC :] + jnp.dot(
                    beyond.astype(bf16), va[h, over, :], preferred_element_type=f32
                )
                acc = jnp.concatenate([acc[: tile - PIC], low], axis=0)
            sums.append(acc)
        outs = []
        for h in range(2):
            acc = sums[h]
            column = width if h == 0 else 0
            total = acc[:, column : column + 1]
            outs.append(acc / total)
            with_shift(h, rows, best[h] + jnp.log(total))
        inside, _ = head_lanes((tile, lanes), 0, width)
        out = jnp.where(inside, outs[0], outs[1])
        wide[rows, :] = out
        count_here = tile // BLOCK
        groups = slice(i * count_here, (i + 1) * count_here)
        att[groups] = out.astype(bf16).reshape(count_here, BLOCK, lanes)
        out_copies += start_all(
            [
                pltpu.make_async_copy(att.at[groups], att_out.at[groups], out_sems.at[2 + 3 * i]),
                pltpu.make_async_copy(wide.at[rows], wide_out.at[rows], out_sems.at[3 + 3 * i]),
                pltpu.make_async_copy(
                    qa.at[:, rows], q_out.at[:, rows], out_sems.at[4 + 3 * i]
                ),
            ]
        )
    wait_all(out_copies)


def attention_forward(blocks, matrices, vectors, pattern, rank, starts, slopes, extra, tile=512):
    rows, model = blocks[0].shape
    seq = 8 * rows
    lanes = model // 8
    heads = jax.ShapeDtypeStruct((2, seq, lanes), bf16)
    return pl.pallas_call(
        functools.partial(forward_kernel, lanes // 2, tile, starts.shape[1]),
        out_shape=(
            jax.ShapeDtypeStruct((8, rows, lanes), bf16),
            jax.ShapeDtypeStruct((seq, lanes), f32),
            heads,
            heads,
            heads,
            jax.ShapeDtypeStruct((seq, model), bf16),
        ),
        in_specs=[smem()] * 3 + [hbm()] * 11 + [anywhere()] * EXTRA,
        out_specs=(hbm(),) * 6,
        scratch_shapes=[
            pltpu.VMEM((seq, model), bf16),
            pltpu.VMEM((model, 3 * lanes), bf16),
            pltpu.VMEM(vectors.shape, bf16),
            pltpu.VMEM((2, seq, lanes), bf16),
            pltpu.VMEM((2, seq, lanes), bf16),
            pltpu.VMEM((2, seq, lanes), bf16),
            pltpu.VMEM((2, seq, lanes), bf16),
            pltpu.VMEM((8, rows, lanes), bf16),
            pltpu.VMEM((seq, lanes), f32),
            pltpu.SemaphoreType.DMA((8,)),
            pltpu.SemaphoreType.DMA((5,)),
            pltpu.SemaphoreType.DMA((8,)),
            pltpu.SemaphoreType.DMA((2 + 3 * (seq // tile),)),
        ],
        compiler_params=params(56),
        cost_estimate=cost(20),
        name="attention_forward",
    )(rank, starts, slopes, *blocks, matrices, vectors, pattern, extra)


def backward_kernel(waits, width, tile, count, starts_ref, *refs):
    q_in, k_in, v_in, kt_in, wide_in, got_in = refs[:6]
    abs_out, rel_out, bias_out, mid_out = refs[6 + waits : 10 + waits]
    qa, ka, va, kt, wide, grads, mid, da, dq_ref, dk_ref, dv_ref = refs[10 + waits : 21 + waits]
    both_ref, flip_ref, mid_flip, bias_ref, in_sems, out_sems = refs[21 + waits :]
    seq, lanes = wide.shape
    factor = width**-0.5
    first = start_all(
        [
            pltpu.make_async_copy(wide_in, wide, in_sems.at[0]),
            pltpu.make_async_copy(got_in.at[:, :, 0:lanes], grads, in_sems.at[1]),
        ]
    )
    rest = start_all(
        [
            pltpu.make_async_copy(q_in, qa, in_sems.at[2]),
            pltpu.make_async_copy(k_in, ka, in_sems.at[3]),
            pltpu.make_async_copy(v_in, va, in_sems.at[4]),
            pltpu.make_async_copy(kt_in, kt, in_sems.at[5]),
            pltpu.make_async_copy(got_in.at[:, :, lanes : 2 * lanes], mid, in_sems.at[6]),
        ]
    )
    wait_all(first)

    def prologue(t, carry):
        rows = pl.ds(pl.multiple_of(t * BLOCK, BLOCK), BLOCK)
        g = grads[t].astype(f32)
        product = g * wide[rows, :]
        for h in range(2):
            inside, spare = head_lanes((BLOCK, lanes), h, width)
            delta = jnp.sum(jnp.where(inside, product, 0.0), axis=1, keepdims=True)
            parts = split3(-jnp.broadcast_to(delta, (BLOCK, lanes)))
            da[h, rows, :] = jnp.where(inside, g, pick(spare, parts)).astype(bf16)
        return carry

    lax.fori_loop(0, seq // BLOCK, prologue, 0)
    dq_ref[...] = jnp.zeros(dq_ref.shape, f32)
    wait_all(rest)

    def pair(h, keys, queries, mask, local):
        logits = lax.dot_general(ka[h, keys, :], qa[h, queries, :], NT, preferred_element_type=f32)
        probs = jnp.exp(logits)
        if mask is not None:
            probs = jnp.where(mask(logits.shape), probs, 0.0)
        inner = lax.dot_general(va[h, keys, :], da[h, queries, :], NT, preferred_element_type=f32)
        grad = (probs * inner).astype(bf16)
        dv_ref[h, local, :] += jnp.dot(
            probs.astype(bf16), da[h, queries, :], preferred_element_type=f32
        )
        dk_ref[h, local, :] += jnp.dot(grad, qa[h, queries, :], preferred_element_type=f32)
        rows = slice(h * width, (h + 1) * width)
        dq_ref[rows, queries] += jnp.dot(kt[rows, keys], grad, preferred_element_type=f32)

    bias_ref[...] = jnp.zeros(bias_ref.shape, f32)
    out_copies = []

    def send(t, part, value, flipped):
        columns = slice(part * lanes, (part + 1) * lanes)
        rows = slice(t * BLOCK, (t + 1) * BLOCK)
        both_ref[rows, columns] = value.astype(bf16)
        flip_ref[columns, rows] = flipped.astype(bf16)
        bias_ref[:, columns] += jnp.sum(value.astype(bf16).astype(f32), axis=0, keepdims=True)

    for j in range(seq // tile):
        base = j * tile
        dk_ref[...] = jnp.zeros(dk_ref.shape, f32)
        dv_ref[...] = jnp.zeros(dv_ref.shape, f32)

        def mask(first_key, first_query, shape):
            queries = lax.broadcasted_iota(jnp.int32, (1, shape[1]), 1) + first_query
            keys = lax.broadcasted_iota(jnp.int32, shape, 0) + first_key
            return keys < limits(queries, starts_ref, count)

        if base > 0:
            for h in range(2):
                pair(
                    h,
                    slice(base, base + PIC),
                    slice(base - PIC, base),
                    functools.partial(mask, base, base - PIC),
                    slice(0, PIC),
                )
        for h in range(2):
            pair(
                h,
                slice(base, base + tile),
                slice(base, base + tile),
                functools.partial(mask, base, base),
                slice(0, tile),
            )

        def full(i, base=base):
            queries = slice(i * tile, (i + 1) * tile)
            for h in range(2):
                pair(h, slice(base, base + tile), queries, None, slice(0, tile))

        if base + tile < seq:
            for i in range(j + 1, seq // tile):
                full(i)
        inside, _ = head_lanes((BLOCK, lanes), 0, width)
        for t in range(tile // BLOCK):
            part = slice(t * BLOCK, (t + 1) * BLOCK)
            block = j * (tile // BLOCK) + t
            dk = jnp.where(inside, dk_ref[0, part, :], dk_ref[1, part, :])
            dv = jnp.where(inside, dv_ref[0, part, :], dv_ref[1, part, :])
            send(block, 1, dk, dk.T)
            send(block, 2, dv, dv.T)
    for t in range(seq // BLOCK):
        rows = slice(t * BLOCK, (t + 1) * BLOCK)
        dq = dq_ref[:, rows] * factor
        send(t, 0, dq.T, dq)
        mid_flip[:, rows] = mid[t].astype(f32).T.astype(bf16)
        out_copies += start_all(
            [
                pltpu.make_async_copy(both_ref.at[rows], abs_out.at[rows], out_sems.at[2 * t]),
                pltpu.make_async_copy(
                    flip_ref.at[:, rows], rel_out.at[:, rows], out_sems.at[2 * t + 1]
                ),
            ]
        )
    out_copies += start_all(
        [
            pltpu.make_async_copy(bias_ref, bias_out, out_sems.at[2 * (seq // BLOCK)]),
            pltpu.make_async_copy(mid_flip, mid_out, out_sems.at[2 * (seq // BLOCK) + 1]),
        ]
    )
    wait_all(out_copies)


def attention_backward(saved, wide, got, starts, extras, tile=512):
    seq, lanes = wide.shape
    blocks = seq // BLOCK
    return pl.pallas_call(
        functools.partial(backward_kernel, len(extras), lanes // 2, tile, starts.shape[1]),
        out_shape=(
            jax.ShapeDtypeStruct((seq, 3 * lanes), bf16),
            jax.ShapeDtypeStruct((3 * lanes, seq), bf16),
            jax.ShapeDtypeStruct((1, 3 * lanes), f32),
            jax.ShapeDtypeStruct((lanes, seq), bf16),
        ),
        in_specs=[smem()] + [hbm()] * 6 + [anywhere()] * len(extras),
        out_specs=(hbm(),) * 4,
        scratch_shapes=[
            pltpu.VMEM((2, seq, lanes), bf16),
            pltpu.VMEM((2, seq, lanes), bf16),
            pltpu.VMEM((2, seq, lanes), bf16),
            pltpu.VMEM((lanes, seq), bf16),
            pltpu.VMEM((seq, lanes), f32),
            pltpu.VMEM((blocks, BLOCK, lanes), bf16),
            pltpu.VMEM((blocks, BLOCK, lanes), bf16),
            pltpu.VMEM((2, seq, lanes), bf16),
            pltpu.VMEM((lanes, seq), f32),
            pltpu.VMEM((2, tile, lanes), f32),
            pltpu.VMEM((2, tile, lanes), f32),
            pltpu.VMEM((seq, 3 * lanes), bf16),
            pltpu.VMEM((3 * lanes, seq), bf16),
            pltpu.VMEM((lanes, seq), bf16),
            pltpu.VMEM((1, 3 * lanes), f32),
            pltpu.SemaphoreType.DMA((7,)),
            pltpu.SemaphoreType.DMA((2 * blocks + 2,)),
        ],
        compiler_params=params(56),
        cost_estimate=cost(21),
        name="attention_backward",
    )(starts, *saved, wide, got, *extras)


def normalize(value):
    centered = value - jnp.mean(value, axis=1, keepdims=True)
    inverse = lax.rsqrt(jnp.mean(centered * centered, axis=1, keepdims=True) + EPSILON)
    return centered * inverse, inverse


def whole(shape):
    return pl.BlockSpec(shape, lambda *_: (0,) * len(shape))


def gate(arrays, waits):
    count = len(arrays)
    return pl.pallas_call(
        lambda *refs: None,
        out_shape=tuple(jax.ShapeDtypeStruct(array.shape, array.dtype) for array in arrays),
        in_specs=[anywhere()] * (count + len(waits)),
        out_specs=(anywhere(),) * count,
        input_output_aliases={k: k for k in range(count)},
        cost_estimate=cost(1),
        name="gate",
    )(*arrays, *waits)


def project_kernel(
    heads_ref, tokens_ref, weights_ref, vectors_ref, extra_ref, middle_ref, hidden_ref, attended_ref
):
    lanes = heads_ref.shape[2]
    for g in range(heads_ref.shape[0]):
        attended_ref[:, g * lanes : (g + 1) * lanes] = heads_ref[g]
    vecs = vectors_ref[...].astype(f32)
    middle = (
        tokens_ref[...].astype(f32)
        + jnp.dot(attended_ref[...], weights_ref[...], preferred_element_type=f32)
        + vecs[4:5]
    )
    middle_ref[...] = middle
    normed, _ = normalize(middle)
    hidden_ref[...] = (normed * vecs[5:6] + vecs[6:7]).astype(bf16)


def project_norm(heads, tokens, matrices, vectors, extra):
    rows, model = tokens.shape
    return pl.pallas_call(
        project_kernel,
        grid=(1,),
        out_shape=(
            jax.ShapeDtypeStruct((rows, model), f32),
            jax.ShapeDtypeStruct((rows, model), bf16),
        ),
        in_specs=[
            whole(heads.shape),
            whole(tokens.shape),
            pl.BlockSpec((model, model), lambda i: (0, 3)),
            whole(vectors.shape),
            anywhere(),
        ],
        out_specs=(whole((rows, model)),) * 2,
        scratch_shapes=[pltpu.VMEM((rows, model), bf16)],
        compiler_params=params(40),
        cost_estimate=cost(3),
        name="project_norm",
    )(heads, tokens, matrices, vectors, extra)


def gelu_parts(pre):
    square = pre * pre
    half = 0.5 * (1.0 + jnp.tanh(GELU_SCALE * (pre + GELU_CUBE * square * pre)))
    act = pre * half
    slope = half + 2.0 * act * (1.0 - half) * (GELU_SCALE * (1.0 + 3.0 * GELU_CUBE * square))
    return act, slope


def norm_pull(grad, gain, normed, inverse):
    scaled = grad * gain
    return inverse * (
        scaled
        - jnp.mean(scaled, axis=1, keepdims=True)
        - normed * jnp.mean(scaled * normed, axis=1, keepdims=True)
    )


def feed_kernel(chunk, *refs):
    hidden_in, middle_in, cotangent_in, vectors_in, bias_in, matrices_in = refs[:6]
    layer_out, grad_mid_out, heads_out, sums_out = refs[6:10]
    hidden, middle, cotangent, vecs_ref, bias, up, down, proj = refs[10:18]
    layer, grad_mid_ref, heads, sums, down_acc, two_acc, in_sems, w_sems, out_sems = refs[18:]
    model = hidden.shape[1]
    count = up.shape[0]
    first = start_all(
        [
            pltpu.make_async_copy(source, target, in_sems.at[k])
            for k, (source, target) in enumerate(
                ((hidden_in, hidden), (cotangent_in, cotangent), (bias_in, bias))
            )
        ]
    )
    weights = []
    for i in range(count):
        for part, ref in ((0, up), (1, down)):
            start = 4 * model + part * count * chunk + i * chunk
            weights.append(
                pltpu.make_async_copy(
                    matrices_in.at[:, start : start + chunk], ref.at[i], w_sems.at[2 * i + part]
                )
            )
    start_all(weights)
    rest = start_all(
        [
            pltpu.make_async_copy(middle_in, middle, in_sems.at[3]),
            pltpu.make_async_copy(vectors_in, vecs_ref, in_sems.at[4]),
            pltpu.make_async_copy(
                matrices_in.at[:, 3 * model : 4 * model], proj, in_sems.at[5]
            ),
        ]
    )
    wait_all(first)
    for i in range(count):
        weights[2 * i].wait()
        pre = jnp.dot(hidden[...], up[i], preferred_element_type=f32)
        pre = pre + bias[:, i * chunk : (i + 1) * chunk]
        weights[2 * i + 1].wait()
        grad_act = jnp.dot(cotangent[...], down[i], preferred_element_type=f32)
        act, slope = gelu_parts(pre)
        grad_pre = (grad_act * slope).astype(bf16)
        down_part = lax.dot_general(act.astype(bf16), down[i], NT, preferred_element_type=f32)
        two_part = lax.dot_general(grad_pre, up[i], NT, preferred_element_type=f32)
        if i == 0:
            down_acc[...] = down_part
            two_acc[...] = two_part
        else:
            down_acc[...] += down_part
            two_acc[...] += two_part
    wait_all(rest)
    vecs = vecs_ref[...].astype(f32)
    grad_two = two_acc[...]
    mid = middle[...]
    normed, inverse = normalize(mid)
    upstream = cotangent[...].astype(f32)
    grad_mid = upstream + norm_pull(grad_two, vecs[5:6], normed, inverse)
    low = grad_mid.astype(bf16)
    grads = lax.dot_general(low, proj[...], NT, preferred_element_type=f32).astype(bf16)
    groups, _, double = heads.shape
    lanes = double // 2
    for g in range(groups):
        heads[g, :, 0:lanes] = grads[:, g * lanes : (g + 1) * lanes]
        heads[g, :, lanes:double] = low[:, g * lanes : (g + 1) * lanes]
    out_copies = [pltpu.make_async_copy(heads, heads_out, out_sems.at[0])]
    out_copies[0].start()
    grad_mid_ref[...] = grad_mid
    layer[...] = (mid + down_acc[...] + vecs[7:8]).astype(bf16)
    rows = [grad_mid, grad_two * normed, grad_two, upstream]
    for k, value in enumerate(rows):
        sums[k : k + 1, :] = jnp.sum(value, axis=0, keepdims=True)
    out_copies += start_all(
        [
            pltpu.make_async_copy(layer, layer_out, out_sems.at[1]),
            pltpu.make_async_copy(grad_mid_ref, grad_mid_out, out_sems.at[2]),
            pltpu.make_async_copy(sums, sums_out, out_sems.at[3]),
        ]
    )
    wait_all(out_copies)


def feed_forward(hidden, up_bias, middle, cotangent, vectors, matrices, chunk=2048):
    rows, model = hidden.shape
    ff_width = up_bias.shape[1]
    count = ff_width // chunk
    outs = (
        jax.ShapeDtypeStruct((rows, model), bf16),
        jax.ShapeDtypeStruct((rows, model), f32),
        jax.ShapeDtypeStruct((8, rows, model // 4), bf16),
        jax.ShapeDtypeStruct((4, model), f32),
    )
    return pl.pallas_call(
        functools.partial(feed_kernel, chunk),
        out_shape=outs,
        in_specs=[hbm()] * 6,
        out_specs=(hbm(),) * 4,
        scratch_shapes=[
            pltpu.VMEM((rows, model), bf16),
            pltpu.VMEM((rows, model), f32),
            pltpu.VMEM((rows, model), bf16),
            pltpu.VMEM(vectors.shape, bf16),
            pltpu.VMEM((1, ff_width), f32),
            pltpu.VMEM((count, model, chunk), bf16),
            pltpu.VMEM((count, model, chunk), bf16),
            pltpu.VMEM((model, model), bf16),
        ]
        + [pltpu.VMEM(out.shape, out.dtype) for out in outs]
        + [
            pltpu.VMEM((rows, model), f32),
            pltpu.VMEM((rows, model), f32),
            pltpu.SemaphoreType.DMA((6,)),
            pltpu.SemaphoreType.DMA((2 * count,)),
            pltpu.SemaphoreType.DMA((4,)),
        ],
        compiler_params=params(40),
        cost_estimate=cost(14),
        name="feed_forward",
    )(hidden, middle, cotangent, vectors, up_bias, matrices)


def units_kernel(waits, rank_ref, *refs):
    blocks, heads = refs[:8], refs[8:16]
    cotangent_in, bias_in, matrices_in, vectors_in = refs[16:20]
    early_out, sums_out, attended_out = refs[20 + waits : 23 + waits]
    tokens, attended, hidden, cotangent, proj, vecs_ref = refs[23 + waits : 29 + waits]
    bias, up, down, act_ref, grad_ref, low, sums, grad_act = refs[29 + waits : 37 + waits]
    w_sems, c_sems, in_sems, head_sems, out_sems = refs[37 + waits :]
    seq, model = hidden.shape
    units = up.shape[1]
    lanes = model // 8
    rank = rank_ref[0]
    first = pl.multiple_of(rank * units, units)
    weights = []
    for part, ref in ((1, down), (0, up)):
        source = pl.ds(pl.multiple_of((4 + 4 * part) * model + first, units), units)
        weights.append(
            pltpu.make_async_copy(matrices_in.at[:, source], ref, w_sems.at[3 + part])
        )
    weights[0].start()
    pieces = [slice(n * 2 * BLOCK, (n + 1) * 2 * BLOCK) for n in range(4)]
    early_copies = start_all(
        [
            pltpu.make_async_copy(cotangent_in.at[piece], cotangent.at[piece], c_sems.at[n])
            for n, piece in enumerate(pieces)
        ]
    )
    copies = [
        pltpu.make_async_copy(bias_in.at[:, pl.ds(first, units)], bias, w_sems.at[0]),
        pltpu.make_async_copy(vectors_in, vecs_ref, w_sems.at[1]),
        pltpu.make_async_copy(matrices_in.at[:, 3 * model : 4 * model], proj, w_sems.at[2]),
    ]
    start_all(copies)
    loads = []
    for k in range(8):
        columns = pl.ds(pl.multiple_of((rank ^ k) * lanes, lanes), lanes)
        loads.append(
            pltpu.make_async_copy(heads[k], attended.at[:, :, columns], head_sems.at[k])
        )
    for k in range(8):
        rows = pl.ds(pl.multiple_of((rank ^ k) * BLOCK, BLOCK), BLOCK)
        loads.append(pltpu.make_async_copy(blocks[k], tokens.at[rows], in_sems.at[k]))
    start_all(loads)
    weights[1].start()
    weights[0].wait()
    for piece, copy in zip(pieces, early_copies):
        copy.wait()
        grad_act[piece, :] = jnp.dot(cotangent[piece, :], down[...], preferred_element_type=f32)
    wait_all(copies + loads)
    out_copies = [pltpu.make_async_copy(attended, attended_out, w_sems.at[6])]
    out_copies[0].start()
    vecs = vecs_ref[...].astype(f32)
    sums[...] = jnp.zeros(sums.shape, f32)
    for part in range(4):
        rows = slice(part * 2 * BLOCK, (part + 1) * 2 * BLOCK)
        heads_here = attended[2 * part : 2 * part + 2].reshape(2 * BLOCK, model)
        middle = (
            tokens[rows, :].astype(f32)
            + jnp.dot(heads_here, proj[...], preferred_element_type=f32)
            + vecs[4:5]
        )
        normed, _ = normalize(middle)
        hidden[rows, :] = (normed * vecs[5:6] + vecs[6:7]).astype(bf16)
        if part == 0:
            weights[1].wait()
        pre = jnp.dot(hidden[rows, :], up[...], preferred_element_type=f32) + bias[...]
        act, slope = gelu_parts(pre)
        grad_pre = grad_act[rows, :] * slope
        act_ref[:, rows] = act.T.astype(bf16)
        grad_ref[:, rows] = grad_pre.T.astype(bf16)
        sums[...] += jnp.sum(grad_pre.astype(bf16).astype(f32), axis=0, keepdims=True)
    quarter = model // 4
    copy = pltpu.make_async_copy(sums, sums_out, w_sems.at[0])
    copy.start()
    out_copies.append(copy)
    for block in range(4):
        columns = slice(block * quarter, (block + 1) * quarter)
        for n, (left, right) in enumerate(((grad_ref, hidden), (act_ref, cotangent))):
            value = jnp.dot(left[...], right[:, columns], preferred_element_type=f32)
            low[block, :, n * units : (n + 1) * units] = value.T.astype(bf16)
        copy = pltpu.make_async_copy(low.at[block], early_out.at[block], out_sems.at[block])
        copy.start()
        out_copies.append(copy)
    wait_all(out_copies)


def own_units(rank, blocks, heads, cotangent, up_bias, matrices, vectors, extras):
    rows, model = blocks[0].shape
    seq = 8 * rows
    units = up_bias.shape[1] // 8
    attended = (8, rows, model)
    return pl.pallas_call(
        functools.partial(units_kernel, len(extras)),
        out_shape=(
            jax.ShapeDtypeStruct((4, model // 4, 2 * units), bf16),
            jax.ShapeDtypeStruct((1, units), f32),
            jax.ShapeDtypeStruct(attended, bf16),
        ),
        in_specs=[smem()] + [hbm()] * 20 + [anywhere()] * len(extras),
        out_specs=(hbm(),) * 3,
        scratch_shapes=[
            pltpu.VMEM((seq, model), bf16),
            pltpu.VMEM(attended, bf16),
            pltpu.VMEM((seq, model), bf16),
            pltpu.VMEM((seq, model), bf16),
            pltpu.VMEM((model, model), bf16),
            pltpu.VMEM(vectors.shape, bf16),
            pltpu.VMEM((1, units), f32),
            pltpu.VMEM((model, units), bf16),
            pltpu.VMEM((model, units), bf16),
            pltpu.VMEM((units, seq), bf16),
            pltpu.VMEM((units, seq), bf16),
            pltpu.VMEM((4, model // 4, 2 * units), bf16),
            pltpu.VMEM((1, units), f32),
            pltpu.VMEM((seq, units), f32),
            pltpu.SemaphoreType.DMA((7,)),
            pltpu.SemaphoreType.DMA((4,)),
            pltpu.SemaphoreType.DMA((8,)),
            pltpu.SemaphoreType.DMA((8,)),
            pltpu.SemaphoreType.DMA((4,)),
        ],
        compiler_params=params(56),
        cost_estimate=cost(1),
        name="own_units",
    )(rank, *blocks, *heads, cotangent, up_bias, matrices, vectors, *extras)


def late_kernel(depth_ref, grads_in, hidden_in, mid_in, attended_in, *refs):
    outs = refs[:4]
    grads, hidden, mid, attended, total, low, in_sems, out_sems = refs[4:]
    columns, model = total.shape
    quarter = model // 4
    first = grads.shape[0]
    copies = start_all(
        [
            pltpu.make_async_copy(source, target, in_sems.at[n])
            for n, (source, target) in enumerate(
                (
                    (grads_in, grads),
                    (hidden_in, hidden),
                    (mid_in, mid),
                    (attended_in, attended),
                )
            )
        ]
    )
    wait_all(copies[:2])
    total[:first, :] = jnp.dot(grads[...], hidden[...], preferred_element_type=f32)
    wait_all(copies[2:])
    total[first:, :] = jnp.dot(mid[...], attended[...], preferred_element_type=f32)
    depth = depth_ref[0]
    near = depth ^ 1
    out_copies = []
    for n, (block, target) in enumerate(
        ((3 - near, outs[0]), (near, outs[1]), (3 - depth, outs[2]), (depth, outs[3]))
    ):
        lane = pl.ds(pl.multiple_of(block * quarter, quarter), quarter)
        if n < 2:
            low[n] = total[:, lane].astype(bf16)
            copy = pltpu.make_async_copy(low.at[n], target, out_sems.at[n])
        else:
            copy = pltpu.make_async_copy(total.at[:, lane], target, out_sems.at[n])
        copy.start()
        out_copies.append(copy)
    wait_all(out_copies)


def late_weights(depth, grads, hidden, mid, attended):
    seq, model = hidden.shape
    columns = grads.shape[0] + mid.shape[0]
    quarter = model // 4
    return pl.pallas_call(
        late_kernel,
        out_shape=(jax.ShapeDtypeStruct((columns, quarter), bf16),) * 2
        + (jax.ShapeDtypeStruct((columns, quarter), f32),) * 2,
        in_specs=[smem()] + [hbm()] * 4,
        out_specs=(hbm(),) * 4,
        scratch_shapes=[
            pltpu.VMEM(grads.shape, bf16),
            pltpu.VMEM(hidden.shape, bf16),
            pltpu.VMEM(mid.shape, bf16),
            pltpu.VMEM(attended.shape, bf16),
            pltpu.VMEM((columns, model), f32),
            pltpu.VMEM((2, columns, quarter), bf16),
            pltpu.SemaphoreType.DMA((4,)),
            pltpu.SemaphoreType.DMA((4,)),
        ],
        compiler_params=params(56),
        cost_estimate=cost(5),
        name="late_weights",
    )(depth, grads, hidden, mid, attended)


def flip_kernel(parts, *refs):
    total = refs[0][...].reshape(refs[0].shape[-2:]).astype(f32)
    for ref in refs[1:parts]:
        total = total + ref[...].astype(f32)
    refs[-1][...] = total.T.astype(bf16)


def flip_sum(arrays, waits, name):
    columns, rows = arrays[0].shape[-2:]
    return pl.pallas_call(
        functools.partial(flip_kernel, len(arrays)),
        grid=(1,),
        out_shape=jax.ShapeDtypeStruct((rows, columns), bf16),
        in_specs=[whole(array.shape) for array in arrays] + [anywhere()] * len(waits),
        out_specs=whole((rows, columns)),
        compiler_params=params(56),
        cost_estimate=cost(0.1),
        name=name,
    )(*arrays, *waits)


def final_kernel(
    heads_ref, weights_ref, tokens_ref, grad_mid_ref, vectors_ref, *refs
):
    out_ref, sums_ref, acc_ref, lhs = refs[-4:]
    step = pl.program_id(0)
    lanes = heads_ref.shape[2] // 3

    @pl.when(step == 0)
    def _():
        acc_ref[...] = jnp.zeros(acc_ref.shape, f32)

    source = pl.ds(pl.multiple_of(step * lanes, lanes), lanes)
    for g in range(heads_ref.shape[0]):
        lhs[:, g * lanes : (g + 1) * lanes] = heads_ref[g, :, source]
    acc_ref[...] += lax.dot_general(lhs[...], weights_ref[...], NT, preferred_element_type=f32)

    @pl.when(step == pl.num_programs(0) - 1)
    def _():
        vecs = vectors_ref[...].astype(f32)
        grad = acc_ref[...]
        normed, inverse = normalize(tokens_ref[...].astype(f32))
        out_ref[...] = grad_mid_ref[...] + norm_pull(grad, vecs[0:1], normed, inverse)
        sums_ref[0:1, :] = jnp.sum(grad * normed, axis=0, keepdims=True)
        sums_ref[1:2, :] = jnp.sum(grad, axis=0, keepdims=True)


def token_gradient(heads, matrices, tokens, grad_mid, vectors, extras):
    rows, model = tokens.shape
    return pl.pallas_call(
        final_kernel,
        grid=(3,),
        out_shape=(
            jax.ShapeDtypeStruct((rows, model), f32),
            jax.ShapeDtypeStruct((2, model), f32),
        ),
        in_specs=[
            whole(heads.shape),
            pl.BlockSpec((model, model), lambda i: (0, i)),
            whole((rows, model)),
            whole((rows, model)),
            whole(vectors.shape),
        ]
        + [anywhere()] * len(extras),
        out_specs=(whole((rows, model)), whole((2, model))),
        scratch_shapes=[pltpu.VMEM((rows, model), f32), pltpu.VMEM((rows, model), bf16)],
        compiler_params=params(56),
        cost_estimate=cost(6),
        name="token_gradient",
    )(heads, matrices, tokens, grad_mid, vectors, *extras)


def vector_pieces_kernel(rank_ref, one_ref, bias_ref, two_ref, units_ref, *refs):
    states, out_ref = refs[:3], refs[-1]
    rank = rank_ref[0]
    lanes = out_ref.shape[2]
    out_ref[...] = jnp.zeros(out_ref.shape, f32)
    copies = out_ref.shape[0] // 8
    for b in range(8):
        columns = slice(b * lanes, (b + 1) * lanes)
        for c in range(copies):
            out_ref[copies * b + c, 0:2, :] = one_ref[:, columns]
            out_ref[copies * b + c, 4:8, :] = two_ref[:, columns]
    rows, own = states[0].shape
    packed = jnp.concatenate(
        [ref[...] for ref in states] + [jnp.zeros((rows, lanes - 3 * own), f32)], axis=1
    )
    for b in range(out_ref.shape[0]):
        out_ref[b, 12 : 12 + rows, :] = packed
    for c in range(copies):
        out_ref[copies * rank + c, 2:3, :] = bias_ref[:, 0:lanes]
        out_ref[copies * rank + c, 3:4, :] = bias_ref[:, 2 * lanes : 3 * lanes]
    pieces = units_ref.shape[1] // lanes
    for n in range(pieces):
        place = rank * pieces + n
        for c in range(copies):
            out_ref[copies * (place % 8) + c, pl.ds(8 + place // 8, 1), :] = units_ref[
                :, n * lanes : (n + 1) * lanes
            ]


def vector_pieces(rank, one, bias, two, units, states, devices, waits):
    lanes = one.shape[1] // 8
    return pl.pallas_call(
        vector_pieces_kernel,
        grid=(1,),
        out_shape=jax.ShapeDtypeStruct((devices, 24, lanes), f32),
        in_specs=[smem(), whole(one.shape), whole(bias.shape), whole(two.shape), whole(units.shape)]
        + [whole(state.shape) for state in states]
        + [anywhere()] * len(waits),
        out_specs=whole((devices, 24, lanes)),
        compiler_params=params(40),
        cost_estimate=cost(0.01),
        name="vector_pieces",
    )(rank, one, bias, two, units, *states, *waits)


def adam(master, first, second, gradient, decay_rate):
    correction = 1.0 - BETA**STEP
    moment = BETA * first + (1.0 - BETA) * gradient
    variance = BETA * second + (1.0 - BETA) * gradient * gradient
    direction = moment / correction / (jnp.sqrt(variance / correction) + ADAM_EPSILON)
    return moment, variance, master - RATE * (direction + decay_rate * master)


def vector_update_kernel(root, place_ref, got_ref, *refs):
    outs, copied_ref = refs[-4:-1], refs[-1]
    lanes = got_ref.shape[2]
    rows, own = outs[0].shape
    gradient = jnp.sum(got_ref[:, :16, :], axis=0) * root
    shard = place_ref[0] % 4
    first = place_ref[0] - shard
    columns = lax.broadcasted_iota(jnp.int32, (16, lanes), 1) // own
    total = jnp.zeros((16, lanes), f32)
    for k in range(4):
        other = shard ^ k
        shifted = pltpu.roll(gradient, lax.rem(lanes - other * own, lanes), 1)[:rows, :own]
        packed = got_ref[first + other, 12 : 12 + rows, :]
        states = [packed[:, n * own : (n + 1) * own] for n in range(3)]
        values = adam(*states, shifted, 0.0)
        if k == 0:
            for ref, value in zip(outs, values):
                ref[...] = value
        wide = jnp.concatenate([values[2], jnp.zeros((rows, lanes - own), f32)], axis=1)
        wide = jnp.concatenate([wide, jnp.zeros((16 - rows, lanes), f32)], axis=0)
        total = jnp.where(columns == other, pltpu.roll(wide, other * own, 1), total)
    copied_ref[...] = total[:rows].astype(bf16)


def vector_update(place, got, rows, own, root, extras):
    lanes = got.shape[2]
    mine = jax.ShapeDtypeStruct((rows, own), f32)
    return pl.pallas_call(
        functools.partial(vector_update_kernel, root),
        grid=(1,),
        out_shape=(mine, mine, mine, jax.ShapeDtypeStruct((rows, lanes), bf16)),
        in_specs=[smem(), whole(got.shape)] + [anywhere()] * len(extras),
        out_specs=(whole((rows, own)),) * 3 + (whole((rows, lanes)),),
        compiler_params=params(40),
        cost_estimate=cost(0.01),
        name="vector_update",
    )(place, got, *extras)


def update_kernel(root, got_ref, *refs):
    states, outs = refs[:3], refs[-5:-2]
    copied_ref, gradient_ref = refs[-2:]
    lanes = got_ref.shape[2]
    for g in range(got_ref.shape[0]):
        gradient_ref[:, g * lanes : (g + 1) * lanes] = got_ref[g].astype(f32)
    values = adam(*[ref[...] for ref in states], gradient_ref[...] * root, DECAY_RATE)
    for ref, value in zip(outs, values):
        ref[...] = value
    copied_ref[...] = values[2].astype(bf16)


def matrix_update(got, states, previous, extras, first, parts, root, name):
    groups, rows, packed = got.shape
    lanes = packed // parts
    block = groups * lanes
    total = states[0].shape[1]
    start = first // block
    state = pl.BlockSpec((rows, block), lambda i: (0, start + i))
    return pl.pallas_call(
        functools.partial(update_kernel, root),
        grid=(parts,),
        out_shape=(jax.ShapeDtypeStruct((rows, total), f32),) * 3
        + (jax.ShapeDtypeStruct((rows, parts * block), bf16),),
        in_specs=[pl.BlockSpec((groups, rows, lanes), lambda i: (0, 0, i))]
        + [state] * 3
        + [anywhere()] * (len(previous) + len(extras)),
        out_specs=(state,) * 3 + (pl.BlockSpec((rows, block), lambda i: (0, i)),),
        scratch_shapes=[pltpu.VMEM((rows, block), f32)],
        input_output_aliases={4 + k: k for k in range(len(previous))},
        compiler_params=params(56),
        cost_estimate=cost(4),
        name=name,
    )(got, *states, *previous, *extras)


def place_kernel(late_blocks, shard_ref, *refs):
    out_ref = refs[-1]
    rows = refs[0].shape[0]
    for first, chosen in ((0, pl.program_id(0) < late_blocks), (4, pl.program_id(0) >= late_blocks)):

        @pl.when(chosen)
        def _(first=first):
            for k in range(4):
                place = pl.multiple_of((shard_ref[0] ^ k) * rows, rows)
                out_ref[pl.ds(place, rows), :] = refs[first + k][...]


def place_copies(shard, late, early):
    rows = late[0].shape[0]
    block = 2048
    count = late[0].shape[1] // block
    total = count * block + early[0].shape[1]
    return pl.pallas_call(
        functools.partial(place_kernel, count),
        grid=(total // block,),
        out_shape=jax.ShapeDtypeStruct((4 * rows, total), bf16),
        in_specs=[smem()]
        + [pl.BlockSpec((rows, block), lambda i: (0, jnp.minimum(i, count - 1)))] * 4
        + [pl.BlockSpec((rows, block), lambda i: (0, jnp.maximum(i - count, 0)))] * 4,
        out_specs=pl.BlockSpec((4 * rows, block), lambda i: (0, i)),
        compiler_params=params(40),
        cost_estimate=cost(0.01),
        name="place_copies",
    )(shard, *late, *early)


def fits_sequence_plan(mesh):
    return mesh.shape["dp"] == 4 and mesh.shape["ctx"] == 2 and mesh.shape["shard"] == 4


EVERY = ("dp", "ctx", "shard")
SEQUENCE = ("ctx", "shard")


def swap(array, axis, bit):
    count = lax.axis_size(axis)
    return lax.ppermute(array, axis, [(i, i ^ bit) for i in range(count)])


def gather_blocks(block, ready=True):
    over_ctx = swap(block, "ctx", 1)
    over_y = swap(block, "shard", 2)
    over_core = swap(block, "shard", 1)
    even = (lax.axis_index("shard") % 2 == 0) & ready
    relay = jnp.where(even, over_ctx, over_y)
    opposite = lax.ppermute(relay, SEQUENCE, [(i, i ^ (4 if i % 2 else 2)) for i in range(8)])
    ctx_core = swap(over_ctx, "shard", 1)
    y_core = swap(over_y, "shard", 1)
    opposite_core = swap(opposite, "shard", 1)
    return relay, [
        block, over_core, over_y, y_core, over_ctx, ctx_core, opposite, opposite_core
    ]


def gather_direct(block):
    straight = [
        block,
        swap(block, "shard", 2),
        swap(block, "ctx", 1),
        lax.ppermute(block, SEQUENCE, [(i, i ^ 6) for i in range(8)]),
    ]
    return [array for first in straight for array in (first, swap(first, "shard", 1))]


def gather_rows(array):
    return lax.all_gather(array, SEQUENCE, axis=0, tiled=True)


def exchange(array, axes=SEQUENCE):
    return lax.all_to_all(array, axes, 0, 0, tiled=True)


def dot_tn(left, right):
    return lax.dot_general(left, right, (((0,), (0,)), ((), ())), preferred_element_type=f32)


def dot_nt(left, right):
    return lax.dot_general(left, right, NT, preferred_element_type=f32)


def dot_nn(left, right):
    return jnp.dot(left, right, preferred_element_type=f32)


def shift_dp(array, distance):
    return lax.ppermute(array, "dp", [(i, (i + distance) % 4) for i in range(4)])


def gather_shards(array):
    over_core = swap(array, "shard", 1)
    over_y = swap(array, "shard", 2)
    return [array, over_core, over_y, swap(over_y, "shard", 1)]


def sequence_shards(
    tokens,
    cotangent,
    picture_starts,
    matrices,
    vectors,
    master_matrices,
    master_vectors,
    first_matrices,
    first_vectors,
    second_matrices,
    second_vectors,
):
    row_count, width = tokens.shape
    ff_width = (matrices.shape[1] - 4 * width) // 2
    group = 8
    shard = lax.axis_index("shard")
    rank = lax.axis_index("ctx") * 4 + shard
    depth = lax.axis_index("dp")
    lanes = width // group
    units = ff_width // group
    own_rows = master_matrices.shape[0]
    seq = group * row_count
    head = rank * 2 + jnp.arange(2)
    slopes = jnp.exp2(-8.0 * (head.astype(f32) + 1.0) / HEADS)
    rank_array = rank.astype(jnp.int32).reshape(1)
    shard_array = shard.astype(jnp.int32).reshape(1)
    vector_rows = vectors.astype(f32)
    up_bias = vector_rows[8:].reshape(1, ff_width)

    with jax.named_scope("prepare"):
        pattern = key_pattern(picture_starts, slopes, seq, lanes)
    with jax.named_scope("gather_tokens"):
        ready = pattern[0, 0, lanes // 2 + 3] == 1.0
        passed, token_blocks = gather_blocks(tokens, ready)
    with jax.named_scope("gather_cotangent"):
        zero = passed[0, 0] * 0
        cotangent_late = cotangent + zero
        cotangent_all = gather_rows(cotangent_late)
    attended_heads, attended_wide, *saved, hidden_all = attention_forward(
        token_blocks,
        matrices,
        vectors,
        pattern,
        rank_array,
        picture_starts,
        slopes,
        cotangent_late,
    )
    with jax.named_scope("attended_exchange"):
        attended_got = exchange(attended_heads)
    with jax.named_scope("transpose_keys"):
        half = lanes // 2
        keys_low = saved[1]
        keys_transposed = jnp.concatenate(
            [keys_low[0, :, :half], keys_low[1, :, half:]], axis=1
        ).T
    middle, hidden_two = project_norm(
        attended_got, tokens, matrices, vectors, keys_transposed
    )
    with jax.named_scope("gather_attended"):
        head_blocks = gather_direct(attended_heads)
    layer_output, grad_mid, grad_out, sums_two = feed_forward(
        hidden_two, up_bias, middle, cotangent, vectors, matrices
    )
    with jax.named_scope("grad_attended_exchange"):
        grad_got = exchange(grad_out)
    early, unit_sums, attended_all = own_units(
        rank_array,
        token_blocks,
        head_blocks,
        cotangent_all,
        up_bias,
        matrices,
        vectors,
        [grad_out],
    )
    with jax.named_scope("grad_feed"):
        (early,) = gate([early], [grad_got])
        early_sum = lax.psum_scatter(early, "dp", scatter_dimension=0, tiled=True)
    grad_abs, grad_flipped, bias_sums, mid_flipped = attention_backward(
        (*saved, keys_transposed), attended_wide, grad_got, picture_starts, [early]
    )
    with jax.named_scope("grad_qkv_exchange"):
        grad_tokens = exchange(grad_abs.reshape(group, row_count, 3 * lanes))
    with jax.named_scope("grad_late"):
        near_far, near, relay, late_own = late_weights(
            depth.astype(jnp.int32).reshape(1), grad_flipped, hidden_all, mid_flipped, attended_all.reshape(seq, width)
        )
        beside = [(i, i ^ 1) for i in range(4)]
        relay = (relay + lax.ppermute(near_far, "dp", beside).astype(f32)).astype(bf16)
        near = lax.ppermute(near, "dp", beside)
        far = lax.ppermute(relay, "dp", [(i, 3 - i) for i in range(4)])
    with jax.named_scope("early_rows"):
        (early_sum,) = gate([early_sum], [grad_tokens, relay])
        early_got = exchange(early_sum.reshape(group, own_rows, 2 * units))
    token_grads, sums_one = token_gradient(
        grad_tokens, matrices, tokens, grad_mid, vectors, [early_sum]
    )
    with jax.named_scope("late_rows"):
        late_sum = flip_sum([late_own, near, far], [early_got, sums_one], "late_rows")
        late_got = exchange(late_sum.reshape(group, own_rows, 4 * lanes))
    root = (row_count * lax.axis_size("dp") * group) ** (-0.5)
    matrix_states = (master_matrices, first_matrices, second_matrices)
    *early_states, early_copy = matrix_update(
        early_got, matrix_states, (), [late_got], 4 * width, 2, root, "early_update"
    )
    with jax.named_scope("early_copies"):
        early_copied = gather_shards(early_copy)
    moment_w, variance_w, updated_w, late_copy = matrix_update(
        late_got,
        matrix_states,
        early_states,
        [],
        0,
        4,
        root,
        "late_update",
    )
    with jax.named_scope("grad_vectors"):
        vector_states = (master_vectors, first_vectors, second_vectors)
        pieces = vector_pieces(
            rank_array, sums_one, bias_sums, sums_two, unit_sums, vector_states, 32, [late_copy]
        )
        vectors_got = exchange(pieces, EVERY)
    with jax.named_scope("late_copies"):
        late_copied = gather_shards(late_copy)
    copied_w = place_copies(shard_array, late_copied, early_copied)
    moment_v, variance_v, updated_v, copied_v = vector_update(
        (depth * group + rank).astype(jnp.int32).reshape(1),
        vectors_got,
        *master_vectors.shape,
        root,
        [early_copied[3]],
    )
    return (
        layer_output,
        token_grads,
        moment_w,
        moment_v,
        variance_w,
        variance_v,
        updated_w,
        updated_v,
        copied_w,
        copied_v,
    )


def solution(mesh):
    in_specs = (
        P(("dp", "ctx", "shard"), None),
        P(("dp", "ctx", "shard"), None),
        P("dp", None),
        P(),
        P(),
        P(("dp", "ctx", "shard"), None),
        P(None, ("dp", "ctx", "shard")),
        P(("dp", "ctx", "shard"), None),
        P(None, ("dp", "ctx", "shard")),
        P(("dp", "ctx", "shard"), None),
        P(None, ("dp", "ctx", "shard")),
    )
    out_specs = (
        P(("dp", "ctx", "shard"), None),
        P(("dp", "ctx", "shard"), None),
        P(("dp", "ctx", "shard"), None),
        P(None, ("dp", "ctx", "shard")),
        P(("dp", "ctx", "shard"), None),
        P(None, ("dp", "ctx", "shard")),
        P(("dp", "ctx", "shard"), None),
        P(None, ("dp", "ctx", "shard")),
        P(("dp", "ctx"), None),
        P(None, ("dp", "ctx")),
    )
    body = sequence_shards if fits_sequence_plan(mesh) else general_shards
    return jax.shard_map(body, mesh=mesh, in_specs=in_specs, out_specs=out_specs, check_vma=False)
```
